32 devices in a mesh: groups: 2 (over y), cell: 4 (over z), gene: 2 (over x), sub: 2 (over core).
Axes of the slice: x: 2, y: 2, z: 4, core: 2. Of those that a mesh axis runs over, the one named last changes fastest.
Arguments:
- counts_x: bfloat16 [8192, 32768], P(('groups', 'cell'), ('gene', 'sub')), parts along dimension 0, may hold values from 0 to 4, as said below
- tile_mask: int32 [32, 128], P(('groups', 'cell'), ('gene', 'sub')), parts along dimension 0, may hold values from 0 to 1, as said below
- tile_counts: int32 [32, 128], P(('groups', 'cell'), ('gene', 'sub')), parts along dimension 0, may hold values from 1 to 4
- gene_factor: bfloat16 [512, 32768], P('groups', ('gene', 'sub')), parts along dimension 0, as said below
- prev_factor: bfloat16 [8192, 256], P(('groups', 'cell')), parts along dimension 0, may hold values from 0 to 2, as said below
Outputs:
- new_factor: bfloat16 [8192, 256], P(('groups', 'cell')), parts along dimension 0
- factor_gram: float32 [512, 256], P('groups'), parts along dimension 0
- data_products: float32 [65536, 256], P(('groups', 'gene', 'sub', 'cell')), parts along dimension 0
The draws below stay inside these ranges and needn't reach their ends.
There are 2 independent parts, one for each index of `groups`. The reference program is written for one: setup_inputs(seed, part) draws one part's arguments, and reference() takes and returns one part's arrays. A program takes and returns all parts, laid end to end along the dimension named above; each array names one. Nothing has to cross between parts.
Inputs may be any that keep to these rules, and one draw needn't show every extreme that they name: `tile_mask`: 1 marks a stored tile, 0 an empty one. `gene_factor`: nonnegative. `counts_x`: nonnegative. `prev_factor`: nonnegative.
All inputs are finite; a program needn't handle non-finite values.
Results may differ from the reference program's by a relative error of at most 0.008.
Values may be sent and summed in bfloat16 or wider, within the bound.
No kernel may reach another device: no remote copies, remote signals or barrier semaphores. Data moves between devices by JAX's collectives and lax.ppermute only.
A program may use at most 192 MiB of HBM per device.

```python
import jax
import jax.numpy as jnp
from jax import lax

TILE = 256
K = 256
GENES = 32768
ITERS = 3
CELLS = 4096


def draw_counts_x(key, part):
    key = jax.random.fold_in(key, 5)
    first, second = jax.random.split(key, 2)
    present = (jax.random.randint(first, (CELLS, GENES), 0, 100) < 2).astype(jnp.float32)
    values = jax.random.uniform(second, (CELLS, GENES), jnp.float32, 0.0, 4.0)
    return (present * values).astype(jnp.bfloat16)


def draw_tile_mask(key, part):
    key = jax.random.fold_in(key, 11)
    first, second = jax.random.split(key)
    density = jax.random.randint(first, (CELLS // TILE, 1), 1, 5)
    pick = jax.random.randint(second, (CELLS // TILE, GENES // TILE), 0, 4)
    return (pick < density).astype(jnp.int32)


def draw_gene_factor(key, part):
    key = jax.random.fold_in(key, 23)
    first, second, third, fourth, fifth = jax.random.split(key, 5)
    spread = 0.2 / GENES ** 0.5
    own = jax.random.uniform(first, (K, GENES), jnp.float32)
    own = own * jax.random.randint(second, (K, GENES), 0, 2).astype(jnp.float32)
    shared = jax.random.uniform(third, (8, GENES), jnp.float32)
    shared = shared * jax.random.randint(fourth, (8, GENES), 0, 2).astype(jnp.float32)
    member = jax.random.randint(fifth, (K,), 0, 8)
    values = (own + 1.5 * jnp.take(shared, member, axis=0)) * spread
    return values.astype(jnp.bfloat16)


def draw_prev_factor(key, part):
    key = jax.random.fold_in(key, 31)
    first, second = jax.random.split(key)
    values = jax.random.uniform(first, (CELLS, K), jnp.float32, 0.0, 2.0)
    present = jax.random.randint(second, (CELLS, K), 0, 2).astype(jnp.float32)
    return (values * present).astype(jnp.bfloat16)


def with_ends(array, stream_key, low, largest):
    index_at = [jax.random.randint(jax.random.fold_in(stream_key, axis), (), 0, length) for axis, length in enumerate(array.shape)]
    main_axis = array.shape.index(max(array.shape))
    beside = index_at[:main_axis] + [(index_at[main_axis] + 1) % array.shape[main_axis]] + index_at[main_axis + 1:]
    return array.at[tuple(index_at)].set(low).at[tuple(beside)].set(largest)


def setup_inputs(seed: int = 0, part: int = 0) -> dict:
    key_of = jax.random.split(jax.random.key(seed), 6)
    part_splits = jax.random.split(jax.random.fold_in(key_of[5], part), 6)
    return {
        "counts_x": draw_counts_x(jax.random.fold_in(jax.random.fold_in(key_of[5], part), 71), part),
        "tile_mask": draw_tile_mask(jax.random.fold_in(jax.random.fold_in(key_of[5], part), 71), part),
        "tile_counts": with_ends(jax.random.randint(part_splits[2], (CELLS // TILE, GENES // TILE), 1, 5), jax.random.fold_in(part_splits[2], 1), 1, 4).astype(jnp.int32),
        "gene_factor": draw_gene_factor(jax.random.fold_in(jax.random.fold_in(key_of[5], part), 71), part),
        "prev_factor": draw_prev_factor(jax.random.fold_in(jax.random.fold_in(key_of[5], part), 71), part),
    }


def scale_rows(block, factor_row):
    shaped = block.astype(jnp.float32).reshape(TILE, GENES // TILE, TILE)
    return (shaped * factor_row[None, :, None]).reshape(TILE, GENES).astype(jnp.bfloat16)

def reference(counts_x, tile_mask, tile_counts, gene_factor, prev_factor):
    factor = tile_mask.astype(jnp.float32) / tile_counts.astype(jnp.float32)
    blocks = counts_x.reshape(CELLS // TILE, TILE, GENES)
    scaled = lax.map(lambda pair: scale_rows(pair[0], pair[1]), (blocks, factor)).reshape(CELLS, GENES)
    gram = lax.dot_general(gene_factor.astype(jnp.float32), gene_factor.astype(jnp.float32), (((1,), (1,)), ((), ())), preferred_element_type=jnp.float32)
    rho = jnp.trace(gram) / K
    eye = jnp.eye(K, dtype=jnp.float32)
    lower = jnp.linalg.cholesky(gram + rho * eye)
    inverse = jax.scipy.linalg.cho_solve((lower, True), eye)
    cross = lax.dot_general(scaled.astype(jnp.float32), gene_factor.astype(jnp.float32), (((1,), (1,)), ((), ())), preferred_element_type=jnp.float32)
    zvalue = prev_factor.astype(jnp.float32)
    uvalue = jnp.zeros_like(zvalue)
    for step in range(ITERS):
        vvalue = jnp.dot(cross + rho * (zvalue - uvalue), inverse, precision=lax.Precision.HIGHEST)
        zvalue = jnp.maximum(vvalue + uvalue, 0.0)
        uvalue = uvalue + vvalue - zvalue
    new_factor = zvalue.astype(jnp.bfloat16)
    factor_gram = lax.dot_general(new_factor.astype(jnp.float32), new_factor.astype(jnp.float32), (((0,), (0,)), ((), ())), preferred_element_type=jnp.float32)
    data_products = lax.dot_general(scaled.astype(jnp.float32), new_factor.astype(jnp.float32), (((0,), (0,)), ((), ())), preferred_element_type=jnp.float32)
    return (new_factor, factor_gram, data_products)
```

```python
import functools

import jax
import jax.numpy as jnp
from jax import lax
from jax.experimental import pallas as pl
from jax.experimental.pallas import tpu as pltpu
from jax.sharding import PartitionSpec as P

ITERS = 3
F32 = jnp.float32
BF16 = jnp.bfloat16
VMEM_LIMIT = 48 * 1024 * 1024


def params():
    return pltpu.CompilerParams(vmem_limit_bytes=VMEM_LIMIT)


def cost(flops, bytes_accessed):
    return pl.CostEstimate(flops=flops, bytes_accessed=bytes_accessed, transcendentals=0)


def contract_last(left, right):
    return lax.dot_general(
        left, right, (((1,), (1,)), ((), ())), preferred_element_type=F32
    )


def cross_kernel(tile, meta, factor, counts, genes, theirs, mine, total):
    step = pl.program_id(0)
    row_tiles = counts.shape[0] // tile
    gene_tiles = counts.shape[1] // tile
    half = counts.shape[0] // 2
    for row in range(row_tiles):
        rows = pl.ds(row * tile, tile)
        parts = [
            (
                counts[rows, pl.ds(col * tile, tile)].astype(F32)
                * factor[row, step * gene_tiles + col]
            ).astype(BF16)
            for col in range(gene_tiles)
        ]
        part = contract_last(jnp.concatenate(parts, axis=1), genes[...])

        @pl.when(step == 0)
        def _(rows=rows, part=part):
            total[rows, :] = part

        @pl.when(step > 0)
        def _(rows=rows, part=part):
            total[rows, :] += part

    @pl.when(step == pl.num_programs(0) - 1)
    def _():
        sub = meta[0]
        mine[...] = total[pl.ds(pl.multiple_of(sub * half, half), half), :]
        theirs[...] = total[pl.ds(pl.multiple_of((1 - sub) * half, half), half), :]


def cross_parts(meta, factor, counts, genes, tile):
    rows, columns = counts.shape
    width = genes.shape[0]
    wide = min(1024, columns)
    half = jax.ShapeDtypeStruct((rows // 2, width), F32)
    return pl.pallas_call(
        functools.partial(cross_kernel, tile),
        out_shape=(half, half),
        grid_spec=pltpu.PrefetchScalarGridSpec(
            num_scalar_prefetch=1,
            grid=(columns // wide,),
            in_specs=[
                pl.BlockSpec(memory_space=pltpu.SMEM),
                pl.BlockSpec((rows, wide), lambda i, m: (0, i)),
                pl.BlockSpec((width, wide), lambda i, m: (0, i)),
            ],
            out_specs=(
                pl.BlockSpec((rows // 2, width), lambda i, m: (0, 0)),
                pl.BlockSpec((rows // 2, width), lambda i, m: (0, 0)),
            ),
            scratch_shapes=[pltpu.VMEM((rows, width), F32)],
        ),
        compiler_params=params(),
        cost_estimate=cost(2 * rows * columns * width, 2 * rows * columns),
        name="cross",
    )(meta, factor, counts, genes)


def halves(value):
    high = value.astype(BF16)
    return high, (value - high.astype(F32)).astype(BF16)


def product3(left, right):
    left_high, left_low = left
    right_high, right_low = right
    dot = functools.partial(jnp.dot, preferred_element_type=F32)
    return dot(left_high, right_high) + (
        dot(left_high, right_low) + dot(left_low, right_high)
    )


def inverse_kernel(gram_a, gram_b, inverse, rho_out):
    gram = gram_a[...] + gram_b[...]
    width = gram.shape[0]
    shape = (width, width)
    diagonal = lax.broadcasted_iota(jnp.int32, shape, 0) == lax.broadcasted_iota(
        jnp.int32, shape, 1
    )
    eye = jnp.where(diagonal, 1.0, 0.0).astype(F32)
    rho = jnp.sum(gram * eye) / width
    rho_out[0, 0] = rho
    scale = 1.0 / jnp.full((1, 1), rho, F32)
    matrix = gram * scale + eye
    low = 2.0 / (width + 2.0)
    guess = low * eye
    image = low * matrix
    first = True
    while True:
        low = low * (2.0 - low)
        gain = 2.0 / (1.0 + low)
        low = gain * low
        done = 1.0 - low < 2e-3
        step = halves(gain * (2.0 * eye - image))
        if first:
            guess = guess[0:1, 0:1] * (gain * (2.0 * eye - image))
        else:
            guess = product3(halves(guess), step)
        first = False
        if done:
            break
        image = product3(halves(image), step)
    rest = eye - jnp.dot(
        matrix, guess, preferred_element_type=F32, precision=lax.Precision.HIGHEST
    )
    rest_halves = halves(rest)
    series = rest + product3(rest_halves, rest_halves)
    inverse[...] = (guess + product3(halves(guess), halves(series))) * scale


def shifted_inverse(gram_a, gram_b):
    width = gram_a.shape[0]
    whole = pl.BlockSpec(memory_space=pltpu.VMEM)
    return pl.pallas_call(
        inverse_kernel,
        out_shape=(
            jax.ShapeDtypeStruct((width, width), F32),
            jax.ShapeDtypeStruct((1, 1), F32),
        ),
        in_specs=[whole, whole],
        out_specs=(whole, pl.BlockSpec(memory_space=pltpu.SMEM)),
        compiler_params=params(),
        cost_estimate=cost(2 * 60 * width**3, 12 * width**2),
        name="inverse",
    )(gram_a, gram_b)


def admm_kernel(meta, rho_ref, cross_a, cross_b, inverse, start, rows_out, columns_out):
    rho = rho_ref[0, 0]
    cross = cross_a[...] + cross_b[...]
    inverse_halves = halves(inverse[...])
    zvalue = start[...].astype(F32)
    uvalue = jnp.zeros_like(zvalue)
    for _ in range(ITERS):
        vvalue = product3(halves(cross + rho * (zvalue - uvalue)), inverse_halves)
        zvalue = jnp.maximum(vvalue + uvalue, 0.0)
        uvalue = uvalue + vvalue - zvalue
    rows_out[...] = zvalue.astype(BF16)
    columns_out[...] = zvalue.T.astype(BF16)


def admm(meta, rho, cross_a, cross_b, inverse, start):
    rows, width = cross_a.shape
    tall = lambda: pl.BlockSpec((rows, width), lambda i, m: (0, 0))
    return pl.pallas_call(
        admm_kernel,
        out_shape=(
            jax.ShapeDtypeStruct((rows, width), BF16),
            jax.ShapeDtypeStruct((width, rows), BF16),
        ),
        grid_spec=pltpu.PrefetchScalarGridSpec(
            num_scalar_prefetch=1,
            grid=(1,),
            in_specs=[
                pl.BlockSpec(memory_space=pltpu.SMEM),
                tall(),
                tall(),
                pl.BlockSpec((width, width), lambda i, m: (0, 0)),
                pl.BlockSpec((rows, width), lambda i, m: (m[0], 0)),
            ],
            out_specs=(
                tall(),
                pl.BlockSpec((width, rows), lambda i, m: (0, 0)),
            ),
        ),
        compiler_params=params(),
        cost_estimate=cost(2 * 9 * rows * width**2, 12 * rows * width),
        name="admm",
    )(meta, rho, cross_a, cross_b, inverse, start)


def chunk_product(tile, gene, meta, factor, counts, own, other):
    half = counts.shape[0] // 2
    sub = meta[0]
    column = gene // tile
    total = None
    for first, left in ((sub, own), (1 - sub, other)):
        parts = [
            (
                counts[pl.ds(pl.multiple_of(first * half + r * tile, tile), tile), :].astype(F32)
                * factor[first * (half // tile) + r, column]
            ).astype(BF16)
            for r in range(half // tile)
        ]
        part = jnp.dot(
            left[...], jnp.concatenate(parts, axis=0), preferred_element_type=F32
        )
        total = part if total is None else total + part
    return total


class Plan:
    def __init__(self, cells, columns, tile):
        self.cells = cells
        self.block = columns // cells
        self.chunks = 2 if self.block % (4 * tile) == 0 else 1
        self.chunk = self.block // self.chunks
        self.wide = min(tile, self.chunk)
        self.steps = self.chunk // self.wide

    def valid(self, shift, meta):
        target = meta[1] + shift
        return jnp.logical_and(target >= 0, target < self.cells)

    def place(self, shift, chunk, step, meta):
        target = lax.rem(meta[1] + shift + self.cells, self.cells)
        place = target * (self.block // self.wide) + chunk * self.steps + step
        return jnp.where(self.valid(shift, meta), place, 0)


def send_kernel(plan, tile, shift, chunk, with_arrived, meta, factor, counts, own, other, *refs):
    out = refs[-1]

    @pl.when(plan.valid(shift, meta))
    def _():
        gene = plan.place(shift, chunk, pl.program_id(0), meta) * plan.wide
        total = chunk_product(tile, gene, meta, factor, counts, own, other)
        if with_arrived:
            total = total + refs[0][...].astype(F32)
        out[...] = total.astype(BF16)


def send_chunk(plan, tile, shift, chunk, meta, factor, counts, own, other, arrived):
    rows = counts.shape[0]
    width = own.shape[0]
    wide = plan.wide
    halved = lambda: pl.BlockSpec((width, rows // 2), lambda i, m: (0, 0))
    piece = lambda: pl.BlockSpec((width, wide), lambda i, m: (0, i))
    extra = [] if arrived is None else [arrived]
    return pl.pallas_call(
        functools.partial(send_kernel, plan, tile, shift, chunk, arrived is not None),
        out_shape=jax.ShapeDtypeStruct((width, plan.chunk), BF16),
        grid_spec=pltpu.PrefetchScalarGridSpec(
            num_scalar_prefetch=1,
            grid=(plan.steps,),
            in_specs=[
                pl.BlockSpec(memory_space=pltpu.SMEM),
                pl.BlockSpec(
                    (rows, wide), lambda i, m: (0, plan.place(shift, chunk, i, m))
                ),
                halved(),
                halved(),
            ]
            + [piece() for _ in extra],
            out_specs=piece(),
        ),
        compiler_params=params(),
        cost_estimate=cost(2 * rows * width * plan.chunk, 2 * rows * plan.chunk),
        name="products_send",
    )(meta, factor, counts, own, other, *extra)


def keep_kernel(plan, tile, chunk, meta, factor, counts, own, other, from_left, from_right, *refs):
    gene = plan.place(0, chunk, pl.program_id(0), meta) * plan.wide
    total = chunk_product(tile, gene, meta, factor, counts, own, other)
    total = total + (from_left[...].astype(F32) + from_right[...].astype(F32))
    refs[-1][...] = total.T


def keep_chunk(plan, tile, chunk, meta, factor, counts, own, other, from_left, from_right, out):
    rows = counts.shape[0]
    width = own.shape[0]
    wide = plan.wide
    halved = lambda: pl.BlockSpec((width, rows // 2), lambda i, m: (0, 0))
    piece = lambda: pl.BlockSpec((width, wide), lambda i, m: (0, i))
    extra = [] if out is None else [out]
    return pl.pallas_call(
        functools.partial(keep_kernel, plan, tile, chunk),
        out_shape=jax.ShapeDtypeStruct((plan.block, width), F32),
        grid_spec=pltpu.PrefetchScalarGridSpec(
            num_scalar_prefetch=1,
            grid=(plan.steps,),
            in_specs=[
                pl.BlockSpec(memory_space=pltpu.SMEM),
                pl.BlockSpec(
                    (rows, wide), lambda i, m: (0, plan.place(0, chunk, i, m))
                ),
                halved(),
                halved(),
                piece(),
                piece(),
            ]
            + [pl.BlockSpec(memory_space=pl.ANY) for _ in extra],
            out_specs=pl.BlockSpec((wide, width), lambda i, m: (chunk * plan.steps + i, 0)),
        ),
        input_output_aliases={7: 0} if extra else {},
        compiler_params=params(),
        cost_estimate=cost(2 * rows * width * plan.chunk, 2 * rows * plan.chunk),
        name="products_keep",
    )(meta, factor, counts, own, other, from_left, from_right, *extra)


def swap(value, axis, size, step):
    return lax.ppermute(value, axis, [(i, i ^ step) for i in range(size)])


def pair_sums(value, axis, size, last):
    step = 1
    while step < size:
        arrived = swap(value, axis, size, step)
        step *= 2
        if step >= size and not last:
            return value, arrived
        value = value + arrived
    return value


def shards(sizes, counts, tile_mask, tile_counts, gene_factor, prev_factor):
    cells, genes, subs = sizes
    rows, columns = counts.shape
    width = gene_factor.shape[0]
    tile = rows // tile_mask.shape[0]
    sub = lax.axis_index("sub")
    cell = lax.axis_index("cell")
    meta = jnp.stack([sub, cell]).astype(jnp.int32)
    factor = tile_mask.astype(F32) / tile_counts.astype(F32)

    gram = contract_last(gene_factor, gene_factor)
    gram = pair_sums(gram, "sub", subs, True)
    gram_a, gram_b = pair_sums(gram, "gene", genes, False)
    theirs, mine = cross_parts(meta, factor, counts, gene_factor, tile)
    cross = mine + swap(theirs, "sub", subs, 1)
    cross_a, cross_b = pair_sums(cross, "gene", genes, False)
    inverse, rho = shifted_inverse(gram_a, gram_b)
    own_rows, own = admm(meta, rho, cross_a, cross_b, inverse, prev_factor)
    other = swap(own, "sub", subs, 1)

    plan = Plan(cells, columns, tile)
    rightward = [(i, i + 1) for i in range(cells - 1)]
    leftward = [(i + 1, i) for i in range(cells - 1)]
    from_left = [None] * plan.chunks
    from_right = [None] * plan.chunks
    for phase in range(1, cells):
        for chunk in range(plan.chunks):
            right = send_chunk(
                plan, tile, cells - phase, chunk, meta, factor, counts, own, other, from_left[chunk]
            )
            left = send_chunk(
                plan, tile, phase - cells, chunk, meta, factor, counts, own, other, from_right[chunk]
            )
            pairs = [pair for pair in rightward if pair[0] < phase]
            from_left[chunk] = lax.ppermute(right, "cell", pairs)
            pairs = [pair for pair in leftward if pair[0] >= cells - phase]
            from_right[chunk] = lax.ppermute(left, "cell", pairs)
    data_products = None
    for chunk in range(plan.chunks):
        data_products = keep_chunk(
            plan, tile, chunk, meta, factor, counts, own, other,
            from_left[chunk], from_right[chunk], data_products,
        )

    other_rows = swap(own_rows, "sub", subs, 1)
    new_factor = jnp.where(
        sub == 0,
        jnp.concatenate([own_rows, other_rows], axis=0),
        jnp.concatenate([other_rows, own_rows], axis=0),
    )
    share = width // (genes * subs)
    first = (lax.axis_index("gene") * subs + sub) * share
    gram_rows = contract_last(lax.dynamic_slice_in_dim(own, first, share, 0), own)
    gram_rows += contract_last(lax.dynamic_slice_in_dim(other, first, share, 0), other)
    gram_rows = pair_sums(gram_rows, "cell", cells, True)
    factor_gram = lax.all_gather(gram_rows, ("gene", "sub"), axis=0, tiled=True)
    return (new_factor, factor_gram, data_products)


def solution(mesh):
    sizes = (mesh.shape["cell"], mesh.shape["gene"], mesh.shape["sub"])
    return jax.shard_map(
        functools.partial(shards, sizes),
        mesh=mesh,
        in_specs=(
            P(("groups", "cell"), ("gene", "sub")),
            P(("groups", "cell"), ("gene", "sub")),
            P(("groups", "cell"), ("gene", "sub")),
            P("groups", ("gene", "sub")),
            P(("groups", "cell"), None),
        ),
        out_specs=(
            P(("groups", "cell"), None),
            P("groups", None),
            P(("groups", "gene", "sub", "cell"), None),
        ),
        check_vma=False,
    )
```

```python
import functools

import jax
import jax.numpy as jnp
from jax import lax
from jax.experimental import pallas as pl
from jax.experimental.pallas import tpu as pltpu
from jax.sharding import PartitionSpec as P

ITERS = 3
F32 = jnp.float32
BF16 = jnp.bfloat16
MIB = 1024 * 1024


def params(limit=48):
    return pltpu.CompilerParams(vmem_limit_bytes=limit * MIB)


def cost(flops, bytes_accessed):
    return pl.CostEstimate(flops=flops, bytes_accessed=bytes_accessed, transcendentals=0)


def contract_last(left, right):
    return lax.dot_general(
        left, right, (((1,), (1,)), ((), ())), preferred_element_type=F32
    )


def gram_kernel(genes, tile_mask, tile_counts, gram, turned, factor):
    step = pl.program_id(0)
    turned[...] = genes[...].T
    part = jnp.dot(genes[...], turned[...], preferred_element_type=F32)

    @pl.when(step == 0)
    def _():
        gram[...] = part
        factor[...] = tile_mask[...].astype(F32) / tile_counts[...].astype(F32)

    @pl.when(step > 0)
    def _():
        gram[...] += part


def gram_parts(genes, tile_mask, tile_counts):
    width, columns = genes.shape
    wide = min(1024, columns)
    tiles = pl.BlockSpec(tile_mask.shape, lambda i: (0, 0))
    return pl.pallas_call(
        gram_kernel,
        out_shape=(
            jax.ShapeDtypeStruct((width, width), F32),
            jax.ShapeDtypeStruct((columns, width), BF16),
            jax.ShapeDtypeStruct(tile_mask.shape, F32),
        ),
        grid=(columns // wide,),
        in_specs=[pl.BlockSpec((width, wide), lambda i: (0, i)), tiles, tiles],
        out_specs=(
            pl.BlockSpec((width, width), lambda i: (0, 0)),
            pl.BlockSpec((wide, width), lambda i: (i, 0)),
            tiles,
        ),
        compiler_params=params(60),
        cost_estimate=cost(2 * width * width * columns, 4 * width * columns),
        name="gram",
    )(genes, tile_mask, tile_counts)


def cross_kernel(tile, meta, factor, counts, turned, theirs, mine, total, scaled):
    step = pl.program_id(0)
    row_tiles = counts.shape[0] // tile
    gene_tiles = counts.shape[1] // tile
    half = counts.shape[0] // 2
    for row in range(row_tiles):
        for col in range(gene_tiles):
            at = (pl.ds(row * tile, tile), pl.ds(col * tile, tile))
            scale = factor[row, step * gene_tiles + col]
            scaled[at] = (counts[at].astype(F32) * scale).astype(BF16)
    part = jnp.dot(scaled[...], turned[...], preferred_element_type=F32)

    @pl.when(step == 0)
    def _():
        total[...] = part

    @pl.when(step > 0)
    def _():
        total[...] += part

    @pl.when(step == pl.num_programs(0) - 1)
    def _():
        sub = meta[0]
        mine[...] = total[pl.ds(pl.multiple_of(sub * half, half), half), :]
        theirs[...] = total[pl.ds(pl.multiple_of((1 - sub) * half, half), half), :]


def cross_parts(meta, factor, counts, turned, tile):
    rows, columns = counts.shape
    width = turned.shape[1]
    wide = min(1024, columns)
    half = jax.ShapeDtypeStruct((rows // 2, width), F32)
    return pl.pallas_call(
        functools.partial(cross_kernel, tile),
        out_shape=(half, half),
        grid_spec=pltpu.PrefetchScalarGridSpec(
            num_scalar_prefetch=1,
            grid=(columns // wide,),
            in_specs=[
                pl.BlockSpec(memory_space=pltpu.SMEM),
                pl.BlockSpec((rows, wide), lambda i, m: (0, i)),
                pl.BlockSpec((wide, width), lambda i, m: (i, 0)),
            ],
            out_specs=(
                pl.BlockSpec((rows // 2, width), lambda i, m: (0, 0)),
                pl.BlockSpec((rows // 2, width), lambda i, m: (0, 0)),
            ),
            scratch_shapes=[
                pltpu.VMEM((rows, width), F32),
                pltpu.VMEM((rows, wide), BF16),
            ],
        ),
        compiler_params=params(60),
        cost_estimate=cost(2 * rows * columns * width, 2 * rows * columns),
        name="cross",
    )(meta, factor, counts, turned)


def halves(value):
    high = value.astype(BF16)
    return high, (value - high.astype(F32)).astype(BF16)


def product3(left, right):
    left_high, left_low = left
    right_high, right_low = right
    dot = functools.partial(jnp.dot, preferred_element_type=F32)
    return dot(left_high, right_high) + (
        dot(left_high, right_low) + dot(left_low, right_high)
    )


def inverse_kernel(gram_a, gram_b, inverse, rho_out):
    gram = gram_a[...] + gram_b[...]
    width = gram.shape[0]
    shape = (width, width)
    diagonal = lax.broadcasted_iota(jnp.int32, shape, 0) == lax.broadcasted_iota(
        jnp.int32, shape, 1
    )
    eye = jnp.where(diagonal, 1.0, 0.0).astype(F32)
    rho = jnp.sum(gram * eye) / width
    rho_out[0, 0] = rho
    scale = 1.0 / jnp.full((1, 1), rho, F32)
    matrix = gram * scale + eye
    low = 2.0 / (width + 2.0)
    guess = low * eye
    image = low * matrix
    first = True
    while True:
        low = low * (2.0 - low)
        gain = 2.0 / (1.0 + low)
        low = gain * low
        done = 1.0 - low < 2e-3
        step = halves(gain * (2.0 * eye - image))
        if first:
            guess = guess[0:1, 0:1] * (gain * (2.0 * eye - image))
        else:
            guess = product3(halves(guess), step)
        first = False
        if done:
            break
        image = product3(halves(image), step)
    rest = eye - jnp.dot(
        matrix, guess, preferred_element_type=F32, precision=lax.Precision.HIGHEST
    )
    rest_halves = halves(rest)
    series = rest + product3(rest_halves, rest_halves)
    inverse[...] = (guess + product3(halves(guess), halves(series))) * scale


def shifted_inverse(gram_a, gram_b):
    width = gram_a.shape[0]
    whole = pl.BlockSpec(memory_space=pltpu.VMEM)
    return pl.pallas_call(
        inverse_kernel,
        out_shape=(
            jax.ShapeDtypeStruct((width, width), F32),
            jax.ShapeDtypeStruct((1, 1), F32),
        ),
        in_specs=[whole, whole],
        out_specs=(whole, pl.BlockSpec(memory_space=pltpu.SMEM)),
        compiler_params=params(),
        cost_estimate=cost(2 * 60 * width**3, 12 * width**2),
        name="inverse",
    )(gram_a, gram_b)


def admm_kernel(meta, rho_ref, cross_a, cross_b, inverse, start, columns_out):
    rho = rho_ref[0, 0]
    cross = cross_a[...] + cross_b[...]
    inverse_halves = halves(inverse[...])
    zvalue = start[...].astype(F32)
    uvalue = jnp.zeros_like(zvalue)
    for _ in range(ITERS):
        vvalue = product3(halves(cross + rho * (zvalue - uvalue)), inverse_halves)
        zvalue = jnp.maximum(vvalue + uvalue, 0.0)
        uvalue = uvalue + vvalue - zvalue
    columns_out[...] = zvalue.T.astype(BF16)


def admm(meta, rho, cross_a, cross_b, inverse, start):
    rows, width = cross_a.shape
    tall = lambda: pl.BlockSpec((rows, width), lambda i, m: (0, 0))
    return pl.pallas_call(
        admm_kernel,
        out_shape=jax.ShapeDtypeStruct((width, rows), BF16),
        grid_spec=pltpu.PrefetchScalarGridSpec(
            num_scalar_prefetch=1,
            grid=(1,),
            in_specs=[
                pl.BlockSpec(memory_space=pltpu.SMEM),
                tall(),
                tall(),
                pl.BlockSpec((width, width), lambda i, m: (0, 0)),
                pl.BlockSpec((rows, width), lambda i, m: (m[2], 0)),
            ],
            out_specs=pl.BlockSpec((width, rows), lambda i, m: (0, 0)),
        ),
        compiler_params=params(),
        cost_estimate=cost(2 * 9 * rows * width**2, 12 * rows * width),
        name="admm",
    )(meta, rho, cross_a, cross_b, inverse, start)


def chunk_product(tile, gene, meta, factor, counts, own, other):
    half = counts.shape[0] // 2
    sub = meta[0]
    column = gene // tile
    total = None
    for first, left in ((sub, own), (1 - sub, other)):
        parts = [
            (
                counts[pl.ds(pl.multiple_of(first * half + r * tile, tile), tile), :].astype(F32)
                * factor[first * (half // tile) + r, column]
            ).astype(BF16)
            for r in range(half // tile)
        ]
        part = jnp.dot(
            left[...], jnp.concatenate(parts, axis=0), preferred_element_type=F32
        )
        total = part if total is None else total + part
    return total


def products_kernel(tile, wide, place, meta, factor, counts, own, other, out):
    gene = place(pl.program_id(0), pl.program_id(1)) * wide
    total = chunk_product(tile, gene, meta, factor, counts, own, other)
    out[...] = total.astype(BF16).reshape(out.shape)


def products(cells, chunks, chunk, tile, meta, factor, counts, own, other):
    rows, columns = counts.shape
    width = own.shape[0]
    block = columns // cells
    part = block // chunks
    wide = min(tile, part)
    place = lambda o, i: o * (block // wide) + chunk * (part // wide) + i
    halved = lambda: pl.BlockSpec((width, rows // 2), lambda o, i, m: (0, 0))
    return pl.pallas_call(
        functools.partial(products_kernel, tile, wide, place),
        out_shape=jax.ShapeDtypeStruct((cells, width, part), BF16),
        grid_spec=pltpu.PrefetchScalarGridSpec(
            num_scalar_prefetch=1,
            grid=(cells, part // wide),
            in_specs=[
                pl.BlockSpec(memory_space=pltpu.SMEM),
                pl.BlockSpec((rows, wide), lambda o, i, m: (0, place(o, i))),
                halved(),
                halved(),
            ],
            out_specs=pl.BlockSpec((1, width, wide), lambda o, i, m: (o, 0, i)),
        ),
        compiler_params=params(),
        cost_estimate=cost(2 * rows * width * part * cells, 2 * rows * part * cells),
        name="products",
    )(meta, factor, counts, own, other)


def swap(value, axis, size, step):
    return lax.ppermute(value, axis, [(i, i ^ step) for i in range(size)])


def pair_sums(value, axis, size):
    step = 1
    while step < size:
        value = value + swap(value, axis, size, step)
        step *= 2
    return value


def split_sums(value, axis, size):
    index = lax.axis_index(axis)
    step = size // 2
    while True:
        upper = (index // step) % 2 == 1
        low, high = jnp.split(value, 2, axis=0)
        kept = jnp.where(upper, high, low)
        arrived = swap(jnp.where(upper, low, high), axis, size, step)
        step //= 2
        if step == 0:
            return kept, arrived
        value = kept + arrived


def join_columns(value, axis, size):
    index = lax.axis_index(axis)
    step = 1
    while step < size:
        arrived = swap(value, axis, size, step)
        value = jnp.where(
            (index // step) % 2 == 0,
            jnp.concatenate([value, arrived], axis=1),
            jnp.concatenate([arrived, value], axis=1),
        )
        step *= 2
    return value


def shards(sizes, counts, tile_mask, tile_counts, gene_factor, prev_factor):
    cells, genes, subs = sizes
    rows, columns = counts.shape
    width = gene_factor.shape[0]
    tile = rows // tile_mask.shape[0]
    sub = lax.axis_index("sub")
    cell = lax.axis_index("cell")
    place = sub * genes + lax.axis_index("gene")
    meta = jnp.stack([sub, cell, place]).astype(jnp.int32)

    gram, turned, factor = gram_parts(gene_factor, tile_mask, tile_counts)
    gram = pair_sums(gram, "gene", genes)
    gram_other = swap(gram, "sub", subs, 1)
    theirs, mine = cross_parts(meta, factor, counts, turned, tile)
    cross = mine + swap(theirs, "sub", subs, 1)
    cross_a, cross_b = split_sums(cross, "gene", genes)
    inverse, rho = shifted_inverse(gram, gram_other)
    share = admm(meta, rho, cross_a, cross_b, inverse, prev_factor)
    own = join_columns(share, "gene", genes)
    other = swap(own, "sub", subs, 1)

    block = columns // cells
    chunks = 2 if block % (2 * tile) == 0 else 1
    pieces = []
    for chunk in range(chunks):
        part = products(cells, chunks, chunk, tile, meta, factor, counts, own, other)
        part = lax.psum_scatter(part, "cell", scatter_dimension=0)
        pieces.append(part.T.astype(F32))
    data_products = jnp.concatenate(pieces, axis=0)

    whole = jnp.where(
        sub == 0,
        jnp.concatenate([own, other], axis=1),
        jnp.concatenate([other, own], axis=1),
    )
    new_factor = whole.T
    part = width // (genes * subs)
    first = (lax.axis_index("gene") * subs + sub) * part
    gram_rows = contract_last(lax.dynamic_slice_in_dim(whole, first, part, 0), whole)
    gram_rows = pair_sums(gram_rows, "cell", cells)
    factor_gram = lax.all_gather(gram_rows, ("gene", "sub"), axis=0, tiled=True)
    return (new_factor, factor_gram, data_products)


def solution(mesh):
    sizes = (mesh.shape["cell"], mesh.shape["gene"], mesh.shape["sub"])
    return jax.shard_map(
        functools.partial(shards, sizes),
        mesh=mesh,
        in_specs=(
            P(("groups", "cell"), ("gene", "sub")),
            P(("groups", "cell"), ("gene", "sub")),
            P(("groups", "cell"), ("gene", "sub")),
            P("groups", ("gene", "sub")),
            P(("groups", "cell"), None),
        ),
        out_specs=(
            P(("groups", "cell"), None),
            P("groups", None),
            P(("groups", "gene", "sub", "cell"), None),
        ),
        check_vma=False,
    )
```

```python
import functools

import jax
import jax.numpy as jnp
from jax import lax
from jax.experimental import pallas as pl
from jax.experimental.pallas import tpu as pltpu
from jax.sharding import PartitionSpec as P

ITERS = 3
F32 = jnp.float32
BF16 = jnp.bfloat16
MIB = 1024 * 1024


def params(limit=48):
    return pltpu.CompilerParams(vmem_limit_bytes=limit * MIB)


def cost(flops, bytes_accessed):
    return pl.CostEstimate(flops=flops, bytes_accessed=bytes_accessed, transcendentals=0)


def contract_last(left, right):
    return lax.dot_general(
        left, right, (((1,), (1,)), ((), ())), preferred_element_type=F32
    )


def cross_tile(counts, scales, genes, row):
    tile = counts.shape[0] // scales.shape[0]
    block = counts[row * tile : (row + 1) * tile].astype(F32)
    return contract_last((block * scales[row : row + 1]).astype(BF16), genes)


def halves(value):
    high = value.astype(BF16)
    return high, (value - high.astype(F32)).astype(BF16)


def product3(left, right):
    left_high, left_low = left
    right_high, right_low = right
    dot = functools.partial(jnp.dot, preferred_element_type=F32)
    return dot(left_high, right_high) + (
        dot(left_high, right_low) + dot(left_low, right_high)
    )


def inverse_kernel(gram_a, gram_b, inverse, rho_out):
    gram = gram_a[...] + gram_b[...]
    width = gram.shape[0]
    shape = (width, width)
    diagonal = lax.broadcasted_iota(jnp.int32, shape, 0) == lax.broadcasted_iota(
        jnp.int32, shape, 1
    )
    eye = jnp.where(diagonal, 1.0, 0.0).astype(F32)
    rho = jnp.sum(gram * eye) / width
    rho_out[0, 0] = rho
    scale = 1.0 / jnp.full((1, 1), rho, F32)
    matrix = gram * scale + eye
    low = 2.0 / (width + 2.0)
    guess = low * eye
    image = low * matrix
    first = True
    while True:
        low = low * (2.0 - low)
        gain = 2.0 / (1.0 + low)
        low = gain * low
        done = 1.0 - low < 2e-3
        step = halves(gain * (2.0 * eye - image))
        if first:
            guess = guess[0:1, 0:1] * (gain * (2.0 * eye - image))
        else:
            guess = product3(halves(guess), step)
        first = False
        if done:
            break
        image = product3(halves(image), step)
    rest = eye - jnp.dot(
        matrix, guess, preferred_element_type=F32, precision=lax.Precision.HIGHEST
    )
    rest_halves = halves(rest)
    series = rest + product3(rest_halves, rest_halves)
    inverse[...] = (guess + product3(halves(guess), halves(series))) * scale


def shifted_inverse(gram_a, gram_b):
    width = gram_a.shape[0]
    whole = pl.BlockSpec(memory_space=pltpu.VMEM)
    return pl.pallas_call(
        inverse_kernel,
        out_shape=(
            jax.ShapeDtypeStruct((width, width), F32),
            jax.ShapeDtypeStruct((1, 1), F32),
        ),
        in_specs=[whole, whole],
        out_specs=(whole, pl.BlockSpec(memory_space=pltpu.SMEM)),
        compiler_params=params(),
        cost_estimate=cost(2 * 60 * width**3, 12 * width**2),
        name="inverse",
    )(gram_a, gram_b)


def admm_kernel(meta, rho_ref, cross_a, cross_b, inverse, start, columns_out):
    rho = rho_ref[0, 0]
    cross = cross_a[...] + cross_b[...]
    inverse_halves = halves(inverse[...])
    zvalue = start[...].astype(F32)
    uvalue = jnp.zeros_like(zvalue)
    for _ in range(ITERS):
        vvalue = product3(halves(cross + rho * (zvalue - uvalue)), inverse_halves)
        zvalue = jnp.maximum(vvalue + uvalue, 0.0)
        uvalue = uvalue + vvalue - zvalue
    columns_out[...] = zvalue.T.astype(BF16)


def admm(meta, rho, cross_a, cross_b, inverse, start):
    rows, width = cross_a.shape
    tall = lambda: pl.BlockSpec((rows, width), lambda i, m: (0, 0))
    return pl.pallas_call(
        admm_kernel,
        out_shape=jax.ShapeDtypeStruct((width, rows), BF16),
        grid_spec=pltpu.PrefetchScalarGridSpec(
            num_scalar_prefetch=1,
            grid=(1,),
            in_specs=[
                pl.BlockSpec(memory_space=pltpu.SMEM),
                tall(),
                tall(),
                pl.BlockSpec((width, width), lambda i, m: (0, 0)),
                pl.BlockSpec((rows, width), lambda i, m: (m[2], 0)),
            ],
            out_specs=pl.BlockSpec((width, rows), lambda i, m: (0, 0)),
        ),
        compiler_params=params(),
        cost_estimate=cost(2 * 9 * rows * width**2, 12 * rows * width),
        name="admm",
    )(meta, rho, cross_a, cross_b, inverse, start)


def tile_products(tile, gene, meta, factor, counts, own, other):
    rows, wide = counts.shape
    half = rows // 2
    sub = meta[0]
    span = min(tile, wide)
    total = None
    for first, left in ((sub, own), (1 - sub, other)):
        parts = [
            [
                (
                    counts[
                        pl.ds(pl.multiple_of(first * half + r * tile, tile), tile),
                        pl.ds(c * span, span),
                    ].astype(F32)
                    * factor[first * (half // tile) + r, gene // tile + c]
                ).astype(BF16)
                for c in range(wide // span)
            ]
            for r in range(half // tile)
        ]
        right = jnp.concatenate([jnp.concatenate(row, axis=1) for row in parts], axis=0)
        part = jnp.dot(left[...], right, preferred_element_type=F32)
        total = part if total is None else total + part
    return total


def products_kernel(tile, wide, place, meta, factor, counts, own, other, out):
    gene = place(pl.program_id(0), pl.program_id(1), meta) * wide
    total = tile_products(tile, gene, meta, factor, counts, own, other)
    out[...] = total.astype(out.dtype).reshape(out.shape)


def products(block_of, blocks, block, start, chunk, dtype, tile, meta, factor, counts, own, other):
    rows = counts.shape[0]
    width = own.shape[0]
    wide = 2 * tile if chunk % (2 * tile) == 0 else min(tile, chunk)

    def place(o, i, m):
        return block_of(o, m) * (block // wide) + start // wide + i

    halved = lambda: pl.BlockSpec((width, rows // 2), lambda o, i, m: (0, 0))
    return pl.pallas_call(
        functools.partial(products_kernel, tile, wide, place),
        out_shape=jax.ShapeDtypeStruct((blocks, width, chunk), dtype),
        grid_spec=pltpu.PrefetchScalarGridSpec(
            num_scalar_prefetch=1,
            grid=(blocks, chunk // wide),
            in_specs=[
                pl.BlockSpec(memory_space=pltpu.SMEM),
                pl.BlockSpec((rows, wide), lambda o, i, m: (0, place(o, i, m))),
                halved(),
                halved(),
            ],
            out_specs=pl.BlockSpec((1, width, wide), lambda o, i, m: (o, 0, i)),
        ),
        compiler_params=params(40),
        cost_estimate=cost(1, 1),
        name="products",
    )(meta, factor, counts, own, other)


def keep_kernel(meta, total, first, second, *refs):
    value = total[0] + (first[...].astype(F32) + second[...].astype(F32))
    refs[-1][...] = value.T


def keep(block, start, meta, totals, first, second, out):
    width, chunk = first.shape
    wide = min(512, chunk)
    piece = lambda: pl.BlockSpec((width, wide), lambda i, m: (0, i))
    extra = [] if out is None else [out]
    return pl.pallas_call(
        keep_kernel,
        out_shape=jax.ShapeDtypeStruct((block, width), F32),
        grid_spec=pltpu.PrefetchScalarGridSpec(
            num_scalar_prefetch=1,
            grid=(chunk // wide,),
            in_specs=[
                pl.BlockSpec((1, width, wide), lambda i, m: (m[1], 0, i)),
                piece(),
                piece(),
            ]
            + [pl.BlockSpec(memory_space=pl.ANY) for _ in extra],
            out_specs=pl.BlockSpec((wide, width), lambda i, m: (start // wide + i, 0)),
        ),
        input_output_aliases={4: 0} if extra else {},
        compiler_params=params(40),
        cost_estimate=cost(3 * width * chunk, 12 * width * chunk),
        name="keep",
    )(meta, totals, first, second, *extra)


class Line:
    def __init__(self, size, cell):
        self.size = size
        self.cell = cell

    def pairs(self, phase, parity):
        links = range(parity, self.size - 1, 2)
        right = [(i, i + 1) for i in links if i < phase]
        left = [(i + 1, i) for i in links if i + 1 >= self.size - phase]
        return right + left

    def block(self, phase, parity):
        to_right = (self.cell & 1) == parity
        block = self.cell + jnp.where(to_right, self.size - phase, phase)
        return jnp.where(block >= self.size, block - self.size, block)

    def send(self, value, phase, parity):
        return lax.ppermute(value, "cell", self.pairs(phase, parity))


def swap(value, axis, size, step):
    return lax.ppermute(value, axis, [(i, i ^ step) for i in range(size)])


def pair_sums(value, axis, size):
    step = 1
    while step < size:
        value = value + swap(value, axis, size, step)
        step *= 2
    return value


def split_sums(value, axis, size):
    index = lax.axis_index(axis)
    step = size // 2
    while True:
        upper = (index & step) != 0
        low, high = jnp.split(value, 2, axis=0)
        kept = jnp.where(upper, high, low)
        arrived = swap(jnp.where(upper, low, high), axis, size, step)
        step //= 2
        if step == 0:
            return kept, arrived
        value = kept + arrived


def join(value, axis, size, dim):
    index = lax.axis_index(axis)
    step = 1
    while step < size:
        arrived = swap(value, axis, size, step)
        value = jnp.where(
            (index & step) == 0,
            jnp.concatenate([value, arrived], axis=dim),
            jnp.concatenate([arrived, value], axis=dim),
        )
        step *= 2
    return value


def after(value, event):
    return lax.optimization_barrier((value, event))


def chunk_sizes(block):
    if block % 2048 == 0:
        return [block // 4, block // 4, block // 2]
    return [block]


def shards(sizes, counts, tile_mask, tile_counts, gene_factor, prev_factor):
    cells, genes, subs = sizes
    rows, columns = counts.shape
    width = gene_factor.shape[0]
    tile = rows // tile_mask.shape[0]
    sub = lax.axis_index("sub")
    cell = lax.axis_index("cell")
    gene = lax.axis_index("gene")
    line = Line(cells, cell)
    meta = jnp.stack([sub, cell, sub * genes + gene, line.block(1, 0)]).astype(jnp.int32)
    factor = tile_mask.astype(F32) / tile_counts.astype(F32)

    gram = contract_last(gene_factor, gene_factor)
    factor, gram = after(factor, gram)
    gram = pair_sums(gram, "gene", genes)
    row_tiles = rows // tile
    early = row_tiles // 4 * 3
    scales = jnp.broadcast_to(factor[:, :, None], factor.shape + (tile,))
    scales = scales.reshape(row_tiles, columns)
    cross = [cross_tile(counts, scales, gene_factor, row) for row in range(early)]
    scales, gram = after(scales, gram)
    gram_other = swap(gram, "sub", subs, 1)
    cross += [cross_tile(counts, scales, gene_factor, row) for row in range(early, row_tiles)]
    low = jnp.concatenate(cross[: row_tiles // 2], axis=0)
    high = jnp.concatenate(cross[row_tiles // 2 :], axis=0)
    arrived = swap(jnp.where(sub == 0, high, low), "sub", subs, 1)
    cross = jnp.where(sub == 0, low, high) + arrived
    cross_a, cross_b = split_sums(cross, "gene", genes)
    inverse, rho = shifted_inverse(gram, gram_other)
    share = admm(meta, rho, cross_a, cross_b, inverse, prev_factor)
    own = join(share, "gene", genes, 1)
    other = swap(own, "sub", subs, 1)

    block = columns // cells
    chunks = chunk_sizes(block)
    starts = [sum(chunks[:i]) for i in range(len(chunks))]
    arrived = [[], []]
    for start, chunk in zip(starts, chunks):
        first = products(
            lambda o, m: m[3], 1, block, start, chunk, BF16, tile, meta, factor, counts, own, other
        )[0]
        meta, first = after(meta, first)
        for parity in (0, 1):
            sends = line.pairs(1, parity)
            arrived[parity].append(line.send(first, 1, parity) if sends else None)
    totals = []
    for index, (start, chunk) in enumerate(zip(starts, chunks)):
        meta, arrived[0][index] = after(meta, arrived[0][index])
        total = products(
            lambda o, m: o, cells, block, start, chunk, F32, tile, meta, factor, counts, own, other
        )
        meta, total = after(meta, total)
        totals.append(total)
    for phase in range(2, cells):
        for index, total in enumerate(totals):
            values = []
            for parity in (0, 1):
                value = lax.dynamic_index_in_dim(total, line.block(phase, parity), 0, False)
                before = arrived[1 - parity][index]
                if before is not None:
                    value = value + before.astype(F32)
                values.append(value.astype(BF16))
            for parity in (0, 1):
                arrived[parity][index] = line.send(values[parity], phase, parity)
    data_products = None
    for index, start in enumerate(starts):
        data_products = keep(
            block, start, meta, totals[index], arrived[0][index], arrived[1][index], data_products
        )

    own, _ = after(own, totals[0])
    whole = jnp.where(
        sub == 0,
        jnp.concatenate([own, other], axis=1),
        jnp.concatenate([other, own], axis=1),
    )
    new_factor = whole.T
    part = width // (genes * subs)
    gram_rows = contract_last(
        lax.dynamic_slice_in_dim(whole, (gene * subs + sub) * part, part, 0), whole
    )
    step = 1
    while step < cells:
        gram_rows = gram_rows.astype(BF16)
        gram_rows = gram_rows.astype(F32) + swap(gram_rows, "cell", cells, step).astype(F32)
        step *= 2
    factor_gram = join(join(gram_rows, "sub", subs, 0), "gene", genes, 0)
    return (new_factor, factor_gram, data_products)


def solution(mesh):
    sizes = (mesh.shape["cell"], mesh.shape["gene"], mesh.shape["sub"])
    return jax.shard_map(
        functools.partial(shards, sizes),
        mesh=mesh,
        in_specs=(
            P(("groups", "cell"), ("gene", "sub")),
            P(("groups", "cell"), ("gene", "sub")),
            P(("groups", "cell"), ("gene", "sub")),
            P("groups", ("gene", "sub")),
            P(("groups", "cell"), None),
        ),
        out_specs=(
            P(("groups", "cell"), None),
            P("groups", None),
            P(("groups", "gene", "sub", "cell"), None),
        ),
        check_vma=False,
    )
```

```python
import functools

import jax
import jax.numpy as jnp
from jax import lax
from jax.experimental import pallas as pl
from jax.experimental.pallas import tpu as pltpu
from jax.sharding import PartitionSpec as P

ITERS = 3
F32 = jnp.float32
BF16 = jnp.bfloat16
MIB = 1024 * 1024


def params(limit=48):
    return pltpu.CompilerParams(vmem_limit_bytes=limit * MIB)


def cost(flops, bytes_accessed):
    return pl.CostEstimate(flops=flops, bytes_accessed=bytes_accessed, transcendentals=0)


def contract_last(left, right):
    return lax.dot_general(
        left, right, (((1,), (1,)), ((), ())), preferred_element_type=F32
    )


def cross_tile(counts, scales, genes, row):
    tile = counts.shape[0] // scales.shape[0]
    block = counts[row * tile : (row + 1) * tile].astype(F32)
    return contract_last((block * scales[row : row + 1]).astype(BF16), genes)


def halves(value):
    high = value.astype(BF16)
    return high, (value - high.astype(F32)).astype(BF16)


def product3(left, right):
    left_high, left_low = left
    right_high, right_low = right
    dot = functools.partial(jnp.dot, preferred_element_type=F32)
    return dot(left_high, right_high) + (
        dot(left_high, right_low) + dot(left_low, right_high)
    )


def inverse_kernel(gram_a, gram_b, inverse, rho_out):
    gram = gram_a[...] + gram_b[...]
    width = gram.shape[0]
    shape = (width, width)
    diagonal = lax.broadcasted_iota(jnp.int32, shape, 0) == lax.broadcasted_iota(
        jnp.int32, shape, 1
    )
    eye = jnp.where(diagonal, 1.0, 0.0).astype(F32)
    rho = jnp.sum(gram * eye) / width
    rho_out[0, 0] = rho
    scale = 1.0 / jnp.full((1, 1), rho, F32)
    matrix = gram * scale + eye
    low = 2.0 / (width + 2.0)
    guess = low * eye
    image = low * matrix
    first = True
    while True:
        low = low * (2.0 - low)
        gain = 2.0 / (1.0 + low)
        low = gain * low
        done = 1.0 - low < 2e-3
        step = halves(gain * (2.0 * eye - image))
        if first:
            guess = guess[0:1, 0:1] * (gain * (2.0 * eye - image))
        else:
            guess = product3(halves(guess), step)
        first = False
        if done:
            break
        image = product3(halves(image), step)
    rest = eye - jnp.dot(
        matrix, guess, preferred_element_type=F32, precision=lax.Precision.HIGHEST
    )
    rest_halves = halves(rest)
    series = rest + product3(rest_halves, rest_halves)
    inverse[...] = (guess + product3(halves(guess), halves(series))) * scale


def shifted_inverse(gram_a, gram_b):
    width = gram_a.shape[0]
    whole = pl.BlockSpec(memory_space=pltpu.VMEM)
    return pl.pallas_call(
        inverse_kernel,
        out_shape=(
            jax.ShapeDtypeStruct((width, width), F32),
            jax.ShapeDtypeStruct((1, 1), F32),
        ),
        in_specs=[whole, whole],
        out_specs=(whole, pl.BlockSpec(memory_space=pltpu.SMEM)),
        compiler_params=params(),
        cost_estimate=cost(2 * 60 * width**3, 12 * width**2),
        name="inverse",
    )(gram_a, gram_b)


def admm_kernel(meta, rho_ref, cross_a, cross_b, inverse, start, columns_out):
    rho = rho_ref[0, 0]
    cross = cross_a[...] + cross_b[...]
    inverse_halves = halves(inverse[...])
    zvalue = start[...].astype(F32)
    uvalue = jnp.zeros_like(zvalue)
    for _ in range(ITERS):
        vvalue = product3(halves(cross + rho * (zvalue - uvalue)), inverse_halves)
        zvalue = jnp.maximum(vvalue + uvalue, 0.0)
        uvalue = uvalue + vvalue - zvalue
    columns_out[...] = zvalue.T.astype(BF16)


def admm(meta, rho, cross_a, cross_b, inverse, start):
    rows, width = cross_a.shape
    tall = lambda: pl.BlockSpec((rows, width), lambda i, m: (0, 0))
    return pl.pallas_call(
        admm_kernel,
        out_shape=jax.ShapeDtypeStruct((width, rows), BF16),
        grid_spec=pltpu.PrefetchScalarGridSpec(
            num_scalar_prefetch=1,
            grid=(1,),
            in_specs=[
                pl.BlockSpec(memory_space=pltpu.SMEM),
                tall(),
                tall(),
                pl.BlockSpec((width, width), lambda i, m: (0, 0)),
                pl.BlockSpec((rows, width), lambda i, m: (m[2], 0)),
            ],
            out_specs=pl.BlockSpec((width, rows), lambda i, m: (0, 0)),
        ),
        compiler_params=params(),
        cost_estimate=cost(2 * 9 * rows * width**2, 12 * rows * width),
        name="admm",
    )(meta, rho, cross_a, cross_b, inverse, start)


def tile_products(tile, gene, meta, factor, counts, own, other):
    rows, wide = counts.shape
    half = rows // 2
    sub = meta[0]
    span = min(tile, wide)
    total = None
    for first, left in ((sub, own), (1 - sub, other)):
        parts = [
            [
                (
                    counts[
                        pl.ds(pl.multiple_of(first * half + r * tile, tile), tile),
                        pl.ds(c * span, span),
                    ].astype(F32)
                    * factor[first * (half // tile) + r, gene // tile + c]
                ).astype(BF16)
                for c in range(wide // span)
            ]
            for r in range(half // tile)
        ]
        right = jnp.concatenate([jnp.concatenate(row, axis=1) for row in parts], axis=0)
        part = jnp.dot(left[...], right, preferred_element_type=F32)
        total = part if total is None else total + part
    return total


def products_kernel(tile, wide, place, meta, factor, counts, own, other, *outs):
    step, order = pl.program_id(0), pl.program_id(1)
    gene = place(step, order, meta) * wide
    total = tile_products(tile, gene, meta, factor, counts, own, other)
    outs[0][...] = total.astype(outs[0].dtype).reshape(outs[0].shape)
    if len(outs) > 1:

        @pl.when(order == meta[4])
        def _():
            outs[1][...] = total.astype(outs[1].dtype)


def products(only_first, cells, start, chunk, tile, meta, factor, counts, own, other):
    rows, columns = counts.shape
    width = own.shape[0]
    block = columns // cells
    blocks = 1 if only_first else cells
    wide = 2 * tile if chunk % (2 * tile) == 0 else min(tile, chunk)

    def place(i, o, m):
        return (m[3] if only_first else o) * (block // wide) + start // wide + i

    halved = lambda: pl.BlockSpec((width, rows // 2), lambda i, o, m: (0, 0))
    flat = pl.BlockSpec((width, wide), lambda i, o, m: (0, i))
    operand = jax.ShapeDtypeStruct((width, chunk), BF16)
    if only_first:
        out_shape, out_specs = (operand,), (flat,)
    else:
        out_shape = (jax.ShapeDtypeStruct((cells, width, chunk), F32), operand)
        out_specs = (pl.BlockSpec((1, width, wide), lambda i, o, m: (o, 0, i)), flat)
    return pl.pallas_call(
        functools.partial(products_kernel, tile, wide, place),
        out_shape=out_shape,
        grid_spec=pltpu.PrefetchScalarGridSpec(
            num_scalar_prefetch=1,
            grid=(chunk // wide, blocks),
            in_specs=[
                pl.BlockSpec(memory_space=pltpu.SMEM),
                pl.BlockSpec((rows, wide), lambda i, o, m: (0, place(i, o, m))),
                halved(),
                halved(),
            ],
            out_specs=out_specs,
        ),
        compiler_params=params(48),
        cost_estimate=cost(1, 1),
        name="products",
    )(meta, factor, counts, own, other)


def operand_kernel(meta, total, before, out):
    out[...] = (total[0] + before[...].astype(F32)).astype(BF16)


def operand(slot, meta, total, before):
    width, chunk = before.shape
    flat = lambda: pl.BlockSpec((width, chunk), lambda i, m: (0, 0))
    return pl.pallas_call(
        operand_kernel,
        out_shape=jax.ShapeDtypeStruct((width, chunk), BF16),
        grid_spec=pltpu.PrefetchScalarGridSpec(
            num_scalar_prefetch=1,
            grid=(1,),
            in_specs=[
                pl.BlockSpec((1, width, chunk), lambda i, m: (m[slot], 0, 0)),
                flat(),
            ],
            out_specs=flat(),
        ),
        compiler_params=params(24),
        cost_estimate=cost(1, 1),
        name="operand",
    )(meta, total, before)


def keep_kernel(meta, total, first, second, *refs):
    value = total[0] + (first[...].astype(F32) + second[...].astype(F32))
    refs[-1][...] = value.T


def keep(block, start, meta, totals, first, second, out):
    width, chunk = first.shape
    wide = min(512, chunk)
    piece = lambda: pl.BlockSpec((width, wide), lambda i, m: (0, i))
    extra = [] if out is None else [out]
    return pl.pallas_call(
        keep_kernel,
        out_shape=jax.ShapeDtypeStruct((block, width), F32),
        grid_spec=pltpu.PrefetchScalarGridSpec(
            num_scalar_prefetch=1,
            grid=(chunk // wide,),
            in_specs=[
                pl.BlockSpec((1, width, wide), lambda i, m: (m[1], 0, i)),
                piece(),
                piece(),
            ]
            + [pl.BlockSpec(memory_space=pl.ANY) for _ in extra],
            out_specs=pl.BlockSpec((wide, width), lambda i, m: (start // wide + i, 0)),
        ),
        input_output_aliases={4: 0} if extra else {},
        compiler_params=params(24),
        cost_estimate=cost(1, 1),
        name="keep",
    )(meta, totals, first, second, *extra)


class Line:
    def __init__(self, size, cell):
        self.size = size
        self.cell = cell

    def pairs(self, phase, parity):
        links = range(parity, self.size - 1, 2)
        right = [(i, i + 1) for i in links if i < phase]
        left = [(i + 1, i) for i in links if i + 1 >= self.size - phase]
        return right + left

    def block(self, phase, parity):
        to_right = (self.cell & 1) == parity
        block = self.cell + jnp.where(to_right, self.size - phase, phase)
        return jnp.where(block >= self.size, block - self.size, block)

    def send(self, value, phase, parity):
        return lax.ppermute(value, "cell", self.pairs(phase, parity))


def swap(value, axis, size, step):
    return lax.ppermute(value, axis, [(i, i ^ step) for i in range(size)])


def pair_sums(value, axis, size):
    step = 1
    while step < size:
        value = value + swap(value, axis, size, step)
        step *= 2
    return value


def split_sums(value, axis, size):
    index = lax.axis_index(axis)
    step = size // 2
    while True:
        upper = (index & step) != 0
        low, high = jnp.split(value, 2, axis=0)
        kept = jnp.where(upper, high, low)
        arrived = swap(jnp.where(upper, low, high), axis, size, step)
        step //= 2
        if step == 0:
            return kept, arrived
        value = kept + arrived


def join(value, axis, size, dim):
    index = lax.axis_index(axis)
    step = 1
    while step < size:
        arrived = swap(value, axis, size, step)
        value = jnp.where(
            (index & step) == 0,
            jnp.concatenate([value, arrived], axis=dim),
            jnp.concatenate([arrived, value], axis=dim),
        )
        step *= 2
    return value


def after(value, event):
    return lax.optimization_barrier((value, event))


def chunk_sizes(block):
    return [block // 2, block // 2] if block % 1024 == 0 else [block]


def shards(sizes, counts, tile_mask, tile_counts, gene_factor, prev_factor):
    cells, genes, subs = sizes
    rows, columns = counts.shape
    width = gene_factor.shape[0]
    tile = rows // tile_mask.shape[0]
    sub = lax.axis_index("sub")
    cell = lax.axis_index("cell")
    gene = lax.axis_index("gene")
    line = Line(cells, cell)
    places = [sub, cell, sub * genes + gene, line.block(1, 0), line.block(2, 0)]
    places += [line.block(phase, parity) for phase in range(2, cells) for parity in (0, 1)]
    meta = jnp.stack(places).astype(jnp.int32)
    factor = tile_mask.astype(F32) / tile_counts.astype(F32)

    gram = contract_last(gene_factor, gene_factor)
    factor, gram = after(factor, gram)
    gram = pair_sums(gram, "gene", genes)
    row_tiles = rows // tile
    early = row_tiles // 4 * 3
    scales = jnp.broadcast_to(factor[:, :, None], factor.shape + (tile,))
    scales = scales.reshape(row_tiles, columns)
    cross = [cross_tile(counts, scales, gene_factor, row) for row in range(early)]
    scales, gram = after(scales, gram)
    gram_other = swap(gram, "sub", subs, 1)
    cross += [cross_tile(counts, scales, gene_factor, row) for row in range(early, row_tiles)]
    low = jnp.concatenate(cross[: row_tiles // 2], axis=0)
    high = jnp.concatenate(cross[row_tiles // 2 :], axis=0)
    arrived = swap(jnp.where(sub == 0, high, low), "sub", subs, 1)
    cross = jnp.where(sub == 0, low, high) + arrived
    cross_a, cross_b = split_sums(cross, "gene", genes)
    inverse, rho = shifted_inverse(gram, gram_other)
    share = admm(meta, rho, cross_a, cross_b, inverse, prev_factor)
    own = join(share, "gene", genes, 1)
    other = swap(own, "sub", subs, 1)

    block = columns // cells
    chunks = chunk_sizes(block)
    starts = [sum(chunks[:i]) for i in range(len(chunks))]
    every = range(len(chunks))
    part = width // (genes * subs)

    arrived = {}

    def send(value, phase, parity, index):
        pairs = line.pairs(phase, parity)
        arrived[phase, parity, index] = lax.ppermute(value, "cell", pairs) if pairs else None

    def resend(meta, phase, parity, index):
        before = arrived[phase - 1, 1 - parity, index]
        if before is None:
            value = seconds[index]
        else:
            value = operand(5 + 2 * (phase - 2) + parity, meta, totals[index], before)
            meta, value = after(meta, value)
        send(value, phase, parity, index)
        return meta

    steps = [1 << i for i in range((cells - 1).bit_length())]

    def add_rows(meta, rows_sum):
        rows_arrived = swap(rows_sum, "cell", cells, steps.pop(0))
        rows_arrived, meta = after(rows_arrived, meta)
        total = rows_sum.astype(F32) + rows_arrived.astype(F32)
        return after(meta, total.astype(BF16) if steps else total)

    def gram_rows(half):
        rows_here = lax.dynamic_slice_in_dim(half, (gene * subs + sub) * part, part, 0)
        return contract_last(rows_here, half)

    meta, rows_sum = after(meta, (gram_rows(own) + gram_rows(other)).astype(BF16))
    for index in every:
        (first,) = products(
            True, cells, starts[index], chunks[index], tile, meta, factor, counts, own, other
        )
        meta, first = after(meta, first)
        for parity in (0, 1):
            send(first, 1, parity, index)
        if index == 0:
            meta, rows_sum = add_rows(meta, rows_sum)
    totals, seconds = [], []
    for index in every:
        total, second = products(
            False, cells, starts[index], chunks[index], tile, meta, factor, counts, own, other
        )
        meta, second = after(meta, second)
        totals.append(total)
        seconds.append(second)
        if cells > 2:
            for parity in (0, 1):
                meta = resend(meta, 2, parity, index)
    while steps:
        meta, rows_sum = add_rows(meta, rows_sum)
    new_factor = factor_gram = None
    for phase in range(3, cells):
        for index in every:
            for parity in (0, 1):
                meta = resend(meta, phase, parity, index)
                if new_factor is None:
                    rows_sum = join(rows_sum, "sub", subs, 0)
                    own_late, meta = after(own, meta)
                    whole = jnp.where(
                        sub == 0,
                        jnp.concatenate([own_late, other], axis=1),
                        jnp.concatenate([other, own_late], axis=1),
                    )
                    new_factor = whole.T
                    meta, new_factor = after(meta, new_factor)
                    factor_gram = join(rows_sum, "gene", genes, 0)
                    meta, factor_gram = after(meta, factor_gram)
    data_products = None
    last = cells - 1
    for index in every:
        data_products = keep(
            block, starts[index], meta, totals[index],
            arrived[last, 0, index], arrived[last, 1, index], data_products,
        )
        meta, data_products = after(meta, data_products)
    return (new_factor, factor_gram, data_products)


def solution(mesh):
    sizes = (mesh.shape["cell"], mesh.shape["gene"], mesh.shape["sub"])
    return jax.shard_map(
        functools.partial(shards, sizes),
        mesh=mesh,
        in_specs=(
            P(("groups", "cell"), ("gene", "sub")),
            P(("groups", "cell"), ("gene", "sub")),
            P(("groups", "cell"), ("gene", "sub")),
            P("groups", ("gene", "sub")),
            P(("groups", "cell"), None),
        ),
        out_specs=(
            P(("groups", "cell"), None),
            P("groups", None),
            P(("groups", "gene", "sub", "cell"), None),
        ),
        check_vma=False,
    )
```

```python
import functools

import jax
import jax.numpy as jnp
from jax import lax
from jax.experimental import pallas as pl
from jax.experimental.pallas import tpu as pltpu
from jax.sharding import PartitionSpec as P

ITERS = 3
F32 = jnp.float32
BF16 = jnp.bfloat16
MIB = 1024 * 1024


def params(limit=48):
    return pltpu.CompilerParams(vmem_limit_bytes=limit * MIB)


def cost(flops, bytes_accessed):
    return pl.CostEstimate(flops=flops, bytes_accessed=bytes_accessed, transcendentals=0)


def contract_last(left, right):
    return lax.dot_general(
        left, right, (((1,), (1,)), ((), ())), preferred_element_type=F32
    )


def row_tile_specs(row_tiles, tile, wide, place):
    return [
        pl.BlockSpec((tile, wide), lambda *ids, r=r: (r, place(*ids)))
        for r in range(row_tiles)
    ]


def scaled_rows(tile, row, gene_tile, factor, counts):
    wide = counts.shape[1]
    span = min(tile, wide)
    parts = [
        (
            counts[:, pl.ds(c * span, span)].astype(F32) * factor[row, gene_tile + c]
        ).astype(BF16)
        for c in range(wide // span)
    ]
    return jnp.concatenate(parts, axis=1)


def cross_kernel(tile, first, row_tiles, last, meta, factor, *refs):
    counts, refs = refs[:row_tiles], refs[row_tiles:]
    genes, refs = refs[0], refs[1:]
    before, outs, total = (None, refs[:1], refs[1]) if not last else (refs[0], refs[1:3], refs[3])
    step = pl.program_id(0)
    gene_tile = (first + step) * (genes.shape[1] // tile)

    @pl.when(step == 0)
    def _():
        total[...] = jnp.zeros_like(total) if before is None else before[...]

    for row in range(row_tiles):
        rows = pl.ds(row * tile, tile)
        scaled = scaled_rows(tile, row, gene_tile, factor, counts[row])
        total[rows, :] += contract_last(scaled, genes[...])

    @pl.when(step == pl.num_programs(0) - 1)
    def _():
        if not last:
            outs[0][...] = total[...]
        else:
            half = total.shape[0] // 2
            sub = meta[0]
            outs[0][...] = total[pl.ds(pl.multiple_of((1 - sub) * half, half), half), :]
            outs[1][...] = total[pl.ds(pl.multiple_of(sub * half, half), half), :]


def cross_part(first, steps, wide, tile, meta, factor, counts, genes, before):
    rows, columns = counts.shape
    width = genes.shape[0]
    row_tiles = rows // tile
    last = before is not None
    whole = lambda n: pl.BlockSpec((n, width), lambda i, m: (0, 0))
    sizes = (rows // 2, rows // 2) if last else (rows,)
    return pl.pallas_call(
        functools.partial(cross_kernel, tile, first, row_tiles, last),
        out_shape=tuple(jax.ShapeDtypeStruct((n, width), F32) for n in sizes),
        grid_spec=pltpu.PrefetchScalarGridSpec(
            num_scalar_prefetch=1,
            grid=(steps,),
            in_specs=[pl.BlockSpec(memory_space=pltpu.SMEM)]
            + row_tile_specs(row_tiles, tile, wide, lambda i, m: first + i)
            + [pl.BlockSpec((width, wide), lambda i, m: (0, first + i))]
            + ([whole(rows)] if last else []),
            out_specs=tuple(whole(n) for n in sizes),
            scratch_shapes=[pltpu.VMEM((rows, width), F32)],
        ),
        compiler_params=params(56),
        cost_estimate=cost(1, 1),
        name="cross",
    )(meta, factor, *[counts] * row_tiles, genes, *([before] if last else []))


def halves(value):
    high = value.astype(BF16)
    return high, (value - high.astype(F32)).astype(BF16)


def product3(left, right):
    left_high, left_low = left
    right_high, right_low = right
    dot = functools.partial(jnp.dot, preferred_element_type=F32)
    return dot(left_high, right_high) + (
        dot(left_high, right_low) + dot(left_low, right_high)
    )


def inverse_kernel(gram_a, gram_b, inverse, rho_out):
    gram = gram_a[...] + gram_b[...]
    width = gram.shape[0]
    shape = (width, width)
    diagonal = lax.broadcasted_iota(jnp.int32, shape, 0) == lax.broadcasted_iota(
        jnp.int32, shape, 1
    )
    eye = jnp.where(diagonal, 1.0, 0.0).astype(F32)
    rho = jnp.sum(gram * eye) / width
    rho_out[0, 0] = rho
    scale = 1.0 / jnp.full((1, 1), rho, F32)
    matrix = gram * scale + eye
    low = 2.0 / (width + 2.0)
    guess = low * eye
    image = low * matrix
    first = True
    while True:
        low = low * (2.0 - low)
        gain = 2.0 / (1.0 + low)
        low = gain * low
        done = 1.0 - low < 2e-3
        step = halves(gain * (2.0 * eye - image))
        if first:
            guess = guess[0:1, 0:1] * (gain * (2.0 * eye - image))
        else:
            guess = product3(halves(guess), step)
        first = False
        if done:
            break
        image = product3(halves(image), step)
    rest = eye - jnp.dot(
        matrix, guess, preferred_element_type=F32, precision=lax.Precision.HIGHEST
    )
    rest_halves = halves(rest)
    series = rest + product3(rest_halves, rest_halves)
    inverse[...] = (guess + product3(halves(guess), halves(series))) * scale


def shifted_inverse(gram_a, gram_b):
    width = gram_a.shape[0]
    whole = pl.BlockSpec(memory_space=pltpu.VMEM)
    return pl.pallas_call(
        inverse_kernel,
        out_shape=(
            jax.ShapeDtypeStruct((width, width), F32),
            jax.ShapeDtypeStruct((1, 1), F32),
        ),
        in_specs=[whole, whole],
        out_specs=(whole, pl.BlockSpec(memory_space=pltpu.SMEM)),
        compiler_params=params(),
        cost_estimate=cost(2 * 60 * width**3, 12 * width**2),
        name="inverse",
    )(gram_a, gram_b)


def admm_kernel(meta, rho_ref, cross_a, cross_b, inverse, start, columns_out):
    rho = rho_ref[0, 0]
    cross = cross_a[...] + cross_b[...]
    inverse_halves = halves(inverse[...])
    zvalue = start[...].astype(F32)
    uvalue = jnp.zeros_like(zvalue)
    for _ in range(ITERS):
        vvalue = product3(halves(cross + rho * (zvalue - uvalue)), inverse_halves)
        zvalue = jnp.maximum(vvalue + uvalue, 0.0)
        uvalue = uvalue + vvalue - zvalue
    columns_out[...] = zvalue.T.astype(BF16)


def admm(meta, rho, cross_a, cross_b, inverse, start):
    rows, width = cross_a.shape
    tall = lambda: pl.BlockSpec((rows, width), lambda i, m: (0, 0))
    return pl.pallas_call(
        admm_kernel,
        out_shape=jax.ShapeDtypeStruct((width, rows), BF16),
        grid_spec=pltpu.PrefetchScalarGridSpec(
            num_scalar_prefetch=1,
            grid=(1,),
            in_specs=[
                pl.BlockSpec(memory_space=pltpu.SMEM),
                tall(),
                tall(),
                pl.BlockSpec((width, width), lambda i, m: (0, 0)),
                pl.BlockSpec((rows, width), lambda i, m: (m[2], 0)),
            ],
            out_specs=pl.BlockSpec((width, rows), lambda i, m: (0, 0)),
        ),
        compiler_params=params(),
        cost_estimate=cost(2 * 9 * rows * width**2, 12 * rows * width),
        name="admm",
    )(meta, rho, cross_a, cross_b, inverse, start)


def products_kernel(tile, wide, place, row_tiles, meta, factor, *refs):
    counts, columns, outs = refs[:row_tiles], refs[row_tiles], refs[row_tiles + 1 :]
    step, order = pl.program_id(0), pl.program_id(1)
    gene_tile = place(step, order, meta) * wide // tile
    scaled = [
        scaled_rows(tile, row, gene_tile, factor, counts[row]) for row in range(row_tiles)
    ]
    total = jnp.dot(
        columns[...], jnp.concatenate(scaled, axis=0), preferred_element_type=F32
    ).astype(BF16)
    outs[0][...] = total.reshape(outs[0].shape)
    if len(outs) > 1:

        @pl.when(order == meta[4])
        def _():
            outs[1][...] = total


def products(only_first, cells, start, chunk, tile, meta, factor, counts, columns):
    rows = counts.shape[0]
    width = columns.shape[0]
    block = counts.shape[1] // cells
    blocks = 1 if only_first else cells
    wide = 2 * tile if chunk % (2 * tile) == 0 else min(tile, chunk)
    row_tiles = rows // tile

    def place(i, o, m):
        return (m[3] if only_first else o) * (block // wide) + start // wide + i

    flat = pl.BlockSpec((width, wide), lambda i, o, m: (0, i))
    operand = jax.ShapeDtypeStruct((width, chunk), BF16)
    if only_first:
        out_shape, out_specs = (operand,), (flat,)
    else:
        out_shape = (jax.ShapeDtypeStruct((cells, width, chunk), BF16), operand)
        out_specs = (pl.BlockSpec((1, width, wide), lambda i, o, m: (o, 0, i)), flat)
    return pl.pallas_call(
        functools.partial(products_kernel, tile, wide, place, row_tiles),
        out_shape=out_shape,
        grid_spec=pltpu.PrefetchScalarGridSpec(
            num_scalar_prefetch=1,
            grid=(chunk // wide, blocks),
            in_specs=[pl.BlockSpec(memory_space=pltpu.SMEM)]
            + row_tile_specs(row_tiles, tile, wide, place)
            + [pl.BlockSpec((width, rows), lambda i, o, m: (0, 0))],
            out_specs=out_specs,
        ),
        compiler_params=params(50),
        cost_estimate=cost(1, 1),
        name="products",
    )(meta, factor, *[counts] * row_tiles, columns)


def small(kernel, name, out_shape, meta, *args, specs=None):
    whole = lambda shape: pl.BlockSpec(shape, lambda i, m: (0,) * len(shape))
    return pl.pallas_call(
        kernel,
        out_shape=out_shape,
        grid_spec=pltpu.PrefetchScalarGridSpec(
            num_scalar_prefetch=1,
            grid=(1,),
            in_specs=specs or [whole(arg.shape) for arg in args],
            out_specs=whole(out_shape.shape),
        ),
        compiler_params=params(24),
        cost_estimate=cost(1, 1),
        name=name,
    )(meta, *args)


def turn_kernel(meta, value, out):
    out[...] = value[...].astype(F32).T.astype(out.dtype)


def turn(meta, value):
    shape = jax.ShapeDtypeStruct(value.shape[::-1], value.dtype)
    return small(turn_kernel, "turn", shape, meta, value)


def row_share_kernel(meta, share, columns, out):
    out[...] = contract_last(share[...], columns[...]).astype(out.dtype)


def row_share(slot, part, meta, columns):
    width, rows = columns.shape
    specs = [
        pl.BlockSpec((part, rows), lambda i, m: (m[slot], 0)),
        pl.BlockSpec((width, rows), lambda i, m: (0, 0)),
    ]
    shape = jax.ShapeDtypeStruct((part, width), BF16)
    return small(row_share_kernel, "row_share", shape, meta, columns, columns, specs=specs)


def plus_kernel(meta, left, right, out):
    out[...] = (left[...].astype(F32) + right[...].astype(F32)).astype(out.dtype)


def plus(dtype, meta, left, right):
    shape = jax.ShapeDtypeStruct(left.shape, dtype)
    return small(plus_kernel, "plus", shape, meta, left, right)


def stack_kernel(slot, bit, meta, mine, theirs, out):
    rows = mine.shape[0]
    upper = (meta[slot] & bit) != 0
    out[:rows] = jnp.where(upper, theirs[...], mine[...])
    out[rows:] = jnp.where(upper, mine[...], theirs[...])


def stack(slot, bit, meta, mine, theirs):
    shape = jax.ShapeDtypeStruct((2 * mine.shape[0],) + mine.shape[1:], mine.dtype)
    return small(functools.partial(stack_kernel, slot, bit), "stack", shape, meta, mine, theirs)


def operand_kernel(meta, total, before, out):
    out[...] = (total[0].astype(F32) + before[...].astype(F32)).astype(BF16)


def operand(slot, meta, total, before):
    width, chunk = before.shape
    flat = lambda: pl.BlockSpec((width, chunk), lambda i, m: (0, 0))
    return pl.pallas_call(
        operand_kernel,
        out_shape=jax.ShapeDtypeStruct((width, chunk), BF16),
        grid_spec=pltpu.PrefetchScalarGridSpec(
            num_scalar_prefetch=1,
            grid=(1,),
            in_specs=[
                pl.BlockSpec((1, width, chunk), lambda i, m: (m[slot], 0, 0)),
                flat(),
            ],
            out_specs=flat(),
        ),
        compiler_params=params(24),
        cost_estimate=cost(1, 1),
        name="operand",
    )(meta, total, before)


def keep_kernel(meta, total, first, second, *refs):
    value = total[0].astype(F32) + (first[...].astype(F32) + second[...].astype(F32))
    refs[-1][...] = value.T


def keep(block, start, meta, totals, first, second, out):
    width, chunk = first.shape
    wide = min(512, chunk)
    piece = lambda: pl.BlockSpec((width, wide), lambda i, m: (0, i))
    extra = [] if out is None else [out]
    return pl.pallas_call(
        keep_kernel,
        out_shape=jax.ShapeDtypeStruct((block, width), F32),
        grid_spec=pltpu.PrefetchScalarGridSpec(
            num_scalar_prefetch=1,
            grid=(chunk // wide,),
            in_specs=[
                pl.BlockSpec((1, width, wide), lambda i, m: (m[1], 0, i)),
                piece(),
                piece(),
            ]
            + [pl.BlockSpec(memory_space=pl.ANY) for _ in extra],
            out_specs=pl.BlockSpec((wide, width), lambda i, m: (start // wide + i, 0)),
        ),
        input_output_aliases={4: 0} if extra else {},
        compiler_params=params(24),
        cost_estimate=cost(1, 1),
        name="keep",
    )(meta, totals, first, second, *extra)


class Line:
    def __init__(self, size, cell):
        self.size = size
        self.cell = cell

    def pairs(self, phase, parity):
        links = range(parity, self.size - 1, 2)
        right = [(i, i + 1) for i in links if i < phase]
        left = [(i + 1, i) for i in links if i + 1 >= self.size - phase]
        return right + left

    def block(self, phase, parity):
        to_right = (self.cell & 1) == parity
        block = self.cell + jnp.where(to_right, self.size - phase, phase)
        return jnp.where(block >= self.size, block - self.size, block)

    def send(self, value, phase, parity):
        return lax.ppermute(value, "cell", self.pairs(phase, parity))


def swap(value, axis, size, step):
    return lax.ppermute(value, axis, [(i, i ^ step) for i in range(size)])


def pair_sums(value, axis, size):
    step = 1
    while step < size:
        value = value + swap(value, axis, size, step)
        step *= 2
    return value


def split_sums(value, axis, size):
    index = lax.axis_index(axis)
    step = size // 2
    while True:
        upper = (index & step) != 0
        low, high = jnp.split(value, 2, axis=0)
        kept = jnp.where(upper, high, low)
        arrived = swap(jnp.where(upper, low, high), axis, size, step)
        step //= 2
        if step == 0:
            return kept, arrived
        value = kept + arrived


def join(value, axis, size, dim):
    index = lax.axis_index(axis)
    step = 1
    while step < size:
        arrived = swap(value, axis, size, step)
        value = jnp.where(
            (index & step) == 0,
            jnp.concatenate([value, arrived], axis=dim),
            jnp.concatenate([arrived, value], axis=dim),
        )
        step *= 2
    return value


def after(value, event):
    return lax.optimization_barrier((value, event))


def chunk_sizes(block):
    return [block // 2, block // 2] if block % 1024 == 0 else [block]


def shards(sizes, counts, tile_mask, tile_counts, gene_factor, prev_factor):
    cells, genes, subs = sizes
    rows, columns = counts.shape
    width = gene_factor.shape[0]
    tile = rows // tile_mask.shape[0]
    sub = lax.axis_index("sub")
    cell = lax.axis_index("cell")
    gene = lax.axis_index("gene")
    line = Line(cells, cell)
    places = [sub, cell, sub * genes + gene, line.block(1, 0), line.block(2, 0)]
    places += [gene * subs + sub, gene]
    at_phases = len(places)
    places += [line.block(phase, parity) for phase in range(2, cells) for parity in (0, 1)]
    meta = jnp.stack(places).astype(jnp.int32)
    factor = tile_mask.astype(F32) / tile_counts.astype(F32)

    gram = contract_last(gene_factor, gene_factor)
    factor, gram = after(factor, gram)
    gram = pair_sums(gram, "gene", genes)
    wide = min(1024, columns)
    steps = columns // wide
    early = max(steps * 3 // 4, 1)
    (early_total,) = cross_part(
        0, early, wide, tile, meta, factor, counts, gene_factor, None
    )
    early_total, gram = after(early_total, gram)
    gram_other = swap(gram, "sub", subs, 1)
    theirs, mine = cross_part(
        early, steps - early, wide, tile, meta, factor, counts, gene_factor, early_total
    )
    cross = mine + swap(theirs, "sub", subs, 1)
    cross_a, cross_b = split_sums(cross, "gene", genes)
    inverse, rho = shifted_inverse(gram, gram_other)
    share = admm(meta, rho, cross_a, cross_b, inverse, prev_factor)
    own = join(share, "gene", genes, 1)
    other = swap(own, "sub", subs, 1)
    whole = jnp.where(
        sub == 0,
        jnp.concatenate([own, other], axis=1),
        jnp.concatenate([other, own], axis=1),
    )

    block = columns // cells
    chunks = chunk_sizes(block)
    starts = [sum(chunks[:i]) for i in range(len(chunks))]
    every = range(len(chunks))

    arrived = {}

    def send(value, phase, parity, index):
        pairs = line.pairs(phase, parity)
        arrived[phase, parity, index] = lax.ppermute(value, "cell", pairs) if pairs else None

    def resend(meta, phase, parity, index):
        before = arrived[phase - 1, 1 - parity, index]
        if before is None:
            value = seconds[index]
        else:
            slot = at_phases + 2 * (phase - 2) + parity
            value = operand(slot, meta, totals[index], before)
            meta, value = after(meta, value)
        send(value, phase, parity, index)
        return meta

    hops = [1 << i for i in range((cells - 1).bit_length())]

    def add_rows(meta, rows_sum):
        rows_arrived = swap(rows_sum, "cell", cells, hops.pop(0))
        return after(meta, plus(BF16 if hops else F32, meta, rows_sum, rows_arrived))

    def stack_rows(meta, rows_sum, axis, size, slot, bit):
        rows_arrived = swap(rows_sum, axis, size, bit)
        return after(meta, stack(slot, bit, meta, rows_sum, rows_arrived))

    meta, rows_sum = after(meta, row_share(5, width // (genes * subs), meta, whole))
    for index in every:
        (first,) = products(
            True, cells, starts[index], chunks[index], tile, meta, factor, counts, whole
        )
        meta, first = after(meta, first)
        for parity in (0, 1):
            send(first, 1, parity, index)
        if index == 0:
            meta, rows_sum = add_rows(meta, rows_sum)
    totals, seconds = [], []
    for index in every:
        total, second = products(
            False, cells, starts[index], chunks[index], tile, meta, factor, counts, whole
        )
        meta, second = after(meta, second)
        totals.append(total)
        seconds.append(second)
        for parity in (0, 1):
            meta = resend(meta, 2, parity, index)
    while hops:
        meta, rows_sum = add_rows(meta, rows_sum)
    new_factor = turn(meta, whole)
    meta, new_factor = after(meta, new_factor)
    meta, rows_sum = stack_rows(meta, rows_sum, "sub", subs, 0, 1)
    bits = [1 << i for i in range((genes - 1).bit_length())]
    for phase in range(3, cells):
        for index in every:
            for parity in (0, 1):
                meta = resend(meta, phase, parity, index)
                if bits:
                    meta, rows_sum = stack_rows(meta, rows_sum, "gene", genes, 6, bits.pop(0))
    data_products = None
    last = cells - 1
    for index in every:
        data_products = keep(
            block, starts[index], meta, totals[index],
            arrived[last, 0, index], arrived[last, 1, index], data_products,
        )
        meta, data_products = after(meta, data_products)
    return (new_factor, rows_sum, data_products)


def solution(mesh):
    sizes = (mesh.shape["cell"], mesh.shape["gene"], mesh.shape["sub"])
    return jax.shard_map(
        functools.partial(shards, sizes),
        mesh=mesh,
        in_specs=(
            P(("groups", "cell"), ("gene", "sub")),
            P(("groups", "cell"), ("gene", "sub")),
            P(("groups", "cell"), ("gene", "sub")),
            P("groups", ("gene", "sub")),
            P(("groups", "cell"), None),
        ),
        out_specs=(
            P(("groups", "cell"), None),
            P("groups", None),
            P(("groups", "gene", "sub", "cell"), None),
        ),
        check_vma=False,
    )
```

```python
import functools

import jax
import jax.numpy as jnp
import numpy as np
from jax import lax
from jax.experimental import pallas as pl
from jax.experimental.pallas import tpu as pltpu
from jax.sharding import PartitionSpec as P

ITERS = 3
F32 = jnp.float32
BF16 = jnp.bfloat16
MIB = 1024 * 1024


def params(limit=48):
    return pltpu.CompilerParams(vmem_limit_bytes=limit * MIB)


def cost(flops, bytes_accessed):
    return pl.CostEstimate(flops=flops, bytes_accessed=bytes_accessed, transcendentals=0)


def contract_last(left, right):
    return lax.dot_general(
        left, right, (((1,), (1,)), ((), ())), preferred_element_type=F32
    )


def gram_kernel(pieces, *refs):
    genes, (tile_mask, tile_counts, gram, factor) = refs[:pieces], refs[pieces:]
    part = None
    for piece in genes:
        product = contract_last(piece[...], piece[...])
        part = product if part is None else part + product

    @pl.when(pl.program_id(0) == 0)
    def _():
        gram[...] = part
        factor[...] = tile_mask[...].astype(F32) / tile_counts[...].astype(F32)

    @pl.when(pl.program_id(0) > 0)
    def _():
        gram[...] += part


def gram_part(genes, tile_mask, tile_counts):
    width, columns = genes.shape
    wide = min(1024, columns)
    pieces = min(4, columns // wide)
    tiles = pl.BlockSpec(tile_mask.shape, lambda i: (0, 0))
    return pl.pallas_call(
        functools.partial(gram_kernel, pieces),
        out_shape=(
            jax.ShapeDtypeStruct((width, width), F32),
            jax.ShapeDtypeStruct(tile_mask.shape, F32),
        ),
        grid=(columns // (wide * pieces),),
        in_specs=[
            pl.BlockSpec((width, wide), lambda i, p=p: (0, i * pieces + p))
            for p in range(pieces)
        ]
        + [tiles, tiles],
        out_specs=(pl.BlockSpec((width, width), lambda i: (0, 0)), tiles),
        compiler_params=params(60),
        cost_estimate=cost(1, 1),
        name="gram",
    )(*[genes] * pieces, tile_mask, tile_counts)


def row_tile_specs(row_tiles, tile, wide, place):
    return [
        pl.BlockSpec((tile, wide), lambda *ids, r=r: (r, place(*ids)))
        for r in range(row_tiles)
    ]


def cross_kernel(tile, first, row_tiles, last, meta, factor, *refs):
    counts, refs = refs[:row_tiles], refs[row_tiles:]
    genes, refs = refs[0], refs[1:]
    before, outs, total = (None, refs[:1], refs[1]) if not last else (refs[0], refs[1:3], refs[3])
    step = pl.program_id(0)
    gene_tiles = genes.shape[1] // tile

    @pl.when(step == 0)
    def _():
        total[...] = jnp.zeros_like(total) if before is None else before[...]

    for row in range(row_tiles):
        rows = pl.ds(row * tile, tile)
        part = total[rows, :]
        for col in range(gene_tiles):
            at = pl.ds(col * tile, tile)
            scale = factor[row, (first + step) * gene_tiles + col]
            part += scale * contract_last(counts[row][:, at], genes[:, at])
        total[rows, :] = part

    @pl.when(step == pl.num_programs(0) - 1)
    def _():
        if not last:
            outs[0][...] = total[...]
        else:
            half = total.shape[0] // 2
            sub = meta[0]
            outs[0][...] = total[pl.ds(pl.multiple_of((1 - sub) * half, half), half), :]
            outs[1][...] = total[pl.ds(pl.multiple_of(sub * half, half), half), :]


def cross_part(first, steps, wide, tile, meta, factor, counts, genes, before):
    rows, columns = counts.shape
    width = genes.shape[0]
    row_tiles = rows // tile
    last = before is not None
    whole = lambda n: pl.BlockSpec((n, width), lambda i, m: (0, 0))
    sizes = (rows // 2, rows // 2) if last else (rows,)
    return pl.pallas_call(
        functools.partial(cross_kernel, tile, first, row_tiles, last),
        out_shape=tuple(jax.ShapeDtypeStruct((n, width), F32) for n in sizes),
        grid_spec=pltpu.PrefetchScalarGridSpec(
            num_scalar_prefetch=1,
            grid=(steps,),
            in_specs=[pl.BlockSpec(memory_space=pltpu.SMEM)]
            + row_tile_specs(row_tiles, tile, wide, lambda i, m: first + i)
            + [pl.BlockSpec((width, wide), lambda i, m: (0, first + i))]
            + ([whole(rows)] if last else []),
            out_specs=tuple(whole(n) for n in sizes),
            scratch_shapes=[pltpu.VMEM((rows, width), F32)],
        ),
        compiler_params=params(56),
        cost_estimate=cost(1, 1),
        name="cross",
    )(meta, factor, *[counts] * row_tiles, genes, *([before] if last else []))


def halves(value):
    high = value.astype(BF16)
    return high, (value - high.astype(F32)).astype(BF16)


def product3(left, right):
    left_high, left_low = left
    right_high, right_low = right
    dot = functools.partial(jnp.dot, preferred_element_type=F32)
    return dot(left_high, right_high) + (
        dot(left_high, right_low) + dot(left_low, right_high)
    )


def inverse_kernel(gram_a, gram_b, inverse, rho_out):
    gram = gram_a[...] + gram_b[...]
    width = gram.shape[0]
    shape = (width, width)
    diagonal = lax.broadcasted_iota(jnp.int32, shape, 0) == lax.broadcasted_iota(
        jnp.int32, shape, 1
    )
    eye = jnp.where(diagonal, 1.0, 0.0).astype(F32)
    rho = jnp.sum(gram * eye) / width
    rho_out[0, 0] = rho
    scale = 1.0 / jnp.full((1, 1), rho, F32)
    matrix = gram * scale + eye
    low = 2.0 / (width + 2.0)
    guess = low * eye
    image = low * matrix
    first = True
    while True:
        low = low * (2.0 - low)
        gain = 2.0 / (1.0 + low)
        low = gain * low
        done = 1.0 - low < 2e-3
        step = halves(gain * (2.0 * eye - image))
        if first:
            guess = guess[0:1, 0:1] * (gain * (2.0 * eye - image))
        else:
            guess = product3(halves(guess), step)
        first = False
        if done:
            break
        image = product3(halves(image), step)
    rest = eye - jnp.dot(
        matrix, guess, preferred_element_type=F32, precision=lax.Precision.HIGHEST
    )
    rest_halves = halves(rest)
    series = rest + product3(rest_halves, rest_halves)
    inverse[...] = (guess + product3(halves(guess), halves(series))) * scale


def shifted_inverse(gram_a, gram_b):
    width = gram_a.shape[0]
    whole = pl.BlockSpec(memory_space=pltpu.VMEM)
    return pl.pallas_call(
        inverse_kernel,
        out_shape=(
            jax.ShapeDtypeStruct((width, width), F32),
            jax.ShapeDtypeStruct((1, 1), F32),
        ),
        in_specs=[whole, whole],
        out_specs=(whole, pl.BlockSpec(memory_space=pltpu.SMEM)),
        compiler_params=params(),
        cost_estimate=cost(2 * 60 * width**3, 12 * width**2),
        name="inverse",
    )(gram_a, gram_b)


def admm_kernel(meta, rho_ref, cross_a, cross_b, inverse, start, columns_out):
    rho = rho_ref[0, 0]
    cross = cross_a[...] + cross_b[...]
    inverse_halves = halves(inverse[...])
    zvalue = start[...].astype(F32)
    uvalue = jnp.zeros_like(zvalue)
    for _ in range(ITERS):
        vvalue = product3(halves(cross + rho * (zvalue - uvalue)), inverse_halves)
        zvalue = jnp.maximum(vvalue + uvalue, 0.0)
        uvalue = uvalue + vvalue - zvalue
    columns_out[...] = zvalue.T.astype(BF16)


def admm(meta, rho, cross_a, cross_b, inverse, start):
    rows, width = cross_a.shape
    tall = lambda: pl.BlockSpec((rows, width), lambda i, m: (0, 0))
    return pl.pallas_call(
        admm_kernel,
        out_shape=jax.ShapeDtypeStruct((width, rows), BF16),
        grid_spec=pltpu.PrefetchScalarGridSpec(
            num_scalar_prefetch=1,
            grid=(1,),
            in_specs=[
                pl.BlockSpec(memory_space=pltpu.SMEM),
                tall(),
                tall(),
                pl.BlockSpec((width, width), lambda i, m: (0, 0)),
                pl.BlockSpec((rows, width), lambda i, m: (m[2], 0)),
            ],
            out_specs=pl.BlockSpec((width, rows), lambda i, m: (0, 0)),
        ),
        compiler_params=params(),
        cost_estimate=cost(2 * 9 * rows * width**2, 12 * rows * width),
        name="admm",
    )(meta, rho, cross_a, cross_b, inverse, start)


def products_kernel(tile, wide, place, row_tiles, meta, factor, *refs):
    counts, columns, outs = refs[:row_tiles], refs[row_tiles], refs[row_tiles + 1 :]
    step, order = pl.program_id(0), pl.program_id(1)
    gene_tile = place(step, order, meta) * wide // tile
    span = min(tile, wide)
    for col in range(wide // span):
        at = pl.ds(col * span, span)
        total = None
        for row in range(row_tiles):
            part = jnp.dot(
                columns[:, pl.ds(row * tile, tile)],
                counts[row][:, at],
                preferred_element_type=F32,
            )
            part = factor[row, gene_tile + col] * part
            total = part if total is None else total + part
        total = total.astype(BF16)
        if len(outs) == 1:
            outs[0][:, at] = total
        else:
            outs[0][0, :, at] = total

            @pl.when(order == meta[4])
            def _(at=at, total=total):
                outs[1][:, at] = total


def products(only_first, cells, start, chunk, tile, meta, factor, counts, columns):
    rows = counts.shape[0]
    width = columns.shape[0]
    block = counts.shape[1] // cells
    blocks = 1 if only_first else cells
    wide = 2 * tile if chunk % (2 * tile) == 0 else min(tile, chunk)
    row_tiles = rows // tile

    def place(i, o, m):
        return (m[3] if only_first else o) * (block // wide) + start // wide + i

    flat = pl.BlockSpec((width, wide), lambda i, o, m: (0, i))
    operand = jax.ShapeDtypeStruct((width, chunk), BF16)
    if only_first:
        out_shape, out_specs = (operand,), (flat,)
    else:
        out_shape = (jax.ShapeDtypeStruct((cells, width, chunk), BF16), operand)
        out_specs = (pl.BlockSpec((1, width, wide), lambda i, o, m: (o, 0, i)), flat)
    return pl.pallas_call(
        functools.partial(products_kernel, tile, wide, place, row_tiles),
        out_shape=out_shape,
        grid_spec=pltpu.PrefetchScalarGridSpec(
            num_scalar_prefetch=1,
            grid=(chunk // wide, blocks),
            in_specs=[pl.BlockSpec(memory_space=pltpu.SMEM)]
            + row_tile_specs(row_tiles, tile, wide, place)
            + [pl.BlockSpec((width, rows), lambda i, o, m: (0, 0))],
            out_specs=out_specs,
        ),
        compiler_params=params(50),
        cost_estimate=cost(1, 1),
        name="products",
    )(meta, factor, *[counts] * row_tiles, columns)


def small(kernel, name, out_shape, meta, *args, specs=None):
    whole = lambda shape: pl.BlockSpec(shape, lambda i, m: (0,) * len(shape))
    return pl.pallas_call(
        kernel,
        out_shape=out_shape,
        grid_spec=pltpu.PrefetchScalarGridSpec(
            num_scalar_prefetch=1,
            grid=(1,),
            in_specs=specs or [whole(arg.shape) for arg in args],
            out_specs=whole(out_shape.shape),
        ),
        compiler_params=params(24),
        cost_estimate=cost(1, 1),
        name=name,
    )(meta, *args)


def turn_kernel(meta, value, out):
    out[...] = value[...].astype(F32).T.astype(out.dtype)


def turn(meta, value):
    shape = jax.ShapeDtypeStruct(value.shape[::-1], value.dtype)
    return small(turn_kernel, "turn", shape, meta, value)


def row_share_kernel(meta, share, columns, out):
    out[...] = contract_last(share[...], columns[...]).astype(out.dtype)


def row_share(slot, part, meta, columns):
    width, rows = columns.shape
    specs = [
        pl.BlockSpec((part, rows), lambda i, m: (m[slot], 0)),
        pl.BlockSpec((width, rows), lambda i, m: (0, 0)),
    ]
    shape = jax.ShapeDtypeStruct((part, width), BF16)
    return small(row_share_kernel, "row_share", shape, meta, columns, columns, specs=specs)


def hop_kernel(kind, targets, meta, held, arrived, out):
    reached = meta[1] == targets[0]
    for target in targets[1:]:
        reached = jnp.logical_or(reached, meta[1] == target)
    more = arrived[...].astype(F32)
    base = held[...].astype(F32)
    value = base + more if kind == "sum" else more
    out[...] = jnp.where(reached, value, base).astype(out.dtype)


def hop(kind, targets, meta, held, arrived):
    shape = jax.ShapeDtypeStruct(held.shape, held.dtype)
    return small(functools.partial(hop_kernel, kind, targets), "hop", shape, meta, held, arrived)


def stack_kernel(slot, bit, meta, mine, theirs, out):
    rows = mine.shape[0]
    upper = (meta[slot] & bit) != 0
    out[:rows] = jnp.where(upper, theirs[...], mine[...])
    out[rows:] = jnp.where(upper, mine[...], theirs[...])


def stack(slot, bit, meta, mine, theirs):
    shape = jax.ShapeDtypeStruct((2 * mine.shape[0],) + mine.shape[1:], mine.dtype)
    return small(functools.partial(stack_kernel, slot, bit), "stack", shape, meta, mine, theirs)


def operand_kernel(meta, total, before, out):
    out[...] = (total[0].astype(F32) + before[...].astype(F32)).astype(BF16)


def operand(slot, meta, total, before):
    width, chunk = before.shape
    flat = lambda: pl.BlockSpec((width, chunk), lambda i, m: (0, 0))
    return pl.pallas_call(
        operand_kernel,
        out_shape=jax.ShapeDtypeStruct((width, chunk), BF16),
        grid_spec=pltpu.PrefetchScalarGridSpec(
            num_scalar_prefetch=1,
            grid=(1,),
            in_specs=[
                pl.BlockSpec((1, width, chunk), lambda i, m: (m[slot], 0, 0)),
                flat(),
            ],
            out_specs=flat(),
        ),
        compiler_params=params(24),
        cost_estimate=cost(1, 1),
        name="operand",
    )(meta, total, before)


def keep_kernel(meta, total, first, second, *refs):
    value = total[0].astype(F32) + (first[...].astype(F32) + second[...].astype(F32))
    refs[-1][...] = value.T


def keep(block, start, meta, totals, first, second, out):
    width, chunk = first.shape
    wide = min(512, chunk)
    piece = lambda: pl.BlockSpec((width, wide), lambda i, m: (0, i))
    extra = [] if out is None else [out]
    return pl.pallas_call(
        keep_kernel,
        out_shape=jax.ShapeDtypeStruct((block, width), F32),
        grid_spec=pltpu.PrefetchScalarGridSpec(
            num_scalar_prefetch=1,
            grid=(chunk // wide,),
            in_specs=[
                pl.BlockSpec((1, width, wide), lambda i, m: (m[1], 0, i)),
                piece(),
                piece(),
            ]
            + [pl.BlockSpec(memory_space=pl.ANY) for _ in extra],
            out_specs=pl.BlockSpec((wide, width), lambda i, m: (start // wide + i, 0)),
        ),
        input_output_aliases={4: 0} if extra else {},
        compiler_params=params(24),
        cost_estimate=cost(1, 1),
        name="keep",
    )(meta, totals, first, second, *extra)


class Line:
    def __init__(self, size, cell):
        self.size = size
        self.cell = cell

    def pairs(self, phase, parity):
        links = range(parity, self.size - 1, 2)
        right = [(i, i + 1) for i in links if i < phase]
        left = [(i + 1, i) for i in links if i + 1 >= self.size - phase]
        return right + left

    def block(self, phase, parity):
        to_right = (self.cell & 1) == parity
        block = self.cell + jnp.where(to_right, self.size - phase, phase)
        return jnp.where(block >= self.size, block - self.size, block)

    def send(self, value, phase, parity):
        return lax.ppermute(value, "cell", self.pairs(phase, parity))


def swap(value, axis, size, step):
    return lax.ppermute(value, axis, [(i, i ^ step) for i in range(size)])


def pair_sums(value, axis, size):
    step = 1
    while step < size:
        value = value + swap(value, axis, size, step)
        step *= 2
    return value


def split_sums(value, axis, size):
    index = lax.axis_index(axis)
    step = size // 2
    while True:
        upper = (index & step) != 0
        low, high = jnp.split(value, 2, axis=0)
        kept = jnp.where(upper, high, low)
        arrived = swap(jnp.where(upper, low, high), axis, size, step)
        step //= 2
        if step == 0:
            return kept, arrived
        value = kept + arrived


def join(value, axis, size, dim):
    index = lax.axis_index(axis)
    step = 1
    while step < size:
        arrived = swap(value, axis, size, step)
        value = jnp.where(
            (index & step) == 0,
            jnp.concatenate([value, arrived], axis=dim),
            jnp.concatenate([arrived, value], axis=dim),
        )
        step *= 2
    return value


def after(value, event):
    return lax.optimization_barrier((value, event))


def chunk_sizes(block):
    return [block // 2, block // 2] if block % 1024 == 0 else [block]


def shards(sizes, counts, tile_mask, tile_counts, gene_factor, prev_factor):
    cells, genes, subs = sizes
    rows, columns = counts.shape
    width = gene_factor.shape[0]
    tile = rows // tile_mask.shape[0]
    sub = lax.axis_index("sub")
    cell = lax.axis_index("cell")
    gene = lax.axis_index("gene")
    line = Line(cells, cell)
    blocks = [(1, 0), (2, 0)]
    blocks += [(phase, parity) for phase in range(2, cells) for parity in (0, 1)]
    at_phases = 8
    table = np.zeros((5, at_phases + len(blocks) - 2), np.int32)
    table[1, [0, 5]] = 1
    table[1, 2] = genes
    table[2, 1] = 1
    table[3, [2, 6]] = 1
    table[3, 5] = subs
    for slot, (phase, parity) in zip([3, 4, *range(at_phases, table.shape[1])], blocks):
        ahead = cells - 2 * phase
        table[:, slot] = [phase + (1 - parity) * ahead, 0, 1, 0, (2 * parity - 1) * ahead]
    is_block = np.zeros(table.shape[1], bool)
    is_block[[3, 4, *range(at_phases, table.shape[1])]] = True
    meta = table[0] + sub * table[1] + cell * table[2] + gene * table[3]
    meta = meta + (cell & 1) * table[4]
    meta = jnp.where(is_block & (meta >= cells), meta - cells, meta).astype(jnp.int32)

    gram, factor = gram_part(gene_factor, tile_mask, tile_counts)
    meta, gram = after(meta, gram)
    gram = pair_sums(gram, "gene", genes)
    wide = min(1024, columns)
    steps = columns // wide
    early = max(steps * 3 // 4, 1)
    (early_total,) = cross_part(
        0, early, wide, tile, meta, factor, counts, gene_factor, None
    )
    early_total, gram = after(early_total, gram)
    gram_other = swap(gram, "sub", subs, 1)
    theirs, mine = cross_part(
        early, steps - early, wide, tile, meta, factor, counts, gene_factor, early_total
    )
    cross = mine + swap(theirs, "sub", subs, 1)
    cross_a, cross_b = split_sums(cross, "gene", genes)
    inverse, rho = shifted_inverse(gram, gram_other)
    share = admm(meta, rho, cross_a, cross_b, inverse, prev_factor)
    own = join(share, "gene", genes, 1)
    other = swap(own, "sub", subs, 1)
    whole = jnp.where(
        sub == 0,
        jnp.concatenate([own, other], axis=1),
        jnp.concatenate([other, own], axis=1),
    )

    block = columns // cells
    chunks = chunk_sizes(block)
    starts = [sum(chunks[:i]) for i in range(len(chunks))]
    every = range(len(chunks))

    arrived = {}

    def send(value, phase, parity, index):
        pairs = line.pairs(phase, parity)
        arrived[phase, parity, index] = lax.ppermute(value, "cell", pairs) if pairs else None

    def resend(meta, phase, parity, index):
        before = arrived[phase - 1, 1 - parity, index]
        if before is None:
            value = seconds[index]
        else:
            slot = at_phases + 2 * (phase - 2) + parity
            value = operand(slot, meta, totals[index], before)
            meta, value = after(meta, value)
        send(value, phase, parity, index)
        return meta

    middle = cells // 2
    inward = [[(i, i + 1), (cells - 1 - i, cells - 2 - i)] for i in range(middle - 1)]
    outward = [[(b, a) for a, b in pairs] for pairs in reversed(inward)]
    hops = [("sum", p) for p in inward] + [("sum", [(middle - 1, middle), (middle, middle - 1)])]
    hops += [("copy", p) for p in outward]

    def hop_rows(meta, rows_sum):
        kind, pairs = hops.pop(0)
        rows_arrived = lax.ppermute(rows_sum, "cell", pairs)
        targets = [b for _, b in pairs]
        return after(meta, hop(kind, targets, meta, rows_sum, rows_arrived))

    def stack_rows(meta, rows_sum, axis, size, slot, bit):
        rows_arrived = swap(rows_sum, axis, size, bit)
        return after(meta, stack(slot, bit, meta, rows_sum, rows_arrived))

    meta, rows_sum = after(meta, row_share(5, width // (genes * subs), meta, whole))
    for index in every:
        (first,) = products(
            True, cells, starts[index], chunks[index], tile, meta, factor, counts, whole
        )
        meta, first = after(meta, first)
        for parity in (0, 1):
            send(first, 1, parity, index)
        if index == 0 and hops:
            meta, rows_sum = hop_rows(meta, rows_sum)
    totals, seconds = [], []
    for index in every:
        total, second = products(
            False, cells, starts[index], chunks[index], tile, meta, factor, counts, whole
        )
        meta, second = after(meta, second)
        if hops:
            meta, rows_sum = hop_rows(meta, rows_sum)
        totals.append(total)
        seconds.append(second)
        for parity in (0, 1):
            meta = resend(meta, 2, parity, index)
    while hops:
        meta, rows_sum = hop_rows(meta, rows_sum)
    new_factor = turn(meta, whole)
    meta, new_factor = after(meta, new_factor)
    meta, rows_sum = stack_rows(meta, rows_sum, "sub", subs, 0, 1)
    bits = [1 << i for i in range((genes - 1).bit_length())]
    for phase in range(3, cells):
        for index in every:
            for parity in (1, 0):
                meta = resend(meta, phase, parity, index)
                if bits:
                    meta, rows_sum = stack_rows(meta, rows_sum, "gene", genes, 6, bits.pop(0))
    data_products = None
    last = cells - 1
    for index in every:
        data_products = keep(
            block, starts[index], meta, totals[index],
            arrived[last, 0, index], arrived[last, 1, index], data_products,
        )
        meta, data_products = after(meta, data_products)
    return (new_factor, rows_sum.astype(F32), data_products)


def solution(mesh):
    sizes = (mesh.shape["cell"], mesh.shape["gene"], mesh.shape["sub"])
    return jax.shard_map(
        functools.partial(shards, sizes),
        mesh=mesh,
        in_specs=(
            P(("groups", "cell"), ("gene", "sub")),
            P(("groups", "cell"), ("gene", "sub")),
            P(("groups", "cell"), ("gene", "sub")),
            P("groups", ("gene", "sub")),
            P(("groups", "cell"), None),
        ),
        out_specs=(
            P(("groups", "cell"), None),
            P("groups", None),
            P(("groups", "gene", "sub", "cell"), None),
        ),
        check_vma=False,
    )
```

```python
import functools

import jax
import jax.numpy as jnp
import numpy as np
from jax import lax
from jax.experimental import pallas as pl
from jax.experimental.pallas import tpu as pltpu
from jax.sharding import PartitionSpec as P

ITERS = 3
F32 = jnp.float32
BF16 = jnp.bfloat16
MIB = 1024 * 1024


def params(limit=16):
    return pltpu.CompilerParams(vmem_limit_bytes=limit * MIB)


def away(value):
    return pltpu.with_memory_space_constraint(value, pltpu.HBM)


def held(value):
    return pltpu.with_memory_space_constraint(value, pltpu.VMEM)


def cost(flops, bytes_accessed):
    return pl.CostEstimate(flops=flops, bytes_accessed=bytes_accessed, transcendentals=0)


def contract_last(left, right):
    return lax.dot_general(
        left, right, (((1,), (1,)), ((), ())), preferred_element_type=F32
    )


def row_copies(source, target, first, sems):
    rows = target.shape[0]
    piece = max(rows // sems.shape[0], 16)
    return [
        pltpu.make_async_copy(
            source.at[pl.ds(first + i * piece, piece)],
            target.at[pl.ds(i * piece, piece)],
            sems.at[i],
        )
        for i in range(rows // piece)
    ]


def gram_kernel(tile, genes, counts, tile_mask, tile_counts, gram, factor, genes_held, head, sems_a, sems_b):
    gene_copies = row_copies(genes, genes_held, 0, sems_a)
    head_copies = row_copies(counts, head, 0, sems_b)
    for copy in gene_copies + head_copies:
        copy.start()
    factor[...] = tile_mask[...].astype(F32) / tile_counts[...].astype(F32)
    for copy in gene_copies:
        copy.wait()
    columns = genes.shape[1]
    wide = min(1024, columns)
    part = None
    for start in range(0, columns, wide):
        piece = genes_held[:, start : start + wide]
        product = contract_last(piece, piece)
        part = product if part is None else part + product
    gram[...] = part
    for copy in head_copies:
        copy.wait()


def gram_part(genes, counts, tile, tile_mask, tile_counts):
    width, columns = genes.shape
    here = pl.BlockSpec(memory_space=pltpu.VMEM)
    there = pl.BlockSpec(memory_space=pltpu.HBM)
    return pl.pallas_call(
        functools.partial(gram_kernel, tile),
        out_shape=(
            jax.ShapeDtypeStruct((width, width), F32),
            jax.ShapeDtypeStruct(tile_mask.shape, F32),
            pltpu.VMEM((width, columns), BF16),
            pltpu.VMEM((tile, columns), BF16),
        ),
        in_specs=[there, there, here, here],
        out_specs=(here,) * 4,
        scratch_shapes=[pltpu.SemaphoreType.DMA((4,)), pltpu.SemaphoreType.DMA((4,))],
        compiler_params=params(16),
        cost_estimate=cost(1, 1),
        name="gram",
    )(away(genes), away(counts), tile_mask, tile_counts)


def cross_rows(tile, row, factor, counts, genes):
    gene_tiles = counts.shape[1] // tile
    at_once = min(4, gene_tiles)

    def body(step, part):
        for col in range(at_once):
            place = step * at_once + col
            at = pl.ds(pl.multiple_of(place * tile, tile), tile)
            part += factor[row, place] * contract_last(counts[:, at], genes[:, at])
        return part

    start = jnp.zeros((tile, genes.shape[0]), F32)
    return lax.fori_loop(0, gene_tiles // at_once, body, start)


def cross_early_kernel(tile, factor, head, counts, genes, total, tail, sems):
    rows = tail.shape[0]
    copies = row_copies(counts, tail, tile, sems)
    per_tile = len(copies) // (rows // tile)
    for copy in copies:
        copy.start()
    total[:tile] = cross_rows(tile, 0, factor, head, genes)
    for row in range(1, rows // tile + 1):
        for copy in copies[(row - 1) * per_tile : row * per_tile]:
            copy.wait()
        if row * tile < rows:
            at = slice((row - 1) * tile, row * tile)
            total[row * tile : (row + 1) * tile] = cross_rows(
                tile, row, factor, tail.at[at], genes
            )


def cross_early(tile, factor, head, counts, genes):
    rows, columns = counts.shape
    width = genes.shape[0]
    here = pl.BlockSpec(memory_space=pltpu.VMEM)
    return pl.pallas_call(
        functools.partial(cross_early_kernel, tile),
        out_shape=(
            jax.ShapeDtypeStruct((rows - tile, width), F32),
            pltpu.VMEM((rows - tile, columns), BF16),
        ),
        in_specs=[
            pl.BlockSpec(memory_space=pltpu.SMEM),
            here,
            pl.BlockSpec(memory_space=pltpu.HBM),
            here,
        ],
        out_specs=(here, here),
        scratch_shapes=[pltpu.SemaphoreType.DMA((4 * (rows // tile - 1),))],
        compiler_params=params(16),
        cost_estimate=cost(1, 1),
        name="cross_early",
    )(factor, held(head), away(counts), held(genes))


def cross_late_kernel(tile, meta, factor, early, tail, genes, theirs, mine):
    rows = early.shape[0]
    half = theirs.shape[0]
    last = cross_rows(tile, rows // tile, factor, tail.at[rows - tile :], genes)

    def put(low, high):
        low[...] = early[:half]
        high[: half - tile] = early[half:]
        high[half - tile :] = last

    @pl.when(meta[0] == 0)
    def _():
        put(mine, theirs)

    @pl.when(meta[0] != 0)
    def _():
        put(theirs, mine)


def cross_late(tile, meta, factor, early, tail, genes):
    rows, width = early.shape
    half = jax.ShapeDtypeStruct(((rows + tile) // 2, width), F32)
    here = pl.BlockSpec(memory_space=pltpu.VMEM)
    there = pl.BlockSpec(memory_space=pltpu.SMEM)
    return pl.pallas_call(
        functools.partial(cross_late_kernel, tile),
        out_shape=(half, half),
        in_specs=[there, there, here, here, here],
        out_specs=(here, here),
        compiler_params=params(16),
        cost_estimate=cost(1, 1),
        name="cross_late",
    )(meta, factor, early, held(tail), held(genes))


def halves(value):
    high = value.astype(BF16)
    return high, (value - high.astype(F32)).astype(BF16)


def product3(left, right):
    left_high, left_low = left
    right_high, right_low = right
    dot = functools.partial(jnp.dot, preferred_element_type=F32)
    return dot(left_high, right_high) + (
        dot(left_high, right_low) + dot(left_low, right_high)
    )


def inverse_kernel(gram_a, gram_b, inverse, rho_out):
    gram = gram_a[...] + gram_b[...]
    width = gram.shape[0]
    shape = (width, width)
    diagonal = lax.broadcasted_iota(jnp.int32, shape, 0) == lax.broadcasted_iota(
        jnp.int32, shape, 1
    )
    eye = jnp.where(diagonal, 1.0, 0.0).astype(F32)
    rho = jnp.sum(gram * eye) / width
    rho_out[0, 0] = rho
    scale = 1.0 / jnp.full((1, 1), rho, F32)
    matrix = gram * scale + eye
    low = 2.0 / (width + 2.0)
    guess = low * eye
    image = low * matrix
    first = True
    while True:
        low = low * (2.0 - low)
        gain = 2.0 / (1.0 + low)
        low = gain * low
        done = 1.0 - low < 2e-3
        step = halves(gain * (2.0 * eye - image))
        if first:
            guess = guess[0:1, 0:1] * (gain * (2.0 * eye - image))
        else:
            guess = product3(halves(guess), step)
        first = False
        if done:
            break
        image = product3(halves(image), step)
    rest = eye - jnp.dot(
        matrix, guess, preferred_element_type=F32, precision=lax.Precision.HIGHEST
    )
    rest_halves = halves(rest)
    series = rest + product3(rest_halves, rest_halves)
    inverse[...] = (guess + product3(halves(guess), halves(series))) * scale


def shifted_inverse(gram_a, gram_b):
    width = gram_a.shape[0]
    whole = pl.BlockSpec(memory_space=pltpu.VMEM)
    return pl.pallas_call(
        inverse_kernel,
        out_shape=(
            jax.ShapeDtypeStruct((width, width), F32),
            jax.ShapeDtypeStruct((1, 1), F32),
        ),
        in_specs=[whole, whole],
        out_specs=(whole, pl.BlockSpec(memory_space=pltpu.SMEM)),
        compiler_params=params(),
        cost_estimate=cost(2 * 60 * width**3, 12 * width**2),
        name="inverse",
    )(gram_a, gram_b)


def admm_kernel(meta, rho_ref, cross_a, cross_b, inverse, start, columns_out):
    rho = rho_ref[0, 0]
    cross = cross_a[...] + cross_b[...]
    inverse_halves = halves(inverse[...])
    zvalue = start[...].astype(F32)
    uvalue = jnp.zeros_like(zvalue)
    for _ in range(ITERS):
        vvalue = product3(halves(cross + rho * (zvalue - uvalue)), inverse_halves)
        zvalue = jnp.maximum(vvalue + uvalue, 0.0)
        uvalue = uvalue + vvalue - zvalue
    columns_out[...] = zvalue.T.astype(BF16)


def admm(meta, rho, cross_a, cross_b, inverse, start):
    rows, width = cross_a.shape
    tall = lambda: pl.BlockSpec((rows, width), lambda i, m: (0, 0))
    return pl.pallas_call(
        admm_kernel,
        out_shape=jax.ShapeDtypeStruct((width, rows), BF16),
        grid_spec=pltpu.PrefetchScalarGridSpec(
            num_scalar_prefetch=1,
            grid=(1,),
            in_specs=[
                pl.BlockSpec(memory_space=pltpu.SMEM),
                tall(),
                tall(),
                pl.BlockSpec((width, width), lambda i, m: (0, 0)),
                pl.BlockSpec((rows, width), lambda i, m: (m[2], 0)),
            ],
            out_specs=pl.BlockSpec((width, rows), lambda i, m: (0, 0)),
        ),
        compiler_params=params(),
        cost_estimate=cost(2 * 9 * rows * width**2, 12 * rows * width),
        name="admm",
    )(meta, rho, cross_a, cross_b, inverse, start)


def products_kernel(tile, block, start, chunk, meta, factor, head, tail, columns, *outs):
    only_first = len(outs) == 1
    span = min(tile, chunk)
    wide = 2 * span if chunk % (2 * span) == 0 else span
    steps = chunk // wide
    row_tiles = columns.shape[1] // tile
    blocks = 1 if only_first else outs[0].shape[0]

    @pl.loop(0, blocks * steps)
    def _(turn):
        order, step = (0, turn) if only_first else (turn // steps, lax.rem(turn, steps))
        place = meta[3] if only_first else order
        first = place * block + start + step * wide
        for col in range(wide // span):
            gene = pl.multiple_of(first + col * span, span)
            total = None
            for row in range(row_tiles):
                counts = head if row == 0 else tail.at[(row - 1) * tile : row * tile]
                part = jnp.dot(
                    columns[:, row * tile : (row + 1) * tile],
                    counts[:, pl.ds(gene, span)],
                    preferred_element_type=F32,
                )
                part = factor[row, gene // tile] * part
                total = part if total is None else total + part
            total = total.astype(BF16)
            at = pl.ds(pl.multiple_of(step * wide + col * span, span), span)
            if only_first:
                outs[0][:, at] = total
            else:
                outs[0][order, :, at] = total

                @pl.when(order == meta[4])
                def _(at=at, total=total):
                    outs[1][:, at] = total


def products(only_first, cells, start, chunk, tile, meta, factor, head, tail, columns):
    width = columns.shape[0]
    block = head.shape[1] // cells
    out_shape = (jax.ShapeDtypeStruct((width, chunk), BF16),)
    if not only_first:
        out_shape = (jax.ShapeDtypeStruct((cells, width, chunk), BF16),) + out_shape
    here = pl.BlockSpec(memory_space=pltpu.VMEM)
    there = pl.BlockSpec(memory_space=pltpu.SMEM)
    return pl.pallas_call(
        functools.partial(products_kernel, tile, block, start, chunk),
        out_shape=out_shape,
        in_specs=[there, there, here, here, here],
        out_specs=(here,) * len(out_shape),
        compiler_params=params(16),
        cost_estimate=cost(1, 1),
        name="products",
    )(meta, factor, held(head), held(tail), columns)


def small(kernel, name, out_shape, meta, *args, specs=None):
    whole = lambda shape: pl.BlockSpec(shape, lambda i, m: (0,) * len(shape))
    return pl.pallas_call(
        kernel,
        out_shape=out_shape,
        grid_spec=pltpu.PrefetchScalarGridSpec(
            num_scalar_prefetch=1,
            grid=(1,),
            in_specs=specs or [whole(arg.shape) for arg in args],
            out_specs=whole(out_shape.shape),
        ),
        compiler_params=params(16),
        cost_estimate=cost(1, 1),
        name=name,
    )(meta, *args)


def turn_kernel(meta, value, out):
    out[...] = value[...].astype(F32).T.astype(out.dtype)


def turn(meta, value):
    shape = jax.ShapeDtypeStruct(value.shape[::-1], value.dtype)
    return small(turn_kernel, "turn", shape, meta, value)


def row_share_kernel(meta, share, columns, out):
    out[...] = contract_last(share[...], columns[...]).astype(out.dtype)


def row_share(slot, part, meta, columns):
    width, rows = columns.shape
    specs = [
        pl.BlockSpec((part, rows), lambda i, m: (m[slot], 0)),
        pl.BlockSpec((width, rows), lambda i, m: (0, 0)),
    ]
    shape = jax.ShapeDtypeStruct((part, width), BF16)
    return small(row_share_kernel, "row_share", shape, meta, columns, columns, specs=specs)


def hop_kernel(kind, targets, meta, held, arrived, out):
    reached = meta[1] == targets[0]
    for target in targets[1:]:
        reached = jnp.logical_or(reached, meta[1] == target)
    more = arrived[...].astype(F32)
    base = held[...].astype(F32)
    value = base + more if kind == "sum" else more
    out[...] = jnp.where(reached, value, base).astype(out.dtype)


def hop(kind, targets, meta, held, arrived):
    shape = jax.ShapeDtypeStruct(held.shape, held.dtype)
    return small(functools.partial(hop_kernel, kind, targets), "hop", shape, meta, held, arrived)


def stack_kernel(slot, bit, meta, mine, theirs, out):
    rows = mine.shape[0]
    upper = (meta[slot] & bit) != 0
    out[:rows] = jnp.where(upper, theirs[...], mine[...])
    out[rows:] = jnp.where(upper, mine[...], theirs[...])


def stack(slot, bit, meta, mine, theirs):
    shape = jax.ShapeDtypeStruct((2 * mine.shape[0],) + mine.shape[1:], mine.dtype)
    return small(functools.partial(stack_kernel, slot, bit), "stack", shape, meta, mine, theirs)


def operand_kernel(meta, total, before, out):
    out[...] = (total[0].astype(F32) + before[...].astype(F32)).astype(BF16)


def operand(slot, meta, total, before):
    width, chunk = before.shape
    flat = lambda: pl.BlockSpec((width, chunk), lambda i, m: (0, 0))
    return pl.pallas_call(
        operand_kernel,
        out_shape=jax.ShapeDtypeStruct((width, chunk), BF16),
        grid_spec=pltpu.PrefetchScalarGridSpec(
            num_scalar_prefetch=1,
            grid=(1,),
            in_specs=[
                pl.BlockSpec((1, width, chunk), lambda i, m: (m[slot], 0, 0)),
                flat(),
            ],
            out_specs=flat(),
        ),
        compiler_params=params(16),
        cost_estimate=cost(1, 1),
        name="operand",
    )(meta, total, before)


def keep_kernel(meta, total, first, second, *refs):
    value = total[0].astype(F32) + (first[...].astype(F32) + second[...].astype(F32))
    refs[-1][...] = value.T


def keep(block, start, meta, totals, first, second, out):
    width, chunk = first.shape
    wide = min(512, chunk)
    piece = lambda: pl.BlockSpec((width, wide), lambda i, m: (0, i))
    extra = [] if out is None else [out]
    return pl.pallas_call(
        keep_kernel,
        out_shape=jax.ShapeDtypeStruct((block, width), F32),
        grid_spec=pltpu.PrefetchScalarGridSpec(
            num_scalar_prefetch=1,
            grid=(chunk // wide,),
            in_specs=[
                pl.BlockSpec((1, width, wide), lambda i, m: (m[1], 0, i)),
                piece(),
                piece(),
            ]
            + [pl.BlockSpec(memory_space=pl.ANY) for _ in extra],
            out_specs=pl.BlockSpec((wide, width), lambda i, m: (start // wide + i, 0)),
        ),
        input_output_aliases={4: 0} if extra else {},
        compiler_params=params(16),
        cost_estimate=cost(1, 1),
        name="keep",
    )(meta, totals, first, second, *extra)


class Line:
    def __init__(self, size, cell):
        self.size = size
        self.cell = cell

    def pairs(self, phase, parity):
        links = range(parity, self.size - 1, 2)
        right = [(i, i + 1) for i in links if i < phase]
        left = [(i + 1, i) for i in links if i + 1 >= self.size - phase]
        return right + left

    def block(self, phase, parity):
        to_right = (self.cell & 1) == parity
        block = self.cell + jnp.where(to_right, self.size - phase, phase)
        return jnp.where(block >= self.size, block - self.size, block)

    def send(self, value, phase, parity):
        return lax.ppermute(value, "cell", self.pairs(phase, parity))


def swap(value, axis, size, step):
    return lax.ppermute(value, axis, [(i, i ^ step) for i in range(size)])


def pair_sums(value, axis, size):
    step = 1
    while step < size:
        value = value + swap(value, axis, size, step)
        step *= 2
    return value


def split_sums(value, axis, size):
    index = lax.axis_index(axis)
    step = size // 2
    while True:
        upper = (index & step) != 0
        low, high = jnp.split(value, 2, axis=0)
        kept = jnp.where(upper, high, low)
        arrived = swap(jnp.where(upper, low, high), axis, size, step)
        step //= 2
        if step == 0:
            return kept, arrived
        value = kept + arrived


def join(value, axis, size, dim):
    index = lax.axis_index(axis)
    step = 1
    while step < size:
        arrived = swap(value, axis, size, step)
        value = jnp.where(
            (index & step) == 0,
            jnp.concatenate([value, arrived], axis=dim),
            jnp.concatenate([arrived, value], axis=dim),
        )
        step *= 2
    return value


def after(value, event):
    return lax.optimization_barrier((value, event))


def chunk_sizes(block):
    return [block // 2, block // 2] if block % 1024 == 0 else [block]


def shards(sizes, counts, tile_mask, tile_counts, gene_factor, prev_factor):
    cells, genes, subs = sizes
    rows, columns = counts.shape
    width = gene_factor.shape[0]
    tile = rows // tile_mask.shape[0]
    sub = lax.axis_index("sub")
    cell = lax.axis_index("cell")
    gene = lax.axis_index("gene")
    line = Line(cells, cell)
    blocks = [(1, 0), (2, 0)]
    blocks += [(phase, parity) for phase in range(2, cells) for parity in (0, 1)]
    at_phases = 8
    table = np.zeros((5, at_phases + len(blocks) - 2), np.int32)
    table[1, [0, 5]] = 1
    table[1, 2] = genes
    table[2, 1] = 1
    table[3, [2, 6]] = 1
    table[3, 5] = subs
    for slot, (phase, parity) in zip([3, 4, *range(at_phases, table.shape[1])], blocks):
        ahead = cells - 2 * phase
        table[:, slot] = [phase + (1 - parity) * ahead, 0, 1, 0, (2 * parity - 1) * ahead]
    is_block = np.zeros(table.shape[1], bool)
    is_block[[3, 4, *range(at_phases, table.shape[1])]] = True
    meta = table[0] + sub * table[1] + cell * table[2] + gene * table[3]
    meta = meta + (cell & 1) * table[4]
    meta = jnp.where(is_block & (meta >= cells), meta - cells, meta).astype(jnp.int32)

    gram, factor, genes_held, head = gram_part(
        gene_factor, counts, tile, tile_mask, tile_counts
    )
    gram = pair_sums(gram, "gene", genes)
    early, tail = cross_early(tile, factor, head, counts, genes_held)
    early, gram = after(early, gram)
    gram_other = swap(gram, "sub", subs, 1)
    theirs, mine = cross_late(tile, meta, factor, early, tail, genes_held)
    cross = mine + swap(theirs, "sub", subs, 1)
    cross_a, cross_b = split_sums(cross, "gene", genes)
    inverse, rho = shifted_inverse(gram, gram_other)
    share = admm(meta, rho, cross_a, cross_b, inverse, prev_factor)
    own = join(share, "gene", genes, 1)
    other = swap(own, "sub", subs, 1)
    whole = jnp.where(
        sub == 0,
        jnp.concatenate([own, other], axis=1),
        jnp.concatenate([other, own], axis=1),
    )

    block = columns // cells
    chunks = chunk_sizes(block)
    starts = [sum(chunks[:i]) for i in range(len(chunks))]
    every = range(len(chunks))

    arrived = {}

    def send(value, phase, parity, index):
        pairs = line.pairs(phase, parity)
        arrived[phase, parity, index] = lax.ppermute(value, "cell", pairs) if pairs else None

    def resend(meta, phase, parity, index):
        before = arrived[phase - 1, 1 - parity, index]
        if before is None:
            value = seconds[index]
        else:
            slot = at_phases + 2 * (phase - 2) + parity
            value = operand(slot, meta, totals[index], before)
            meta, value = after(meta, value)
        send(value, phase, parity, index)
        return meta

    middle = cells // 2
    inward = [[(i, i + 1), (cells - 1 - i, cells - 2 - i)] for i in range(middle - 1)]
    outward = [[(b, a) for a, b in pairs] for pairs in reversed(inward)]
    hops = [("sum", p) for p in inward] + [("sum", [(middle - 1, middle), (middle, middle - 1)])]
    hops += [("copy", p) for p in outward]

    def hop_rows(meta, rows_sum):
        kind, pairs = hops.pop(0)
        rows_arrived = lax.ppermute(rows_sum, "cell", pairs)
        targets = [b for _, b in pairs]
        return after(meta, hop(kind, targets, meta, rows_sum, rows_arrived))

    def stack_rows(meta, rows_sum, axis, size, slot, bit):
        rows_arrived = swap(rows_sum, axis, size, bit)
        return after(meta, stack(slot, bit, meta, rows_sum, rows_arrived))

    meta, rows_sum = after(meta, row_share(5, width // (genes * subs), meta, whole))
    for index in every:
        (first,) = products(
            True, cells, starts[index], chunks[index], tile, meta, factor, head, tail, whole
        )
        meta, first = after(meta, first)
        for parity in (0, 1):
            send(first, 1, parity, index)
        if index == 0 and hops:
            meta, rows_sum = hop_rows(meta, rows_sum)
    totals, seconds = [], []
    for index in every:
        total, second = products(
            False, cells, starts[index], chunks[index], tile, meta, factor, head, tail, whole
        )
        meta, second = after(meta, second)
        if hops:
            meta, rows_sum = hop_rows(meta, rows_sum)
        totals.append(total)
        seconds.append(second)
        for parity in (0, 1):
            meta = resend(meta, 2, parity, index)
    while hops:
        meta, rows_sum = hop_rows(meta, rows_sum)
    new_factor = turn(meta, whole)
    meta, new_factor = after(meta, new_factor)
    meta, rows_sum = stack_rows(meta, rows_sum, "sub", subs, 0, 1)
    bits = [1 << i for i in range((genes - 1).bit_length())]
    for phase in range(3, cells):
        for index in every:
            for parity in (0, 1):
                meta = resend(meta, phase, parity, index)
                if bits:
                    meta, rows_sum = stack_rows(meta, rows_sum, "gene", genes, 6, bits.pop(0))
    data_products = None
    last = cells - 1
    for index in every:
        data_products = keep(
            block, starts[index], meta, totals[index],
            arrived[last, 0, index], arrived[last, 1, index], data_products,
        )
        meta, data_products = after(meta, data_products)
    return (new_factor, rows_sum.astype(F32), data_products)


def solution(mesh):
    sizes = (mesh.shape["cell"], mesh.shape["gene"], mesh.shape["sub"])
    return jax.shard_map(
        functools.partial(shards, sizes),
        mesh=mesh,
        in_specs=(
            P(("groups", "cell"), ("gene", "sub")),
            P(("groups", "cell"), ("gene", "sub")),
            P(("groups", "cell"), ("gene", "sub")),
            P("groups", ("gene", "sub")),
            P(("groups", "cell"), None),
        ),
        out_specs=(
            P(("groups", "cell"), None),
            P("groups", None),
            P(("groups", "gene", "sub", "cell"), None),
        ),
        check_vma=False,
    )
```

```python
import functools

import jax
import jax.numpy as jnp
import numpy as np
from jax import lax
from jax.experimental import pallas as pl
from jax.experimental.pallas import tpu as pltpu
from jax.sharding import PartitionSpec as P

ITERS = 3
F32 = jnp.float32
BF16 = jnp.bfloat16
MIB = 1024 * 1024


def params(limit=16):
    return pltpu.CompilerParams(vmem_limit_bytes=limit * MIB)


def away(value):
    return pltpu.with_memory_space_constraint(value, pltpu.HBM)


def held(value):
    return pltpu.with_memory_space_constraint(value, pltpu.VMEM)


def cost(flops, bytes_accessed):
    return pl.CostEstimate(flops=flops, bytes_accessed=bytes_accessed, transcendentals=0)


def contract_last(left, right):
    return lax.dot_general(
        left, right, (((1,), (1,)), ((), ())), preferred_element_type=F32
    )


def row_copies(source, target, first, sems):
    rows = target.shape[0]
    piece = max(rows // sems.shape[0], 16)
    return [
        pltpu.make_async_copy(
            source.at[pl.ds(first + i * piece, piece)],
            target.at[pl.ds(i * piece, piece)],
            sems.at[i],
        )
        for i in range(rows // piece)
    ]


def load_kernel(
    tile, genes, counts, tile_mask, tile_counts,
    gram, factor, theirs, mine, genes_held, counts_held,
    mask_here, counts_here, mask_scalars, counts_scalars, gene_sems, row_sems, small_sems,
):
    small = [(tile_mask, mask_here), (tile_counts, counts_here)]
    small += [(tile_mask, mask_scalars), (tile_counts, counts_scalars)]
    small_copies = [
        pltpu.make_async_copy(source, target, small_sems.at[i])
        for i, (source, target) in enumerate(small)
    ]
    gene_copies = row_copies(genes, genes_held, 0, gene_sems)
    row_starts = row_copies(counts, counts_held, 0, row_sems)
    for copy in small_copies + gene_copies + row_starts:
        copy.start()
    for copy in small_copies:
        copy.wait()
    factor[...] = mask_here[...].astype(F32) / counts_here[...].astype(F32)
    for copy in gene_copies:
        copy.wait()
    columns = genes.shape[1]
    wide = min(1024, columns)
    part = None
    for start in range(0, columns, wide):
        piece = genes_held[:, start : start + wide]
        product = contract_last(piece, piece)
        part = product if part is None else part + product
    gram[...] = part

    rows = counts.shape[0]
    half = rows // 2
    at_once = min(4, columns // tile)

    def scale(row, place):
        above = jnp.full((1, tile), mask_scalars[row, place].astype(F32), F32)
        return above / jnp.full((1, tile), counts_scalars[row, place].astype(F32), F32)

    def half_cross(side, out):
        out[...] = jnp.zeros_like(out)

        @pl.loop(0, columns // (tile * at_once))
        def _(step):
            total = None
            for col in range(at_once):
                place = step * at_once + col
                at = pl.ds(pl.multiple_of(place * tile, tile), tile)
                product = contract_last(
                    genes_held[:, at], counts_held[side * half : (side + 1) * half, at]
                )
                first = side * (half // tile)
                scales = jnp.concatenate(
                    [scale(first + row, place) for row in range(half // tile)], axis=1
                )
                product = scales * product
                total = product if total is None else total + product
            out[...] += total

    core = lax.axis_index("sub")
    per_half = len(row_starts) // 2
    for side in (0, 1):
        for copy in row_starts[side * per_half : (side + 1) * per_half]:
            copy.wait()

        @pl.when(core == side)
        def _(side=side):
            half_cross(side, mine)

        @pl.when(core != side)
        def _(side=side):
            half_cross(side, theirs)


def load(genes, counts, tile_mask, tile_counts):
    width, columns = genes.shape
    rows = counts.shape[0]
    tile = rows // tile_mask.shape[0]
    here = pl.BlockSpec(memory_space=pltpu.VMEM)
    there = pl.BlockSpec(memory_space=pltpu.HBM)
    half = jax.ShapeDtypeStruct((width, rows // 2), F32)
    return pl.pallas_call(
        functools.partial(load_kernel, tile),
        out_shape=(
            jax.ShapeDtypeStruct((width, width), F32),
            jax.ShapeDtypeStruct(tile_mask.shape, F32),
            half,
            half,
            pltpu.VMEM((width, columns), BF16),
            pltpu.VMEM((rows, columns), BF16),
        ),
        in_specs=[there] * 4,
        out_specs=(here,) * 6,
        scratch_shapes=[
            pltpu.VMEM(tile_mask.shape, jnp.int32),
            pltpu.VMEM(tile_mask.shape, jnp.int32),
            pltpu.SMEM(tile_mask.shape, jnp.int32),
            pltpu.SMEM(tile_mask.shape, jnp.int32),
            pltpu.SemaphoreType.DMA((4,)),
            pltpu.SemaphoreType.DMA((16,)),
            pltpu.SemaphoreType.DMA((4,)),
        ],
        compiler_params=params(),
        cost_estimate=cost(1, 1),
        name="load",
    )(away(genes), away(counts), away(tile_mask), away(tile_counts))


def call(kernel, name, out_shape, token, *args, scratch=(), smem=0, aliases=None, out=None):
    here = pl.BlockSpec(memory_space=pltpu.VMEM)
    there = pl.BlockSpec(memory_space=pltpu.SMEM)
    wherever = pl.BlockSpec(memory_space=pl.ANY)
    single = not isinstance(out_shape, tuple)
    specs = [there] * smem + [here] * (len(args) - smem)
    if aliases:
        specs[-1] = wherever
    out = out or here
    return pl.pallas_call(
        lambda token, *refs: kernel(*refs),
        out_shape=out_shape,
        in_specs=[wherever] + specs,
        out_specs=out if single else (out,) * len(out_shape),
        scratch_shapes=list(scratch),
        input_output_aliases=aliases or {},
        compiler_params=params(),
        cost_estimate=cost(1, 1),
        name=name,
    )(token, *args)


def fold_kernel(axis, bit, left, right, kept, sent):
    half = kept.shape[1]
    upper = (lax.axis_index(axis) & bit) != 0

    @pl.when(upper)
    def _():
        kept[...] = left[:, half:] + right[:, half:]
        sent[...] = left[:, :half] + right[:, :half]

    @pl.when(jnp.logical_not(upper))
    def _():
        kept[...] = left[:, :half] + right[:, :half]
        sent[...] = left[:, half:] + right[:, half:]


def fold(axis, bit, token, left, right):
    shape = jax.ShapeDtypeStruct((left.shape[0], left.shape[1] // 2), F32)
    return call(
        functools.partial(fold_kernel, axis, bit), "fold", (shape, shape), token, left, right
    )


def side_kernel(axis, bit, dim, mine, theirs, out):
    size = mine.shape[dim]
    low = (slice(None),) * dim + (slice(0, size),)
    high = (slice(None),) * dim + (slice(size, 2 * size),)
    upper = (lax.axis_index(axis) & bit) != 0

    @pl.when(upper)
    def _():
        out[low], out[high] = theirs[...], mine[...]

    @pl.when(jnp.logical_not(upper))
    def _():
        out[low], out[high] = mine[...], theirs[...]


def side(axis, bit, dim, token, mine, theirs):
    shape = list(mine.shape)
    shape[dim] *= 2
    return call(
        functools.partial(side_kernel, axis, bit, dim),
        "side", jax.ShapeDtypeStruct(tuple(shape), mine.dtype), token, mine, theirs,
    )


def halves(value):
    high = value.astype(BF16)
    return high, (value - high.astype(F32)).astype(BF16)


def product3(left, right):
    left_high, left_low = left
    right_high, right_low = right
    dot = functools.partial(jnp.dot, preferred_element_type=F32)
    return dot(left_high, right_high) + (
        dot(left_high, right_low) + dot(left_low, right_high)
    )


def inverse_kernel(gram_a, gram_b, inverse, rho_out):
    gram = gram_a[...] + gram_b[...]
    width = gram.shape[0]
    shape = (width, width)
    diagonal = lax.broadcasted_iota(jnp.int32, shape, 0) == lax.broadcasted_iota(
        jnp.int32, shape, 1
    )
    eye = jnp.where(diagonal, 1.0, 0.0).astype(F32)
    rho = jnp.sum(gram * eye) / width
    rho_out[...] = jnp.full(rho_out.shape, rho, F32)
    scale = 1.0 / jnp.full((1, 1), rho, F32)
    matrix = gram * scale + eye
    low = 2.0 / (width + 2.0)
    guess = low * eye
    image = low * matrix
    first = True
    while True:
        low = low * (2.0 - low)
        gain = 2.0 / (1.0 + low)
        low = gain * low
        done = 1.0 - low < 2e-3
        step = halves(gain * (2.0 * eye - image))
        if first:
            guess = guess[0:1, 0:1] * (gain * (2.0 * eye - image))
        else:
            guess = product3(halves(guess), step)
        first = False
        if done:
            break
        image = product3(halves(image), step)
    rest = eye - jnp.dot(
        matrix, guess, preferred_element_type=F32, precision=lax.Precision.HIGHEST
    )
    rest_halves = halves(rest)
    series = rest + product3(rest_halves, rest_halves)
    inverse[...] = (guess + product3(halves(guess), halves(series))) * scale


def shifted_inverse(gram_a, gram_b):
    width = gram_a.shape[0]
    whole = pl.BlockSpec(memory_space=pltpu.VMEM)
    return pl.pallas_call(
        inverse_kernel,
        out_shape=(
            jax.ShapeDtypeStruct((width, width), F32),
            jax.ShapeDtypeStruct((8, 128), F32),
        ),
        in_specs=[whole, whole],
        out_specs=(whole, whole),
        compiler_params=params(),
        cost_estimate=cost(2 * 60 * width**3, 12 * width**2),
        name="inverse",
    )(gram_a, gram_b)


def admm_kernel(genes, rho_block, cross_a, cross_b, inverse, start, columns_out):
    rows = cross_a.shape[1]
    place = lax.axis_index("sub") * genes + lax.axis_index("gene")
    rho = rho_block[0:1, 0:1]
    cross = cross_a[...] + cross_b[...]
    inverse_halves = halves(inverse[...])
    zvalue = start[pl.ds(pl.multiple_of(place * rows, rows), rows), :].astype(F32).T
    uvalue = jnp.zeros_like(zvalue)
    for _ in range(ITERS):
        vvalue = product3(inverse_halves, halves(cross + rho * (zvalue - uvalue)))
        zvalue = jnp.maximum(vvalue + uvalue, 0.0)
        uvalue = uvalue + vvalue - zvalue
    columns_out[...] = zvalue.astype(BF16)


def products_kernel(tile, line, start, chunk, factor, counts, columns, *outs):
    only_first = len(outs) == 1
    block = line.block(1 if only_first else 2, 0)
    size = counts.shape[1] // line.size
    span = min(tile, chunk)
    wide = 2 * span if chunk % (2 * span) == 0 else span
    steps = chunk // wide
    row_tiles = columns.shape[1] // tile

    @pl.loop(0, steps if only_first else line.size * steps)
    def _(turn):
        order, step = (block, turn) if only_first else (turn // steps, lax.rem(turn, steps))
        first = pl.multiple_of(order * size + start + step * wide, span)
        total = None
        for row in range(row_tiles):
            part = jnp.dot(
                columns[:, row * tile : (row + 1) * tile],
                counts[row * tile : (row + 1) * tile, pl.ds(first, wide)],
                preferred_element_type=F32,
            )
            scales = [
                jnp.full((1, span), factor[row, (first + col * span) // tile], F32)
                for col in range(wide // span)
            ]
            part = jnp.concatenate(scales, axis=1) * part
            total = part if total is None else total + part
        total = total.astype(BF16)
        at = pl.ds(pl.multiple_of(step * wide, span), wide)
        if only_first:
            outs[0][:, at] = total
        else:
            outs[0][order, :, at] = total

            @pl.when(order == block)
            def _():
                outs[1][:, at] = total


def products(only_first, line, start, chunk, token, factor, counts, columns):
    width, rows = columns.shape
    tile = rows // factor.shape[0]
    out_shape = (jax.ShapeDtypeStruct((width, chunk), BF16),)
    if not only_first:
        out_shape = (jax.ShapeDtypeStruct((line.size, width, chunk), BF16),) + out_shape
    return call(
        functools.partial(products_kernel, tile, line, start, chunk),
        "products", out_shape, token, factor, held(counts), columns, smem=1,
    )


def turn_kernel(value, out):
    out[...] = value[...].astype(F32).T.astype(out.dtype)


def turn(token, value):
    shape = jax.ShapeDtypeStruct(value.shape[::-1], value.dtype)
    return call(turn_kernel, "turn", shape, token, value)


def row_share_kernel(subs, columns, out):
    part = out.shape[0]
    place = lax.axis_index("gene") * subs + lax.axis_index("sub")
    share = columns[pl.ds(pl.multiple_of(place * part, part), part), :]
    out[...] = contract_last(share, columns[...]).astype(out.dtype)


def row_share(subs, part, token, columns):
    shape = jax.ShapeDtypeStruct((part, columns.shape[0]), BF16)
    return call(functools.partial(row_share_kernel, subs), "row_share", shape, token, columns)


def hop_kernel(kind, targets, own, arrived, out):
    cell = lax.axis_index("cell")
    reached = cell == targets[0]
    for target in targets[1:]:
        reached = jnp.logical_or(reached, cell == target)
    more = arrived[...].astype(F32)
    base = own[...].astype(F32)
    value = base + more if kind == "sum" else more
    out[...] = jnp.where(reached, value, base).astype(out.dtype)


def hop(kind, targets, token, own, arrived):
    shape = jax.ShapeDtypeStruct(own.shape, own.dtype)
    return call(functools.partial(hop_kernel, kind, targets), "hop", shape, token, own, arrived)


def operand_kernel(line, phase, parity, total, before, out):
    own = total[line.block(phase, parity)].astype(F32)
    out[...] = (own + before[...].astype(F32)).astype(BF16)


def operand(line, phase, parity, token, total, before):
    shape = jax.ShapeDtypeStruct(before.shape, BF16)
    return call(
        functools.partial(operand_kernel, line, phase, parity),
        "operand", shape, token, total, before,
    )


def keep_kernel(start, total, first, second, *refs):
    out, turned, sems = refs[-3:]
    width, chunk = first.shape
    pieces = sems.shape[0]
    wide = chunk // pieces
    own = total.at[lax.axis_index("cell")]
    copies = []
    for piece in range(pieces):
        at = slice(piece * wide, (piece + 1) * wide)
        value = first[:, at].astype(F32) + second[:, at].astype(F32)
        turned[at] = (own[:, at].astype(F32) + value).T
        copies.append(
            pltpu.make_async_copy(
                turned.at[at], out.at[pl.ds(start + piece * wide, wide)], sems.at[piece]
            )
        )
        copies[-1].start()
    for copy in copies:
        copy.wait()


def keep(block, start, token, total, first, second, out):
    width, chunk = first.shape
    pieces = max(1, chunk // 256)
    return call(
        functools.partial(keep_kernel, start),
        "keep", jax.ShapeDtypeStruct((block, width), F32), token,
        total, first, second, *([] if out is None else [out]),
        scratch=[pltpu.VMEM((chunk, width), F32), pltpu.SemaphoreType.DMA((pieces,))],
        aliases=None if out is None else {4: 0},
        out=pl.BlockSpec(memory_space=pl.ANY),
    )


class Line:
    def __init__(self, size):
        self.size = size

    def pairs(self, phase, parity):
        links = range(parity, self.size - 1, 2)
        right = [(i, i + 1) for i in links if i < phase]
        left = [(i + 1, i) for i in links if i + 1 >= self.size - phase]
        return right + left

    def block(self, phase, parity):
        cell = lax.axis_index("cell")
        to_right = (cell & 1) == parity
        block = cell + jnp.where(to_right, self.size - phase, phase)
        return jnp.where(block >= self.size, block - self.size, block)

    def send(self, value, phase, parity):
        return lax.ppermute(value, "cell", self.pairs(phase, parity))


def swap(value, axis, size, step):
    return lax.ppermute(value, axis, [(i, i ^ step) for i in range(size)])


def pair_sums(value, axis, size, event):
    step = 1
    while step < size:
        arrived, event = after(swap(value, axis, size, step), event)
        value = value + arrived
        step *= 2
    return value


def after(value, event):
    return lax.optimization_barrier((value, event))


def chunk_sizes(block):
    return [block // 2, block // 2] if block % 1024 == 0 else [block]


def shards(sizes, counts, tile_mask, tile_counts, gene_factor, prev_factor):
    cells, genes, subs = sizes
    rows, columns = counts.shape
    width = gene_factor.shape[0]
    line = Line(cells)

    gram, factor, theirs, mine, _, counts_held = load(
        gene_factor, counts, tile_mask, tile_counts
    )
    token = factor
    arrived = swap(theirs, "sub", subs, 1)
    cross_a, cross_b = mine, arrived
    bit = genes // 2
    while bit:
        cross_a, sent = fold("gene", bit, token, cross_a, cross_b)
        cross_b = swap(sent, "gene", genes, bit)
        if bit == genes // 2:
            gram = pair_sums(gram, "gene", genes, cross_a)
        bit //= 2
    gram_other = swap(gram, "sub", subs, 1)
    inverse, rho = shifted_inverse(gram, gram_other)
    share = jax.ShapeDtypeStruct((width, rows // (genes * subs)), BF16)
    columns_held = call(
        functools.partial(admm_kernel, genes),
        "admm", share, token, rho, cross_a, cross_b, inverse, prev_factor,
    )
    bit = 1
    while bit < genes:
        columns_arrived = swap(columns_held, "gene", genes, bit)
        columns_held = side("gene", bit, 1, token, columns_held, columns_arrived)
        bit *= 2
    columns_arrived = swap(columns_held, "sub", subs, 1)
    whole = side("sub", 1, 1, token, columns_held, columns_arrived)

    block = columns // cells
    chunks = chunk_sizes(block)
    starts = [sum(chunks[:i]) for i in range(len(chunks))]
    every = range(len(chunks))

    arrived = {}

    def send(value, phase, parity, index):
        pairs = line.pairs(phase, parity)
        arrived[phase, parity, index] = lax.ppermute(value, "cell", pairs) if pairs else None

    def resend(token, phase, parity, index):
        before = arrived[phase - 1, 1 - parity, index]
        if before is None:
            value = seconds[index]
        else:
            value = operand(line, phase, parity, token, totals[index], before)
            token, value = after(token, value)
        send(value, phase, parity, index)
        return token

    middle = cells // 2
    inward = [[(i, i + 1), (cells - 1 - i, cells - 2 - i)] for i in range(middle - 1)]
    outward = [[(b, a) for a, b in pairs] for pairs in reversed(inward)]
    hops = [("sum", p) for p in inward] + [("sum", [(middle - 1, middle), (middle, middle - 1)])]
    hops += [("copy", p) for p in outward]

    def hop_rows(token, rows_sum):
        kind, pairs = hops.pop(0)
        rows_arrived = lax.ppermute(rows_sum, "cell", pairs)
        targets = [b for _, b in pairs]
        return after(token, hop(kind, targets, token, rows_sum, rows_arrived))

    def side_rows(token, rows_sum, axis, size, bit):
        rows_arrived = swap(rows_sum, axis, size, bit)
        return after(token, side(axis, bit, 0, token, rows_sum, rows_arrived))

    token, rows_sum = after(token, row_share(subs, width // (genes * subs), token, whole))
    for index in every:
        (first,) = products(
            True, line, starts[index], chunks[index], token, factor, counts_held, whole
        )
        token, first = after(token, first)
        for parity in (0, 1):
            send(first, 1, parity, index)
        if index == 0 and hops:
            token, rows_sum = hop_rows(token, rows_sum)
    totals, seconds = [], []
    for index in every:
        total, second = products(
            False, line, starts[index], chunks[index], token, factor, counts_held, whole
        )
        token, second = after(token, second)
        if hops:
            token, rows_sum = hop_rows(token, rows_sum)
        totals.append(total)
        seconds.append(second)
        for parity in (0, 1):
            token = resend(token, 2, parity, index)
    while hops:
        token, rows_sum = hop_rows(token, rows_sum)
    new_factor = turn(token, whole)
    token, new_factor = after(token, new_factor)
    token, rows_sum = side_rows(token, rows_sum, "sub", subs, 1)
    bits = [1 << i for i in range((genes - 1).bit_length())]
    for phase in range(3, cells):
        for index in every:
            for parity in (0, 1):
                token = resend(token, phase, parity, index)
                if bits:
                    token, rows_sum = side_rows(token, rows_sum, "gene", genes, bits.pop(0))
    data_products = None
    last = cells - 1
    for index in every:
        data_products = keep(
            block, starts[index], token, totals[index],
            arrived[last, 0, index], arrived[last, 1, index], data_products,
        )
        token, data_products = after(token, data_products)
    return (new_factor, rows_sum.astype(F32), data_products)


def solution(mesh):
    sizes = (mesh.shape["cell"], mesh.shape["gene"], mesh.shape["sub"])
    return jax.shard_map(
        functools.partial(shards, sizes),
        mesh=mesh,
        in_specs=(
            P(("groups", "cell"), ("gene", "sub")),
            P(("groups", "cell"), ("gene", "sub")),
            P(("groups", "cell"), ("gene", "sub")),
            P("groups", ("gene", "sub")),
            P(("groups", "cell"), None),
        ),
        out_specs=(
            P(("groups", "cell"), None),
            P("groups", None),
            P(("groups", "gene", "sub", "cell"), None),
        ),
        check_vma=False,
    )
```

```python
import functools

import jax
import jax.numpy as jnp
import numpy as np
from jax import lax
from jax.experimental import pallas as pl
from jax.experimental.pallas import tpu as pltpu
from jax.sharding import PartitionSpec as P

ITERS = 3
F32 = jnp.float32
BF16 = jnp.bfloat16
MIB = 1024 * 1024


def params(limit=16):
    return pltpu.CompilerParams(vmem_limit_bytes=limit * MIB)


def away(value):
    return pltpu.with_memory_space_constraint(value, pltpu.HBM)


def held(value):
    return pltpu.with_memory_space_constraint(value, pltpu.VMEM)


def cost(flops, bytes_accessed):
    return pl.CostEstimate(flops=flops, bytes_accessed=bytes_accessed, transcendentals=0)


def contract_last(left, right):
    return lax.dot_general(
        left, right, (((1,), (1,)), ((), ())), preferred_element_type=F32
    )


def row_copies(source, target, first, sems):
    rows = target.shape[0]
    piece = max(rows // sems.shape[0], 16)
    return [
        pltpu.make_async_copy(
            source.at[pl.ds(first + i * piece, piece)],
            target.at[pl.ds(i * piece, piece)],
            sems.at[i],
        )
        for i in range(rows // piece)
    ]


def load_kernel(
    genes, counts, tile_mask, tile_counts, gram, factor, turned, upper,
    genes_here, mask_here, counts_here, gene_sems, row_sems, small_sems,
):
    small_copies = [
        pltpu.make_async_copy(tile_mask, mask_here, small_sems.at[0]),
        pltpu.make_async_copy(tile_counts, counts_here, small_sems.at[1]),
    ]
    gene_copies = row_copies(genes, genes_here, 0, gene_sems)
    upper_copies = row_copies(counts, upper, 0, row_sems)
    for copy in gene_copies + small_copies + upper_copies:
        copy.start()
    for copy in small_copies:
        copy.wait()
    factor[...] = mask_here[...].astype(F32) / counts_here[...].astype(F32)
    for copy in gene_copies:
        copy.wait()
    columns = genes.shape[1]
    wide = min(1024, columns)
    gram[...] = jnp.zeros_like(gram)

    @pl.loop(0, columns // wide)
    def _(step):
        at = pl.ds(pl.multiple_of(step * wide, wide), wide)
        piece = genes_here[:, at]
        turned[at, :] = piece.T
        gram[...] += jnp.dot(piece, turned[at, :], preferred_element_type=F32)

    for copy in upper_copies:
        copy.wait()


def load(genes, counts, tile_mask, tile_counts):
    width, columns = genes.shape
    rows = counts.shape[0]
    here = pl.BlockSpec(memory_space=pltpu.VMEM)
    there = pl.BlockSpec(memory_space=pltpu.HBM)
    return pl.pallas_call(
        load_kernel,
        out_shape=(
            jax.ShapeDtypeStruct((width, width), F32),
            jax.ShapeDtypeStruct(tile_mask.shape, F32),
            pltpu.VMEM((columns, width), BF16),
            pltpu.VMEM((rows // 2, columns), BF16),
        ),
        in_specs=[there] * 4,
        out_specs=(here,) * 4,
        scratch_shapes=[
            pltpu.VMEM((width, columns), BF16),
            pltpu.VMEM(tile_mask.shape, jnp.int32),
            pltpu.VMEM(tile_mask.shape, jnp.int32),
            pltpu.SemaphoreType.DMA((4,)),
            pltpu.SemaphoreType.DMA((8,)),
            pltpu.SemaphoreType.DMA((2,)),
        ],
        compiler_params=params(),
        cost_estimate=cost(1, 1),
        name="load",
    )(away(genes), away(counts), away(tile_mask), away(tile_counts))


def add_cross(first_row, start, stop, factor, counts, turned, total):
    tile = counts.shape[1] // factor.shape[1]
    at_once = min(4, stop - start)

    @pl.loop(start // at_once, stop // at_once)
    def _(step):
        sums = None
        for col in range(at_once):
            place = step * at_once + col
            at = pl.ds(pl.multiple_of(place * tile, tile), tile)
            product = jnp.dot(counts[:, at], turned[at, :], preferred_element_type=F32)
            product = jnp.concatenate(
                [
                    product[row * tile : (row + 1) * tile] * factor[first_row + row, place]
                    for row in range(counts.shape[0] // tile)
                ],
                axis=0,
            )
            sums = product if sums is None else sums + product
        total[...] += sums


def cross_early_kernel(split, factor, upper, turned, counts, high, low, lower, total, sems):
    half = upper.shape[0]
    copies = row_copies(counts, lower, half, sems)
    for copy in copies:
        copy.start()
    gene_tiles = factor.shape[1]
    total[...] = jnp.zeros_like(total)
    add_cross(0, 0, gene_tiles, factor, upper, turned, total)
    high[...] = total[...].T
    for copy in copies:
        copy.wait()
    low[...] = jnp.zeros_like(low)
    add_cross(factor.shape[0] // 2, 0, split, factor, lower, turned, low)


def cross_early(split, factor, upper, turned, counts):
    half, columns = upper.shape
    width = turned.shape[1]
    here = pl.BlockSpec(memory_space=pltpu.VMEM)
    return pl.pallas_call(
        functools.partial(cross_early_kernel, split),
        out_shape=(
            jax.ShapeDtypeStruct((width, half), F32),
            jax.ShapeDtypeStruct((half, width), F32),
            pltpu.VMEM((half, columns), BF16),
        ),
        in_specs=[
            pl.BlockSpec(memory_space=pltpu.SMEM),
            here,
            here,
            pl.BlockSpec(memory_space=pltpu.HBM),
        ],
        out_specs=(here,) * 3,
        scratch_shapes=[pltpu.VMEM((half, width), F32), pltpu.SemaphoreType.DMA((8,))],
        compiler_params=params(),
        cost_estimate=cost(1, 1),
        name="cross_early",
    )(factor, held(upper), held(turned), away(counts))


def cross_late_kernel(split, factor, high, low, lower, turned, theirs, mine, total):
    total[...] = low[...]
    add_cross(factor.shape[0] // 2, split, factor.shape[1], factor, lower, turned, total)

    @pl.when(lax.axis_index("sub") == 0)
    def _():
        mine[...] = high[...]
        theirs[...] = total[...].T

    @pl.when(lax.axis_index("sub") != 0)
    def _():
        theirs[...] = high[...]
        mine[...] = total[...].T


def call(kernel, name, out_shape, token, *args, scratch=(), smem=0, aliases=None, out=None):
    here = pl.BlockSpec(memory_space=pltpu.VMEM)
    there = pl.BlockSpec(memory_space=pltpu.SMEM)
    wherever = pl.BlockSpec(memory_space=pl.ANY)
    single = not isinstance(out_shape, tuple)
    specs = [there] * smem + [here] * (len(args) - smem)
    if aliases:
        specs[-1] = wherever
    out = out or here
    return pl.pallas_call(
        lambda token, *refs: kernel(*refs),
        out_shape=out_shape,
        in_specs=[wherever] + specs,
        out_specs=out if single else (out,) * len(out_shape),
        scratch_shapes=list(scratch),
        input_output_aliases=aliases or {},
        compiler_params=params(),
        cost_estimate=cost(1, 1),
        name=name,
    )(token, *args)


def fold_kernel(axis, bit, left, right, kept, sent):
    half = kept.shape[1]
    upper = (lax.axis_index(axis) & bit) != 0

    @pl.when(upper)
    def _():
        kept[...] = left[:, half:] + right[:, half:]
        sent[...] = left[:, :half] + right[:, :half]

    @pl.when(jnp.logical_not(upper))
    def _():
        kept[...] = left[:, :half] + right[:, :half]
        sent[...] = left[:, half:] + right[:, half:]


def fold(axis, bit, token, left, right):
    shape = jax.ShapeDtypeStruct((left.shape[0], left.shape[1] // 2), F32)
    return call(
        functools.partial(fold_kernel, axis, bit), "fold", (shape, shape), token, left, right
    )


def side_kernel(axis, bit, dim, mine, theirs, out):
    size = mine.shape[dim]
    low = (slice(None),) * dim + (slice(0, size),)
    high = (slice(None),) * dim + (slice(size, 2 * size),)
    upper = (lax.axis_index(axis) & bit) != 0

    @pl.when(upper)
    def _():
        out[low], out[high] = theirs[...], mine[...]

    @pl.when(jnp.logical_not(upper))
    def _():
        out[low], out[high] = mine[...], theirs[...]


def side(axis, bit, dim, token, mine, theirs):
    shape = list(mine.shape)
    shape[dim] *= 2
    return call(
        functools.partial(side_kernel, axis, bit, dim),
        "side", jax.ShapeDtypeStruct(tuple(shape), mine.dtype), token, mine, theirs,
    )


def halves(value):
    high = value.astype(BF16)
    return high, (value - high.astype(F32)).astype(BF16)


def product3(left, right):
    left_high, left_low = left
    right_high, right_low = right
    dot = functools.partial(jnp.dot, preferred_element_type=F32)
    return dot(left_high, right_high) + (
        dot(left_high, right_low) + dot(left_low, right_high)
    )


def inverse_kernel(gram_a, gram_b, inverse, rho_out):
    gram = gram_a[...] + gram_b[...]
    width = gram.shape[0]
    shape = (width, width)
    diagonal = lax.broadcasted_iota(jnp.int32, shape, 0) == lax.broadcasted_iota(
        jnp.int32, shape, 1
    )
    eye = jnp.where(diagonal, 1.0, 0.0).astype(F32)
    rho = jnp.sum(gram * eye) / width
    rho_out[...] = jnp.full(rho_out.shape, rho, F32)
    scale = 1.0 / jnp.full((1, 1), rho, F32)
    matrix = gram * scale + eye
    low = 2.0 / (width + 2.0)
    guess = low * eye
    image = low * matrix
    first = True
    while True:
        low = low * (2.0 - low)
        gain = 2.0 / (1.0 + low)
        low = gain * low
        done = 1.0 - low < 2e-3
        step = halves(gain * (2.0 * eye - image))
        if first:
            guess = guess[0:1, 0:1] * (gain * (2.0 * eye - image))
        else:
            guess = product3(halves(guess), step)
        first = False
        if done:
            break
        image = product3(halves(image), step)
    rest = eye - jnp.dot(
        matrix, guess, preferred_element_type=F32, precision=lax.Precision.HIGHEST
    )
    rest_halves = halves(rest)
    series = rest + product3(rest_halves, rest_halves)
    inverse[...] = (guess + product3(halves(guess), halves(series))) * scale


def shifted_inverse(gram_a, gram_b):
    width = gram_a.shape[0]
    whole = pl.BlockSpec(memory_space=pltpu.VMEM)
    return pl.pallas_call(
        inverse_kernel,
        out_shape=(
            jax.ShapeDtypeStruct((width, width), F32),
            jax.ShapeDtypeStruct((8, 128), F32),
        ),
        in_specs=[whole, whole],
        out_specs=(whole, whole),
        compiler_params=params(),
        cost_estimate=cost(2 * 60 * width**3, 12 * width**2),
        name="inverse",
    )(gram_a, gram_b)


def admm_kernel(genes, rho_block, cross_a, cross_b, inverse, start, columns_out):
    rows = cross_a.shape[1]
    place = lax.axis_index("sub") * genes + lax.axis_index("gene")
    rho = rho_block[0:1, 0:1]
    cross = cross_a[...] + cross_b[...]
    inverse_halves = halves(inverse[...])
    zvalue = start[pl.ds(pl.multiple_of(place * rows, rows), rows), :].astype(F32).T
    uvalue = jnp.zeros_like(zvalue)
    for _ in range(ITERS):
        vvalue = product3(inverse_halves, halves(cross + rho * (zvalue - uvalue)))
        zvalue = jnp.maximum(vvalue + uvalue, 0.0)
        uvalue = uvalue + vvalue - zvalue
    columns_out[...] = zvalue.astype(BF16)


def products_kernel(tile, line, start, chunk, factor, upper, lower, columns, *outs):
    only_first = len(outs) == 1
    block = line.block(1 if only_first else 2, 0)
    size = upper.shape[1] // line.size
    span = min(tile, chunk)
    wide = 2 * span if chunk % (2 * span) == 0 else span
    steps = chunk // wide
    row_tiles = columns.shape[1] // tile

    @pl.loop(0, steps if only_first else line.size * steps)
    def _(turn):
        order, step = (block, turn) if only_first else (turn // steps, lax.rem(turn, steps))
        first = pl.multiple_of(order * size + start + step * wide, span)
        total = None
        for row in range(row_tiles):
            counts, place = (upper, row) if row < row_tiles // 2 else (lower, row - row_tiles // 2)
            part = jnp.dot(
                columns[:, row * tile : (row + 1) * tile],
                counts[place * tile : (place + 1) * tile, pl.ds(first, wide)],
                preferred_element_type=F32,
            )
            scales = [
                jnp.full((1, span), factor[row, (first + col * span) // tile], F32)
                for col in range(wide // span)
            ]
            part = jnp.concatenate(scales, axis=1) * part
            total = part if total is None else total + part
        total = total.astype(BF16)
        at = pl.ds(pl.multiple_of(step * wide, span), wide)
        if only_first:
            outs[0][:, at] = total
        else:
            outs[0][order, :, at] = total

            @pl.when(order == block)
            def _():
                outs[1][:, at] = total


def products(only_first, line, start, chunk, token, factor, upper, lower, columns):
    width, rows = columns.shape
    tile = rows // factor.shape[0]
    out_shape = (jax.ShapeDtypeStruct((width, chunk), BF16),)
    if not only_first:
        out_shape = (jax.ShapeDtypeStruct((line.size, width, chunk), BF16),) + out_shape
    return call(
        functools.partial(products_kernel, tile, line, start, chunk),
        "products", out_shape, token, factor, held(upper), held(lower), columns, smem=1,
    )


def turn_kernel(value, out):
    out[...] = value[...].astype(F32).T.astype(out.dtype)


def turn(token, value):
    shape = jax.ShapeDtypeStruct(value.shape[::-1], value.dtype)
    return call(turn_kernel, "turn", shape, token, value)


def row_share_kernel(columns, out):
    part = out.shape[0]
    place = lax.axis_index("gene")
    share = columns[pl.ds(pl.multiple_of(place * part, part), part), :]
    out[...] = contract_last(share, columns[...]).astype(out.dtype)


def row_share(part, token, columns):
    shape = jax.ShapeDtypeStruct((part, columns.shape[0]), BF16)
    return call(row_share_kernel, "row_share", shape, token, columns)


def plus_kernel(left, right, out):
    out[...] = (left[...].astype(F32) + right[...].astype(F32)).astype(out.dtype)


def hop_kernel(kind, targets, own, arrived, out):
    cell = lax.axis_index("cell")
    reached = cell == targets[0]
    for target in targets[1:]:
        reached = jnp.logical_or(reached, cell == target)
    more = arrived[...].astype(F32)
    base = own[...].astype(F32)
    value = base + more if kind == "sum" else more
    out[...] = jnp.where(reached, value, base).astype(out.dtype)


def hop(kind, targets, token, own, arrived):
    shape = jax.ShapeDtypeStruct(own.shape, own.dtype)
    return call(functools.partial(hop_kernel, kind, targets), "hop", shape, token, own, arrived)


def operand_kernel(line, phase, parity, total, before, out):
    own = total[line.block(phase, parity)].astype(F32)
    out[...] = (own + before[...].astype(F32)).astype(BF16)


def operand(line, phase, parity, token, total, before):
    shape = jax.ShapeDtypeStruct(before.shape, BF16)
    return call(
        functools.partial(operand_kernel, line, phase, parity),
        "operand", shape, token, total, before,
    )


def keep_kernel(start, total, first, second, *refs):
    out, turned, sems = refs[-3:]
    width, chunk = first.shape
    pieces = sems.shape[0]
    wide = chunk // pieces
    own = total.at[lax.axis_index("cell")]
    copies = []
    for piece in range(pieces):
        at = slice(piece * wide, (piece + 1) * wide)
        value = first[:, at].astype(F32) + second[:, at].astype(F32)
        turned[at] = (own[:, at].astype(F32) + value).T
        copies.append(
            pltpu.make_async_copy(
                turned.at[at], out.at[pl.ds(start + piece * wide, wide)], sems.at[piece]
            )
        )
        copies[-1].start()
    for copy in copies:
        copy.wait()


def keep(block, start, token, total, first, second, out):
    width, chunk = first.shape
    pieces = max(1, chunk // 256)
    return call(
        functools.partial(keep_kernel, start),
        "keep", jax.ShapeDtypeStruct((block, width), F32), token,
        total, first, second, *([] if out is None else [out]),
        scratch=[pltpu.VMEM((chunk, width), F32), pltpu.SemaphoreType.DMA((pieces,))],
        aliases=None if out is None else {4: 0},
        out=pl.BlockSpec(memory_space=pl.ANY),
    )


class Line:
    def __init__(self, size):
        self.size = size

    def pairs(self, phase, parity):
        links = range(parity, self.size - 1, 2)
        right = [(i, i + 1) for i in links if i < phase]
        left = [(i + 1, i) for i in links if i + 1 >= self.size - phase]
        return right + left

    def block(self, phase, parity):
        cell = lax.axis_index("cell")
        to_right = (cell & 1) == parity
        block = cell + jnp.where(to_right, self.size - phase, phase)
        return jnp.where(block >= self.size, block - self.size, block)

    def send(self, value, phase, parity):
        return lax.ppermute(value, "cell", self.pairs(phase, parity))


def swap(value, axis, size, step):
    return lax.ppermute(value, axis, [(i, i ^ step) for i in range(size)])


def pair_sums(value, axis, size, event):
    step = 1
    while step < size:
        arrived, event = after(swap(value, axis, size, step), event)
        value = value + arrived
        step *= 2
    return value, event


def after(value, event):
    return lax.optimization_barrier((value, event))


def chunk_sizes(block):
    return [block // 2, block // 2] if block % 1024 == 0 else [block]


def shards(sizes, counts, tile_mask, tile_counts, gene_factor, prev_factor):
    cells, genes, subs = sizes
    rows, columns = counts.shape
    width = gene_factor.shape[0]
    line = Line(cells)

    gram, factor, turned, upper = load(gene_factor, counts, tile_mask, tile_counts)
    token = factor
    split = tile_mask.shape[1] // 8 * 4
    high, low, lower = cross_early(split, factor, upper, turned, counts)
    gram, low = pair_sums(gram, "gene", genes, low)
    half = jax.ShapeDtypeStruct((width, rows // 2), F32)
    theirs, mine = call(
        functools.partial(cross_late_kernel, split), "cross_late", (half, half), token,
        factor, high, low, held(lower), held(turned),
        smem=1, scratch=[pltpu.VMEM((rows // 2, width), F32)],
    )
    arrived = swap(theirs, "sub", subs, 1)
    cross_a, cross_b = mine, arrived
    bit = genes // 2
    while bit:
        cross_a, sent = fold("gene", bit, token, cross_a, cross_b)
        cross_b = swap(sent, "gene", genes, bit)
        bit //= 2
    gram_other = swap(gram, "sub", subs, 1)
    inverse, rho = shifted_inverse(gram, gram_other)
    share = jax.ShapeDtypeStruct((width, rows // (genes * subs)), BF16)
    columns_held = call(
        functools.partial(admm_kernel, genes),
        "admm", share, token, rho, cross_a, cross_b, inverse, prev_factor,
    )
    bit = 1
    while bit < genes:
        columns_arrived = swap(columns_held, "gene", genes, bit)
        columns_held = side("gene", bit, 1, token, columns_held, columns_arrived)
        bit *= 2
    token, rows_sum = after(token, row_share(width // genes, token, columns_held))
    columns_arrived = swap(columns_held, "sub", subs, 1)
    whole = side("sub", 1, 1, token, columns_held, columns_arrived)

    block = columns // cells
    chunks = chunk_sizes(block)
    starts = [sum(chunks[:i]) for i in range(len(chunks))]
    every = range(len(chunks))

    arrived = {}

    def send(value, phase, parity, index):
        pairs = line.pairs(phase, parity)
        arrived[phase, parity, index] = lax.ppermute(value, "cell", pairs) if pairs else None

    def resend(token, phase, parity, index):
        before = arrived[phase - 1, 1 - parity, index]
        if before is None:
            value = seconds[index]
        else:
            value = operand(line, phase, parity, token, totals[index], before)
            token, value = after(token, value)
        send(value, phase, parity, index)
        return token

    middle = cells // 2
    inward = [[(i, i + 1), (cells - 1 - i, cells - 2 - i)] for i in range(middle - 1)]
    outward = [[(b, a) for a, b in pairs] for pairs in reversed(inward)]
    hops = [("sum", p) for p in inward] + [("sum", [(middle - 1, middle), (middle, middle - 1)])]
    hops += [("copy", p) for p in outward]

    def hop_rows(token, rows_sum):
        kind, pairs = hops.pop(0)
        rows_arrived = lax.ppermute(rows_sum, "cell", pairs)
        targets = [b for _, b in pairs]
        return after(token, hop(kind, targets, token, rows_sum, rows_arrived))

    def side_rows(token, rows_sum, axis, size, bit):
        rows_arrived = swap(rows_sum, axis, size, bit)
        return after(token, side(axis, bit, 0, token, rows_sum, rows_arrived))

    for index in every:
        (first,) = products(
            True, line, starts[index], chunks[index], token, factor, upper, lower, whole
        )
        token, first = after(token, first)
        for parity in (0, 1):
            send(first, 1, parity, index)
        if index == 0 and hops:
            token, rows_sum = hop_rows(token, rows_sum)
    totals, seconds = [], []
    for index in every:
        total, second = products(
            False, line, starts[index], chunks[index], token, factor, upper, lower, whole
        )
        token, second = after(token, second)
        if hops:
            token, rows_sum = hop_rows(token, rows_sum)
        totals.append(total)
        seconds.append(second)
        for parity in (0, 1):
            token = resend(token, 2, parity, index)
    while hops:
        token, rows_sum = hop_rows(token, rows_sum)
    new_factor = turn(token, whole)
    token, new_factor = after(token, new_factor)
    rows_arrived = swap(rows_sum, "sub", subs, 1)
    shape = jax.ShapeDtypeStruct(rows_sum.shape, F32)
    token, rows_sum = after(token, call(plus_kernel, "plus", shape, token, rows_sum, rows_arrived))
    bits = [1 << i for i in range((genes - 1).bit_length())]
    for phase in range(3, cells):
        for index in every:
            for parity in (0, 1):
                token = resend(token, phase, parity, index)
                if bits:
                    token, rows_sum = side_rows(token, rows_sum, "gene", genes, bits.pop(0))
    data_products = None
    last = cells - 1
    for index in every:
        data_products = keep(
            block, starts[index], token, totals[index],
            arrived[last, 0, index], arrived[last, 1, index], data_products,
        )
        token, data_products = after(token, data_products)
    return (new_factor, rows_sum, data_products)


def solution(mesh):
    sizes = (mesh.shape["cell"], mesh.shape["gene"], mesh.shape["sub"])
    return jax.shard_map(
        functools.partial(shards, sizes),
        mesh=mesh,
        in_specs=(
            P(("groups", "cell"), ("gene", "sub")),
            P(("groups", "cell"), ("gene", "sub")),
            P(("groups", "cell"), ("gene", "sub")),
            P("groups", ("gene", "sub")),
            P(("groups", "cell"), None),
        ),
        out_specs=(
            P(("groups", "cell"), None),
            P("groups", None),
            P(("groups", "gene", "sub", "cell"), None),
        ),
        check_vma=False,
    )
```

```python
import functools

import jax
import jax.numpy as jnp
import numpy as np
from jax import lax
from jax.experimental import pallas as pl
from jax.experimental.pallas import tpu as pltpu
from jax.sharding import PartitionSpec as P

ITERS = 3
F32 = jnp.float32
BF16 = jnp.bfloat16
MIB = 1024 * 1024


def params(limit=16):
    return pltpu.CompilerParams(vmem_limit_bytes=limit * MIB)


def away(value):
    return pltpu.with_memory_space_constraint(value, pltpu.HBM)


def held(value):
    return pltpu.with_memory_space_constraint(value, pltpu.VMEM)


def cost(flops, bytes_accessed):
    return pl.CostEstimate(flops=flops, bytes_accessed=bytes_accessed, transcendentals=0)


def contract_last(left, right):
    return lax.dot_general(
        left, right, (((1,), (1,)), ((), ())), preferred_element_type=F32
    )


def row_copies(source, target, first, sems):
    rows = target.shape[0]
    piece = max(rows // sems.shape[0], 16)
    return [
        pltpu.make_async_copy(
            source.at[pl.ds(first + i * piece, piece)],
            target.at[pl.ds(i * piece, piece)],
            sems.at[i],
        )
        for i in range(rows // piece)
    ]


def load_kernel(
    genes, counts, tile_mask, tile_counts, gram, factor, turned, theirs,
    genes_here, mask_here, counts_here, gene_sems, row_sems, small_sems,
):
    small_copies = [
        pltpu.make_async_copy(tile_mask, mask_here, small_sems.at[0]),
        pltpu.make_async_copy(tile_counts, counts_here, small_sems.at[1]),
    ]
    gene_copies = row_copies(genes, genes_here, 0, gene_sems)
    half = theirs.shape[0]
    other_core = 1 - lax.axis_index("sub")
    row_starts = row_copies(counts, theirs, pl.multiple_of(other_core * half, half), row_sems)
    for copy in gene_copies + small_copies:
        copy.start()
    for copy in small_copies:
        copy.wait()
    factor[...] = mask_here[...].astype(F32) / counts_here[...].astype(F32)
    for copy in gene_copies:
        copy.wait()
    for copy in row_starts:
        copy.start()
    columns = genes.shape[1]
    wide = min(1024, columns)
    gram[...] = jnp.zeros_like(gram)

    @pl.loop(0, columns // wide)
    def _(step):
        at = pl.ds(pl.multiple_of(step * wide, wide), wide)
        piece = genes_here[:, at]
        turned[at, :] = piece.T
        gram[...] += jnp.dot(piece, turned[at, :], preferred_element_type=F32)

    for copy in row_starts:
        copy.wait()


def load(genes, counts, tile_mask, tile_counts):
    width, columns = genes.shape
    rows = counts.shape[0]
    here = pl.BlockSpec(memory_space=pltpu.VMEM)
    there = pl.BlockSpec(memory_space=pltpu.HBM)
    return pl.pallas_call(
        load_kernel,
        out_shape=(
            jax.ShapeDtypeStruct((width, width), F32),
            jax.ShapeDtypeStruct(tile_mask.shape, F32),
            pltpu.VMEM((columns, width), BF16),
            pltpu.VMEM((rows // 2, columns), BF16),
        ),
        in_specs=[there] * 4,
        out_specs=(here,) * 4,
        scratch_shapes=[
            pltpu.VMEM((width, columns), BF16),
            pltpu.VMEM(tile_mask.shape, jnp.int32),
            pltpu.VMEM(tile_mask.shape, jnp.int32),
            pltpu.SemaphoreType.DMA((4,)),
            pltpu.SemaphoreType.DMA((8,)),
            pltpu.SemaphoreType.DMA((2,)),
        ],
        compiler_params=params(),
        cost_estimate=cost(1, 1),
        name="load",
    )(away(genes), away(counts), away(tile_mask), away(tile_counts))


def add_cross(first_row, start, stop, factor, counts, turned, total):
    tile = counts.shape[1] // factor.shape[1]
    at_once = min(4, stop - start)

    @pl.loop(start // at_once, stop // at_once)
    def _(step):
        sums = None
        for col in range(at_once):
            place = step * at_once + col
            at = pl.ds(pl.multiple_of(place * tile, tile), tile)
            product = jnp.dot(counts[:, at], turned[at, :], preferred_element_type=F32)
            product = jnp.concatenate(
                [
                    product[row * tile : (row + 1) * tile] * factor[first_row + row, place]
                    for row in range(counts.shape[0] // tile)
                ],
                axis=0,
            )
            sums = product if sums is None else sums + product
        total[...] += sums


def cross_early_kernel(
    split, factor, theirs, turned, counts, cross_a, cross_b, low, mine, total, sems
):
    half = theirs.shape[0]
    core = lax.axis_index("sub")
    copies = row_copies(counts, mine, pl.multiple_of(core * half, half), sems)
    for copy in copies:
        copy.start()
    gene_tiles = factor.shape[1]
    row_tiles = factor.shape[0] // 2
    total[...] = jnp.zeros_like(total)
    add_cross((1 - core) * row_tiles, 0, gene_tiles, factor, theirs, turned, total)
    cross_a[...] = total[: half // 2].T
    cross_b[...] = total[half // 2 :].T
    for copy in copies:
        copy.wait()
    low[...] = jnp.zeros_like(low)
    add_cross(core * row_tiles, 0, split, factor, mine, turned, low)


def cross_early(split, factor, theirs, turned, counts):
    half, columns = theirs.shape
    width = turned.shape[1]
    here = pl.BlockSpec(memory_space=pltpu.VMEM)
    return pl.pallas_call(
        functools.partial(cross_early_kernel, split),
        out_shape=(
            jax.ShapeDtypeStruct((width, half // 2), F32),
            jax.ShapeDtypeStruct((width, half // 2), F32),
            jax.ShapeDtypeStruct((half, width), F32),
            pltpu.VMEM((half, columns), BF16),
        ),
        in_specs=[
            pl.BlockSpec(memory_space=pltpu.SMEM),
            here,
            here,
            pl.BlockSpec(memory_space=pltpu.HBM),
        ],
        out_specs=(here,) * 4,
        scratch_shapes=[pltpu.VMEM((half, width), F32), pltpu.SemaphoreType.DMA((8,))],
        compiler_params=params(),
        cost_estimate=cost(1, 1),
        name="cross_early",
    )(factor, held(theirs), held(turned), away(counts))


def cross_late_kernel(split, factor, low, counts, turned, cross, total):
    total[...] = low[...]
    first_row = lax.axis_index("sub") * (factor.shape[0] // 2)
    add_cross(first_row, split, factor.shape[1], factor, counts, turned, total)
    cross[...] = total[...].T


def call(kernel, name, out_shape, token, *args, scratch=(), smem=0, aliases=None, out=None):
    here = pl.BlockSpec(memory_space=pltpu.VMEM)
    there = pl.BlockSpec(memory_space=pltpu.SMEM)
    wherever = pl.BlockSpec(memory_space=pl.ANY)
    single = not isinstance(out_shape, tuple)
    specs = [there] * smem + [here] * (len(args) - smem)
    if aliases:
        specs[-1] = wherever
    out = out or here
    return pl.pallas_call(
        lambda token, *refs: kernel(*refs),
        out_shape=out_shape,
        in_specs=[wherever] + specs,
        out_specs=out if single else (out,) * len(out_shape),
        scratch_shapes=list(scratch),
        input_output_aliases=aliases or {},
        compiler_params=params(),
        cost_estimate=cost(1, 1),
        name=name,
    )(token, *args)


def fold_kernel(axis, bit, left, right, kept, sent):
    half = kept.shape[1]
    upper = (lax.axis_index(axis) & bit) != 0

    @pl.when(upper)
    def _():
        kept[...] = left[:, half:] + right[:, half:]
        sent[...] = left[:, :half] + right[:, :half]

    @pl.when(jnp.logical_not(upper))
    def _():
        kept[...] = left[:, :half] + right[:, :half]
        sent[...] = left[:, half:] + right[:, half:]


def first_fold_kernel(axis, bit, left, right_low, right_high, kept, sent):
    half = kept.shape[1]
    upper = (lax.axis_index(axis) & bit) != 0

    @pl.when(upper)
    def _():
        kept[...] = left[:, half:] + right_high[...]
        sent[...] = left[:, :half] + right_low[...]

    @pl.when(jnp.logical_not(upper))
    def _():
        kept[...] = left[:, :half] + right_low[...]
        sent[...] = left[:, half:] + right_high[...]


def first_fold(axis, bit, token, left, right_low, right_high):
    shape = jax.ShapeDtypeStruct(right_low.shape, F32)
    return call(
        functools.partial(first_fold_kernel, axis, bit),
        "fold", (shape, shape), token, left, right_low, right_high,
    )


def fold(axis, bit, token, left, right):
    shape = jax.ShapeDtypeStruct((left.shape[0], left.shape[1] // 2), F32)
    return call(
        functools.partial(fold_kernel, axis, bit), "fold", (shape, shape), token, left, right
    )


def side_kernel(axis, bit, dim, mine, theirs, out):
    size = mine.shape[dim]
    low = (slice(None),) * dim + (slice(0, size),)
    high = (slice(None),) * dim + (slice(size, 2 * size),)
    upper = (lax.axis_index(axis) & bit) != 0

    @pl.when(upper)
    def _():
        out[low], out[high] = theirs[...], mine[...]

    @pl.when(jnp.logical_not(upper))
    def _():
        out[low], out[high] = mine[...], theirs[...]


def side(axis, bit, dim, token, mine, theirs):
    shape = list(mine.shape)
    shape[dim] *= 2
    return call(
        functools.partial(side_kernel, axis, bit, dim),
        "side", jax.ShapeDtypeStruct(tuple(shape), mine.dtype), token, mine, theirs,
    )


def halves(value):
    high = value.astype(BF16)
    return high, (value - high.astype(F32)).astype(BF16)


def product3(left, right):
    left_high, left_low = left
    right_high, right_low = right
    dot = functools.partial(jnp.dot, preferred_element_type=F32)
    return dot(left_high, right_high) + (
        dot(left_high, right_low) + dot(left_low, right_high)
    )


def inverse_kernel(gram_a, gram_b, inverse, rho_out):
    gram = gram_a[...] + gram_b[...]
    width = gram.shape[0]
    shape = (width, width)
    diagonal = lax.broadcasted_iota(jnp.int32, shape, 0) == lax.broadcasted_iota(
        jnp.int32, shape, 1
    )
    eye = jnp.where(diagonal, 1.0, 0.0).astype(F32)
    rho = jnp.sum(gram * eye) / width
    rho_out[...] = jnp.full(rho_out.shape, rho, F32)
    scale = 1.0 / jnp.full((1, 1), rho, F32)
    matrix = gram * scale + eye
    low = 2.0 / (width + 2.0)
    guess = low * eye
    image = low * matrix
    first = True
    while True:
        low = low * (2.0 - low)
        gain = 2.0 / (1.0 + low)
        low = gain * low
        done = 1.0 - low < 2e-3
        step = halves(gain * (2.0 * eye - image))
        if first:
            guess = guess[0:1, 0:1] * (gain * (2.0 * eye - image))
        else:
            guess = product3(halves(guess), step)
        first = False
        if done:
            break
        image = product3(halves(image), step)
    rest = eye - jnp.dot(
        matrix, guess, preferred_element_type=F32, precision=lax.Precision.HIGHEST
    )
    rest_halves = halves(rest)
    series = rest + product3(rest_halves, rest_halves)
    inverse[...] = (guess + product3(halves(guess), halves(series))) * scale


def shifted_inverse(gram_a, gram_b):
    width = gram_a.shape[0]
    whole = pl.BlockSpec(memory_space=pltpu.VMEM)
    return pl.pallas_call(
        inverse_kernel,
        out_shape=(
            jax.ShapeDtypeStruct((width, width), F32),
            jax.ShapeDtypeStruct((8, 128), F32),
        ),
        in_specs=[whole, whole],
        out_specs=(whole, whole),
        compiler_params=params(),
        cost_estimate=cost(2 * 60 * width**3, 12 * width**2),
        name="inverse",
    )(gram_a, gram_b)


def admm_kernel(genes, rho_block, cross_a, cross_b, inverse, start, columns_out):
    rows = cross_a.shape[1]
    place = lax.axis_index("sub") * genes + lax.axis_index("gene")
    rho = rho_block[0:1, 0:1]
    cross = cross_a[...] + cross_b[...]
    inverse_halves = halves(inverse[...])
    zvalue = start[pl.ds(pl.multiple_of(place * rows, rows), rows), :].astype(F32).T
    uvalue = jnp.zeros_like(zvalue)
    for _ in range(ITERS):
        vvalue = product3(inverse_halves, halves(cross + rho * (zvalue - uvalue)))
        zvalue = jnp.maximum(vvalue + uvalue, 0.0)
        uvalue = uvalue + vvalue - zvalue
    columns_out[...] = zvalue.astype(BF16)


def products_kernel(tile, line, start, chunk, factor, theirs, mine, columns, *outs):
    only_first = len(outs) == 1
    block = line.block(1 if only_first else 2, 0)
    size = mine.shape[1] // line.size
    span = min(tile, chunk)
    wide = 2 * span if chunk % (2 * span) == 0 else span
    steps = chunk // wide
    row_tiles = columns.shape[1] // tile // 2
    core = lax.axis_index("sub")

    @pl.loop(0, steps if only_first else line.size * steps)
    def _(turn):
        order, step = (block, turn) if only_first else (turn // steps, lax.rem(turn, steps))
        first = pl.multiple_of(order * size + start + step * wide, span)
        total = None
        for counts, side, place in [
            (counts, side, place)
            for counts, side in ((theirs, 1 - core), (mine, core))
            for place in range(row_tiles)
        ]:
            row = side * row_tiles + place
            part = jnp.dot(
                columns[:, pl.ds(pl.multiple_of(row * tile, tile), tile)],
                counts[place * tile : (place + 1) * tile, pl.ds(first, wide)],
                preferred_element_type=F32,
            )
            scales = [
                jnp.full((1, span), factor[row, (first + col * span) // tile], F32)
                for col in range(wide // span)
            ]
            part = jnp.concatenate(scales, axis=1) * part
            total = part if total is None else total + part
        total = total.astype(BF16)
        at = pl.ds(pl.multiple_of(step * wide, span), wide)
        if only_first:
            outs[0][:, at] = total
        else:
            outs[0][order, :, at] = total

            @pl.when(order == block)
            def _():
                outs[1][:, at] = total


def products(only_first, line, start, chunk, token, factor, theirs, mine, columns):
    width, rows = columns.shape
    tile = rows // factor.shape[0]
    out_shape = (jax.ShapeDtypeStruct((width, chunk), BF16),)
    if not only_first:
        out_shape = (jax.ShapeDtypeStruct((line.size, width, chunk), BF16),) + out_shape
    return call(
        functools.partial(products_kernel, tile, line, start, chunk),
        "products", out_shape, token, factor, held(theirs), held(mine), columns, smem=1,
    )


def turn_kernel(value, out):
    out[...] = value[...].astype(F32).T.astype(out.dtype)


def turn(token, value):
    shape = jax.ShapeDtypeStruct(value.shape[::-1], value.dtype)
    return call(turn_kernel, "turn", shape, token, value)


def row_share_kernel(columns, out):
    part = out.shape[0]
    place = lax.axis_index("gene")
    share = columns[pl.ds(pl.multiple_of(place * part, part), part), :]
    out[...] = contract_last(share, columns[...]).astype(out.dtype)


def row_share(part, token, columns):
    shape = jax.ShapeDtypeStruct((part, columns.shape[0]), BF16)
    return call(row_share_kernel, "row_share", shape, token, columns)


def plus_kernel(left, right, out):
    out[...] = (left[...].astype(F32) + right[...].astype(F32)).astype(out.dtype)


def hop_kernel(kind, targets, own, arrived, out):
    cell = lax.axis_index("cell")
    reached = cell == targets[0]
    for target in targets[1:]:
        reached = jnp.logical_or(reached, cell == target)
    more = arrived[...].astype(F32)
    base = own[...].astype(F32)
    value = base + more if kind == "sum" else more
    out[...] = jnp.where(reached, value, base).astype(out.dtype)


def hop(kind, targets, token, own, arrived):
    shape = jax.ShapeDtypeStruct(own.shape, own.dtype)
    return call(functools.partial(hop_kernel, kind, targets), "hop", shape, token, own, arrived)


def operand_kernel(line, phase, parity, total, before, out):
    own = total[line.block(phase, parity)].astype(F32)
    out[...] = (own + before[...].astype(F32)).astype(BF16)


def operand(line, phase, parity, token, total, before):
    shape = jax.ShapeDtypeStruct(before.shape, BF16)
    return call(
        functools.partial(operand_kernel, line, phase, parity),
        "operand", shape, token, total, before,
    )


def keep_kernel(start, total, first, second, *refs):
    out, turned, sems = refs[-3:]
    width, chunk = first.shape
    pieces = sems.shape[0]
    wide = chunk // pieces
    own = total.at[lax.axis_index("cell")]
    copies = []
    for piece in range(pieces):
        at = slice(piece * wide, (piece + 1) * wide)
        value = first[:, at].astype(F32) + second[:, at].astype(F32)
        turned[at] = (own[:, at].astype(F32) + value).T
        copies.append(
            pltpu.make_async_copy(
                turned.at[at], out.at[pl.ds(start + piece * wide, wide)], sems.at[piece]
            )
        )
        copies[-1].start()
    for copy in copies:
        copy.wait()


def keep(block, start, token, total, first, second, out):
    width, chunk = first.shape
    pieces = max(1, chunk // 256)
    return call(
        functools.partial(keep_kernel, start),
        "keep", jax.ShapeDtypeStruct((block, width), F32), token,
        total, first, second, *([] if out is None else [out]),
        scratch=[pltpu.VMEM((chunk, width), F32), pltpu.SemaphoreType.DMA((pieces,))],
        aliases=None if out is None else {4: 0},
        out=pl.BlockSpec(memory_space=pl.ANY),
    )


class Line:
    def __init__(self, size):
        self.size = size

    def pairs(self, phase, parity):
        links = range(parity, self.size - 1, 2)
        used = [i for i in links if i < phase or i + 1 >= self.size - phase]
        return [(i, i + 1) for i in used] + [(i + 1, i) for i in used]

    def block(self, phase, parity):
        cell = lax.axis_index("cell")
        to_right = (cell & 1) == parity
        block = cell + jnp.where(to_right, self.size - phase, phase)
        return jnp.where(block >= self.size, block - self.size, block)

    def send(self, value, phase, parity):
        return lax.ppermute(value, "cell", self.pairs(phase, parity))


def swap(value, axis, size, step):
    return lax.ppermute(value, axis, [(i, i ^ step) for i in range(size)])


def pair_sums(value, axis, size, event):
    step = 1
    while step < size:
        arrived, event = after(swap(value, axis, size, step), event)
        value = value + arrived
        step *= 2
    return value, event


def after(value, event):
    return lax.optimization_barrier((value, event))


def chunk_sizes(block):
    return [block // 2, block // 2] if block % 1024 == 0 else [block]


def shards(sizes, counts, tile_mask, tile_counts, gene_factor, prev_factor):
    cells, genes, subs = sizes
    rows, columns = counts.shape
    width = gene_factor.shape[0]
    line = Line(cells)

    gram, factor, turned, theirs = load(gene_factor, counts, tile_mask, tile_counts)
    token = factor
    split = tile_mask.shape[1] // 8 * 4
    theirs_low, theirs_high, low, mine = cross_early(split, factor, theirs, turned, counts)
    gram, low = pair_sums(gram, "gene", genes, low)
    half = jax.ShapeDtypeStruct((width, rows // 2), F32)
    cross_a = call(
        functools.partial(cross_late_kernel, split), "cross_late", half, token,
        factor, low, held(mine), held(turned),
        smem=1, scratch=[pltpu.VMEM((rows // 2, width), F32)],
    )
    arrived_low = swap(theirs_low, "sub", subs, 1)
    arrived_high = swap(theirs_high, "sub", subs, 1)
    bit = genes // 2
    cross_a, sent = first_fold("gene", bit, token, cross_a, arrived_low, arrived_high)
    cross_b = swap(sent, "gene", genes, bit)
    bit //= 2
    while bit:
        cross_a, sent = fold("gene", bit, token, cross_a, cross_b)
        cross_b = swap(sent, "gene", genes, bit)
        bit //= 2
    gram_other = swap(gram, "sub", subs, 1)
    inverse, rho = shifted_inverse(gram, gram_other)
    share = jax.ShapeDtypeStruct((width, rows // (genes * subs)), BF16)
    columns_held = call(
        functools.partial(admm_kernel, genes),
        "admm", share, token, rho, cross_a, cross_b, inverse, prev_factor,
    )
    bit = 1
    while bit < genes:
        columns_arrived = swap(columns_held, "gene", genes, bit)
        columns_held = side("gene", bit, 1, token, columns_held, columns_arrived)
        bit *= 2
    token, rows_sum = after(token, row_share(width // genes, token, columns_held))
    columns_arrived = swap(columns_held, "sub", subs, 1)
    whole = side("sub", 1, 1, token, columns_held, columns_arrived)

    block = columns // cells
    chunks = chunk_sizes(block)
    starts = [sum(chunks[:i]) for i in range(len(chunks))]
    every = range(len(chunks))

    arrived = {}

    def send(value, phase, parity, index):
        pairs = line.pairs(phase, parity)
        arrived[phase, parity, index] = lax.ppermute(value, "cell", pairs) if pairs else None

    def resend(token, phase, parity, index):
        before = arrived[phase - 1, 1 - parity, index]
        if before is None:
            value = seconds[index]
        else:
            value = operand(line, phase, parity, token, totals[index], before)
            token, value = after(token, value)
        send(value, phase, parity, index)
        return token

    middle = cells // 2
    inward = [[(i, i + 1), (cells - 1 - i, cells - 2 - i)] for i in range(middle - 1)]
    outward = [[(b, a) for a, b in pairs] for pairs in reversed(inward)]
    hops = [("sum", p) for p in inward] + [("sum", [(middle - 1, middle), (middle, middle - 1)])]
    hops += [("copy", p) for p in outward]

    def hop_rows(token, rows_sum):
        kind, pairs = hops.pop(0)
        both = sorted(set(pairs) | {(b, a) for a, b in pairs})
        rows_arrived = lax.ppermute(rows_sum, "cell", both)
        targets = [b for _, b in pairs]
        return after(token, hop(kind, targets, token, rows_sum, rows_arrived))

    def side_rows(token, rows_sum, axis, size, bit):
        rows_arrived = swap(rows_sum, axis, size, bit)
        return after(token, side(axis, bit, 0, token, rows_sum, rows_arrived))

    for index in every:
        (first,) = products(
            True, line, starts[index], chunks[index], token, factor, theirs, mine, whole
        )
        token, first = after(token, first)
        for parity in (0, 1):
            send(first, 1, parity, index)
        if index == 0 and hops:
            token, rows_sum = hop_rows(token, rows_sum)
    totals, seconds = [], []
    for index in every:
        total, second = products(
            False, line, starts[index], chunks[index], token, factor, theirs, mine, whole
        )
        token, second = after(token, second)
        if hops:
            token, rows_sum = hop_rows(token, rows_sum)
        totals.append(total)
        seconds.append(second)
        for parity in (0, 1):
            token = resend(token, 2, parity, index)
    while hops:
        token, rows_sum = hop_rows(token, rows_sum)
    new_factor = turn(token, whole)
    token, new_factor = after(token, new_factor)
    rows_arrived = swap(rows_sum, "sub", subs, 1)
    shape = jax.ShapeDtypeStruct(rows_sum.shape, F32)
    token, rows_sum = after(token, call(plus_kernel, "plus", shape, token, rows_sum, rows_arrived))
    bits = [1 << i for i in range((genes - 1).bit_length())]
    for phase in range(3, cells):
        for index in every:
            for parity in (0, 1):
                token = resend(token, phase, parity, index)
                if bits:
                    token, rows_sum = side_rows(token, rows_sum, "gene", genes, bits.pop(0))
    data_products = None
    last = cells - 1
    for index in every:
        data_products = keep(
            block, starts[index], token, totals[index],
            arrived[last, 0, index], arrived[last, 1, index], data_products,
        )
        token, data_products = after(token, data_products)
    return (new_factor, rows_sum, data_products)


def solution(mesh):
    sizes = (mesh.shape["cell"], mesh.shape["gene"], mesh.shape["sub"])
    return jax.shard_map(
        functools.partial(shards, sizes),
        mesh=mesh,
        in_specs=(
            P(("groups", "cell"), ("gene", "sub")),
            P(("groups", "cell"), ("gene", "sub")),
            P(("groups", "cell"), ("gene", "sub")),
            P("groups", ("gene", "sub")),
            P(("groups", "cell"), None),
        ),
        out_specs=(
            P(("groups", "cell"), None),
            P("groups", None),
            P(("groups", "gene", "sub", "cell"), None),
        ),
        check_vma=False,
    )
```

```python
import functools

import jax
import jax.numpy as jnp
import numpy as np
from jax import lax
from jax.experimental import pallas as pl
from jax.experimental.pallas import tpu as pltpu
from jax.sharding import PartitionSpec as P

ITERS = 3
F32 = jnp.float32
BF16 = jnp.bfloat16
MIB = 1024 * 1024


def params(limit=16):
    return pltpu.CompilerParams(vmem_limit_bytes=limit * MIB)


def away(value):
    return pltpu.with_memory_space_constraint(value, pltpu.HBM)


def held(value):
    return pltpu.with_memory_space_constraint(value, pltpu.VMEM)


def cost(flops, bytes_accessed):
    return pl.CostEstimate(flops=flops, bytes_accessed=bytes_accessed, transcendentals=0)


def contract_last(left, right):
    return lax.dot_general(
        left, right, (((1,), (1,)), ((), ())), preferred_element_type=F32
    )


def row_copies(source, target, first, sems):
    rows = target.shape[0]
    piece = max(rows // sems.shape[0], 16)
    return [
        pltpu.make_async_copy(
            source.at[pl.ds(first + i * piece, piece)],
            target.at[pl.ds(i * piece, piece)],
            sems.at[i],
        )
        for i in range(rows // piece)
    ]


def load_kernel(
    genes, counts, tile_mask, tile_counts, gram, factor, turned, theirs,
    genes_here, mask_here, counts_here, gene_sems, row_sems, small_sems,
):
    small_copies = [
        pltpu.make_async_copy(tile_mask, mask_here, small_sems.at[0]),
        pltpu.make_async_copy(tile_counts, counts_here, small_sems.at[1]),
    ]
    gene_copies = row_copies(genes, genes_here, 0, gene_sems)
    half = theirs.shape[0]
    other_core = 1 - lax.axis_index("sub")
    row_starts = row_copies(counts, theirs, pl.multiple_of(other_core * half, half), row_sems)
    for copy in gene_copies + small_copies:
        copy.start()
    for copy in small_copies:
        copy.wait()
    factor[...] = mask_here[...].astype(F32) / counts_here[...].astype(F32)
    for copy in gene_copies:
        copy.wait()
    for copy in row_starts:
        copy.start()
    columns = genes.shape[1]
    wide = min(1024, columns)
    gram[...] = jnp.zeros_like(gram)

    @pl.loop(0, columns // wide)
    def _(step):
        at = pl.ds(pl.multiple_of(step * wide, wide), wide)
        piece = genes_here[:, at]
        turned[at, :] = piece.T
        gram[...] += jnp.dot(piece, turned[at, :], preferred_element_type=F32)

    for copy in row_starts:
        copy.wait()


def load(genes, counts, tile_mask, tile_counts):
    width, columns = genes.shape
    rows = counts.shape[0]
    here = pl.BlockSpec(memory_space=pltpu.VMEM)
    there = pl.BlockSpec(memory_space=pltpu.HBM)
    return pl.pallas_call(
        load_kernel,
        out_shape=(
            jax.ShapeDtypeStruct((width, width), F32),
            jax.ShapeDtypeStruct(tile_mask.shape, F32),
            pltpu.VMEM((columns, width), BF16),
            pltpu.VMEM((rows // 2, columns), BF16),
        ),
        in_specs=[there] * 4,
        out_specs=(here,) * 4,
        scratch_shapes=[
            pltpu.VMEM((width, columns), BF16),
            pltpu.VMEM(tile_mask.shape, jnp.int32),
            pltpu.VMEM(tile_mask.shape, jnp.int32),
            pltpu.SemaphoreType.DMA((4,)),
            pltpu.SemaphoreType.DMA((8,)),
            pltpu.SemaphoreType.DMA((2,)),
        ],
        compiler_params=params(),
        cost_estimate=cost(1, 1),
        name="load",
    )(away(genes), away(counts), away(tile_mask), away(tile_counts))


def scaled(counts, factors):
    tile_rows = counts.shape[0] // len(factors)
    tile_columns = counts.shape[1] // len(factors[0])
    rows = []
    for row, scales in enumerate(factors):
        part = counts[row * tile_rows : (row + 1) * tile_rows]
        rows.append(
            jnp.concatenate(
                [
                    (
                        part[:, col * tile_columns : (col + 1) * tile_columns].astype(F32) * scale
                    ).astype(BF16)
                    for col, scale in enumerate(scales)
                ],
                axis=1,
            )
        )
    return jnp.concatenate(rows, axis=0)


def add_cross(first_row, factor, counts, turned, total):
    gene_tiles = factor.shape[1]
    tile = counts.shape[1] // gene_tiles
    row_tiles = counts.shape[0] // tile
    at_once = min(4, gene_tiles)

    @pl.loop(0, gene_tiles // at_once)
    def _(step):
        at = pl.ds(pl.multiple_of(step * at_once * tile, at_once * tile), at_once * tile)
        factors = [
            [factor[first_row + row, step * at_once + col] for col in range(at_once)]
            for row in range(row_tiles)
        ]
        total[...] += jnp.dot(
            scaled(counts[:, at], factors), turned[at, :], preferred_element_type=F32
        )


def cross_theirs_kernel(factor, theirs, turned, counts, low, high, mine, total, sems):
    half = theirs.shape[0]
    core = lax.axis_index("sub")
    copies = row_copies(counts, mine, pl.multiple_of(core * half, half), sems)
    for copy in copies:
        copy.start()
    total[...] = jnp.zeros_like(total)
    add_cross((1 - core) * (factor.shape[0] // 2), factor, theirs, turned, total)
    low[...] = total[: half // 2].T
    high[...] = total[half // 2 :].T
    for copy in copies:
        copy.wait()


def cross_theirs(factor, theirs, turned, counts):
    half, columns = theirs.shape
    width = turned.shape[1]
    here = pl.BlockSpec(memory_space=pltpu.VMEM)
    piece = jax.ShapeDtypeStruct((width, half // 2), F32)
    return pl.pallas_call(
        cross_theirs_kernel,
        out_shape=(piece, piece, pltpu.VMEM((half, columns), BF16)),
        in_specs=[
            pl.BlockSpec(memory_space=pltpu.SMEM),
            here,
            here,
            pl.BlockSpec(memory_space=pltpu.HBM),
        ],
        out_specs=(here,) * 3,
        scratch_shapes=[pltpu.VMEM((half, width), F32), pltpu.SemaphoreType.DMA((8,))],
        compiler_params=params(),
        cost_estimate=cost(1, 1),
        name="cross_theirs",
    )(factor, held(theirs), held(turned), away(counts))


def cross_piece_kernel(bit, kept, factor, mine, turned, cross, total):
    rows = total.shape[0]
    upper = ((lax.axis_index("gene") & bit) != 0) == kept
    piece = jnp.where(upper, 1, 0)
    first = lax.axis_index("sub") * (factor.shape[0] // 2)
    first += piece * (factor.shape[0] // 4)
    total[...] = jnp.zeros_like(total)
    counts = mine.at[pl.ds(pl.multiple_of(piece * rows, rows), rows)]
    add_cross(first, factor, counts, turned, total)
    cross[...] = total[...].T


def cross_piece(bit, kept, token, factor, mine, turned):
    rows = mine.shape[0] // 2
    width = turned.shape[1]
    return call(
        functools.partial(cross_piece_kernel, bit, kept),
        "cross_piece", jax.ShapeDtypeStruct((width, rows), F32), token,
        factor, held(mine), held(turned),
        smem=1, scratch=[pltpu.VMEM((rows, width), F32)],
    )


def add_piece_kernel(bit, kept, left, low, high, out):
    upper = ((lax.axis_index("gene") & bit) != 0) == kept

    @pl.when(upper)
    def _():
        out[...] = left[...] + high[...]

    @pl.when(jnp.logical_not(upper))
    def _():
        out[...] = left[...] + low[...]


def add_piece(bit, kept, token, left, low, high):
    shape = jax.ShapeDtypeStruct(left.shape, F32)
    return call(
        functools.partial(add_piece_kernel, bit, kept), "add_piece", shape, token, left, low, high
    )


def call(kernel, name, out_shape, token, *args, scratch=(), smem=0, aliases=None, out=None):
    here = pl.BlockSpec(memory_space=pltpu.VMEM)
    there = pl.BlockSpec(memory_space=pltpu.SMEM)
    wherever = pl.BlockSpec(memory_space=pl.ANY)
    single = not isinstance(out_shape, tuple)
    specs = [there] * smem + [here] * (len(args) - smem)
    if aliases:
        specs[-1] = wherever
    out = out or here
    return pl.pallas_call(
        lambda token, *refs: kernel(*refs),
        out_shape=out_shape,
        in_specs=[wherever] + specs,
        out_specs=out if single else (out,) * len(out_shape),
        scratch_shapes=list(scratch),
        input_output_aliases=aliases or {},
        compiler_params=params(),
        cost_estimate=cost(1, 1),
        name=name,
    )(token, *args)


def fold_kernel(axis, bit, left, right, kept, sent):
    half = kept.shape[1]
    upper = (lax.axis_index(axis) & bit) != 0

    @pl.when(upper)
    def _():
        kept[...] = left[:, half:] + right[:, half:]
        sent[...] = left[:, :half] + right[:, :half]

    @pl.when(jnp.logical_not(upper))
    def _():
        kept[...] = left[:, :half] + right[:, :half]
        sent[...] = left[:, half:] + right[:, half:]


def fold(axis, bit, token, left, right):
    shape = jax.ShapeDtypeStruct((left.shape[0], left.shape[1] // 2), F32)
    return call(
        functools.partial(fold_kernel, axis, bit), "fold", (shape, shape), token, left, right
    )


def side_kernel(axis, bit, dim, mine, theirs, out):
    size = mine.shape[dim]
    low = (slice(None),) * dim + (slice(0, size),)
    high = (slice(None),) * dim + (slice(size, 2 * size),)
    upper = (lax.axis_index(axis) & bit) != 0

    @pl.when(upper)
    def _():
        out[low], out[high] = theirs[...], mine[...]

    @pl.when(jnp.logical_not(upper))
    def _():
        out[low], out[high] = mine[...], theirs[...]


def side(axis, bit, dim, token, mine, theirs):
    shape = list(mine.shape)
    shape[dim] *= 2
    return call(
        functools.partial(side_kernel, axis, bit, dim),
        "side", jax.ShapeDtypeStruct(tuple(shape), mine.dtype), token, mine, theirs,
    )


def halves(value):
    high = value.astype(BF16)
    return high, (value - high.astype(F32)).astype(BF16)


def product3(left, right):
    left_high, left_low = left
    right_high, right_low = right
    dot = functools.partial(jnp.dot, preferred_element_type=F32)
    return dot(left_high, right_high) + (
        dot(left_high, right_low) + dot(left_low, right_high)
    )


def inverse_kernel(gram_a, gram_b, inverse, rho_out):
    gram = gram_a[...] + gram_b[...]
    width = gram.shape[0]
    shape = (width, width)
    diagonal = lax.broadcasted_iota(jnp.int32, shape, 0) == lax.broadcasted_iota(
        jnp.int32, shape, 1
    )
    eye = jnp.where(diagonal, 1.0, 0.0).astype(F32)
    rho = jnp.sum(gram * eye) / width
    rho_out[...] = jnp.full(rho_out.shape, rho, F32)
    scale = 1.0 / jnp.full((1, 1), rho, F32)
    matrix = gram * scale + eye
    low = 2.0 / (width + 2.0)
    guess = low * eye
    image = low * matrix
    first = True
    while True:
        low = low * (2.0 - low)
        gain = 2.0 / (1.0 + low)
        low = gain * low
        done = 1.0 - low < 2e-3
        step = halves(gain * (2.0 * eye - image))
        if first:
            guess = guess[0:1, 0:1] * (gain * (2.0 * eye - image))
        else:
            guess = product3(halves(guess), step)
        first = False
        if done:
            break
        image = product3(halves(image), step)
    rest = eye - jnp.dot(
        matrix, guess, preferred_element_type=F32, precision=lax.Precision.HIGHEST
    )
    rest_halves = halves(rest)
    series = rest + product3(rest_halves, rest_halves)
    inverse[...] = (guess + product3(halves(guess), halves(series))) * scale


def shifted_inverse(gram_a, gram_b):
    width = gram_a.shape[0]
    whole = pl.BlockSpec(memory_space=pltpu.VMEM)
    return pl.pallas_call(
        inverse_kernel,
        out_shape=(
            jax.ShapeDtypeStruct((width, width), F32),
            jax.ShapeDtypeStruct((8, 128), F32),
        ),
        in_specs=[whole, whole],
        out_specs=(whole, whole),
        compiler_params=params(),
        cost_estimate=cost(2 * 60 * width**3, 12 * width**2),
        name="inverse",
    )(gram_a, gram_b)


def admm_kernel(genes, rho_block, cross_a, cross_b, inverse, start, columns_out):
    rows = cross_a.shape[1]
    place = lax.axis_index("sub") * genes + lax.axis_index("gene")
    rho = rho_block[0:1, 0:1]
    cross = cross_a[...] + cross_b[...]
    inverse_halves = halves(inverse[...])
    zvalue = start[pl.ds(pl.multiple_of(place * rows, rows), rows), :].astype(F32).T
    uvalue = jnp.zeros_like(zvalue)
    for _ in range(ITERS):
        vvalue = product3(inverse_halves, halves(cross + rho * (zvalue - uvalue)))
        zvalue = jnp.maximum(vvalue + uvalue, 0.0)
        uvalue = uvalue + vvalue - zvalue
    columns_out[...] = zvalue.astype(BF16)


def products_kernel(tile, line, start, chunk, factor, theirs, mine, columns, *outs):
    only_first = len(outs) == 1
    block = line.block(1 if only_first else 2, 0)
    size = mine.shape[1] // line.size
    span = min(tile, chunk)
    wide = 2 * span if chunk % (2 * span) == 0 else span
    steps = chunk // wide
    row_tiles = columns.shape[1] // tile // 2
    core = lax.axis_index("sub")

    @pl.loop(0, steps if only_first else line.size * steps)
    def _(turn):
        order, step = (block, turn) if only_first else (turn // steps, lax.rem(turn, steps))
        first = pl.multiple_of(order * size + start + step * wide, span)
        total = None
        for counts, side in ((theirs, 1 - core), (mine, core)):
            factors = [
                [
                    factor[side * row_tiles + row, (first + col * span) // tile]
                    for col in range(wide // span)
                ]
                for row in range(row_tiles)
            ]
            cells = row_tiles * tile
            part = jnp.dot(
                columns[:, pl.ds(pl.multiple_of(side * cells, cells), cells)],
                scaled(counts[:, pl.ds(first, wide)], factors),
                preferred_element_type=F32,
            )
            total = part if total is None else total + part
        total = total.astype(BF16)
        at = pl.ds(pl.multiple_of(step * wide, span), wide)
        if only_first:
            outs[0][:, at] = total
        else:
            outs[0][order, :, at] = total

            @pl.when(order == block)
            def _():
                outs[1][:, at] = total


def products(only_first, line, start, chunk, token, factor, theirs, mine, columns):
    width, rows = columns.shape
    tile = rows // factor.shape[0]
    out_shape = (jax.ShapeDtypeStruct((width, chunk), BF16),)
    if not only_first:
        out_shape = (jax.ShapeDtypeStruct((line.size, width, chunk), BF16),) + out_shape
    return call(
        functools.partial(products_kernel, tile, line, start, chunk),
        "products", out_shape, token, factor, held(theirs), held(mine), columns, smem=1,
    )


def turn_kernel(value, out):
    out[...] = value[...].astype(F32).T.astype(out.dtype)


def turn(token, value):
    shape = jax.ShapeDtypeStruct(value.shape[::-1], value.dtype)
    return call(turn_kernel, "turn", shape, token, value)


def row_share_kernel(columns, out):
    part = out.shape[0]
    place = lax.axis_index("gene")
    share = columns[pl.ds(pl.multiple_of(place * part, part), part), :]
    out[...] = contract_last(share, columns[...]).astype(out.dtype)


def row_share(part, token, columns):
    shape = jax.ShapeDtypeStruct((part, columns.shape[0]), BF16)
    return call(row_share_kernel, "row_share", shape, token, columns)


def plus_kernel(left, right, out):
    out[...] = (left[...].astype(F32) + right[...].astype(F32)).astype(out.dtype)


def hop_kernel(kind, targets, own, arrived, out):
    cell = lax.axis_index("cell")
    reached = cell == targets[0]
    for target in targets[1:]:
        reached = jnp.logical_or(reached, cell == target)
    more = arrived[...].astype(F32)
    base = own[...].astype(F32)
    value = base + more if kind == "sum" else more
    out[...] = jnp.where(reached, value, base).astype(out.dtype)


def hop(kind, targets, token, own, arrived):
    shape = jax.ShapeDtypeStruct(own.shape, own.dtype)
    return call(functools.partial(hop_kernel, kind, targets), "hop", shape, token, own, arrived)


def operand_kernel(line, phase, parity, total, before, out):
    own = total[line.block(phase, parity)].astype(F32)
    out[...] = (own + before[...].astype(F32)).astype(BF16)


def operand(line, phase, parity, token, total, before):
    shape = jax.ShapeDtypeStruct(before.shape, BF16)
    return call(
        functools.partial(operand_kernel, line, phase, parity),
        "operand", shape, token, total, before,
    )


def keep_kernel(start, total, first, second, *refs):
    out, turned, sems = refs[-3:]
    width, chunk = first.shape
    pieces = sems.shape[0]
    wide = chunk // pieces
    own = total.at[lax.axis_index("cell")]
    copies = []
    for piece in range(pieces):
        at = slice(piece * wide, (piece + 1) * wide)
        value = first[:, at].astype(F32) + second[:, at].astype(F32)
        turned[at] = (own[:, at].astype(F32) + value).T
        copies.append(
            pltpu.make_async_copy(
                turned.at[at], out.at[pl.ds(start + piece * wide, wide)], sems.at[piece]
            )
        )
        copies[-1].start()
    for copy in copies:
        copy.wait()


def keep(block, start, token, total, first, second, out):
    width, chunk = first.shape
    pieces = max(1, chunk // 256)
    return call(
        functools.partial(keep_kernel, start),
        "keep", jax.ShapeDtypeStruct((block, width), F32), token,
        total, first, second, *([] if out is None else [out]),
        scratch=[pltpu.VMEM((chunk, width), F32), pltpu.SemaphoreType.DMA((pieces,))],
        aliases=None if out is None else {4: 0},
        out=pl.BlockSpec(memory_space=pl.ANY),
    )


class Line:
    def __init__(self, size):
        self.size = size

    def pairs(self, phase, parity, exchange=False):
        links = range(parity, self.size - 1, 2)
        right = [(i, i + 1) for i in links if i < phase]
        left = [(i + 1, i) for i in links if i + 1 >= self.size - phase]
        pairs = right + left
        if exchange:
            pairs = sorted(set(pairs) | {(b, a) for a, b in pairs})
        return pairs

    def block(self, phase, parity):
        cell = lax.axis_index("cell")
        to_right = (cell & 1) == parity
        block = cell + jnp.where(to_right, self.size - phase, phase)
        return jnp.where(block >= self.size, block - self.size, block)

    def send(self, value, phase, parity):
        return lax.ppermute(value, "cell", self.pairs(phase, parity))


def swap(value, axis, size, step):
    return lax.ppermute(value, axis, [(i, i ^ step) for i in range(size)])


def pair_sums(value, axis, size, event):
    step = 1
    while step < size:
        arrived, event = after(swap(value, axis, size, step), event)
        value = value + arrived
        step *= 2
    return value, event


def after(value, event):
    return lax.optimization_barrier((value, event))


def chunk_sizes(block):
    return [block // 2, block // 2] if block % 1024 == 0 else [block]


def shards(sizes, counts, tile_mask, tile_counts, gene_factor, prev_factor):
    cells, genes, subs = sizes
    rows, columns = counts.shape
    width = gene_factor.shape[0]
    line = Line(cells)

    gram, factor, turned, theirs = load(gene_factor, counts, tile_mask, tile_counts)
    token = factor
    theirs_low, theirs_high, mine = cross_theirs(factor, theirs, turned, counts)
    arrived_low = swap(theirs_low, "sub", subs, 1)
    arrived_high = swap(theirs_high, "sub", subs, 1)
    bit = genes // 2
    own_sent = cross_piece(bit, False, token, factor, mine, turned)
    sent = add_piece(bit, False, token, own_sent, arrived_low, arrived_high)
    cross_b = swap(sent, "gene", genes, bit)
    gram, (factor_late, _) = pair_sums(gram, "gene", genes, (factor, own_sent))
    cross_a = cross_piece(bit, True, token, factor_late, mine, turned)
    cross_a = add_piece(bit, True, token, cross_a, arrived_low, arrived_high)
    bit //= 2
    while bit:
        cross_a, sent = fold("gene", bit, token, cross_a, cross_b)
        cross_b = swap(sent, "gene", genes, bit)
        bit //= 2
    gram_other = swap(gram, "sub", subs, 1)
    inverse, rho = shifted_inverse(gram, gram_other)
    share = jax.ShapeDtypeStruct((width, rows // (genes * subs)), BF16)
    columns_held = call(
        functools.partial(admm_kernel, genes),
        "admm", share, token, rho, cross_a, cross_b, inverse, prev_factor,
    )
    bit = 1
    while bit < genes:
        columns_arrived = swap(columns_held, "gene", genes, bit)
        columns_held = side("gene", bit, 1, token, columns_held, columns_arrived)
        bit *= 2
    token, rows_sum = after(token, row_share(width // genes, token, columns_held))
    columns_arrived = swap(columns_held, "sub", subs, 1)
    whole = side("sub", 1, 1, token, columns_held, columns_arrived)

    block = columns // cells
    chunks = chunk_sizes(block)
    starts = [sum(chunks[:i]) for i in range(len(chunks))]
    every = range(len(chunks))

    arrived = {}

    def send(value, phase, parity, index):
        pairs = line.pairs(phase, parity, exchange=phase == 1 and index == 0)
        arrived[phase, parity, index] = lax.ppermute(value, "cell", pairs) if pairs else None

    def resend(token, phase, parity, index):
        before = arrived[phase - 1, 1 - parity, index]
        if before is None:
            value = seconds[index]
        else:
            value = operand(line, phase, parity, token, totals[index], before)
            token, value = after(token, value)
        send(value, phase, parity, index)
        return token

    middle = cells // 2
    inward = [[(i, i + 1), (cells - 1 - i, cells - 2 - i)] for i in range(middle - 1)]
    outward = [[(b, a) for a, b in pairs] for pairs in reversed(inward)]
    hops = [("sum", p) for p in inward] + [("sum", [(middle - 1, middle), (middle, middle - 1)])]
    hops += [("copy", p) for p in outward]

    def hop_rows(token, rows_sum):
        kind, pairs = hops.pop(0)
        both = sorted(set(pairs) | {(b, a) for a, b in pairs})
        rows_arrived = lax.ppermute(rows_sum, "cell", both)
        targets = [b for _, b in pairs]
        return after(token, hop(kind, targets, token, rows_sum, rows_arrived))

    def side_rows(token, rows_sum, axis, size, bit):
        rows_arrived = swap(rows_sum, axis, size, bit)
        return after(token, side(axis, bit, 0, token, rows_sum, rows_arrived))

    for index in every:
        (first,) = products(
            True, line, starts[index], chunks[index], token, factor, theirs, mine, whole
        )
        token, first = after(token, first)
        for parity in (0, 1):
            send(first, 1, parity, index)
        if index == 0 and hops:
            token, rows_sum = hop_rows(token, rows_sum)
    totals, seconds = [], []
    for index in every:
        total, second = products(
            False, line, starts[index], chunks[index], token, factor, theirs, mine, whole
        )
        token, second = after(token, second)
        if hops:
            token, rows_sum = hop_rows(token, rows_sum)
        totals.append(total)
        seconds.append(second)
        for parity in (0, 1):
            token = resend(token, 2, parity, index)
    while hops:
        token, rows_sum = hop_rows(token, rows_sum)
    new_factor = turn(token, whole)
    token, new_factor = after(token, new_factor)
    rows_arrived = swap(rows_sum, "sub", subs, 1)
    shape = jax.ShapeDtypeStruct(rows_sum.shape, F32)
    token, rows_sum = after(token, call(plus_kernel, "plus", shape, token, rows_sum, rows_arrived))
    bits = [1 << i for i in range((genes - 1).bit_length())]
    for phase in range(3, cells):
        for index in every:
            for parity in (0, 1):
                token = resend(token, phase, parity, index)
                if bits:
                    token, rows_sum = side_rows(token, rows_sum, "gene", genes, bits.pop(0))
    data_products = None
    last = cells - 1
    for index in every:
        data_products = keep(
            block, starts[index], token, totals[index],
            arrived[last, 0, index], arrived[last, 1, index], data_products,
        )
        token, data_products = after(token, data_products)
    return (new_factor, rows_sum, data_products)


def solution(mesh):
    sizes = (mesh.shape["cell"], mesh.shape["gene"], mesh.shape["sub"])
    return jax.shard_map(
        functools.partial(shards, sizes),
        mesh=mesh,
        in_specs=(
            P(("groups", "cell"), ("gene", "sub")),
            P(("groups", "cell"), ("gene", "sub")),
            P(("groups", "cell"), ("gene", "sub")),
            P("groups", ("gene", "sub")),
            P(("groups", "cell"), None),
        ),
        out_specs=(
            P(("groups", "cell"), None),
            P("groups", None),
            P(("groups", "gene", "sub", "cell"), None),
        ),
        check_vma=False,
    )
```

```python
import functools

import jax
import jax.numpy as jnp
import numpy as np
from jax import lax
from jax.experimental import pallas as pl
from jax.experimental.pallas import tpu as pltpu
from jax.sharding import PartitionSpec as P

ITERS = 3
F32 = jnp.float32
BF16 = jnp.bfloat16
MIB = 1024 * 1024


def params(limit=16):
    return pltpu.CompilerParams(vmem_limit_bytes=limit * MIB)


def away(value):
    return pltpu.with_memory_space_constraint(value, pltpu.HBM)


def held(value):
    return pltpu.with_memory_space_constraint(value, pltpu.VMEM)


def cost(flops, bytes_accessed):
    return pl.CostEstimate(flops=flops, bytes_accessed=bytes_accessed, transcendentals=0)


def contract_last(left, right):
    return lax.dot_general(
        left, right, (((1,), (1,)), ((), ())), preferred_element_type=F32
    )


def row_copies(source, target, first, sems):
    rows = target.shape[0]
    piece = max(rows // sems.shape[0], 16)
    return [
        pltpu.make_async_copy(
            source.at[pl.ds(first + i * piece, piece)],
            target.at[pl.ds(i * piece, piece)],
            sems.at[i],
        )
        for i in range(rows // piece)
    ]


def pieces_of(rows, bit):
    core = lax.axis_index("sub")
    upper = (lax.axis_index("gene") & bit) != 0
    half, quarter = rows // 2, rows // 4
    mine = core * half
    kept = jnp.where(upper, quarter, 0)
    return [
        pl.multiple_of((1 - core) * half, quarter),
        pl.multiple_of(mine + quarter - kept, quarter),
        pl.multiple_of(mine + kept, quarter),
    ]


def load_kernel(
    bit, genes, counts, tile_mask, tile_counts, gram, scales, turned, first,
    genes_here, mask_here, counts_here, gene_sems, row_sems, sent_sems, small_sems,
):
    small_copies = [
        pltpu.make_async_copy(tile_mask, mask_here, small_sems.at[0]),
        pltpu.make_async_copy(tile_counts, counts_here, small_sems.at[1]),
    ]
    gene_copies = row_copies(genes, genes_here, 0, gene_sems)
    rows = counts.shape[0]
    half = rows // 2
    theirs, sent, _ = pieces_of(rows, bit)
    row_starts = row_copies(counts, first.at[:half], theirs, row_sems)
    row_starts += row_copies(counts, first.at[half:], sent, sent_sems)
    for copy in gene_copies + small_copies:
        copy.start()
    for copy in small_copies:
        copy.wait()
    ratio = mask_here[...].astype(F32) / counts_here[...].astype(F32)
    columns = genes.shape[1]
    tile = columns // ratio.shape[1]
    for row in range(ratio.shape[0]):
        for col in range(ratio.shape[1]):
            scales[row * 8 : row * 8 + 8, col * tile : (col + 1) * tile] = jnp.broadcast_to(
                ratio[row : row + 1, col : col + 1], (8, tile)
            )
    for copy in gene_copies:
        copy.wait()
    for copy in row_starts:
        copy.start()
    wide = min(1024, columns)
    gram[...] = jnp.zeros_like(gram)

    @pl.loop(0, columns // wide)
    def _(step):
        at = pl.ds(pl.multiple_of(step * wide, wide), wide)
        piece = genes_here[:, at]
        turned[at, :] = piece.T
        gram[...] += jnp.dot(piece, turned[at, :], preferred_element_type=F32)

    for copy in row_starts:
        copy.wait()


def load(bit, genes, counts, tile_mask, tile_counts):
    width, columns = genes.shape
    rows = counts.shape[0]
    here = pl.BlockSpec(memory_space=pltpu.VMEM)
    there = pl.BlockSpec(memory_space=pltpu.HBM)
    return pl.pallas_call(
        functools.partial(load_kernel, bit),
        out_shape=(
            jax.ShapeDtypeStruct((width, width), F32),
            jax.ShapeDtypeStruct((tile_mask.shape[0] * 8, columns), F32),
            pltpu.VMEM((columns, width), BF16),
            pltpu.VMEM((rows // 4 * 3, columns), BF16),
        ),
        in_specs=[there] * 4,
        out_specs=(here,) * 4,
        scratch_shapes=[
            pltpu.VMEM((width, columns), BF16),
            pltpu.VMEM(tile_mask.shape, jnp.int32),
            pltpu.VMEM(tile_mask.shape, jnp.int32),
            pltpu.SemaphoreType.DMA((4,)),
            pltpu.SemaphoreType.DMA((8,)),
            pltpu.SemaphoreType.DMA((4,)),
            pltpu.SemaphoreType.DMA((2,)),
        ],
        compiler_params=params(),
        cost_estimate=cost(1, 1),
        name="load",
    )(away(genes), away(counts), away(tile_mask), away(tile_counts))


def scaled(counts, at, row_tiles, scales):
    tile = counts.shape[0] // len(row_tiles)
    return jnp.concatenate(
        [
            (
                counts[i * tile : (i + 1) * tile, at].astype(F32)
                * scales[pl.ds(pl.multiple_of(row * 8, 8), 8), at][0:1]
            ).astype(BF16)
            for i, row in enumerate(row_tiles)
        ],
        axis=0,
    )


def cross_rows(row_tiles, scales, counts, turned, total):
    columns = counts.shape[1]
    wide = min(1024, columns)
    total[...] = jnp.zeros_like(total)

    @pl.loop(0, columns // wide)
    def _(step):
        at = pl.ds(pl.multiple_of(step * wide, wide), wide)
        total[...] += jnp.dot(
            scaled(counts, at, row_tiles, scales), turned[at, :], preferred_element_type=F32
        )


def tiles_from(start, rows, tile):
    return [start // tile + i for i in range(rows // tile)]


def cross_first_kernel(bit, scales, first, turned, counts, low, high, sent, kept, total, sems):
    rows = counts.shape[0]
    half, quarter, tile = rows // 2, rows // 4, rows // (scales.shape[0] // 8)
    theirs_at, sent_at, kept_at = pieces_of(rows, bit)
    copies = row_copies(counts, kept, kept_at, sems)
    for copy in copies:
        copy.start()
    row_tiles = tiles_from(theirs_at, half, tile) + tiles_from(sent_at, quarter, tile)
    cross_rows(row_tiles, scales, first, turned, total)
    low[...] = total[:quarter].T
    high[...] = total[quarter:half].T
    sent[...] = total[half:].T
    for copy in copies:
        copy.wait()


def cross_first(bit, scales, first, turned, counts):
    rows, columns = counts.shape
    width = turned.shape[1]
    here = pl.BlockSpec(memory_space=pltpu.VMEM)
    piece = jax.ShapeDtypeStruct((width, rows // 4), F32)
    return pl.pallas_call(
        functools.partial(cross_first_kernel, bit),
        out_shape=(piece, piece, piece, pltpu.VMEM((rows // 4, columns), BF16)),
        in_specs=[here, here, here, pl.BlockSpec(memory_space=pltpu.HBM)],
        out_specs=(here,) * 4,
        scratch_shapes=[pltpu.VMEM(first.shape[:1] + (width,), F32), pltpu.SemaphoreType.DMA((4,))],
        compiler_params=params(),
        cost_estimate=cost(1, 1),
        name="cross_first",
    )(scales, held(first), held(turned), away(counts))


def cross_kept_kernel(bit, scales, kept, turned, cross, total):
    rows = kept.shape[0] * 4
    tile = rows // (scales.shape[0] // 8)
    row_tiles = tiles_from(pieces_of(rows, bit)[2], rows // 4, tile)
    cross_rows(row_tiles, scales, kept, turned, total)
    cross[...] = total[...].T


def cross_kept(bit, token, scales, kept, turned):
    rows, width = kept.shape[0], turned.shape[1]
    return call(
        functools.partial(cross_kept_kernel, bit),
        "cross_kept", jax.ShapeDtypeStruct((width, rows), F32), token,
        scales, held(kept), held(turned), scratch=[pltpu.VMEM((rows, width), F32)],
    )


def add_piece_kernel(bit, kept, left, low, high, out):
    upper = ((lax.axis_index("gene") & bit) != 0) == kept

    @pl.when(upper)
    def _():
        out[...] = left[...] + high[...]

    @pl.when(jnp.logical_not(upper))
    def _():
        out[...] = left[...] + low[...]


def add_piece(bit, kept, token, left, low, high):
    shape = jax.ShapeDtypeStruct(left.shape, F32)
    return call(
        functools.partial(add_piece_kernel, bit, kept), "add_piece", shape, token, left, low, high
    )


def call(kernel, name, out_shape, token, *args, scratch=(), aliases=None, out=None):
    here = pl.BlockSpec(memory_space=pltpu.VMEM)
    wherever = pl.BlockSpec(memory_space=pl.ANY)
    single = not isinstance(out_shape, tuple)
    specs = [here] * len(args)
    if aliases:
        specs[-1] = wherever
    out = out or here
    return pl.pallas_call(
        lambda token, *refs: kernel(*refs),
        out_shape=out_shape,
        in_specs=[wherever] + specs,
        out_specs=out if single else (out,) * len(out_shape),
        scratch_shapes=list(scratch),
        input_output_aliases=aliases or {},
        compiler_params=params(),
        cost_estimate=cost(1, 1),
        name=name,
    )(token, *args)


def fold_kernel(axis, bit, left, right, kept, sent):
    half = kept.shape[1]
    upper = (lax.axis_index(axis) & bit) != 0

    @pl.when(upper)
    def _():
        kept[...] = left[:, half:] + right[:, half:]
        sent[...] = left[:, :half] + right[:, :half]

    @pl.when(jnp.logical_not(upper))
    def _():
        kept[...] = left[:, :half] + right[:, :half]
        sent[...] = left[:, half:] + right[:, half:]


def fold(axis, bit, token, left, right):
    shape = jax.ShapeDtypeStruct((left.shape[0], left.shape[1] // 2), F32)
    return call(
        functools.partial(fold_kernel, axis, bit), "fold", (shape, shape), token, left, right
    )


def side_kernel(axis, bit, dim, mine, theirs, out):
    size = mine.shape[dim]
    low = (slice(None),) * dim + (slice(0, size),)
    high = (slice(None),) * dim + (slice(size, 2 * size),)
    upper = (lax.axis_index(axis) & bit) != 0

    @pl.when(upper)
    def _():
        out[low], out[high] = theirs[...], mine[...]

    @pl.when(jnp.logical_not(upper))
    def _():
        out[low], out[high] = mine[...], theirs[...]


def side(axis, bit, dim, token, mine, theirs):
    shape = list(mine.shape)
    shape[dim] *= 2
    return call(
        functools.partial(side_kernel, axis, bit, dim),
        "side", jax.ShapeDtypeStruct(tuple(shape), mine.dtype), token, mine, theirs,
    )


def halves(value):
    high = value.astype(BF16)
    return high, (value - high.astype(F32)).astype(BF16)


def product3(left, right):
    left_high, left_low = left
    right_high, right_low = right
    dot = functools.partial(jnp.dot, preferred_element_type=F32)
    return dot(left_high, right_high) + (
        dot(left_high, right_low) + dot(left_low, right_high)
    )


def inverse_kernel(gram_a, gram_b, inverse, rho_out):
    gram = gram_a[...] + gram_b[...]
    width = gram.shape[0]
    shape = (width, width)
    diagonal = lax.broadcasted_iota(jnp.int32, shape, 0) == lax.broadcasted_iota(
        jnp.int32, shape, 1
    )
    eye = jnp.where(diagonal, 1.0, 0.0).astype(F32)
    rho = jnp.sum(gram * eye) / width
    rho_out[...] = jnp.full(rho_out.shape, rho, F32)
    scale = 1.0 / jnp.full((1, 1), rho, F32)
    matrix = gram * scale + eye
    low = 2.0 / (width + 2.0)
    guess = low * eye
    image = low * matrix
    first = True
    while True:
        low = low * (2.0 - low)
        gain = 2.0 / (1.0 + low)
        low = gain * low
        done = 1.0 - low < 2e-3
        step = halves(gain * (2.0 * eye - image))
        if first:
            guess = guess[0:1, 0:1] * (gain * (2.0 * eye - image))
        else:
            guess = product3(halves(guess), step)
        first = False
        if done:
            break
        image = product3(halves(image), step)
    rest = eye - jnp.dot(
        matrix, guess, preferred_element_type=F32, precision=lax.Precision.HIGHEST
    )
    rest_halves = halves(rest)
    series = rest + product3(rest_halves, rest_halves)
    inverse[...] = (guess + product3(halves(guess), halves(series))) * scale


def shifted_inverse(gram_a, gram_b):
    width = gram_a.shape[0]
    whole = pl.BlockSpec(memory_space=pltpu.VMEM)
    return pl.pallas_call(
        inverse_kernel,
        out_shape=(
            jax.ShapeDtypeStruct((width, width), F32),
            jax.ShapeDtypeStruct((8, 128), F32),
        ),
        in_specs=[whole, whole],
        out_specs=(whole, whole),
        compiler_params=params(),
        cost_estimate=cost(2 * 60 * width**3, 12 * width**2),
        name="inverse",
    )(gram_a, gram_b)


def admm_kernel(genes, rho_block, cross_a, cross_b, inverse, start, columns_out):
    rows = cross_a.shape[1]
    place = lax.axis_index("sub") * genes + lax.axis_index("gene")
    rho = rho_block[0:1, 0:1]
    cross = cross_a[...] + cross_b[...]
    inverse_halves = halves(inverse[...])
    zvalue = start[pl.ds(pl.multiple_of(place * rows, rows), rows), :].astype(F32).T
    uvalue = jnp.zeros_like(zvalue)
    for _ in range(ITERS):
        vvalue = product3(inverse_halves, halves(cross + rho * (zvalue - uvalue)))
        zvalue = jnp.maximum(vvalue + uvalue, 0.0)
        uvalue = uvalue + vvalue - zvalue
    columns_out[...] = zvalue.astype(BF16)


def products_kernel(tile, bit, line, start, chunk, scales, first, kept, columns, *outs):
    only_first = len(outs) == 1
    block = line.block(1 if only_first else 2, 0)
    size = first.shape[1] // line.size
    span = min(tile, chunk)
    wide = 2 * span if chunk % (2 * span) == 0 else span
    steps = chunk // wide
    rows = columns.shape[1]
    half = rows // 2
    theirs_at, sent_at, kept_at = pieces_of(rows, bit)
    groups = [
        (first.at[:half], theirs_at),
        (first.at[half:], sent_at),
        (kept, kept_at),
    ]

    @pl.loop(0, steps if only_first else line.size * steps)
    def _(turn):
        order, step = (block, turn) if only_first else (turn // steps, lax.rem(turn, steps))
        genes = pl.ds(pl.multiple_of(order * size + start + step * wide, span), wide)
        total = None
        for counts, place in groups:
            cells = counts.shape[0]
            part = jnp.dot(
                columns[:, pl.ds(place, cells)],
                scaled(counts, genes, tiles_from(place, cells, tile), scales),
                preferred_element_type=F32,
            )
            total = part if total is None else total + part
        total = total.astype(BF16)
        at = pl.ds(pl.multiple_of(step * wide, span), wide)
        if only_first:
            outs[0][:, at] = total
        else:
            outs[0][order, :, at] = total

            @pl.when(order == block)
            def _():
                outs[1][:, at] = total


def products(only_first, bit, line, start, chunk, token, scales, first, kept, columns):
    width, rows = columns.shape
    tile = rows // (scales.shape[0] // 8)
    out_shape = (jax.ShapeDtypeStruct((width, chunk), BF16),)
    if not only_first:
        out_shape = (jax.ShapeDtypeStruct((line.size, width, chunk), BF16),) + out_shape
    return call(
        functools.partial(products_kernel, tile, bit, line, start, chunk),
        "products", out_shape, token, scales, held(first), held(kept), columns,
    )


def turn_kernel(value, out):
    out[...] = value[...].astype(F32).T.astype(out.dtype)


def turn(token, value):
    shape = jax.ShapeDtypeStruct(value.shape[::-1], value.dtype)
    return call(turn_kernel, "turn", shape, token, value)


def row_share_kernel(columns, out):
    part = out.shape[0]
    place = lax.axis_index("gene")
    share = columns[pl.ds(pl.multiple_of(place * part, part), part), :]
    out[...] = contract_last(share, columns[...]).astype(out.dtype)


def row_share(part, token, columns):
    shape = jax.ShapeDtypeStruct((part, columns.shape[0]), BF16)
    return call(row_share_kernel, "row_share", shape, token, columns)


def plus_kernel(left, right, out):
    out[...] = (left[...].astype(F32) + right[...].astype(F32)).astype(out.dtype)


def hop_kernel(kind, targets, own, arrived, out):
    cell = lax.axis_index("cell")
    reached = cell == targets[0]
    for target in targets[1:]:
        reached = jnp.logical_or(reached, cell == target)
    more = arrived[...].astype(F32)
    base = own[...].astype(F32)
    value = base + more if kind == "sum" else more
    out[...] = jnp.where(reached, value, base).astype(out.dtype)


def hop(kind, targets, token, own, arrived):
    shape = jax.ShapeDtypeStruct(own.shape, own.dtype)
    return call(functools.partial(hop_kernel, kind, targets), "hop", shape, token, own, arrived)


def operand_kernel(line, phase, parity, total, before, out):
    own = total[line.block(phase, parity)].astype(F32)
    out[...] = (own + before[...].astype(F32)).astype(BF16)


def operand(line, phase, parity, token, total, before):
    shape = jax.ShapeDtypeStruct(before.shape, BF16)
    return call(
        functools.partial(operand_kernel, line, phase, parity),
        "operand", shape, token, total, before,
    )


def keep_kernel(start, total, first, second, *refs):
    out, turned, sems = refs[-3:]
    width, chunk = first.shape
    pieces = sems.shape[0]
    wide = chunk // pieces
    own = total.at[lax.axis_index("cell")]
    copies = []
    for piece in range(pieces):
        at = slice(piece * wide, (piece + 1) * wide)
        value = first[:, at].astype(F32) + second[:, at].astype(F32)
        turned[at] = (own[:, at].astype(F32) + value).T
        copies.append(
            pltpu.make_async_copy(
                turned.at[at], out.at[pl.ds(start + piece * wide, wide)], sems.at[piece]
            )
        )
        copies[-1].start()
    for copy in copies:
        copy.wait()


def keep(block, start, token, total, first, second, out):
    width, chunk = first.shape
    pieces = max(1, chunk // 256)
    return call(
        functools.partial(keep_kernel, start),
        "keep", jax.ShapeDtypeStruct((block, width), F32), token,
        total, first, second, *([] if out is None else [out]),
        scratch=[pltpu.VMEM((chunk, width), F32), pltpu.SemaphoreType.DMA((pieces,))],
        aliases=None if out is None else {4: 0},
        out=pl.BlockSpec(memory_space=pl.ANY),
    )


class Line:
    def __init__(self, size):
        self.size = size

    def pairs(self, phase, parity, exchange=False):
        links = range(parity, self.size - 1, 2)
        right = [(i, i + 1) for i in links if i < phase]
        left = [(i + 1, i) for i in links if i + 1 >= self.size - phase]
        pairs = right + left
        if exchange:
            pairs = sorted(set(pairs) | {(b, a) for a, b in pairs})
        return pairs

    def block(self, phase, parity):
        cell = lax.axis_index("cell")
        to_right = (cell & 1) == parity
        block = cell + jnp.where(to_right, self.size - phase, phase)
        return jnp.where(block >= self.size, block - self.size, block)

    def send(self, value, phase, parity):
        return lax.ppermute(value, "cell", self.pairs(phase, parity))


def swap(value, axis, size, step):
    return lax.ppermute(value, axis, [(i, i ^ step) for i in range(size)])


def pair_sums(value, axis, size, event):
    step = 1
    while step < size:
        arrived, event = after(swap(value, axis, size, step), event)
        value = value + arrived
        step *= 2
    return value, event


def after(value, event):
    return lax.optimization_barrier((value, event))


def chunk_sizes(block):
    return [block // 2, block // 2] if block % 1024 == 0 else [block]


def shards(sizes, counts, tile_mask, tile_counts, gene_factor, prev_factor):
    cells, genes, subs = sizes
    rows, columns = counts.shape
    width = gene_factor.shape[0]
    line = Line(cells)

    half_bit = bit = genes // 2
    gram, scales, turned, first_rows = load(bit, gene_factor, counts, tile_mask, tile_counts)
    token = scales
    theirs_low, theirs_high, own_sent, kept = cross_first(
        bit, scales, first_rows, turned, counts
    )
    arrived_low = swap(theirs_low, "sub", subs, 1)
    arrived_high = swap(theirs_high, "sub", subs, 1)
    sent = add_piece(bit, False, token, own_sent, arrived_low, arrived_high)
    cross_b = swap(sent, "gene", genes, bit)
    gram, (scales_late, _) = pair_sums(gram, "gene", genes, (scales, own_sent))
    cross_a = cross_kept(bit, token, scales_late, kept, turned)
    cross_a = add_piece(bit, True, token, cross_a, arrived_low, arrived_high)
    bit //= 2
    while bit:
        cross_a, sent = fold("gene", bit, token, cross_a, cross_b)
        cross_b = swap(sent, "gene", genes, bit)
        bit //= 2
    gram_other = swap(gram, "sub", subs, 1)
    inverse, rho = shifted_inverse(gram, gram_other)
    share = jax.ShapeDtypeStruct((width, rows // (genes * subs)), BF16)
    columns_held = call(
        functools.partial(admm_kernel, genes),
        "admm", share, token, rho, cross_a, cross_b, inverse, prev_factor,
    )
    bit = 1
    while bit < genes:
        columns_arrived = swap(columns_held, "gene", genes, bit)
        columns_held = side("gene", bit, 1, token, columns_held, columns_arrived)
        bit *= 2
    token, rows_sum = after(token, row_share(width // genes, token, columns_held))
    columns_arrived = swap(columns_held, "sub", subs, 1)
    whole = side("sub", 1, 1, token, columns_held, columns_arrived)

    block = columns // cells
    chunks = chunk_sizes(block)
    starts = [sum(chunks[:i]) for i in range(len(chunks))]
    every = range(len(chunks))

    arrived = {}

    def send(value, phase, parity, index):
        pairs = line.pairs(phase, parity, exchange=phase == 1 and index == 0)
        arrived[phase, parity, index] = lax.ppermute(value, "cell", pairs) if pairs else None

    def resend(token, phase, parity, index):
        before = arrived[phase - 1, 1 - parity, index]
        if before is None:
            value = seconds[index]
        else:
            value = operand(line, phase, parity, token, totals[index], before)
            token, value = after(token, value)
        send(value, phase, parity, index)
        return token

    middle = cells // 2
    inward = [[(i, i + 1), (cells - 1 - i, cells - 2 - i)] for i in range(middle - 1)]
    outward = [[(b, a) for a, b in pairs] for pairs in reversed(inward)]
    hops = [("sum", p) for p in inward] + [("sum", [(middle - 1, middle), (middle, middle - 1)])]
    hops += [("copy", p) for p in outward]

    def hop_rows(token, rows_sum):
        kind, pairs = hops.pop(0)
        both = sorted(set(pairs) | {(b, a) for a, b in pairs})
        rows_arrived = lax.ppermute(rows_sum, "cell", both)
        targets = [b for _, b in pairs]
        return after(token, hop(kind, targets, token, rows_sum, rows_arrived))

    def side_rows(token, rows_sum, axis, size, bit):
        rows_arrived = swap(rows_sum, axis, size, bit)
        return after(token, side(axis, bit, 0, token, rows_sum, rows_arrived))

    for index in every:
        (first,) = products(
            True, half_bit, line, starts[index], chunks[index], token, scales, first_rows, kept, whole
        )
        token, first = after(token, first)
        for parity in (0, 1):
            send(first, 1, parity, index)
        if index == 0 and hops:
            token, rows_sum = hop_rows(token, rows_sum)
    totals, seconds = [], []
    for index in every:
        total, second = products(
            False, half_bit, line, starts[index], chunks[index], token, scales, first_rows, kept, whole
        )
        token, second = after(token, second)
        if hops:
            token, rows_sum = hop_rows(token, rows_sum)
        totals.append(total)
        seconds.append(second)
        for parity in (0, 1):
            token = resend(token, 2, parity, index)
    while hops:
        token, rows_sum = hop_rows(token, rows_sum)
    new_factor = turn(token, whole)
    token, new_factor = after(token, new_factor)
    rows_arrived = swap(rows_sum, "sub", subs, 1)
    shape = jax.ShapeDtypeStruct(rows_sum.shape, F32)
    token, rows_sum = after(token, call(plus_kernel, "plus", shape, token, rows_sum, rows_arrived))
    bits = [1 << i for i in range((genes - 1).bit_length())]
    for phase in range(3, cells):
        for index in every:
            for parity in (0, 1):
                token = resend(token, phase, parity, index)
                if bits:
                    token, rows_sum = side_rows(token, rows_sum, "gene", genes, bits.pop(0))
    data_products = None
    last = cells - 1
    for index in every:
        data_products = keep(
            block, starts[index], token, totals[index],
            arrived[last, 0, index], arrived[last, 1, index], data_products,
        )
        token, data_products = after(token, data_products)
    return (new_factor, rows_sum, data_products)


def solution(mesh):
    sizes = (mesh.shape["cell"], mesh.shape["gene"], mesh.shape["sub"])
    return jax.shard_map(
        functools.partial(shards, sizes),
        mesh=mesh,
        in_specs=(
            P(("groups", "cell"), ("gene", "sub")),
            P(("groups", "cell"), ("gene", "sub")),
            P(("groups", "cell"), ("gene", "sub")),
            P("groups", ("gene", "sub")),
            P(("groups", "cell"), None),
        ),
        out_specs=(
            P(("groups", "cell"), None),
            P("groups", None),
            P(("groups", "gene", "sub", "cell"), None),
        ),
        check_vma=False,
    )
```

```python
import functools

import jax
import jax.numpy as jnp
import numpy as np
from jax import lax
from jax.experimental import pallas as pl
from jax.experimental.pallas import tpu as pltpu
from jax.sharding import PartitionSpec as P

ITERS = 3
F32 = jnp.float32
BF16 = jnp.bfloat16
MIB = 1024 * 1024


def params(limit=16):
    return pltpu.CompilerParams(vmem_limit_bytes=limit * MIB)


def away(value):
    return pltpu.with_memory_space_constraint(value, pltpu.HBM)


def held(value):
    return pltpu.with_memory_space_constraint(value, pltpu.VMEM)


def cost(flops, bytes_accessed):
    return pl.CostEstimate(flops=flops, bytes_accessed=bytes_accessed, transcendentals=0)


def contract_last(left, right):
    return lax.dot_general(
        left, right, (((1,), (1,)), ((), ())), preferred_element_type=F32
    )


def row_copies(source, target, first, sems):
    rows = target.shape[0]
    piece = max(rows // sems.shape[0], 16)
    return [
        pltpu.make_async_copy(
            source.at[pl.ds(first + i * piece, piece)],
            target.at[pl.ds(i * piece, piece)],
            sems.at[i],
        )
        for i in range(rows // piece)
    ]


def pieces_of(rows, bit, kept):
    core = lax.axis_index("sub")
    upper = ((lax.axis_index("gene") & bit) != 0) == kept
    half, quarter = rows // 2, rows // 4
    place = jnp.where(upper, quarter, 0)
    return [
        pl.multiple_of((1 - core) * half + place, quarter),
        pl.multiple_of(core * half + place, quarter),
    ]


def piece_copies(bit, kept, counts, target, sems):
    quarter = counts.shape[0] // 4
    copies = []
    for i, place in enumerate(pieces_of(counts.shape[0], bit, kept)):
        copies += row_copies(
            counts, target.at[i * quarter : (i + 1) * quarter], place, sems.at[i * 4 : i * 4 + 4]
        )
    return copies


def load_kernel(
    bit, genes, counts, tile_mask, tile_counts, gram, scales, turned, first,
    genes_here, mask_here, counts_here, gene_sems, row_sems, small_sems,
):
    small_copies = [
        pltpu.make_async_copy(tile_mask, mask_here, small_sems.at[0]),
        pltpu.make_async_copy(tile_counts, counts_here, small_sems.at[1]),
    ]
    gene_copies = row_copies(genes, genes_here, 0, gene_sems)
    row_starts = piece_copies(bit, False, counts, first, row_sems)
    for copy in gene_copies + small_copies:
        copy.start()
    for copy in small_copies:
        copy.wait()
    ratio = mask_here[...].astype(F32) / counts_here[...].astype(F32)
    columns = genes.shape[1]
    tile = columns // ratio.shape[1]
    for row in range(ratio.shape[0]):
        for col in range(ratio.shape[1]):
            scales[row * 8 : row * 8 + 8, col * tile : (col + 1) * tile] = jnp.broadcast_to(
                ratio[row : row + 1, col : col + 1], (8, tile)
            )
    for copy in gene_copies:
        copy.wait()
    for copy in row_starts:
        copy.start()
    wide = min(1024, columns)
    gram[...] = jnp.zeros_like(gram)

    @pl.loop(0, columns // wide)
    def _(step):
        at = pl.ds(pl.multiple_of(step * wide, wide), wide)
        piece = genes_here[:, at]
        turned[at, :] = piece.T
        gram[...] += jnp.dot(piece, turned[at, :], preferred_element_type=F32)

    for copy in row_starts:
        copy.wait()


def load(bit, genes, counts, tile_mask, tile_counts):
    width, columns = genes.shape
    rows = counts.shape[0]
    here = pl.BlockSpec(memory_space=pltpu.VMEM)
    there = pl.BlockSpec(memory_space=pltpu.HBM)
    return pl.pallas_call(
        functools.partial(load_kernel, bit),
        out_shape=(
            jax.ShapeDtypeStruct((width, width), F32),
            jax.ShapeDtypeStruct((tile_mask.shape[0] * 8, columns), F32),
            pltpu.VMEM((columns, width), BF16),
            pltpu.VMEM((rows // 2, columns), BF16),
        ),
        in_specs=[there] * 4,
        out_specs=(here,) * 4,
        scratch_shapes=[
            pltpu.VMEM((width, columns), BF16),
            pltpu.VMEM(tile_mask.shape, jnp.int32),
            pltpu.VMEM(tile_mask.shape, jnp.int32),
            pltpu.SemaphoreType.DMA((4,)),
            pltpu.SemaphoreType.DMA((8,)),
            pltpu.SemaphoreType.DMA((2,)),
        ],
        compiler_params=params(),
        cost_estimate=cost(1, 1),
        name="load",
    )(away(genes), away(counts), away(tile_mask), away(tile_counts))


def scaled(counts, at, row_tiles, scales):
    tile = counts.shape[0] // len(row_tiles)
    return jnp.concatenate(
        [
            (
                counts[i * tile : (i + 1) * tile, at].astype(F32)
                * scales[pl.ds(pl.multiple_of(row * 8, 8), 8), at][0:1]
            ).astype(BF16)
            for i, row in enumerate(row_tiles)
        ],
        axis=0,
    )


def cross_rows(row_tiles, scales, counts, turned, total):
    columns = counts.shape[1]
    wide = min(1024, columns)
    total[...] = jnp.zeros_like(total)

    @pl.loop(0, columns // wide)
    def _(step):
        at = pl.ds(pl.multiple_of(step * wide, wide), wide)
        total[...] += jnp.dot(
            scaled(counts, at, row_tiles, scales), turned[at, :], preferred_element_type=F32
        )


def tiles_of(bit, kept, rows, tile):
    quarter = rows // 4
    return [
        place // tile + i
        for place in pieces_of(rows, bit, kept)
        for i in range(quarter // tile)
    ]


def cross_kernel(bit, kept, rows, scales, held_rows, turned, *refs):
    (low, high, mine), total = refs[-5:-2] if kept else refs[1:4], refs[-2]
    if not kept:
        copies = piece_copies(bit, True, refs[0], refs[4], refs[-1])
        for copy in copies:
            copy.start()
    quarter, tile = rows // 4, rows // (scales.shape[0] // 8)
    cross_rows(tiles_of(bit, kept, rows, tile), scales, held_rows, turned, total)
    low[...] = total[: quarter // 2].T
    high[...] = total[quarter // 2 : quarter].T
    mine[...] = total[quarter:].T
    if not kept:
        for copy in copies:
            copy.wait()


def cross(bit, kept, scales, held_rows, turned, counts):
    rows, columns = counts.shape
    width = turned.shape[1]
    here = pl.BlockSpec(memory_space=pltpu.VMEM)
    piece = jax.ShapeDtypeStruct((width, rows // 4), F32)
    small_piece = jax.ShapeDtypeStruct((width, rows // 8), F32)
    out_shape = (small_piece, small_piece, piece)
    in_specs, args = [here] * 3, [scales, held(held_rows), held(turned)]
    if not kept:
        out_shape += (pltpu.VMEM((rows // 2, columns), BF16),)
        in_specs.append(pl.BlockSpec(memory_space=pltpu.HBM))
        args.append(away(counts))
    return pl.pallas_call(
        functools.partial(cross_kernel, bit, kept, rows),
        out_shape=out_shape,
        in_specs=in_specs,
        out_specs=(here,) * len(out_shape),
        scratch_shapes=[pltpu.VMEM((rows // 2, width), F32), pltpu.SemaphoreType.DMA((8,))],
        compiler_params=params(),
        cost_estimate=cost(1, 1),
        name="cross_kept" if kept else "cross_sent",
    )(*args)


def plus_pieces_kernel(left, low, high, out):
    half = low.shape[1]
    out[:, :half] = left[:, :half] + low[...]
    out[:, half:] = left[:, half:] + high[...]


def call(kernel, name, out_shape, token, *args, scratch=(), aliases=None, out=None):
    here = pl.BlockSpec(memory_space=pltpu.VMEM)
    wherever = pl.BlockSpec(memory_space=pl.ANY)
    single = not isinstance(out_shape, tuple)
    specs = [here] * len(args)
    if aliases:
        specs[-1] = wherever
    out = out or here
    return pl.pallas_call(
        lambda token, *refs: kernel(*refs),
        out_shape=out_shape,
        in_specs=[wherever] + specs,
        out_specs=out if single else (out,) * len(out_shape),
        scratch_shapes=list(scratch),
        input_output_aliases=aliases or {},
        compiler_params=params(),
        cost_estimate=cost(1, 1),
        name=name,
    )(token, *args)


def fold_kernel(axis, bit, left, right, kept, sent):
    half = kept.shape[1]
    upper = (lax.axis_index(axis) & bit) != 0

    @pl.when(upper)
    def _():
        kept[...] = left[:, half:] + right[:, half:]
        sent[...] = left[:, :half] + right[:, :half]

    @pl.when(jnp.logical_not(upper))
    def _():
        kept[...] = left[:, :half] + right[:, :half]
        sent[...] = left[:, half:] + right[:, half:]


def fold(axis, bit, token, left, right):
    shape = jax.ShapeDtypeStruct((left.shape[0], left.shape[1] // 2), F32)
    return call(
        functools.partial(fold_kernel, axis, bit), "fold", (shape, shape), token, left, right
    )


def side_kernel(axis, bit, dim, mine, theirs, out):
    size = mine.shape[dim]
    low = (slice(None),) * dim + (slice(0, size),)
    high = (slice(None),) * dim + (slice(size, 2 * size),)
    upper = (lax.axis_index(axis) & bit) != 0

    @pl.when(upper)
    def _():
        out[low], out[high] = theirs[...], mine[...]

    @pl.when(jnp.logical_not(upper))
    def _():
        out[low], out[high] = mine[...], theirs[...]


def side(axis, bit, dim, token, mine, theirs):
    shape = list(mine.shape)
    shape[dim] *= 2
    return call(
        functools.partial(side_kernel, axis, bit, dim),
        "side", jax.ShapeDtypeStruct(tuple(shape), mine.dtype), token, mine, theirs,
    )


def halves(value):
    high = value.astype(BF16)
    return high, (value - high.astype(F32)).astype(BF16)


def product3(left, right):
    left_high, left_low = left
    right_high, right_low = right
    dot = functools.partial(jnp.dot, preferred_element_type=F32)
    return dot(left_high, right_high) + (
        dot(left_high, right_low) + dot(left_low, right_high)
    )


def inverse_kernel(gram_a, gram_b, inverse, rho_out):
    gram = gram_a[...] + gram_b[...]
    width = gram.shape[0]
    shape = (width, width)
    diagonal = lax.broadcasted_iota(jnp.int32, shape, 0) == lax.broadcasted_iota(
        jnp.int32, shape, 1
    )
    eye = jnp.where(diagonal, 1.0, 0.0).astype(F32)
    rho = jnp.sum(gram * eye) / width
    rho_out[...] = jnp.full(rho_out.shape, rho, F32)
    scale = 1.0 / jnp.full((1, 1), rho, F32)
    matrix = gram * scale + eye
    low = 2.0 / (width + 2.0)
    guess = low * eye
    image = low * matrix
    first = True
    while True:
        low = low * (2.0 - low)
        gain = 2.0 / (1.0 + low)
        low = gain * low
        done = 1.0 - low < 2e-3
        step = halves(gain * (2.0 * eye - image))
        if first:
            guess = guess[0:1, 0:1] * (gain * (2.0 * eye - image))
        else:
            guess = product3(halves(guess), step)
        first = False
        if done:
            break
        image = product3(halves(image), step)
    rest = eye - jnp.dot(
        matrix, guess, preferred_element_type=F32, precision=lax.Precision.HIGHEST
    )
    rest_halves = halves(rest)
    series = rest + product3(rest_halves, rest_halves)
    inverse[...] = (guess + product3(halves(guess), halves(series))) * scale


def shifted_inverse(gram_a, gram_b):
    width = gram_a.shape[0]
    whole = pl.BlockSpec(memory_space=pltpu.VMEM)
    return pl.pallas_call(
        inverse_kernel,
        out_shape=(
            jax.ShapeDtypeStruct((width, width), F32),
            jax.ShapeDtypeStruct((8, 128), F32),
        ),
        in_specs=[whole, whole],
        out_specs=(whole, whole),
        compiler_params=params(),
        cost_estimate=cost(1, 1),
        name="inverse",
    )(gram_a, gram_b)


def admm_kernel(genes, rho_block, cross_a, cross_b, inverse, start, columns_out):
    rows = cross_a.shape[1]
    place = lax.axis_index("sub") * genes + lax.axis_index("gene")
    rho = rho_block[0:1, 0:1]
    cross = cross_a[...] + cross_b[...]
    inverse_halves = halves(inverse[...])
    zvalue = start[pl.ds(pl.multiple_of(place * rows, rows), rows), :].astype(F32).T
    uvalue = jnp.zeros_like(zvalue)
    for _ in range(ITERS):
        vvalue = product3(inverse_halves, halves(cross + rho * (zvalue - uvalue)))
        zvalue = jnp.maximum(vvalue + uvalue, 0.0)
        uvalue = uvalue + vvalue - zvalue
    columns_out[...] = zvalue.astype(BF16)


def products_kernel(tile, bit, line, start, chunk, scales, sent, kept, columns, *outs):
    only_first = len(outs) == 1
    block = line.block(1 if only_first else 2, 0)
    size = kept.shape[1] // line.size
    span = min(tile, chunk)
    wide = 2 * span if chunk % (2 * span) == 0 else span
    steps = chunk // wide
    rows = columns.shape[1]
    quarter = rows // 4
    groups = [(sent, False), (kept, True)]

    @pl.loop(0, steps if only_first else line.size * steps)
    def _(turn):
        order, step = (block, turn) if only_first else (turn // steps, lax.rem(turn, steps))
        genes = pl.ds(pl.multiple_of(order * size + start + step * wide, span), wide)
        total = None
        for counts, stays in groups:
            cells = [columns[:, pl.ds(at, quarter)] for at in pieces_of(rows, bit, stays)]
            part = jnp.dot(
                jnp.concatenate(cells, axis=1),
                scaled(counts, genes, tiles_of(bit, stays, rows, tile), scales),
                preferred_element_type=F32,
            )
            total = part if total is None else total + part
        total = total.astype(BF16)
        at = pl.ds(pl.multiple_of(step * wide, span), wide)
        if only_first:
            outs[0][:, at] = total
        else:
            outs[0][order, :, at] = total

            @pl.when(order == block)
            def _():
                outs[1][:, at] = total


def products(only_first, bit, line, start, chunk, token, scales, sent, kept, columns):
    width, rows = columns.shape
    tile = rows // (scales.shape[0] // 8)
    out_shape = (jax.ShapeDtypeStruct((width, chunk), BF16),)
    if not only_first:
        out_shape = (jax.ShapeDtypeStruct((line.size, width, chunk), BF16),) + out_shape
    return call(
        functools.partial(products_kernel, tile, bit, line, start, chunk),
        "products", out_shape, token, scales, held(sent), held(kept), columns,
    )


def turn_kernel(value, out):
    out[...] = value[...].astype(F32).T.astype(out.dtype)


def turn(token, value):
    shape = jax.ShapeDtypeStruct(value.shape[::-1], value.dtype)
    return call(turn_kernel, "turn", shape, token, value)


def row_share_kernel(columns, out):
    part = out.shape[0]
    place = lax.axis_index("gene")
    share = columns[pl.ds(pl.multiple_of(place * part, part), part), :]
    out[...] = contract_last(share, columns[...]).astype(out.dtype)


def row_share(part, token, columns):
    shape = jax.ShapeDtypeStruct((part, columns.shape[0]), BF16)
    return call(row_share_kernel, "row_share", shape, token, columns)


def plus_kernel(left, right, out):
    out[...] = (left[...].astype(F32) + right[...].astype(F32)).astype(out.dtype)


def hop_kernel(kind, targets, own, arrived, out):
    cell = lax.axis_index("cell")
    reached = cell == targets[0]
    for target in targets[1:]:
        reached = jnp.logical_or(reached, cell == target)
    more = arrived[...].astype(F32)
    base = own[...].astype(F32)
    value = base + more if kind == "sum" else more
    out[...] = jnp.where(reached, value, base).astype(out.dtype)


def hop(kind, targets, token, own, arrived):
    shape = jax.ShapeDtypeStruct(own.shape, own.dtype)
    return call(functools.partial(hop_kernel, kind, targets), "hop", shape, token, own, arrived)


def operand_kernel(line, phase, parity, total, before, out):
    own = total[line.block(phase, parity)].astype(F32)
    out[...] = (own + before[...].astype(F32)).astype(BF16)


def operand(line, phase, parity, token, total, before):
    shape = jax.ShapeDtypeStruct(before.shape, BF16)
    return call(
        functools.partial(operand_kernel, line, phase, parity),
        "operand", shape, token, total, before,
    )


def keep_kernel(start, total, first, second, *refs):
    out, turned, sems = refs[-3:]
    width, chunk = first.shape
    pieces = sems.shape[0]
    wide = chunk // pieces
    own = total.at[lax.axis_index("cell")]
    copies = []
    for piece in range(pieces):
        at = slice(piece * wide, (piece + 1) * wide)
        value = first[:, at].astype(F32) + second[:, at].astype(F32)
        turned[at] = (own[:, at].astype(F32) + value).T
        copies.append(
            pltpu.make_async_copy(
                turned.at[at], out.at[pl.ds(start + piece * wide, wide)], sems.at[piece]
            )
        )
        copies[-1].start()
    for copy in copies:
        copy.wait()


def keep(block, start, token, total, first, second, out):
    width, chunk = first.shape
    pieces = max(1, chunk // 256)
    return call(
        functools.partial(keep_kernel, start),
        "keep", jax.ShapeDtypeStruct((block, width), F32), token,
        total, first, second, *([] if out is None else [out]),
        scratch=[pltpu.VMEM((chunk, width), F32), pltpu.SemaphoreType.DMA((pieces,))],
        aliases=None if out is None else {4: 0},
        out=pl.BlockSpec(memory_space=pl.ANY),
    )


class Line:
    def __init__(self, size):
        self.size = size

    def pairs(self, phase, parity, exchange=False):
        links = range(parity, self.size - 1, 2)
        right = [(i, i + 1) for i in links if i < phase]
        left = [(i + 1, i) for i in links if i + 1 >= self.size - phase]
        pairs = right + left
        if exchange:
            pairs = sorted(set(pairs) | {(b, a) for a, b in pairs})
        return pairs

    def block(self, phase, parity):
        cell = lax.axis_index("cell")
        to_right = (cell & 1) == parity
        block = cell + jnp.where(to_right, self.size - phase, phase)
        return jnp.where(block >= self.size, block - self.size, block)

    def send(self, value, phase, parity):
        return lax.ppermute(value, "cell", self.pairs(phase, parity))


def swap(value, axis, size, step):
    return lax.ppermute(value, axis, [(i, i ^ step) for i in range(size)])


def pair_sums(value, axis, size, event):
    step = 1
    while step < size:
        arrived, event = after(swap(value, axis, size, step), event)
        value = value + arrived
        step *= 2
    return value, event


def after(value, event):
    return lax.optimization_barrier((value, event))


def chunk_sizes(block):
    return [block // 2, block // 2] if block % 1024 == 0 else [block]


def shards(sizes, counts, tile_mask, tile_counts, gene_factor, prev_factor):
    cells, genes, subs = sizes
    rows, columns = counts.shape
    width = gene_factor.shape[0]
    line = Line(cells)

    half_bit = bit = genes // 2
    gram, scales, turned, sent_rows = load(bit, gene_factor, counts, tile_mask, tile_counts)
    token = scales
    piece = jax.ShapeDtypeStruct((width, rows // 4), F32)
    low, high, mine, kept_rows = cross(bit, False, scales, sent_rows, turned, counts)
    low, high = [swap(value, "sub", subs, 1) for value in (low, high)]
    sent = call(plus_pieces_kernel, "plus", piece, token, mine, low, high)
    cross_b = swap(sent, "gene", genes, bit)
    gram, (scales_late, _) = pair_sums(gram, "gene", genes, (scales, sent))
    low, high, mine = cross(bit, True, scales_late, kept_rows, turned, counts)
    low, high = [swap(value, "sub", subs, 1) for value in (low, high)]
    gram_other = swap(gram, "sub", subs, 1)
    inverse, rho = shifted_inverse(gram, gram_other)
    token_late, inverse = after(token, inverse)
    cross_a = call(plus_pieces_kernel, "plus", piece, token_late, mine, low, high)
    bit //= 2
    while bit:
        cross_a, sent = fold("gene", bit, token, cross_a, cross_b)
        cross_b = swap(sent, "gene", genes, bit)
        bit //= 2
    share = jax.ShapeDtypeStruct((width, rows // (genes * subs)), BF16)
    columns_held = call(
        functools.partial(admm_kernel, genes),
        "admm", share, token, rho, cross_a, cross_b, inverse, prev_factor,
    )
    bit = 1
    while bit < genes:
        columns_arrived = swap(columns_held, "gene", genes, bit)
        columns_held = side("gene", bit, 1, token, columns_held, columns_arrived)
        bit *= 2
    token, rows_sum = after(token, row_share(width // genes, token, columns_held))
    columns_arrived = swap(columns_held, "sub", subs, 1)
    whole = side("sub", 1, 1, token, columns_held, columns_arrived)

    block = columns // cells
    chunks = chunk_sizes(block)
    starts = [sum(chunks[:i]) for i in range(len(chunks))]
    every = range(len(chunks))

    arrived = {}

    def send(value, phase, parity, index):
        pairs = line.pairs(phase, parity, exchange=phase == 1 and index == 0)
        arrived[phase, parity, index] = lax.ppermute(value, "cell", pairs) if pairs else None

    def resend(token, phase, parity, index):
        before = arrived[phase - 1, 1 - parity, index]
        if before is None:
            value = seconds[index]
        else:
            value = operand(line, phase, parity, token, totals[index], before)
            token, value = after(token, value)
        send(value, phase, parity, index)
        return token

    middle = cells // 2
    inward = [[(i, i + 1), (cells - 1 - i, cells - 2 - i)] for i in range(middle - 1)]
    outward = [[(b, a) for a, b in pairs] for pairs in reversed(inward)]
    hops = [("sum", p) for p in inward] + [("sum", [(middle - 1, middle), (middle, middle - 1)])]
    hops += [("copy", p) for p in outward]

    def hop_rows(token, rows_sum):
        kind, pairs = hops.pop(0)
        both = sorted(set(pairs) | {(b, a) for a, b in pairs})
        rows_arrived = lax.ppermute(rows_sum, "cell", both)
        targets = [b for _, b in pairs]
        return after(token, hop(kind, targets, token, rows_sum, rows_arrived))

    def side_rows(token, rows_sum, axis, size, bit):
        rows_arrived = swap(rows_sum, axis, size, bit)
        return after(token, side(axis, bit, 0, token, rows_sum, rows_arrived))

    for index in every:
        (first,) = products(
            True, half_bit, line, starts[index], chunks[index], token, scales, sent_rows, kept_rows, whole
        )
        token, first = after(token, first)
        for parity in (0, 1):
            send(first, 1, parity, index)
        if index == 0 and hops:
            token, rows_sum = hop_rows(token, rows_sum)
    totals, seconds = [], []
    for index in every:
        total, second = products(
            False, half_bit, line, starts[index], chunks[index], token, scales, sent_rows, kept_rows, whole
        )
        token, second = after(token, second)
        if hops:
            token, rows_sum = hop_rows(token, rows_sum)
        totals.append(total)
        seconds.append(second)
        for parity in (0, 1):
            token = resend(token, 2, parity, index)
    while hops:
        token, rows_sum = hop_rows(token, rows_sum)
    new_factor = turn(token, whole)
    token, new_factor = after(token, new_factor)
    rows_arrived = swap(rows_sum, "sub", subs, 1)
    shape = jax.ShapeDtypeStruct(rows_sum.shape, F32)
    token, rows_sum = after(token, call(plus_kernel, "plus", shape, token, rows_sum, rows_arrived))
    bits = [1 << i for i in range((genes - 1).bit_length())]
    for phase in range(3, cells):
        for index in every:
            for parity in (0, 1):
                token = resend(token, phase, parity, index)
                if bits:
                    token, rows_sum = side_rows(token, rows_sum, "gene", genes, bits.pop(0))
    data_products = None
    last = cells - 1
    for index in every:
        data_products = keep(
            block, starts[index], token, totals[index],
            arrived[last, 0, index], arrived[last, 1, index], data_products,
        )
        token, data_products = after(token, data_products)
    return (new_factor, rows_sum, data_products)


def solution(mesh):
    sizes = (mesh.shape["cell"], mesh.shape["gene"], mesh.shape["sub"])
    return jax.shard_map(
        functools.partial(shards, sizes),
        mesh=mesh,
        in_specs=(
            P(("groups", "cell"), ("gene", "sub")),
            P(("groups", "cell"), ("gene", "sub")),
            P(("groups", "cell"), ("gene", "sub")),
            P("groups", ("gene", "sub")),
            P(("groups", "cell"), None),
        ),
        out_specs=(
            P(("groups", "cell"), None),
            P("groups", None),
            P(("groups", "gene", "sub", "cell"), None),
        ),
        check_vma=False,
    )
```

```python
import functools

import jax
import jax.numpy as jnp
import numpy as np
from jax import lax
from jax.experimental import pallas as pl
from jax.experimental.pallas import tpu as pltpu
from jax.sharding import PartitionSpec as P

ITERS = 3
F32 = jnp.float32
BF16 = jnp.bfloat16
MIB = 1024 * 1024


def params(limit=16):
    return pltpu.CompilerParams(vmem_limit_bytes=limit * MIB)


def away(value):
    return pltpu.with_memory_space_constraint(value, pltpu.HBM)


def held(value):
    return pltpu.with_memory_space_constraint(value, pltpu.VMEM)


def cost(flops, bytes_accessed):
    return pl.CostEstimate(flops=flops, bytes_accessed=bytes_accessed, transcendentals=0)


def contract_last(left, right):
    return lax.dot_general(
        left, right, (((1,), (1,)), ((), ())), preferred_element_type=F32
    )


def row_copies(source, target, first, sems):
    rows = target.shape[0]
    piece = max(rows // sems.shape[0], 16)
    return [
        pltpu.make_async_copy(
            source.at[pl.ds(first + i * piece, piece)],
            target.at[pl.ds(i * piece, piece)],
            sems.at[i],
        )
        for i in range(rows // piece)
    ]


def pieces_of(rows, bit, kept):
    core = lax.axis_index("sub")
    upper = ((lax.axis_index("gene") & bit) != 0) == kept
    half, quarter = rows // 2, rows // 4
    place = jnp.where(upper, quarter, 0)
    return [
        pl.multiple_of((1 - core) * half + place, quarter),
        pl.multiple_of(core * half + place, quarter),
    ]


def piece_copies(bit, kept, counts, target, sems):
    quarter = counts.shape[0] // 4
    copies = []
    for i, place in enumerate(pieces_of(counts.shape[0], bit, kept)):
        copies += row_copies(
            counts, target.at[i * quarter : (i + 1) * quarter], place, sems.at[i * 4 : i * 4 + 4]
        )
    return copies


def load_kernel(
    bit, genes, counts, tile_mask, tile_counts, gram, scales, turned, first,
    genes_here, mask_here, counts_here, gene_sems, row_sems, small_sems,
):
    small_copies = [
        pltpu.make_async_copy(tile_mask, mask_here, small_sems.at[0]),
        pltpu.make_async_copy(tile_counts, counts_here, small_sems.at[1]),
    ]
    gene_copies = row_copies(genes, genes_here, 0, gene_sems)
    row_starts = piece_copies(bit, False, counts, first, row_sems)
    for copy in gene_copies + small_copies:
        copy.start()
    for copy in small_copies:
        copy.wait()
    ratio = mask_here[...].astype(F32) / counts_here[...].astype(F32)
    columns = genes.shape[1]
    tile = columns // ratio.shape[1]
    for row in range(ratio.shape[0]):
        for col in range(ratio.shape[1]):
            scales[row * 8 : row * 8 + 8, col * tile : (col + 1) * tile] = jnp.broadcast_to(
                ratio[row : row + 1, col : col + 1], (8, tile)
            )
    for copy in gene_copies:
        copy.wait()
    for copy in row_starts:
        copy.start()
    wide = min(1024, columns)
    gram[...] = jnp.zeros_like(gram)

    @pl.loop(0, columns // wide)
    def _(step):
        at = pl.ds(pl.multiple_of(step * wide, wide), wide)
        piece = genes_here[:, at]
        turned[at, :] = piece.T
        gram[...] += jnp.dot(piece, turned[at, :], preferred_element_type=F32)

    for copy in row_starts:
        copy.wait()


def load(bit, genes, counts, tile_mask, tile_counts):
    width, columns = genes.shape
    rows = counts.shape[0]
    here = pl.BlockSpec(memory_space=pltpu.VMEM)
    there = pl.BlockSpec(memory_space=pltpu.HBM)
    return pl.pallas_call(
        functools.partial(load_kernel, bit),
        out_shape=(
            jax.ShapeDtypeStruct((width, width), F32),
            jax.ShapeDtypeStruct((tile_mask.shape[0] * 8, columns), F32),
            pltpu.VMEM((columns, width), BF16),
            pltpu.VMEM((rows // 2, columns), BF16),
        ),
        in_specs=[there] * 4,
        out_specs=(here,) * 4,
        scratch_shapes=[
            pltpu.VMEM((width, columns), BF16),
            pltpu.VMEM(tile_mask.shape, jnp.int32),
            pltpu.VMEM(tile_mask.shape, jnp.int32),
            pltpu.SemaphoreType.DMA((4,)),
            pltpu.SemaphoreType.DMA((8,)),
            pltpu.SemaphoreType.DMA((2,)),
        ],
        compiler_params=params(),
        cost_estimate=cost(1, 1),
        name="load",
    )(away(genes), away(counts), away(tile_mask), away(tile_counts))


def scaled(counts, at, row_tiles, scales):
    tile = counts.shape[0] // len(row_tiles)
    return jnp.concatenate(
        [
            (
                counts[i * tile : (i + 1) * tile, at].astype(F32)
                * scales[pl.ds(pl.multiple_of(row * 8, 8), 8), at][0:1]
            ).astype(BF16)
            for i, row in enumerate(row_tiles)
        ],
        axis=0,
    )


def cross_rows(row_tiles, scales, counts, turned, total):
    columns = counts.shape[1]
    wide = min(1024, columns)
    total[...] = jnp.zeros_like(total)

    @pl.loop(0, columns // wide)
    def _(step):
        at = pl.ds(pl.multiple_of(step * wide, wide), wide)
        total[...] += jnp.dot(
            scaled(counts, at, row_tiles, scales), turned[at, :], preferred_element_type=F32
        )


def tiles_of(bit, kept, rows, tile):
    quarter = rows // 4
    return [
        place // tile + i
        for place in pieces_of(rows, bit, kept)
        for i in range(quarter // tile)
    ]


def cross_kernel(bit, kept, rows, scales, held_rows, turned, *refs):
    (low, high, mine), total = refs[-5:-2] if kept else refs[1:4], refs[-2]
    if not kept:
        copies = piece_copies(bit, True, refs[0], refs[4], refs[-1])
        for copy in copies:
            copy.start()
    quarter, tile = rows // 4, rows // (scales.shape[0] // 8)
    cross_rows(tiles_of(bit, kept, rows, tile), scales, held_rows, turned, total)
    low[...] = total[: quarter // 2].T
    high[...] = total[quarter // 2 : quarter].T
    mine[...] = total[quarter:].T
    if not kept:
        for copy in copies:
            copy.wait()


def cross(bit, kept, scales, held_rows, turned, counts):
    rows, columns = counts.shape
    width = turned.shape[1]
    here = pl.BlockSpec(memory_space=pltpu.VMEM)
    piece = jax.ShapeDtypeStruct((width, rows // 4), F32)
    small_piece = jax.ShapeDtypeStruct((width, rows // 8), F32)
    out_shape = (small_piece, small_piece, piece)
    in_specs, args = [here] * 3, [scales, held(held_rows), held(turned)]
    if not kept:
        out_shape += (pltpu.VMEM((rows // 2, columns), BF16),)
        in_specs.append(pl.BlockSpec(memory_space=pltpu.HBM))
        args.append(away(counts))
    return pl.pallas_call(
        functools.partial(cross_kernel, bit, kept, rows),
        out_shape=out_shape,
        in_specs=in_specs,
        out_specs=(here,) * len(out_shape),
        scratch_shapes=[pltpu.VMEM((rows // 2, width), F32), pltpu.SemaphoreType.DMA((8,))],
        compiler_params=params(),
        cost_estimate=cost(1, 1),
        name="cross_kept" if kept else "cross_sent",
    )(*args)


def plus_pieces_kernel(left, low, high, out):
    half = low.shape[1]
    out[:, :half] = left[:, :half] + low[...]
    out[:, half:] = left[:, half:] + high[...]


def call(kernel, name, out_shape, token, *args, scratch=(), aliases=None, out=None):
    here = pl.BlockSpec(memory_space=pltpu.VMEM)
    wherever = pl.BlockSpec(memory_space=pl.ANY)
    single = not isinstance(out_shape, tuple)
    specs = [here] * len(args)
    if aliases:
        specs[-1] = wherever
    out = out or here
    return pl.pallas_call(
        lambda token, *refs: kernel(*refs),
        out_shape=out_shape,
        in_specs=[wherever] + specs,
        out_specs=out if single else (out,) * len(out_shape),
        scratch_shapes=list(scratch),
        input_output_aliases=aliases or {},
        compiler_params=params(),
        cost_estimate=cost(1, 1),
        name=name,
    )(token, *args)


def fold_kernel(axis, bit, left, right, kept, sent):
    half = kept.shape[1]
    upper = (lax.axis_index(axis) & bit) != 0

    @pl.when(upper)
    def _():
        kept[...] = left[:, half:] + right[:, half:]
        sent[...] = left[:, :half] + right[:, :half]

    @pl.when(jnp.logical_not(upper))
    def _():
        kept[...] = left[:, :half] + right[:, :half]
        sent[...] = left[:, half:] + right[:, half:]


def fold(axis, bit, token, left, right):
    shape = jax.ShapeDtypeStruct((left.shape[0], left.shape[1] // 2), F32)
    return call(
        functools.partial(fold_kernel, axis, bit), "fold", (shape, shape), token, left, right
    )


def side_kernel(axis, bit, dim, mine, theirs, out):
    size = mine.shape[dim]
    low = (slice(None),) * dim + (slice(0, size),)
    high = (slice(None),) * dim + (slice(size, 2 * size),)
    upper = (lax.axis_index(axis) & bit) != 0

    @pl.when(upper)
    def _():
        out[low], out[high] = theirs[...], mine[...]

    @pl.when(jnp.logical_not(upper))
    def _():
        out[low], out[high] = mine[...], theirs[...]


def side(axis, bit, dim, token, mine, theirs):
    shape = list(mine.shape)
    shape[dim] *= 2
    return call(
        functools.partial(side_kernel, axis, bit, dim),
        "side", jax.ShapeDtypeStruct(tuple(shape), mine.dtype), token, mine, theirs,
    )


def halves(value):
    high = value.astype(BF16)
    return high, (value - high.astype(F32)).astype(BF16)


def product3(left, right):
    left_high, left_low = left
    right_high, right_low = right
    dot = functools.partial(jnp.dot, preferred_element_type=F32)
    rows = left_high.shape[0]
    both = dot(jnp.concatenate([left_high, left_low], axis=0), right_high)
    return both[:rows] + (dot(left_high, right_low) + both[rows:])


def inverse_kernel(gram_a, gram_b, inverse, rho_out):
    gram = gram_a[...] + gram_b[...]
    width = gram.shape[0]
    shape = (width, width)
    diagonal = lax.broadcasted_iota(jnp.int32, shape, 0) == lax.broadcasted_iota(
        jnp.int32, shape, 1
    )
    eye = jnp.where(diagonal, 1.0, 0.0).astype(F32)
    rho = jnp.sum(gram * eye) / width
    rho_out[...] = jnp.full(rho_out.shape, rho, F32)
    scale = 1.0 / jnp.full((1, 1), rho, F32)
    matrix = gram * scale + eye
    low = 2.0 / (width + 2.0)
    guess = low * eye
    image = low * matrix
    first = True
    while True:
        low = low * (2.0 - low)
        gain = 2.0 / (1.0 + low)
        low = gain * low
        done = 1.0 - low < 2e-3
        step = halves(gain * (2.0 * eye - image))
        if first:
            guess = guess[0:1, 0:1] * (gain * (2.0 * eye - image))
            image = product3(halves(image), step)
        elif done:
            guess = product3(halves(guess), step)
            break
        else:
            both = product3(halves(jnp.concatenate([guess, image], axis=0)), step)
            guess, image = both[:width], both[width:]
        first = False
    rest = eye - jnp.dot(
        matrix, guess, preferred_element_type=F32, precision=lax.Precision.HIGHEST
    )
    rest_halves = halves(rest)
    series = rest + product3(rest_halves, rest_halves)
    inverse[...] = (guess + product3(halves(guess), halves(series))) * scale


def shifted_inverse(gram_a, gram_b):
    width = gram_a.shape[0]
    whole = pl.BlockSpec(memory_space=pltpu.VMEM)
    return pl.pallas_call(
        inverse_kernel,
        out_shape=(
            jax.ShapeDtypeStruct((width, width), F32),
            jax.ShapeDtypeStruct((8, 128), F32),
        ),
        in_specs=[whole, whole],
        out_specs=(whole, whole),
        compiler_params=params(),
        cost_estimate=cost(1, 1),
        name="inverse",
    )(gram_a, gram_b)


def admm_kernel(genes, rho_block, cross_a, cross_b, inverse, start, columns_out):
    rows = cross_a.shape[1]
    place = lax.axis_index("sub") * genes + lax.axis_index("gene")
    rho = rho_block[0:1, 0:1]
    cross = cross_a[...] + cross_b[...]
    inverse_halves = halves(inverse[...])
    zvalue = start[pl.ds(pl.multiple_of(place * rows, rows), rows), :].astype(F32).T
    uvalue = jnp.zeros_like(zvalue)
    for _ in range(ITERS):
        vvalue = product3(inverse_halves, halves(cross + rho * (zvalue - uvalue)))
        zvalue = jnp.maximum(vvalue + uvalue, 0.0)
        uvalue = uvalue + vvalue - zvalue
    columns_out[...] = zvalue.astype(BF16)


def products_kernel(tile, bit, line, start, chunk, scales, sent, kept, columns, *outs):
    only_first = len(outs) == 1
    block = line.block(1 if only_first else 2, 0)
    size = kept.shape[1] // line.size
    span = min(tile, chunk)
    wide = 2 * span if chunk % (2 * span) == 0 else span
    steps = chunk // wide
    rows = columns.shape[1]
    quarter = rows // 4
    groups = [(sent, False), (kept, True)]

    turns = jnp.where(line.sends(1, 0), steps, 0) if only_first else line.size * steps

    @pl.loop(0, turns)
    def _(turn):
        order, step = (block, turn) if only_first else (turn // steps, lax.rem(turn, steps))
        genes = pl.ds(pl.multiple_of(order * size + start + step * wide, span), wide)
        total = None
        for counts, stays in groups:
            cells = [columns[:, pl.ds(at, quarter)] for at in pieces_of(rows, bit, stays)]
            part = jnp.dot(
                jnp.concatenate(cells, axis=1),
                scaled(counts, genes, tiles_of(bit, stays, rows, tile), scales),
                preferred_element_type=F32,
            )
            total = part if total is None else total + part
        total = total.astype(BF16)
        at = pl.ds(pl.multiple_of(step * wide, span), wide)
        if only_first:
            outs[0][:, at] = total
        else:
            outs[0][order, :, at] = total

            @pl.when(order == block)
            def _():
                outs[1][:, at] = total


def products(only_first, bit, line, start, chunk, token, scales, sent, kept, columns):
    width, rows = columns.shape
    tile = rows // (scales.shape[0] // 8)
    out_shape = (jax.ShapeDtypeStruct((width, chunk), BF16),)
    if not only_first:
        out_shape = (jax.ShapeDtypeStruct((line.size, width, chunk), BF16),) + out_shape
    return call(
        functools.partial(products_kernel, tile, bit, line, start, chunk),
        "products", out_shape, token, scales, held(sent), held(kept), columns,
    )


def turn_kernel(value, out):
    out[...] = value[...].astype(F32).T.astype(out.dtype)


def turn(token, value):
    shape = jax.ShapeDtypeStruct(value.shape[::-1], value.dtype)
    return call(turn_kernel, "turn", shape, token, value)


def row_share_kernel(columns, out):
    part = out.shape[0]
    place = lax.axis_index("gene")
    share = columns[pl.ds(pl.multiple_of(place * part, part), part), :]
    out[...] = contract_last(share, columns[...]).astype(out.dtype)


def row_share(part, token, columns):
    shape = jax.ShapeDtypeStruct((part, columns.shape[0]), BF16)
    return call(row_share_kernel, "row_share", shape, token, columns)


def plus_kernel(left, right, out):
    out[...] = (left[...].astype(F32) + right[...].astype(F32)).astype(out.dtype)


def hop_kernel(kind, targets, own, arrived, out):
    cell = lax.axis_index("cell")
    reached = cell == targets[0]
    for target in targets[1:]:
        reached = jnp.logical_or(reached, cell == target)
    more = arrived[...].astype(F32)
    base = own[...].astype(F32)
    value = base + more if kind == "sum" else more
    out[...] = jnp.where(reached, value, base).astype(out.dtype)


def hop(kind, targets, token, own, arrived):
    shape = jax.ShapeDtypeStruct(own.shape, own.dtype)
    return call(functools.partial(hop_kernel, kind, targets), "hop", shape, token, own, arrived)


def operand_kernel(line, phase, parity, total, before, out):
    own = total[line.block(phase, parity)].astype(F32)
    out[...] = (own + before[...].astype(F32)).astype(BF16)


def operand(line, phase, parity, token, total, before):
    shape = jax.ShapeDtypeStruct(before.shape, BF16)
    return call(
        functools.partial(operand_kernel, line, phase, parity),
        "operand", shape, token, total, before,
    )


def keep_kernel(start, total, first, second, *refs):
    out, turned, sems = refs[-3:]
    width, chunk = first.shape
    pieces = sems.shape[0]
    wide = chunk // pieces
    own = total.at[lax.axis_index("cell")]
    copies = []
    for piece in range(pieces):
        at = slice(piece * wide, (piece + 1) * wide)
        value = first[:, at].astype(F32) + second[:, at].astype(F32)
        turned[at] = (own[:, at].astype(F32) + value).T
        copies.append(
            pltpu.make_async_copy(
                turned.at[at], out.at[pl.ds(start + piece * wide, wide)], sems.at[piece]
            )
        )
        copies[-1].start()
    for copy in copies:
        copy.wait()


def keep(block, start, token, total, first, second, out):
    width, chunk = first.shape
    pieces = max(1, chunk // 256)
    return call(
        functools.partial(keep_kernel, start),
        "keep", jax.ShapeDtypeStruct((block, width), F32), token,
        total, first, second, *([] if out is None else [out]),
        scratch=[pltpu.VMEM((chunk, width), F32), pltpu.SemaphoreType.DMA((pieces,))],
        aliases=None if out is None else {4: 0},
        out=pl.BlockSpec(memory_space=pl.ANY),
    )


class Line:
    def __init__(self, size):
        self.size = size

    def pairs(self, phase, parity):
        links = range(parity, self.size - 1, 2)
        right = [(i, i + 1) for i in links if i < phase]
        left = [(i + 1, i) for i in links if i + 1 >= self.size - phase]
        return right + left

    def sends(self, phase, parity):
        cell = lax.axis_index("cell")
        ahead = self.size - phase
        to_right = (cell & 1) == parity
        return jnp.where(to_right, cell + ahead < self.size, cell >= ahead)

    def block(self, phase, parity):
        cell = lax.axis_index("cell")
        to_right = (cell & 1) == parity
        block = cell + jnp.where(to_right, self.size - phase, phase)
        return jnp.where(block >= self.size, block - self.size, block)

    def send(self, value, phase, parity):
        return lax.ppermute(value, "cell", self.pairs(phase, parity))


def swap(value, axis, size, step):
    return lax.ppermute(value, axis, [(i, i ^ step) for i in range(size)])


def pair_sums(value, axis, size, event):
    step = 1
    while step < size:
        arrived, event = after(swap(value, axis, size, step), event)
        value = value + arrived
        step *= 2
    return value, event


def after(value, event):
    return lax.optimization_barrier((value, event))


def chunk_sizes(block):
    return [block // 2, block // 2] if block % 1024 == 0 else [block]


def shards(sizes, counts, tile_mask, tile_counts, gene_factor, prev_factor):
    cells, genes, subs = sizes
    rows, columns = counts.shape
    width = gene_factor.shape[0]
    line = Line(cells)

    half_bit = bit = genes // 2
    gram, scales, turned, sent_rows = load(bit, gene_factor, counts, tile_mask, tile_counts)
    token = scales
    piece = jax.ShapeDtypeStruct((width, rows // 4), F32)
    low, high, mine, kept_rows = cross(bit, False, scales, sent_rows, turned, counts)
    low, high = [swap(value, "sub", subs, 1) for value in (low, high)]
    sent = call(plus_pieces_kernel, "plus", piece, token, mine, low, high)
    cross_b = swap(sent, "gene", genes, bit)
    gram, (scales_late, _) = pair_sums(gram, "gene", genes, (scales, sent))
    low, high, mine = cross(bit, True, scales_late, kept_rows, turned, counts)
    low, high = [swap(value, "sub", subs, 1) for value in (low, high)]
    gram_other = swap(gram, "sub", subs, 1)
    inverse, rho = shifted_inverse(gram, gram_other)
    token_late, inverse = after(token, inverse)
    cross_a = call(plus_pieces_kernel, "plus", piece, token_late, mine, low, high)
    bit //= 2
    while bit:
        cross_a, sent = fold("gene", bit, token, cross_a, cross_b)
        cross_b = swap(sent, "gene", genes, bit)
        bit //= 2
    share = jax.ShapeDtypeStruct((width, rows // (genes * subs)), BF16)
    columns_held = call(
        functools.partial(admm_kernel, genes),
        "admm", share, token, rho, cross_a, cross_b, inverse, prev_factor,
    )
    bit = 1
    while bit < genes:
        columns_arrived = swap(columns_held, "gene", genes, bit)
        columns_held = side("gene", bit, 1, token, columns_held, columns_arrived)
        bit *= 2
    token, rows_sum = after(token, row_share(width // genes, token, columns_held))
    columns_arrived = swap(columns_held, "sub", subs, 1)
    whole = side("sub", 1, 1, token, columns_held, columns_arrived)

    block = columns // cells
    chunks = chunk_sizes(block)
    starts = [sum(chunks[:i]) for i in range(len(chunks))]
    every = range(len(chunks))

    arrived = {}

    def send(value, phase, parity, index):
        pairs = line.pairs(phase, parity)
        arrived[phase, parity, index] = lax.ppermute(value, "cell", pairs) if pairs else None

    def resend(token, phase, parity, index):
        before = arrived[phase - 1, 1 - parity, index]
        if before is None:
            value = seconds[index]
        else:
            value = operand(line, phase, parity, token, totals[index], before)
            token, value = after(token, value)
        send(value, phase, parity, index)
        return token

    middle = cells // 2
    inward = [[(i, i + 1), (cells - 1 - i, cells - 2 - i)] for i in range(middle - 1)]
    outward = [[(b, a) for a, b in pairs] for pairs in reversed(inward)]
    hops = [("sum", p) for p in inward] + [("sum", [(middle - 1, middle), (middle, middle - 1)])]
    hops += [("copy", p) for p in outward]

    def hop_rows(token, rows_sum):
        kind, pairs = hops.pop(0)
        both = sorted(set(pairs) | {(b, a) for a, b in pairs})
        rows_arrived = lax.ppermute(rows_sum, "cell", both)
        targets = [b for _, b in pairs]
        return after(token, hop(kind, targets, token, rows_sum, rows_arrived))

    def side_rows(token, rows_sum, axis, size, bit):
        rows_arrived = swap(rows_sum, axis, size, bit)
        return after(token, side(axis, bit, 0, token, rows_sum, rows_arrived))

    for index in every:
        (first,) = products(
            True, half_bit, line, starts[index], chunks[index], token, scales, sent_rows, kept_rows, whole
        )
        token, first = after(token, first)
        for parity in (0, 1):
            send(first, 1, parity, index)
        if index == 0 and hops:
            token, rows_sum = hop_rows(token, rows_sum)
    totals, seconds = [], []
    for index in every:
        total, second = products(
            False, half_bit, line, starts[index], chunks[index], token, scales, sent_rows, kept_rows, whole
        )
        token, second = after(token, second)
        if hops:
            token, rows_sum = hop_rows(token, rows_sum)
        totals.append(total)
        seconds.append(second)
        for parity in (0, 1):
            token = resend(token, 2, parity, index)
    while hops:
        token, rows_sum = hop_rows(token, rows_sum)
    new_factor = turn(token, whole)
    token, new_factor = after(token, new_factor)
    rows_arrived = swap(rows_sum, "sub", subs, 1)
    shape = jax.ShapeDtypeStruct(rows_sum.shape, F32)
    token, rows_sum = after(token, call(plus_kernel, "plus", shape, token, rows_sum, rows_arrived))
    bits = [1 << i for i in range((genes - 1).bit_length())]
    for phase in range(3, cells):
        for index in every:
            for parity in (0, 1):
                token = resend(token, phase, parity, index)
                if bits:
                    token, rows_sum = side_rows(token, rows_sum, "gene", genes, bits.pop(0))
    data_products = None
    last = cells - 1
    for index in every:
        data_products = keep(
            block, starts[index], token, totals[index],
            arrived[last, 0, index], arrived[last, 1, index], data_products,
        )
        token, data_products = after(token, data_products)
    return (new_factor, rows_sum, data_products)


def solution(mesh):
    sizes = (mesh.shape["cell"], mesh.shape["gene"], mesh.shape["sub"])
    return jax.shard_map(
        functools.partial(shards, sizes),
        mesh=mesh,
        in_specs=(
            P(("groups", "cell"), ("gene", "sub")),
            P(("groups", "cell"), ("gene", "sub")),
            P(("groups", "cell"), ("gene", "sub")),
            P("groups", ("gene", "sub")),
            P(("groups", "cell"), None),
        ),
        out_specs=(
            P(("groups", "cell"), None),
            P("groups", None),
            P(("groups", "gene", "sub", "cell"), None),
        ),
        check_vma=False,
    )
```

```python
import functools

import jax
import jax.numpy as jnp
import numpy as np
from jax import lax
from jax.experimental import pallas as pl
from jax.experimental.pallas import tpu as pltpu
from jax.sharding import PartitionSpec as P

ITERS = 3
F32 = jnp.float32
BF16 = jnp.bfloat16
MIB = 1024 * 1024


def params(limit=16):
    return pltpu.CompilerParams(vmem_limit_bytes=limit * MIB)


def away(value):
    return pltpu.with_memory_space_constraint(value, pltpu.HBM)


def held(value):
    return pltpu.with_memory_space_constraint(value, pltpu.VMEM)


def cost(flops, bytes_accessed):
    return pl.CostEstimate(flops=flops, bytes_accessed=bytes_accessed, transcendentals=0)


def contract_last(left, right):
    return lax.dot_general(
        left, right, (((1,), (1,)), ((), ())), preferred_element_type=F32
    )


def row_copies(source, target, first, sems):
    rows = target.shape[0]
    piece = max(rows // sems.shape[0], 16)
    return [
        pltpu.make_async_copy(
            source.at[pl.ds(first + i * piece, piece)],
            target.at[pl.ds(i * piece, piece)],
            sems.at[i],
        )
        for i in range(rows // piece)
    ]


def pieces_of(rows, bit, kept):
    core = lax.axis_index("sub")
    upper = ((lax.axis_index("gene") & bit) != 0) == kept
    half, quarter = rows // 2, rows // 4
    place = jnp.where(upper, quarter, 0)
    return [
        pl.multiple_of((1 - core) * half + place, quarter),
        pl.multiple_of(core * half + place, quarter),
    ]


def piece_copies(bit, kept, counts, target, sems):
    quarter = counts.shape[0] // 4
    copies = []
    for i, place in enumerate(pieces_of(counts.shape[0], bit, kept)):
        copies += row_copies(
            counts, target.at[i * quarter : (i + 1) * quarter], place, sems.at[i * 4 : i * 4 + 4]
        )
    return copies


def load_kernel(
    bit, genes, counts, tile_mask, tile_counts, gram, scales, turned, first,
    genes_here, mask_here, counts_here, gene_sems, row_sems, small_sems,
):
    small_copies = [
        pltpu.make_async_copy(tile_mask, mask_here, small_sems.at[0]),
        pltpu.make_async_copy(tile_counts, counts_here, small_sems.at[1]),
    ]
    gene_copies = row_copies(genes, genes_here, 0, gene_sems)
    row_starts = piece_copies(bit, False, counts, first, row_sems)
    for copy in gene_copies + small_copies:
        copy.start()
    for copy in small_copies:
        copy.wait()
    ratio = mask_here[...].astype(F32) / counts_here[...].astype(F32)
    columns = genes.shape[1]
    tile = columns // ratio.shape[1]
    for row in range(ratio.shape[0]):
        for col in range(ratio.shape[1]):
            scales[row * 8 : row * 8 + 8, col * tile : (col + 1) * tile] = jnp.broadcast_to(
                ratio[row : row + 1, col : col + 1], (8, tile)
            )
    for copy in gene_copies:
        copy.wait()
    for copy in row_starts:
        copy.start()
    wide = min(1024, columns)
    gram[...] = jnp.zeros_like(gram)

    @pl.loop(0, columns // wide)
    def _(step):
        at = pl.ds(pl.multiple_of(step * wide, wide), wide)
        piece = genes_here[:, at]
        turned[at, :] = piece.T
        gram[...] += jnp.dot(piece, turned[at, :], preferred_element_type=F32)

    for copy in row_starts:
        copy.wait()


def load(bit, genes, counts, tile_mask, tile_counts):
    width, columns = genes.shape
    rows = counts.shape[0]
    here = pl.BlockSpec(memory_space=pltpu.VMEM)
    there = pl.BlockSpec(memory_space=pltpu.HBM)
    return pl.pallas_call(
        functools.partial(load_kernel, bit),
        out_shape=(
            jax.ShapeDtypeStruct((width, width), F32),
            jax.ShapeDtypeStruct((tile_mask.shape[0] * 8, columns), F32),
            pltpu.VMEM((columns, width), BF16),
            pltpu.VMEM((rows // 2, columns), BF16),
        ),
        in_specs=[there] * 4,
        out_specs=(here,) * 4,
        scratch_shapes=[
            pltpu.VMEM((width, columns), BF16),
            pltpu.VMEM(tile_mask.shape, jnp.int32),
            pltpu.VMEM(tile_mask.shape, jnp.int32),
            pltpu.SemaphoreType.DMA((4,)),
            pltpu.SemaphoreType.DMA((8,)),
            pltpu.SemaphoreType.DMA((2,)),
        ],
        compiler_params=params(),
        cost_estimate=cost(1, 1),
        name="load",
    )(away(genes), away(counts), away(tile_mask), away(tile_counts))


def scaled(counts, at, row_tiles, scales):
    tile = counts.shape[0] // len(row_tiles)
    return jnp.concatenate(
        [
            (
                counts[i * tile : (i + 1) * tile, at].astype(F32)
                * scales[pl.ds(pl.multiple_of(row * 8, 8), 8), at][0:1]
            ).astype(BF16)
            for i, row in enumerate(row_tiles)
        ],
        axis=0,
    )


def cross_rows(row_tiles, scales, counts, turned, total):
    columns = counts.shape[1]
    wide = min(1024, columns)
    total[...] = jnp.zeros_like(total)

    @pl.loop(0, columns // wide)
    def _(step):
        at = pl.ds(pl.multiple_of(step * wide, wide), wide)
        total[...] += jnp.dot(
            scaled(counts, at, row_tiles, scales), turned[at, :], preferred_element_type=F32
        )


def tiles_of(bit, kept, rows, tile):
    quarter = rows // 4
    return [
        place // tile + i
        for place in pieces_of(rows, bit, kept)
        for i in range(quarter // tile)
    ]


def cross_kernel(bit, kept, rows, scales, held_rows, turned, *refs):
    (low, high, mine), total = refs[-5:-2] if kept else refs[1:4], refs[-2]
    if not kept:
        copies = piece_copies(bit, True, refs[0], refs[4], refs[-1])
        for copy in copies:
            copy.start()
    quarter, tile = rows // 4, rows // (scales.shape[0] // 8)
    cross_rows(tiles_of(bit, kept, rows, tile), scales, held_rows, turned, total)
    low[...] = total[: quarter // 2].T
    high[...] = total[quarter // 2 : quarter].T
    mine[...] = total[quarter:].T
    if not kept:
        for copy in copies:
            copy.wait()


def cross(bit, kept, scales, held_rows, turned, counts):
    rows, columns = counts.shape
    width = turned.shape[1]
    here = pl.BlockSpec(memory_space=pltpu.VMEM)
    piece = jax.ShapeDtypeStruct((width, rows // 4), F32)
    small_piece = jax.ShapeDtypeStruct((width, rows // 8), F32)
    out_shape = (small_piece, small_piece, piece)
    in_specs, args = [here] * 3, [scales, held(held_rows), held(turned)]
    if not kept:
        out_shape += (pltpu.VMEM((rows // 2, columns), BF16),)
        in_specs.append(pl.BlockSpec(memory_space=pltpu.HBM))
        args.append(away(counts))
    return pl.pallas_call(
        functools.partial(cross_kernel, bit, kept, rows),
        out_shape=out_shape,
        in_specs=in_specs,
        out_specs=(here,) * len(out_shape),
        scratch_shapes=[pltpu.VMEM((rows // 2, width), F32), pltpu.SemaphoreType.DMA((8,))],
        compiler_params=params(),
        cost_estimate=cost(1, 1),
        name="cross_kept" if kept else "cross_sent",
    )(*args)


def plus_pieces_kernel(left, low, high, out):
    half = low.shape[1]
    out[:, :half] = left[:, :half] + low[...]
    out[:, half:] = left[:, half:] + high[...]


def call(kernel, name, out_shape, token, *args, scratch=(), aliases=None, out=None):
    here = pl.BlockSpec(memory_space=pltpu.VMEM)
    wherever = pl.BlockSpec(memory_space=pl.ANY)
    single = not isinstance(out_shape, tuple)
    specs = [here] * len(args)
    if aliases:
        specs[-1] = wherever
    out = out or here
    return pl.pallas_call(
        lambda token, *refs: kernel(*refs),
        out_shape=out_shape,
        in_specs=[wherever] + specs,
        out_specs=out if single else (out,) * len(out_shape),
        scratch_shapes=list(scratch),
        input_output_aliases=aliases or {},
        compiler_params=params(),
        cost_estimate=cost(1, 1),
        name=name,
    )(token, *args)


def fold_kernel(axis, bit, left, right, kept, sent):
    half = kept.shape[1]
    upper = (lax.axis_index(axis) & bit) != 0

    @pl.when(upper)
    def _():
        kept[...] = left[:, half:] + right[:, half:]
        sent[...] = left[:, :half] + right[:, :half]

    @pl.when(jnp.logical_not(upper))
    def _():
        kept[...] = left[:, :half] + right[:, :half]
        sent[...] = left[:, half:] + right[:, half:]


def fold(axis, bit, token, left, right):
    shape = jax.ShapeDtypeStruct((left.shape[0], left.shape[1] // 2), F32)
    return call(
        functools.partial(fold_kernel, axis, bit), "fold", (shape, shape), token, left, right
    )


def side_kernel(axis, bit, dim, mine, theirs, out):
    size = mine.shape[dim]
    low = (slice(None),) * dim + (slice(0, size),)
    high = (slice(None),) * dim + (slice(size, 2 * size),)
    upper = (lax.axis_index(axis) & bit) != 0

    @pl.when(upper)
    def _():
        out[low], out[high] = theirs[...], mine[...]

    @pl.when(jnp.logical_not(upper))
    def _():
        out[low], out[high] = mine[...], theirs[...]


def side(axis, bit, dim, token, mine, theirs):
    shape = list(mine.shape)
    shape[dim] *= 2
    return call(
        functools.partial(side_kernel, axis, bit, dim),
        "side", jax.ShapeDtypeStruct(tuple(shape), mine.dtype), token, mine, theirs,
    )


def halves(value):
    high = value.astype(BF16)
    return high, (value - high.astype(F32)).astype(BF16)


def product3(left, right):
    left_high, left_low = left
    right_high, right_low = right
    dot = functools.partial(jnp.dot, preferred_element_type=F32)
    return dot(left_high, right_high) + (
        dot(left_high, right_low) + dot(left_low, right_high)
    )


def inverse_kernel(gram_in, inverse, rho_out):
    gram = gram_in[...]
    width = gram.shape[0]
    shape = (width, width)
    diagonal = lax.broadcasted_iota(jnp.int32, shape, 0) == lax.broadcasted_iota(
        jnp.int32, shape, 1
    )
    eye = jnp.where(diagonal, 1.0, 0.0).astype(F32)
    rho = jnp.sum(gram * eye) / width
    rho_out[...] = jnp.full(rho_out.shape, rho, F32)
    scale = 1.0 / jnp.full((1, 1), rho, F32)
    matrix = gram * scale + eye
    low = 2.0 / (width + 2.0)
    guess = low * eye
    image = low * matrix
    first = True
    while True:
        low = low * (2.0 - low)
        gain = 2.0 / (1.0 + low)
        low = gain * low
        done = 1.0 - low < 2e-3
        step = halves(gain * (2.0 * eye - image))
        if first:
            guess = guess[0:1, 0:1] * (gain * (2.0 * eye - image))
        else:
            guess = product3(halves(guess), step)
        first = False
        if done:
            break
        image = product3(halves(image), step)
    rest = eye - jnp.dot(
        matrix, guess, preferred_element_type=F32, precision=lax.Precision.HIGHEST
    )
    rest_halves = halves(rest)
    series = rest + product3(rest_halves, rest_halves)
    inverse[...] = (guess + product3(halves(guess), halves(series))) * scale


def shifted_inverse(gram):
    width = gram.shape[0]
    whole = pl.BlockSpec(memory_space=pltpu.VMEM)
    return pl.pallas_call(
        inverse_kernel,
        out_shape=(
            jax.ShapeDtypeStruct((width, width), F32),
            jax.ShapeDtypeStruct((8, 128), F32),
        ),
        in_specs=[whole],
        out_specs=(whole, whole),
        compiler_params=params(),
        cost_estimate=cost(1, 1),
        name="inverse",
    )(gram)


def admm_kernel(genes, rho_block, cross_a, cross_b, inverse, start, columns_out):
    rows = cross_a.shape[1]
    place = lax.axis_index("sub") * genes + lax.axis_index("gene")
    rho = rho_block[0:1, 0:1]
    cross = cross_a[...] + cross_b[...]
    inverse_halves = halves(inverse[...])
    zvalue = start[pl.ds(pl.multiple_of(place * rows, rows), rows), :].astype(F32).T
    uvalue = jnp.zeros_like(zvalue)
    for _ in range(ITERS):
        vvalue = product3(inverse_halves, halves(cross + rho * (zvalue - uvalue)))
        zvalue = jnp.maximum(vvalue + uvalue, 0.0)
        uvalue = uvalue + vvalue - zvalue
    columns_out[...] = zvalue.astype(BF16)


def products_kernel(tile, bit, line, start, chunk, scales, sent, kept, columns, *outs):
    only_first = len(outs) == 1
    block = line.block(1 if only_first else 2, 0)
    size = kept.shape[1] // line.size
    span = min(tile, chunk)
    wide = 2 * span if chunk % (2 * span) == 0 else span
    steps = chunk // wide
    rows = columns.shape[1]
    quarter = rows // 4
    groups = [(sent, False), (kept, True)]

    @pl.loop(0, steps if only_first else line.size * steps)
    def _(turn):
        order, step = (block, turn) if only_first else (turn // steps, lax.rem(turn, steps))
        genes = pl.ds(pl.multiple_of(order * size + start + step * wide, span), wide)
        total = None
        for counts, stays in groups:
            cells = [columns[:, pl.ds(at, quarter)] for at in pieces_of(rows, bit, stays)]
            part = jnp.dot(
                jnp.concatenate(cells, axis=1),
                scaled(counts, genes, tiles_of(bit, stays, rows, tile), scales),
                preferred_element_type=F32,
            )
            total = part if total is None else total + part
        total = total.astype(BF16)
        at = pl.ds(pl.multiple_of(step * wide, span), wide)
        if only_first:
            outs[0][:, at] = total
        else:
            outs[0][order, :, at] = total

            @pl.when(order == block)
            def _():
                outs[1][:, at] = total


def products(only_first, bit, line, start, chunk, token, scales, sent, kept, columns):
    width, rows = columns.shape
    tile = rows // (scales.shape[0] // 8)
    out_shape = (jax.ShapeDtypeStruct((width, chunk), BF16),)
    if not only_first:
        out_shape = (jax.ShapeDtypeStruct((line.size, width, chunk), BF16),) + out_shape
    return call(
        functools.partial(products_kernel, tile, bit, line, start, chunk),
        "products", out_shape, token, scales, held(sent), held(kept), columns,
    )


def turn_kernel(value, out):
    out[...] = value[...].astype(F32).T.astype(out.dtype)


def turn(token, value):
    shape = jax.ShapeDtypeStruct(value.shape[::-1], value.dtype)
    return call(turn_kernel, "turn", shape, token, value)


def row_share_kernel(columns, out):
    part = out.shape[0]
    place = lax.axis_index("gene")
    share = columns[pl.ds(pl.multiple_of(place * part, part), part), :]
    out[...] = contract_last(share, columns[...]).astype(out.dtype)


def row_share(part, token, columns):
    shape = jax.ShapeDtypeStruct((part, columns.shape[0]), BF16)
    return call(row_share_kernel, "row_share", shape, token, columns)


def plus_kernel(left, right, out):
    out[...] = (left[...].astype(F32) + right[...].astype(F32)).astype(out.dtype)


def hop_kernel(kind, targets, own, arrived, out):
    cell = lax.axis_index("cell")
    reached = cell == targets[0]
    for target in targets[1:]:
        reached = jnp.logical_or(reached, cell == target)
    more = arrived[...].astype(F32)
    base = own[...].astype(F32)
    value = base + more if kind == "sum" else more
    out[...] = jnp.where(reached, value, base).astype(out.dtype)


def hop(kind, targets, token, own, arrived):
    shape = jax.ShapeDtypeStruct(own.shape, own.dtype)
    return call(functools.partial(hop_kernel, kind, targets), "hop", shape, token, own, arrived)


def operand_kernel(line, phase, parity, total, before, *outs):
    own = total.at[line.block(phase, parity)]
    start = 0
    for out in outs:
        at = slice(start, start + out.shape[1])
        out[...] = (own[:, at].astype(F32) + before[:, at].astype(F32)).astype(BF16)
        start += out.shape[1]


def operand(line, phase, parity, parts, token, total, before):
    width = before.shape[0]
    return call(
        functools.partial(operand_kernel, line, phase, parity),
        "operand", tuple(jax.ShapeDtypeStruct((width, part), BF16) for part in parts),
        token, total, before,
    )


def keep_kernel(start, skip, total, first, second, *refs):
    out, turned, sems = refs[-3:]
    pieces = sems.shape[0]
    wide = first.shape[1] // pieces
    own = total.at[lax.axis_index("cell")]
    copies = []
    for piece in range(pieces):
        at = slice(piece * wide, (piece + 1) * wide)
        there = slice(skip + piece * wide, skip + (piece + 1) * wide)
        value = first[:, at].astype(F32) + second[:, there].astype(F32)
        turned[at] = (own[:, there].astype(F32) + value).T
        copies.append(
            pltpu.make_async_copy(
                turned.at[at], out.at[pl.ds(start + skip + piece * wide, wide)], sems.at[piece]
            )
        )
        copies[-1].start()
    for copy in copies:
        copy.wait()


def keep(block, start, skip, token, total, first, second, out):
    width, chunk = first.shape
    pieces = max(1, chunk // 256)
    return call(
        functools.partial(keep_kernel, start, skip),
        "keep", jax.ShapeDtypeStruct((block, width), F32), token,
        total, first, second, *([] if out is None else [out]),
        scratch=[pltpu.VMEM((chunk, width), F32), pltpu.SemaphoreType.DMA((pieces,))],
        aliases=None if out is None else {4: 0},
        out=pl.BlockSpec(memory_space=pl.ANY),
    )


class Line:
    def __init__(self, size):
        self.size = size

    def pairs(self, phase, parity, exchange=False):
        links = range(parity, self.size - 1, 2)
        right = [(i, i + 1) for i in links if i < phase]
        left = [(i + 1, i) for i in links if i + 1 >= self.size - phase]
        pairs = right + left
        if exchange:
            pairs = sorted(set(pairs) | {(b, a) for a, b in pairs})
        return pairs

    def block(self, phase, parity):
        cell = lax.axis_index("cell")
        to_right = (cell & 1) == parity
        block = cell + jnp.where(to_right, self.size - phase, phase)
        return jnp.where(block >= self.size, block - self.size, block)

    def send(self, value, phase, parity):
        return lax.ppermute(value, "cell", self.pairs(phase, parity))


def swap(value, axis, size, step):
    return lax.ppermute(value, axis, [(i, i ^ step) for i in range(size)])


def pair_sums(value, axis, size, event):
    step = 1
    while step < size:
        arrived, event = after(swap(value, axis, size, step), event)
        value = value + arrived
        step *= 2
    return value, event


def after(value, event):
    return lax.optimization_barrier((value, event))


def chunk_sizes(block):
    return [block // 2, block // 2] if block % 1024 == 0 else [block]


def shards(sizes, counts, tile_mask, tile_counts, gene_factor, prev_factor):
    cells, genes, subs = sizes
    rows, columns = counts.shape
    width = gene_factor.shape[0]
    line = Line(cells)

    half_bit = bit = genes // 2
    gram, scales, turned, sent_rows = load(bit, gene_factor, counts, tile_mask, tile_counts)
    token = scales
    piece = jax.ShapeDtypeStruct((width, rows // 4), F32)
    gram_other = swap(gram, "sub", subs, 1)
    low, high, mine, kept_rows = cross(bit, False, scales, sent_rows, turned, counts)
    low, high = [swap(value, "sub", subs, 1) for value in (low, high)]
    token_sent, mine = after(token, mine)
    gram_half, _ = fold("sub", 1, token_sent, gram, gram_other)
    token_sent, gram_half = after(token, gram_half)
    sent = call(plus_pieces_kernel, "plus", piece, token_sent, mine, low, high)
    cross_b = swap(sent, "gene", genes, bit)
    scales_late, _ = after(scales, sent)
    low, high, mine = cross(bit, True, scales_late, kept_rows, turned, counts)
    low, high = [swap(value, "sub", subs, 1) for value in (low, high)]
    gram_half, (mine, _) = pair_sums(gram_half, "gene", genes, (mine, scales))
    gram = side("sub", 1, 1, token, gram_half, swap(gram_half, "sub", subs, 1))
    inverse, rho = shifted_inverse(gram)
    token_late, inverse = after(token, inverse)
    cross_a = call(plus_pieces_kernel, "plus", piece, token_late, mine, low, high)
    bit //= 2
    while bit:
        cross_a, sent = fold("gene", bit, token, cross_a, cross_b)
        cross_b = swap(sent, "gene", genes, bit)
        bit //= 2
    share = jax.ShapeDtypeStruct((width, rows // (genes * subs)), BF16)
    columns_held = call(
        functools.partial(admm_kernel, genes),
        "admm", share, token, rho, cross_a, cross_b, inverse, prev_factor,
    )
    bit = 1
    while bit < genes:
        columns_arrived = swap(columns_held, "gene", genes, bit)
        columns_held = side("gene", bit, 1, token, columns_held, columns_arrived)
        bit *= 2
    token, rows_sum = after(token, row_share(width // genes, token, columns_held))
    columns_arrived = swap(columns_held, "sub", subs, 1)
    whole = side("sub", 1, 1, token, columns_held, columns_arrived)

    block = columns // cells
    chunks = chunk_sizes(block)
    starts = [sum(chunks[:i]) for i in range(len(chunks))]
    every = range(len(chunks))

    arrived = {}
    last_part = []

    def send(value, phase, parity, index):
        pairs = line.pairs(phase, parity, exchange=phase == 1 and index == 0)
        arrived[phase, parity, index] = lax.ppermute(value, "cell", pairs) if pairs else None

    def resend(token, phase, parity, index):
        before = arrived[phase - 1, 1 - parity, index]
        if before is None:
            value = seconds[index]
        else:
            chunk = chunks[index]
            parts = (chunk,)
            if phase == cells - 1 and parity == 0 and index == every[-1] and chunk >= 1024:
                parts = (chunk // 4 * 3, chunk // 4)
            values = operand(line, phase, parity, parts, token, totals[index], before)
            token, values = after(token, values)
            value, rest = values[0], values[1:]
            for part in rest:
                last_part.append(lax.ppermute(part, "cell", line.pairs(phase, parity)))
        send(value, phase, parity, index)
        return token

    middle = cells // 2
    inward = [[(i, i + 1), (cells - 1 - i, cells - 2 - i)] for i in range(middle - 1)]
    outward = [[(b, a) for a, b in pairs] for pairs in reversed(inward)]
    hops = [("sum", p) for p in inward] + [("sum", [(middle - 1, middle), (middle, middle - 1)])]
    hops += [("copy", p) for p in outward]

    def hop_rows(token, rows_sum):
        kind, pairs = hops.pop(0)
        both = sorted(set(pairs) | {(b, a) for a, b in pairs})
        rows_arrived = lax.ppermute(rows_sum, "cell", both)
        targets = [b for _, b in pairs]
        return after(token, hop(kind, targets, token, rows_sum, rows_arrived))

    def side_rows(token, rows_sum, axis, size, bit):
        rows_arrived = swap(rows_sum, axis, size, bit)
        return after(token, side(axis, bit, 0, token, rows_sum, rows_arrived))

    for index in every:
        (first,) = products(
            True, half_bit, line, starts[index], chunks[index], token, scales, sent_rows, kept_rows, whole
        )
        token, first = after(token, first)
        for parity in (0, 1):
            send(first, 1, parity, index)
        if index == 0 and hops:
            token, rows_sum = hop_rows(token, rows_sum)
    totals, seconds = [], []
    for index in every:
        total, second = products(
            False, half_bit, line, starts[index], chunks[index], token, scales, sent_rows, kept_rows, whole
        )
        token, second = after(token, second)
        if hops:
            token, rows_sum = hop_rows(token, rows_sum)
        totals.append(total)
        seconds.append(second)
        for parity in (0, 1):
            token = resend(token, 2, parity, index)
    while hops:
        token, rows_sum = hop_rows(token, rows_sum)
    new_factor = turn(token, whole)
    token, new_factor = after(token, new_factor)
    rows_arrived = swap(rows_sum, "sub", subs, 1)
    shape = jax.ShapeDtypeStruct(rows_sum.shape, F32)
    token, rows_sum = after(token, call(plus_kernel, "plus", shape, token, rows_sum, rows_arrived))
    bits = [1 << i for i in range((genes - 1).bit_length())]
    for phase in range(3, cells):
        for index in every:
            for parity in (0, 1):
                token = resend(token, phase, parity, index)
                if bits:
                    token, rows_sum = side_rows(token, rows_sum, "gene", genes, bits.pop(0))
    data_products = None
    last = cells - 1
    for index in every:
        parts = [arrived[last, 0, index]] + (last_part if index == every[-1] else [])
        skip = 0
        for part in parts:
            data_products = keep(
                block, starts[index], skip, token, totals[index],
                part, arrived[last, 1, index], data_products,
            )
            token, data_products = after(token, data_products)
            skip += part.shape[1]
    return (new_factor, rows_sum, data_products)


def solution(mesh):
    sizes = (mesh.shape["cell"], mesh.shape["gene"], mesh.shape["sub"])
    return jax.shard_map(
        functools.partial(shards, sizes),
        mesh=mesh,
        in_specs=(
            P(("groups", "cell"), ("gene", "sub")),
            P(("groups", "cell"), ("gene", "sub")),
            P(("groups", "cell"), ("gene", "sub")),
            P("groups", ("gene", "sub")),
            P(("groups", "cell"), None),
        ),
        out_specs=(
            P(("groups", "cell"), None),
            P("groups", None),
            P(("groups", "gene", "sub", "cell"), None),
        ),
        check_vma=False,
    )
```

```python
import functools

import jax
import jax.numpy as jnp
import numpy as np
from jax import lax
from jax.experimental import pallas as pl
from jax.experimental.pallas import tpu as pltpu
from jax.sharding import PartitionSpec as P

ITERS = 3
F32 = jnp.float32
BF16 = jnp.bfloat16
MIB = 1024 * 1024


def params(limit=16):
    return pltpu.CompilerParams(vmem_limit_bytes=limit * MIB)


def away(value):
    return pltpu.with_memory_space_constraint(value, pltpu.HBM)


def held(value):
    return pltpu.with_memory_space_constraint(value, pltpu.VMEM)


def cost(flops, bytes_accessed):
    return pl.CostEstimate(flops=flops, bytes_accessed=bytes_accessed, transcendentals=0)


def contract_last(left, right):
    return lax.dot_general(
        left, right, (((1,), (1,)), ((), ())), preferred_element_type=F32
    )


def row_copies(source, target, first, sems):
    rows = target.shape[0]
    piece = max(rows // sems.shape[0], 16)
    return [
        pltpu.make_async_copy(
            source.at[pl.ds(first + i * piece, piece)],
            target.at[pl.ds(i * piece, piece)],
            sems.at[i],
        )
        for i in range(rows // piece)
    ]


def pieces_of(rows, bit, kept):
    core = lax.axis_index("sub")
    upper = ((lax.axis_index("gene") & bit) != 0) == kept
    half, quarter = rows // 2, rows // 4
    place = jnp.where(upper, quarter, 0)
    return [
        pl.multiple_of((1 - core) * half + place, quarter),
        pl.multiple_of(core * half + place, quarter),
    ]


def piece_copies(bit, kept, counts, target, sems):
    quarter = counts.shape[0] // 4
    copies = []
    for i, place in enumerate(pieces_of(counts.shape[0], bit, kept)):
        copies += row_copies(
            counts, target.at[i * quarter : (i + 1) * quarter], place, sems.at[i * 4 : i * 4 + 4]
        )
    return copies


def load_kernel(
    bit, genes, counts, tile_mask, tile_counts, gram, scales, turned, first,
    genes_here, mask_here, counts_here, gene_sems, row_sems, small_sems,
):
    small_copies = [
        pltpu.make_async_copy(tile_mask, mask_here, small_sems.at[0]),
        pltpu.make_async_copy(tile_counts, counts_here, small_sems.at[1]),
    ]
    gene_copies = row_copies(genes, genes_here, 0, gene_sems)
    row_starts = piece_copies(bit, False, counts, first, row_sems)
    for copy in gene_copies + small_copies:
        copy.start()
    for copy in small_copies:
        copy.wait()
    ratio = mask_here[...].astype(F32) / counts_here[...].astype(F32)
    columns = genes.shape[1]
    tile = columns // ratio.shape[1]
    for row in range(ratio.shape[0]):
        for col in range(ratio.shape[1]):
            scales[row * 8 : row * 8 + 8, col * tile : (col + 1) * tile] = jnp.broadcast_to(
                ratio[row : row + 1, col : col + 1], (8, tile)
            )
    for copy in gene_copies:
        copy.wait()
    for copy in row_starts:
        copy.start()
    wide = min(1024, columns)
    gram[...] = jnp.zeros_like(gram)

    @pl.loop(0, columns // wide)
    def _(step):
        at = pl.ds(pl.multiple_of(step * wide, wide), wide)
        piece = genes_here[:, at]
        turned[at, :] = piece.T
        gram[...] += jnp.dot(piece, turned[at, :], preferred_element_type=F32)

    for copy in row_starts:
        copy.wait()


def load(bit, genes, counts, tile_mask, tile_counts):
    width, columns = genes.shape
    rows = counts.shape[0]
    here = pl.BlockSpec(memory_space=pltpu.VMEM)
    there = pl.BlockSpec(memory_space=pltpu.HBM)
    return pl.pallas_call(
        functools.partial(load_kernel, bit),
        out_shape=(
            jax.ShapeDtypeStruct((width, width), F32),
            jax.ShapeDtypeStruct((tile_mask.shape[0] * 8, columns), F32),
            pltpu.VMEM((columns, width), BF16),
            pltpu.VMEM((rows // 2, columns), BF16),
        ),
        in_specs=[there] * 4,
        out_specs=(here,) * 4,
        scratch_shapes=[
            pltpu.VMEM((width, columns), BF16),
            pltpu.VMEM(tile_mask.shape, jnp.int32),
            pltpu.VMEM(tile_mask.shape, jnp.int32),
            pltpu.SemaphoreType.DMA((4,)),
            pltpu.SemaphoreType.DMA((8,)),
            pltpu.SemaphoreType.DMA((2,)),
        ],
        compiler_params=params(),
        cost_estimate=cost(1, 1),
        name="load",
    )(away(genes), away(counts), away(tile_mask), away(tile_counts))


def scaled(counts, at, row_tiles, scales):
    tile = counts.shape[0] // len(row_tiles)
    return jnp.concatenate(
        [
            (
                counts[i * tile : (i + 1) * tile, at].astype(F32)
                * scales[pl.ds(pl.multiple_of(row * 8, 8), 8), at][0:1]
            ).astype(BF16)
            for i, row in enumerate(row_tiles)
        ],
        axis=0,
    )


def cross_rows(row_tiles, scales, counts, turned, total):
    columns = counts.shape[1]
    wide = min(1024, columns)
    total[...] = jnp.zeros_like(total)

    @pl.loop(0, columns // wide)
    def _(step):
        at = pl.ds(pl.multiple_of(step * wide, wide), wide)
        total[...] += jnp.dot(
            scaled(counts, at, row_tiles, scales), turned[at, :], preferred_element_type=F32
        )


def tiles_of(bit, kept, rows, tile):
    quarter = rows // 4
    return [
        place // tile + i
        for place in pieces_of(rows, bit, kept)
        for i in range(quarter // tile)
    ]


def cross_kernel(bit, kept, rows, scales, held_rows, turned, *refs):
    (low, high, mine), total = refs[-5:-2] if kept else refs[1:4], refs[-2]
    if not kept:
        copies = piece_copies(bit, True, refs[0], refs[4], refs[-1])
        for copy in copies:
            copy.start()
    quarter, tile = rows // 4, rows // (scales.shape[0] // 8)
    cross_rows(tiles_of(bit, kept, rows, tile), scales, held_rows, turned, total)
    low[...] = total[: quarter // 2].T
    high[...] = total[quarter // 2 : quarter].T
    mine[...] = total[quarter:].T
    if not kept:
        for copy in copies:
            copy.wait()


def cross(bit, kept, scales, held_rows, turned, counts):
    rows, columns = counts.shape
    width = turned.shape[1]
    here = pl.BlockSpec(memory_space=pltpu.VMEM)
    piece = jax.ShapeDtypeStruct((width, rows // 4), F32)
    small_piece = jax.ShapeDtypeStruct((width, rows // 8), F32)
    out_shape = (small_piece, small_piece, piece)
    in_specs, args = [here] * 3, [scales, held(held_rows), held(turned)]
    if not kept:
        out_shape += (pltpu.VMEM((rows // 2, columns), BF16),)
        in_specs.append(pl.BlockSpec(memory_space=pltpu.HBM))
        args.append(away(counts))
    return pl.pallas_call(
        functools.partial(cross_kernel, bit, kept, rows),
        out_shape=out_shape,
        in_specs=in_specs,
        out_specs=(here,) * len(out_shape),
        scratch_shapes=[pltpu.VMEM((rows // 2, width), F32), pltpu.SemaphoreType.DMA((8,))],
        compiler_params=params(),
        cost_estimate=cost(1, 1),
        name="cross_kept" if kept else "cross_sent",
    )(*args)


def plus_pieces_kernel(left, low, high, out):
    half = low.shape[1]
    out[:, :half] = left[:, :half] + low[...]
    out[:, half:] = left[:, half:] + high[...]


def call(kernel, name, out_shape, token, *args, scratch=(), aliases=None, out=None):
    here = pl.BlockSpec(memory_space=pltpu.VMEM)
    wherever = pl.BlockSpec(memory_space=pl.ANY)
    single = not isinstance(out_shape, tuple)
    specs = [here] * len(args)
    if aliases:
        specs[-1] = wherever
    out = out or here
    return pl.pallas_call(
        lambda token, *refs: kernel(*refs),
        out_shape=out_shape,
        in_specs=[wherever] + specs,
        out_specs=out if single else (out,) * len(out_shape),
        scratch_shapes=list(scratch),
        input_output_aliases=aliases or {},
        compiler_params=params(),
        cost_estimate=cost(1, 1),
        name=name,
    )(token, *args)


def fold_kernel(axis, bit, left, right, kept, sent):
    half = kept.shape[1]
    upper = (lax.axis_index(axis) & bit) != 0

    @pl.when(upper)
    def _():
        kept[...] = left[:, half:] + right[:, half:]
        sent[...] = left[:, :half] + right[:, :half]

    @pl.when(jnp.logical_not(upper))
    def _():
        kept[...] = left[:, :half] + right[:, :half]
        sent[...] = left[:, half:] + right[:, half:]


def half_sum_kernel(axis, left, right, out):
    half = out.shape[1]
    upper = lax.axis_index(axis) != 0

    @pl.when(upper)
    def _():
        out[...] = left[:, half:] + right[:, half:]

    @pl.when(jnp.logical_not(upper))
    def _():
        out[...] = left[:, :half] + right[:, :half]


def fold(axis, bit, token, left, right):
    shape = jax.ShapeDtypeStruct((left.shape[0], left.shape[1] // 2), F32)
    return call(
        functools.partial(fold_kernel, axis, bit), "fold", (shape, shape), token, left, right
    )


def side_kernel(axis, bit, dim, mine, theirs, out):
    size = mine.shape[dim]
    low = (slice(None),) * dim + (slice(0, size),)
    high = (slice(None),) * dim + (slice(size, 2 * size),)
    upper = (lax.axis_index(axis) & bit) != 0

    @pl.when(upper)
    def _():
        out[low], out[high] = theirs[...], mine[...]

    @pl.when(jnp.logical_not(upper))
    def _():
        out[low], out[high] = mine[...], theirs[...]


def side(axis, bit, dim, token, mine, theirs):
    shape = list(mine.shape)
    shape[dim] *= 2
    return call(
        functools.partial(side_kernel, axis, bit, dim),
        "side", jax.ShapeDtypeStruct(tuple(shape), mine.dtype), token, mine, theirs,
    )


def halves(value):
    high = value.astype(BF16)
    return high, (value - high.astype(F32)).astype(BF16)


def product3(left, right):
    left_high, left_low = left
    right_high, right_low = right
    dot = functools.partial(jnp.dot, preferred_element_type=F32)
    return dot(left_high, right_high) + (
        dot(left_high, right_low) + dot(left_low, right_high)
    )


def inverse_kernel(gram_in, inverse, rho_out):
    gram = gram_in[...]
    width = gram.shape[0]
    shape = (width, width)
    diagonal = lax.broadcasted_iota(jnp.int32, shape, 0) == lax.broadcasted_iota(
        jnp.int32, shape, 1
    )
    eye = jnp.where(diagonal, 1.0, 0.0).astype(F32)
    rho = jnp.sum(gram * eye) / width
    rho_out[...] = jnp.full(rho_out.shape, rho, F32)
    scale = 1.0 / jnp.full((1, 1), rho, F32)
    matrix = gram * scale + eye
    low = 2.0 / (width + 2.0)
    guess = low * eye
    image = low * matrix
    first = True
    while True:
        low = low * (2.0 - low)
        gain = 2.0 / (1.0 + low)
        low = gain * low
        done = 1.0 - low < 2e-3
        step = halves(gain * (2.0 * eye - image))
        if first:
            guess = guess[0:1, 0:1] * (gain * (2.0 * eye - image))
        else:
            guess = product3(halves(guess), step)
        first = False
        if done:
            break
        image = product3(halves(image), step)
    rest = eye - jnp.dot(
        matrix, guess, preferred_element_type=F32, precision=lax.Precision.HIGHEST
    )
    rest_halves = halves(rest)
    series = rest + product3(rest_halves, rest_halves)
    inverse[...] = (guess + product3(halves(guess), halves(series))) * scale


def shifted_inverse(gram):
    width = gram.shape[0]
    whole = pl.BlockSpec(memory_space=pltpu.VMEM)
    return pl.pallas_call(
        inverse_kernel,
        out_shape=(
            jax.ShapeDtypeStruct((width, width), F32),
            jax.ShapeDtypeStruct((8, 128), F32),
        ),
        in_specs=[whole],
        out_specs=(whole, whole),
        compiler_params=params(),
        cost_estimate=cost(1, 1),
        name="inverse",
    )(gram)


def admm_kernel(genes, rho_block, cross_a, cross_b, inverse, start, columns_out):
    rows = cross_a.shape[1]
    place = lax.axis_index("sub") * genes + lax.axis_index("gene")
    rho = rho_block[0:1, 0:1]
    cross = cross_a[...] + cross_b[...]
    inverse_halves = halves(inverse[...])
    zvalue = start[pl.ds(pl.multiple_of(place * rows, rows), rows), :].astype(F32).T
    uvalue = jnp.zeros_like(zvalue)
    for _ in range(ITERS):
        vvalue = product3(inverse_halves, halves(cross + rho * (zvalue - uvalue)))
        zvalue = jnp.maximum(vvalue + uvalue, 0.0)
        uvalue = uvalue + vvalue - zvalue
    columns_out[...] = zvalue.astype(BF16)


def products_kernel(tile, bit, line, start, chunk, scales, sent, kept, columns, *outs):
    only_first = len(outs) == 1
    block = line.block(1 if only_first else 2, 0)
    size = kept.shape[1] // line.size
    span = min(tile, chunk)
    wide = 2 * span if chunk % (2 * span) == 0 else span
    steps = chunk // wide
    rows = columns.shape[1]
    quarter = rows // 4
    groups = [(sent, False), (kept, True)]

    @pl.loop(0, steps if only_first else line.size * steps)
    def _(turn):
        order, step = (block, turn) if only_first else (turn // steps, lax.rem(turn, steps))
        genes = pl.ds(pl.multiple_of(order * size + start + step * wide, span), wide)
        total = None
        for counts, stays in groups:
            cells = [columns[:, pl.ds(at, quarter)] for at in pieces_of(rows, bit, stays)]
            part = jnp.dot(
                jnp.concatenate(cells, axis=1),
                scaled(counts, genes, tiles_of(bit, stays, rows, tile), scales),
                preferred_element_type=F32,
            )
            total = part if total is None else total + part
        total = total.astype(BF16)
        at = pl.ds(pl.multiple_of(step * wide, span), wide)
        if only_first:
            outs[0][:, at] = total
        else:
            outs[0][order, :, at] = total

            @pl.when(order == block)
            def _():
                outs[1][:, at] = total


def products(only_first, bit, line, start, chunk, token, scales, sent, kept, columns):
    width, rows = columns.shape
    tile = rows // (scales.shape[0] // 8)
    out_shape = (jax.ShapeDtypeStruct((width, chunk), BF16),)
    if not only_first:
        out_shape = (jax.ShapeDtypeStruct((line.size, width, chunk), BF16),) + out_shape
    return call(
        functools.partial(products_kernel, tile, bit, line, start, chunk),
        "products", out_shape, token, scales, held(sent), held(kept), columns,
    )


def turn_kernel(value, out):
    out[...] = value[...].astype(F32).T.astype(out.dtype)


def turn(token, value):
    shape = jax.ShapeDtypeStruct(value.shape[::-1], value.dtype)
    return call(turn_kernel, "turn", shape, token, value)


def row_share_kernel(columns, out):
    part = out.shape[0]
    place = lax.axis_index("gene")
    share = columns[pl.ds(pl.multiple_of(place * part, part), part), :]
    out[...] = contract_last(share, columns[...]).astype(out.dtype)


def row_share(part, token, columns):
    shape = jax.ShapeDtypeStruct((part, columns.shape[0]), BF16)
    return call(row_share_kernel, "row_share", shape, token, columns)


def plus_kernel(left, right, out):
    out[...] = (left[...].astype(F32) + right[...].astype(F32)).astype(out.dtype)


def hop_kernel(kind, targets, own, arrived, out):
    cell = lax.axis_index("cell")
    reached = cell == targets[0]
    for target in targets[1:]:
        reached = jnp.logical_or(reached, cell == target)
    more = arrived[...].astype(F32)
    base = own[...].astype(F32)
    value = base + more if kind == "sum" else more
    out[...] = jnp.where(reached, value, base).astype(out.dtype)


def hop(kind, targets, token, own, arrived):
    shape = jax.ShapeDtypeStruct(own.shape, own.dtype)
    return call(functools.partial(hop_kernel, kind, targets), "hop", shape, token, own, arrived)


def operand_kernel(line, phase, parity, total, before, *outs):
    own = total.at[line.block(phase, parity)]
    start = 0
    for out in outs:
        at = slice(start, start + out.shape[1])
        out[...] = (own[:, at].astype(F32) + before[:, at].astype(F32)).astype(BF16)
        start += out.shape[1]


def operand(line, phase, parity, parts, token, total, before):
    width = before.shape[0]
    return call(
        functools.partial(operand_kernel, line, phase, parity),
        "operand", tuple(jax.ShapeDtypeStruct((width, part), BF16) for part in parts),
        token, total, before,
    )


def keep_kernel(start, skip, total, first, second, *refs):
    out, turned, sems = refs[-3:]
    pieces = sems.shape[0]
    wide = first.shape[1] // pieces
    own = total.at[lax.axis_index("cell")]
    copies = []
    for piece in range(pieces):
        at = slice(piece * wide, (piece + 1) * wide)
        there = slice(skip + piece * wide, skip + (piece + 1) * wide)
        value = first[:, at].astype(F32) + second[:, there].astype(F32)
        turned[at] = (own[:, there].astype(F32) + value).T
        copies.append(
            pltpu.make_async_copy(
                turned.at[at], out.at[pl.ds(start + skip + piece * wide, wide)], sems.at[piece]
            )
        )
        copies[-1].start()
    for copy in copies:
        copy.wait()


def keep(block, start, skip, token, total, first, second, out):
    width, chunk = first.shape
    pieces = max(1, chunk // 256)
    return call(
        functools.partial(keep_kernel, start, skip),
        "keep", jax.ShapeDtypeStruct((block, width), F32), token,
        total, first, second, *([] if out is None else [out]),
        scratch=[pltpu.VMEM((chunk, width), F32), pltpu.SemaphoreType.DMA((pieces,))],
        aliases=None if out is None else {4: 0},
        out=pl.BlockSpec(memory_space=pl.ANY),
    )


class Line:
    def __init__(self, size):
        self.size = size

    def pairs(self, phase, parity, exchange=False):
        links = range(parity, self.size - 1, 2)
        right = [(i, i + 1) for i in links if i < phase]
        left = [(i + 1, i) for i in links if i + 1 >= self.size - phase]
        pairs = right + left
        if exchange:
            pairs = sorted(set(pairs) | {(b, a) for a, b in pairs})
        return pairs

    def block(self, phase, parity):
        cell = lax.axis_index("cell")
        to_right = (cell & 1) == parity
        block = cell + jnp.where(to_right, self.size - phase, phase)
        return jnp.where(block >= self.size, block - self.size, block)

    def send(self, value, phase, parity):
        return lax.ppermute(value, "cell", self.pairs(phase, parity))


def swap(value, axis, size, step):
    return lax.ppermute(value, axis, [(i, i ^ step) for i in range(size)])


def pair_sums(value, axis, size, event):
    step = 1
    while step < size:
        arrived, event = after(swap(value, axis, size, step), event)
        value = value + arrived
        step *= 2
    return value, event


def after(value, event):
    return lax.optimization_barrier((value, event))


def chunk_sizes(block):
    return [block // 2, block // 2] if block % 1024 == 0 else [block]


def shards(sizes, counts, tile_mask, tile_counts, gene_factor, prev_factor):
    cells, genes, subs = sizes
    rows, columns = counts.shape
    width = gene_factor.shape[0]
    line = Line(cells)

    half_bit = bit = genes // 2
    gram, scales, turned, sent_rows = load(bit, gene_factor, counts, tile_mask, tile_counts)
    token = scales
    piece = jax.ShapeDtypeStruct((width, rows // 4), F32)
    gram_other = swap(gram, "sub", subs, 1)
    low, high, mine, kept_rows = cross(bit, False, scales, sent_rows, turned, counts)
    low, high = [swap(value, "sub", subs, 1) for value in (low, high)]
    token_sent, mine = after(token, mine)
    half = jax.ShapeDtypeStruct((width, width // 2), F32)
    gram_half = call(
        functools.partial(half_sum_kernel, "sub"), "half_sum", half, token_sent, gram, gram_other
    )
    token_sent, gram_half = after(token, gram_half)
    sent = call(plus_pieces_kernel, "plus", piece, token_sent, mine, low, high)
    cross_b = swap(sent, "gene", genes, bit)
    scales_late, _ = after(scales, sent)
    low, high, mine = cross(bit, True, scales_late, kept_rows, turned, counts)
    low, high = [swap(value, "sub", subs, 1) for value in (low, high)]
    gram_half, (mine, _) = pair_sums(gram_half, "gene", genes, (mine, scales))
    gram = side("sub", 1, 1, token, gram_half, swap(gram_half, "sub", subs, 1))
    inverse, rho = shifted_inverse(gram)
    token_late, inverse = after(token, inverse)
    cross_a = call(plus_pieces_kernel, "plus", piece, token_late, mine, low, high)
    bit //= 2
    while bit:
        cross_a, sent = fold("gene", bit, token, cross_a, cross_b)
        cross_b = swap(sent, "gene", genes, bit)
        bit //= 2
    share = jax.ShapeDtypeStruct((width, rows // (genes * subs)), BF16)
    columns_held = call(
        functools.partial(admm_kernel, genes),
        "admm", share, token, rho, cross_a, cross_b, inverse, prev_factor,
    )
    bit = 1
    while bit < genes:
        columns_arrived = swap(columns_held, "gene", genes, bit)
        columns_held = side("gene", bit, 1, token, columns_held, columns_arrived)
        bit *= 2
    token, rows_sum = after(token, row_share(width // genes, token, columns_held))
    columns_arrived = swap(columns_held, "sub", subs, 1)
    whole = side("sub", 1, 1, token, columns_held, columns_arrived)

    block = columns // cells
    chunks = chunk_sizes(block)
    starts = [sum(chunks[:i]) for i in range(len(chunks))]
    every = range(len(chunks))

    arrived = {}
    last_part = []

    def send(value, phase, parity, index):
        pairs = line.pairs(phase, parity, exchange=phase == 1 and index == 0)
        arrived[phase, parity, index] = lax.ppermute(value, "cell", pairs) if pairs else None

    def resend(token, phase, parity, index):
        before = arrived[phase - 1, 1 - parity, index]
        if before is None:
            value = seconds[index]
        else:
            chunk = chunks[index]
            parts = (chunk,)
            if phase == cells - 1 and parity == 0 and index == every[-1] and chunk >= 1024:
                parts = (chunk // 4 * 3, chunk // 4)
            values = operand(line, phase, parity, parts, token, totals[index], before)
            token, values = after(token, values)
            value, rest = values[0], values[1:]
            for part in rest:
                last_part.append(lax.ppermute(part, "cell", line.pairs(phase, parity)))
        send(value, phase, parity, index)
        return token

    middle = cells // 2
    inward = [[(i, i + 1), (cells - 1 - i, cells - 2 - i)] for i in range(middle - 1)]
    outward = [[(b, a) for a, b in pairs] for pairs in reversed(inward)]
    hops = [("sum", p) for p in inward] + [("sum", [(middle - 1, middle), (middle, middle - 1)])]
    hops += [("copy", p) for p in outward]

    def hop_rows(token, rows_sum):
        kind, pairs = hops.pop(0)
        both = sorted(set(pairs) | {(b, a) for a, b in pairs})
        rows_arrived = lax.ppermute(rows_sum, "cell", both)
        targets = [b for _, b in pairs]
        return after(token, hop(kind, targets, token, rows_sum, rows_arrived))

    def side_rows(token, rows_sum, axis, size, bit):
        rows_arrived = swap(rows_sum, axis, size, bit)
        return after(token, side(axis, bit, 0, token, rows_sum, rows_arrived))

    for index in every:
        (first,) = products(
            True, half_bit, line, starts[index], chunks[index], token, scales, sent_rows, kept_rows, whole
        )
        token, first = after(token, first)
        for parity in (0, 1):
            send(first, 1, parity, index)
        if index == 0 and hops:
            token, rows_sum = hop_rows(token, rows_sum)
    totals, seconds = [], []
    for index in every:
        total, second = products(
            False, half_bit, line, starts[index], chunks[index], token, scales, sent_rows, kept_rows, whole
        )
        token, second = after(token, second)
        if hops:
            token, rows_sum = hop_rows(token, rows_sum)
        totals.append(total)
        seconds.append(second)
        for parity in (0, 1):
            token = resend(token, 2, parity, index)
    while hops:
        token, rows_sum = hop_rows(token, rows_sum)
    new_factor = turn(token, whole)
    token, new_factor = after(token, new_factor)
    rows_arrived = swap(rows_sum, "sub", subs, 1)
    shape = jax.ShapeDtypeStruct(rows_sum.shape, F32)
    token, rows_sum = after(token, call(plus_kernel, "plus", shape, token, rows_sum, rows_arrived))
    bits = [1 << i for i in range((genes - 1).bit_length())]
    for phase in range(3, cells):
        for index in every:
            for parity in (0, 1):
                token = resend(token, phase, parity, index)
                if bits:
                    token, rows_sum = side_rows(token, rows_sum, "gene", genes, bits.pop(0))
    data_products = None
    last = cells - 1
    for index in every:
        parts = [arrived[last, 0, index]] + (last_part if index == every[-1] else [])
        skip = 0
        for part in parts:
            data_products = keep(
                block, starts[index], skip, token, totals[index],
                part, arrived[last, 1, index], data_products,
            )
            token, data_products = after(token, data_products)
            skip += part.shape[1]
    return (new_factor, rows_sum, data_products)


def solution(mesh):
    sizes = (mesh.shape["cell"], mesh.shape["gene"], mesh.shape["sub"])
    return jax.shard_map(
        functools.partial(shards, sizes),
        mesh=mesh,
        in_specs=(
            P(("groups", "cell"), ("gene", "sub")),
            P(("groups", "cell"), ("gene", "sub")),
            P(("groups", "cell"), ("gene", "sub")),
            P("groups", ("gene", "sub")),
            P(("groups", "cell"), None),
        ),
        out_specs=(
            P(("groups", "cell"), None),
            P("groups", None),
            P(("groups", "gene", "sub", "cell"), None),
        ),
        check_vma=False,
    )
```

```python
import functools

import jax
import jax.numpy as jnp
import numpy as np
from jax import lax
from jax.experimental import pallas as pl
from jax.experimental.pallas import tpu as pltpu
from jax.sharding import PartitionSpec as P

ITERS = 3
F32 = jnp.float32
BF16 = jnp.bfloat16
MIB = 1024 * 1024


def params(limit=16):
    return pltpu.CompilerParams(vmem_limit_bytes=limit * MIB)


def away(value):
    return pltpu.with_memory_space_constraint(value, pltpu.HBM)


def held(value):
    return pltpu.with_memory_space_constraint(value, pltpu.VMEM)


def cost(flops, bytes_accessed):
    return pl.CostEstimate(flops=flops, bytes_accessed=bytes_accessed, transcendentals=0)


def contract_last(left, right):
    return lax.dot_general(
        left, right, (((1,), (1,)), ((), ())), preferred_element_type=F32
    )


def row_copies(source, target, first, sems):
    rows = target.shape[0]
    piece = max(rows // sems.shape[0], 16)
    return [
        pltpu.make_async_copy(
            source.at[pl.ds(first + i * piece, piece)],
            target.at[pl.ds(i * piece, piece)],
            sems.at[i],
        )
        for i in range(rows // piece)
    ]


def pieces_of(rows, bit, kept):
    core = lax.axis_index("sub")
    upper = ((lax.axis_index("gene") & bit) != 0) == kept
    half, quarter = rows // 2, rows // 4
    place = jnp.where(upper, quarter, 0)
    return [
        pl.multiple_of((1 - core) * half + place, quarter),
        pl.multiple_of(core * half + place, quarter),
    ]


def piece_copies(bit, kept, counts, target, sems):
    quarter = counts.shape[0] // 4
    copies = []
    for i, place in enumerate(pieces_of(counts.shape[0], bit, kept)):
        copies += row_copies(
            counts, target.at[i * quarter : (i + 1) * quarter], place, sems.at[i * 4 : i * 4 + 4]
        )
    return copies


def load_kernel(
    bit, genes, counts, tile_mask, tile_counts, gram, scales, turned, first,
    genes_here, mask_here, counts_here, gene_sems, row_sems, small_sems,
):
    small_copies = [
        pltpu.make_async_copy(tile_mask, mask_here, small_sems.at[0]),
        pltpu.make_async_copy(tile_counts, counts_here, small_sems.at[1]),
    ]
    gene_copies = row_copies(genes, genes_here, 0, gene_sems)
    row_starts = piece_copies(bit, False, counts, first, row_sems)
    for copy in gene_copies + small_copies:
        copy.start()
    for copy in small_copies:
        copy.wait()
    ratio = mask_here[...].astype(F32) / counts_here[...].astype(F32)
    columns = genes.shape[1]
    tile = columns // ratio.shape[1]
    for row in range(ratio.shape[0]):
        for col in range(ratio.shape[1]):
            scales[row * 8 : row * 8 + 8, col * tile : (col + 1) * tile] = jnp.broadcast_to(
                ratio[row : row + 1, col : col + 1], (8, tile)
            )
    for copy in gene_copies:
        copy.wait()
    for copy in row_starts:
        copy.start()
    wide = min(1024, columns)
    gram[...] = jnp.zeros_like(gram)

    @pl.loop(0, columns // wide)
    def _(step):
        at = pl.ds(pl.multiple_of(step * wide, wide), wide)
        piece = genes_here[:, at]
        turned[at, :] = piece.T
        gram[...] += jnp.dot(piece, turned[at, :], preferred_element_type=F32)

    for copy in row_starts:
        copy.wait()


def load(bit, genes, counts, tile_mask, tile_counts):
    width, columns = genes.shape
    rows = counts.shape[0]
    here = pl.BlockSpec(memory_space=pltpu.VMEM)
    there = pl.BlockSpec(memory_space=pltpu.HBM)
    return pl.pallas_call(
        functools.partial(load_kernel, bit),
        out_shape=(
            jax.ShapeDtypeStruct((width, width), F32),
            jax.ShapeDtypeStruct((tile_mask.shape[0] * 8, columns), F32),
            pltpu.VMEM((columns, width), BF16),
            pltpu.VMEM((rows // 2, columns), BF16),
        ),
        in_specs=[there] * 4,
        out_specs=(here,) * 4,
        scratch_shapes=[
            pltpu.VMEM((width, columns), BF16),
            pltpu.VMEM(tile_mask.shape, jnp.int32),
            pltpu.VMEM(tile_mask.shape, jnp.int32),
            pltpu.SemaphoreType.DMA((4,)),
            pltpu.SemaphoreType.DMA((8,)),
            pltpu.SemaphoreType.DMA((2,)),
        ],
        compiler_params=params(),
        cost_estimate=cost(1, 1),
        name="load",
    )(away(genes), away(counts), away(tile_mask), away(tile_counts))


def scaled(counts, at, row_tiles, scales):
    tile = counts.shape[0] // len(row_tiles)
    return jnp.concatenate(
        [
            (
                counts[i * tile : (i + 1) * tile, at].astype(F32)
                * scales[pl.ds(pl.multiple_of(row * 8, 8), 8), at][0:1]
            ).astype(BF16)
            for i, row in enumerate(row_tiles)
        ],
        axis=0,
    )


def cross_rows(row_tiles, scales, counts, turned, total):
    columns = counts.shape[1]
    wide = min(2048, columns)
    total[...] = jnp.zeros_like(total)

    @pl.loop(0, columns // wide)
    def _(step):
        at = pl.ds(pl.multiple_of(step * wide, wide), wide)
        total[...] += jnp.dot(
            scaled(counts, at, row_tiles, scales), turned[at, :], preferred_element_type=F32
        )


def tiles_of(bit, kept, rows, tile):
    quarter = rows // 4
    return [
        place // tile + i
        for place in pieces_of(rows, bit, kept)
        for i in range(quarter // tile)
    ]


def cross_kernel(bit, kept, rows, scales, held_rows, turned, *refs):
    (low, high, mine), total = refs[-5:-2] if kept else refs[1:4], refs[-2]
    if not kept:
        copies = piece_copies(bit, True, refs[0], refs[4], refs[-1])
        for copy in copies:
            copy.start()
    quarter, tile = rows // 4, rows // (scales.shape[0] // 8)
    cross_rows(tiles_of(bit, kept, rows, tile), scales, held_rows, turned, total)
    low[...] = total[: quarter // 2].T
    high[...] = total[quarter // 2 : quarter].T
    mine[...] = total[quarter:].T
    if not kept:
        for copy in copies:
            copy.wait()


def cross(bit, kept, scales, held_rows, turned, counts):
    rows, columns = counts.shape
    width = turned.shape[1]
    here = pl.BlockSpec(memory_space=pltpu.VMEM)
    piece = jax.ShapeDtypeStruct((width, rows // 4), F32)
    small_piece = jax.ShapeDtypeStruct((width, rows // 8), F32)
    out_shape = (small_piece, small_piece, piece)
    in_specs, args = [here] * 3, [scales, held(held_rows), held(turned)]
    if not kept:
        out_shape += (pltpu.VMEM((rows // 2, columns), BF16),)
        in_specs.append(pl.BlockSpec(memory_space=pltpu.HBM))
        args.append(away(counts))
    return pl.pallas_call(
        functools.partial(cross_kernel, bit, kept, rows),
        out_shape=out_shape,
        in_specs=in_specs,
        out_specs=(here,) * len(out_shape),
        scratch_shapes=[pltpu.VMEM((rows // 2, width), F32), pltpu.SemaphoreType.DMA((8,))],
        compiler_params=params(),
        cost_estimate=cost(1, 1),
        name="cross_kept" if kept else "cross_sent",
    )(*args)


def plus_pieces_kernel(left, low, high, out):
    half = low.shape[1]
    out[:, :half] = left[:, :half] + low[...]
    out[:, half:] = left[:, half:] + high[...]


def call(kernel, name, out_shape, token, *args, scratch=(), aliases=None, out=None):
    here = pl.BlockSpec(memory_space=pltpu.VMEM)
    wherever = pl.BlockSpec(memory_space=pl.ANY)
    single = not isinstance(out_shape, tuple)
    specs = [here] * len(args)
    if aliases:
        specs[-1] = wherever
    out = out or here
    return pl.pallas_call(
        lambda token, *refs: kernel(*refs),
        out_shape=out_shape,
        in_specs=[wherever] + specs,
        out_specs=out if single else (out,) * len(out_shape),
        scratch_shapes=list(scratch),
        input_output_aliases=aliases or {},
        compiler_params=params(),
        cost_estimate=cost(1, 1),
        name=name,
    )(token, *args)


def fold_kernel(axis, bit, left, right, kept, sent):
    half = kept.shape[1]
    upper = (lax.axis_index(axis) & bit) != 0

    @pl.when(upper)
    def _():
        kept[...] = left[:, half:] + right[:, half:]
        sent[...] = left[:, :half] + right[:, :half]

    @pl.when(jnp.logical_not(upper))
    def _():
        kept[...] = left[:, :half] + right[:, :half]
        sent[...] = left[:, half:] + right[:, half:]


def half_sum_kernel(axis, left, right, out):
    half = out.shape[1]
    upper = lax.axis_index(axis) != 0

    @pl.when(upper)
    def _():
        out[...] = left[:, half:] + right[:, half:]

    @pl.when(jnp.logical_not(upper))
    def _():
        out[...] = left[:, :half] + right[:, :half]


def fold(axis, bit, token, left, right):
    shape = jax.ShapeDtypeStruct((left.shape[0], left.shape[1] // 2), F32)
    return call(
        functools.partial(fold_kernel, axis, bit), "fold", (shape, shape), token, left, right
    )


def side_kernel(axis, bit, dim, mine, theirs, out):
    size = mine.shape[dim]
    low = (slice(None),) * dim + (slice(0, size),)
    high = (slice(None),) * dim + (slice(size, 2 * size),)
    upper = (lax.axis_index(axis) & bit) != 0

    @pl.when(upper)
    def _():
        out[low], out[high] = theirs[...], mine[...]

    @pl.when(jnp.logical_not(upper))
    def _():
        out[low], out[high] = mine[...], theirs[...]


def side(axis, bit, dim, token, mine, theirs):
    shape = list(mine.shape)
    shape[dim] *= 2
    return call(
        functools.partial(side_kernel, axis, bit, dim),
        "side", jax.ShapeDtypeStruct(tuple(shape), mine.dtype), token, mine, theirs,
    )


def halves(value):
    high = value.astype(BF16)
    return high, (value - high.astype(F32)).astype(BF16)


def product3(left, right):
    left_high, left_low = left
    right_high, right_low = right
    dot = functools.partial(jnp.dot, preferred_element_type=F32)
    return dot(left_high, right_high) + (
        dot(left_high, right_low) + dot(left_low, right_high)
    )


def inverse_kernel(gram_in, inverse, rho_out):
    gram = gram_in[...]
    width = gram.shape[0]
    shape = (width, width)
    diagonal = lax.broadcasted_iota(jnp.int32, shape, 0) == lax.broadcasted_iota(
        jnp.int32, shape, 1
    )
    eye = jnp.where(diagonal, 1.0, 0.0).astype(F32)
    rho = jnp.sum(gram * eye) / width
    rho_out[...] = jnp.full(rho_out.shape, rho, F32)
    scale = 1.0 / jnp.full((1, 1), rho, F32)
    matrix = gram * scale + eye
    low = 2.0 / (width + 2.0)
    guess = low * eye
    image = low * matrix
    first = True
    while True:
        low = low * (2.0 - low)
        gain = 2.0 / (1.0 + low)
        low = gain * low
        done = 1.0 - low < 2e-3
        step = halves(gain * (2.0 * eye - image))
        if first:
            guess = guess[0:1, 0:1] * (gain * (2.0 * eye - image))
        else:
            guess = product3(halves(guess), step)
        first = False
        if done:
            break
        image = product3(halves(image), step)
    rest = eye - jnp.dot(
        matrix, guess, preferred_element_type=F32, precision=lax.Precision.HIGHEST
    )
    rest_halves = halves(rest)
    series = rest + product3(rest_halves, rest_halves)
    inverse[...] = (guess + product3(halves(guess), halves(series))) * scale


def shifted_inverse(gram):
    width = gram.shape[0]
    whole = pl.BlockSpec(memory_space=pltpu.VMEM)
    return pl.pallas_call(
        inverse_kernel,
        out_shape=(
            jax.ShapeDtypeStruct((width, width), F32),
            jax.ShapeDtypeStruct((8, 128), F32),
        ),
        in_specs=[whole],
        out_specs=(whole, whole),
        compiler_params=params(),
        cost_estimate=cost(1, 1),
        name="inverse",
    )(gram)


def admm_kernel(genes, rho_block, cross_a, cross_b, inverse, start, columns_out):
    rows = cross_a.shape[1]
    place = lax.axis_index("sub") * genes + lax.axis_index("gene")
    rho = rho_block[0:1, 0:1]
    cross = cross_a[...] + cross_b[...]
    inverse_halves = halves(inverse[...])
    zvalue = start[pl.ds(pl.multiple_of(place * rows, rows), rows), :].astype(F32).T
    uvalue = jnp.zeros_like(zvalue)
    for _ in range(ITERS):
        vvalue = product3(inverse_halves, halves(cross + rho * (zvalue - uvalue)))
        zvalue = jnp.maximum(vvalue + uvalue, 0.0)
        uvalue = uvalue + vvalue - zvalue
    columns_out[...] = zvalue.astype(BF16)


def products_kernel(tile, bit, line, start, chunk, scales, sent, kept, columns, *outs):
    only_first = len(outs) == 1
    block = line.block(1 if only_first else 2, 0)
    size = kept.shape[1] // line.size
    span = min(tile, chunk)
    wide = 2 * span if chunk % (2 * span) == 0 else span
    steps = chunk // wide
    rows = columns.shape[1]
    quarter = rows // 4
    groups = [(sent, False), (kept, True)]

    @pl.loop(0, steps if only_first else line.size * steps)
    def _(turn):
        order, step = (block, turn) if only_first else (turn // steps, lax.rem(turn, steps))
        genes = pl.ds(pl.multiple_of(order * size + start + step * wide, span), wide)
        total = None
        for counts, stays in groups:
            cells = [columns[:, pl.ds(at, quarter)] for at in pieces_of(rows, bit, stays)]
            part = jnp.dot(
                jnp.concatenate(cells, axis=1),
                scaled(counts, genes, tiles_of(bit, stays, rows, tile), scales),
                preferred_element_type=F32,
            )
            total = part if total is None else total + part
        total = total.astype(BF16)
        at = pl.ds(pl.multiple_of(step * wide, span), wide)
        if only_first:
            outs[0][:, at] = total
        else:
            outs[0][order, :, at] = total

            @pl.when(order == block)
            def _():
                outs[1][:, at] = total


def products(only_first, bit, line, start, chunk, token, scales, sent, kept, columns):
    width, rows = columns.shape
    tile = rows // (scales.shape[0] // 8)
    out_shape = (jax.ShapeDtypeStruct((width, chunk), BF16),)
    if not only_first:
        out_shape = (jax.ShapeDtypeStruct((line.size, width, chunk), BF16),) + out_shape
    return call(
        functools.partial(products_kernel, tile, bit, line, start, chunk),
        "products", out_shape, token, scales, held(sent), held(kept), columns,
    )


def turn_kernel(value, out):
    out[...] = value[...].astype(F32).T.astype(out.dtype)


def turn(token, value):
    shape = jax.ShapeDtypeStruct(value.shape[::-1], value.dtype)
    return call(turn_kernel, "turn", shape, token, value)


def row_share_kernel(columns, out):
    part = out.shape[0]
    place = lax.axis_index("gene")
    share = columns[pl.ds(pl.multiple_of(place * part, part), part), :]
    out[...] = contract_last(share, columns[...]).astype(out.dtype)


def row_share(part, token, columns):
    shape = jax.ShapeDtypeStruct((part, columns.shape[0]), BF16)
    return call(row_share_kernel, "row_share", shape, token, columns)


def plus_kernel(left, right, out):
    out[...] = (left[...].astype(F32) + right[...].astype(F32)).astype(out.dtype)


def hop_kernel(kind, targets, own, arrived, out):
    cell = lax.axis_index("cell")
    reached = cell == targets[0]
    for target in targets[1:]:
        reached = jnp.logical_or(reached, cell == target)
    more = arrived[...].astype(F32)
    base = own[...].astype(F32)
    value = base + more if kind == "sum" else more
    out[...] = jnp.where(reached, value, base).astype(out.dtype)


def hop(kind, targets, token, own, arrived):
    shape = jax.ShapeDtypeStruct(own.shape, own.dtype)
    return call(functools.partial(hop_kernel, kind, targets), "hop", shape, token, own, arrived)


def operand_kernel(line, phase, parity, total, before, *outs):
    own = total.at[line.block(phase, parity)]
    start = 0
    for out in outs:
        at = slice(start, start + out.shape[1])
        out[...] = (own[:, at].astype(F32) + before[:, at].astype(F32)).astype(BF16)
        start += out.shape[1]


def operand(line, phase, parity, parts, token, total, before):
    width = before.shape[0]
    return call(
        functools.partial(operand_kernel, line, phase, parity),
        "operand", tuple(jax.ShapeDtypeStruct((width, part), BF16) for part in parts),
        token, total, before,
    )


def keep_kernel(start, skip, total, first, second, *refs):
    out, turned, sems = refs[-3:]
    pieces = sems.shape[0]
    wide = first.shape[1] // pieces
    own = total.at[lax.axis_index("cell")]
    copies = []
    for piece in range(pieces):
        at = slice(piece * wide, (piece + 1) * wide)
        there = slice(skip + piece * wide, skip + (piece + 1) * wide)
        value = first[:, at].astype(F32) + second[:, there].astype(F32)
        turned[at] = (own[:, there].astype(F32) + value).T
        copies.append(
            pltpu.make_async_copy(
                turned.at[at], out.at[pl.ds(start + skip + piece * wide, wide)], sems.at[piece]
            )
        )
        copies[-1].start()
    for copy in copies:
        copy.wait()


def keep(block, start, skip, token, total, first, second, out):
    width, chunk = first.shape
    pieces = max(1, chunk // 256)
    return call(
        functools.partial(keep_kernel, start, skip),
        "keep", jax.ShapeDtypeStruct((block, width), F32), token,
        total, first, second, *([] if out is None else [out]),
        scratch=[pltpu.VMEM((chunk, width), F32), pltpu.SemaphoreType.DMA((pieces,))],
        aliases=None if out is None else {4: 0},
        out=pl.BlockSpec(memory_space=pl.ANY),
    )


class Line:
    def __init__(self, size):
        self.size = size

    def pairs(self, phase, parity, exchange=False):
        links = range(parity, self.size - 1, 2)
        right = [(i, i + 1) for i in links if i < phase]
        left = [(i + 1, i) for i in links if i + 1 >= self.size - phase]
        pairs = right + left
        if exchange:
            pairs = sorted(set(pairs) | {(b, a) for a, b in pairs})
        return pairs

    def block(self, phase, parity):
        cell = lax.axis_index("cell")
        to_right = (cell & 1) == parity
        block = cell + jnp.where(to_right, self.size - phase, phase)
        return jnp.where(block >= self.size, block - self.size, block)

    def send(self, value, phase, parity):
        return lax.ppermute(value, "cell", self.pairs(phase, parity))


def swap(value, axis, size, step):
    return lax.ppermute(value, axis, [(i, i ^ step) for i in range(size)])


def pair_sums(value, axis, size, event):
    step = 1
    while step < size:
        arrived, event = after(swap(value, axis, size, step), event)
        value = value + arrived
        step *= 2
    return value, event


def after(value, event):
    return lax.optimization_barrier((value, event))


def chunk_sizes(block):
    return [block // 2, block // 2] if block % 1024 == 0 else [block]


def shards(sizes, counts, tile_mask, tile_counts, gene_factor, prev_factor):
    cells, genes, subs = sizes
    rows, columns = counts.shape
    width = gene_factor.shape[0]
    line = Line(cells)

    half_bit = bit = genes // 2
    gram, scales, turned, sent_rows = load(bit, gene_factor, counts, tile_mask, tile_counts)
    token = scales
    piece = jax.ShapeDtypeStruct((width, rows // 4), F32)
    gram_other = swap(gram, "sub", subs, 1)
    low, high, mine, kept_rows = cross(bit, False, scales, sent_rows, turned, counts)
    low, high = [swap(value, "sub", subs, 1) for value in (low, high)]
    token_sent, mine = after(token, mine)
    half = jax.ShapeDtypeStruct((width, width // 2), F32)
    gram_half = call(
        functools.partial(half_sum_kernel, "sub"), "half_sum", half, token_sent, gram, gram_other
    )
    token_sent, gram_half = after(token, gram_half)
    sent = call(plus_pieces_kernel, "plus", piece, token_sent, mine, low, high)
    cross_b = swap(sent, "gene", genes, bit)
    scales_late, _ = after(scales, sent)
    low, high, mine = cross(bit, True, scales_late, kept_rows, turned, counts)
    low, high = [swap(value, "sub", subs, 1) for value in (low, high)]
    gram_half, (mine, _) = pair_sums(gram_half, "gene", genes, (mine, scales))
    gram = side("sub", 1, 1, token, gram_half, swap(gram_half, "sub", subs, 1))
    inverse, rho = shifted_inverse(gram)
    token_late, inverse = after(token, inverse)
    cross_a = call(plus_pieces_kernel, "plus", piece, token_late, mine, low, high)
    bit //= 2
    while bit:
        cross_a, sent = fold("gene", bit, token, cross_a, cross_b)
        cross_b = swap(sent, "gene", genes, bit)
        bit //= 2
    share = jax.ShapeDtypeStruct((width, rows // (genes * subs)), BF16)
    columns_held = call(
        functools.partial(admm_kernel, genes),
        "admm", share, token, rho, cross_a, cross_b, inverse, prev_factor,
    )
    bit = 1
    while bit < genes:
        columns_arrived = swap(columns_held, "gene", genes, bit)
        columns_held = side("gene", bit, 1, token, columns_held, columns_arrived)
        bit *= 2
    token, rows_sum = after(token, row_share(width // genes, token, columns_held))
    columns_arrived = swap(columns_held, "sub", subs, 1)
    whole = side("sub", 1, 1, token, columns_held, columns_arrived)

    block = columns // cells
    chunks = chunk_sizes(block)
    starts = [sum(chunks[:i]) for i in range(len(chunks))]
    every = range(len(chunks))

    arrived = {}
    last_part = []

    def send(value, phase, parity, index):
        pairs = line.pairs(phase, parity, exchange=phase == 1 and index == 0)
        arrived[phase, parity, index] = lax.ppermute(value, "cell", pairs) if pairs else None

    def resend(token, phase, parity, index):
        before = arrived[phase - 1, 1 - parity, index]
        if before is None:
            value = seconds[index]
        else:
            chunk = chunks[index]
            parts = (chunk,)
            if phase == cells - 1 and parity == 0 and index == every[-1] and chunk >= 1024:
                parts = (chunk // 4 * 3, chunk // 4)
            values = operand(line, phase, parity, parts, token, totals[index], before)
            token, values = after(token, values)
            value, rest = values[0], values[1:]
            for part in rest:
                last_part.append(lax.ppermute(part, "cell", line.pairs(phase, parity)))
        send(value, phase, parity, index)
        return token

    middle = cells // 2
    inward = [[(i, i + 1), (cells - 1 - i, cells - 2 - i)] for i in range(middle - 1)]
    outward = [[(b, a) for a, b in pairs] for pairs in reversed(inward)]
    hops = [("sum", p) for p in inward] + [("sum", [(middle - 1, middle), (middle, middle - 1)])]
    hops += [("copy", p) for p in outward]

    def hop_rows(token, rows_sum):
        kind, pairs = hops.pop(0)
        both = sorted(set(pairs) | {(b, a) for a, b in pairs})
        rows_arrived = lax.ppermute(rows_sum, "cell", both)
        targets = [b for _, b in pairs]
        return after(token, hop(kind, targets, token, rows_sum, rows_arrived))

    def side_rows(token, rows_sum, axis, size, bit):
        rows_arrived = swap(rows_sum, axis, size, bit)
        return after(token, side(axis, bit, 0, token, rows_sum, rows_arrived))

    for index in every:
        (first,) = products(
            True, half_bit, line, starts[index], chunks[index], token, scales, sent_rows, kept_rows, whole
        )
        token, first = after(token, first)
        for parity in (0, 1):
            send(first, 1, parity, index)
        if index == 0 and hops:
            token, rows_sum = hop_rows(token, rows_sum)
    totals, seconds = [], []
    for index in every:
        total, second = products(
            False, half_bit, line, starts[index], chunks[index], token, scales, sent_rows, kept_rows, whole
        )
        token, second = after(token, second)
        if hops:
            token, rows_sum = hop_rows(token, rows_sum)
        totals.append(total)
        seconds.append(second)
        for parity in (0, 1):
            token = resend(token, 2, parity, index)
    while hops:
        token, rows_sum = hop_rows(token, rows_sum)
    new_factor = turn(token, whole)
    token, new_factor = after(token, new_factor)
    rows_arrived = swap(rows_sum, "sub", subs, 1)
    shape = jax.ShapeDtypeStruct(rows_sum.shape, F32)
    token, rows_sum = after(token, call(plus_kernel, "plus", shape, token, rows_sum, rows_arrived))
    bits = [1 << i for i in range((genes - 1).bit_length())]
    for phase in range(3, cells):
        for index in every:
            for parity in (0, 1):
                token = resend(token, phase, parity, index)
                if bits:
                    token, rows_sum = side_rows(token, rows_sum, "gene", genes, bits.pop(0))
    data_products = None
    last = cells - 1
    for index in every:
        parts = [arrived[last, 0, index]] + (last_part if index == every[-1] else [])
        skip = 0
        for part in parts:
            data_products = keep(
                block, starts[index], skip, token, totals[index],
                part, arrived[last, 1, index], data_products,
            )
            token, data_products = after(token, data_products)
            skip += part.shape[1]
    return (new_factor, rows_sum, data_products)


def solution(mesh):
    sizes = (mesh.shape["cell"], mesh.shape["gene"], mesh.shape["sub"])
    return jax.shard_map(
        functools.partial(shards, sizes),
        mesh=mesh,
        in_specs=(
            P(("groups", "cell"), ("gene", "sub")),
            P(("groups", "cell"), ("gene", "sub")),
            P(("groups", "cell"), ("gene", "sub")),
            P("groups", ("gene", "sub")),
            P(("groups", "cell"), None),
        ),
        out_specs=(
            P(("groups", "cell"), None),
            P("groups", None),
            P(("groups", "gene", "sub", "cell"), None),
        ),
        check_vma=False,
    )
```

```python
import functools

import jax
import jax.numpy as jnp
import numpy as np
from jax import lax
from jax.experimental import pallas as pl
from jax.experimental.pallas import tpu as pltpu
from jax.sharding import PartitionSpec as P

ITERS = 3
F32 = jnp.float32
BF16 = jnp.bfloat16
MIB = 1024 * 1024


def params(limit=16):
    return pltpu.CompilerParams(vmem_limit_bytes=limit * MIB)


def away(value):
    return pltpu.with_memory_space_constraint(value, pltpu.HBM)


def held(value):
    return pltpu.with_memory_space_constraint(value, pltpu.VMEM)


def cost(flops, bytes_accessed):
    return pl.CostEstimate(flops=flops, bytes_accessed=bytes_accessed, transcendentals=0)


def contract_last(left, right):
    return lax.dot_general(
        left, right, (((1,), (1,)), ((), ())), preferred_element_type=F32
    )


def row_copies(source, target, first, sems):
    rows = target.shape[0]
    piece = max(rows // sems.shape[0], 16)
    return [
        pltpu.make_async_copy(
            source.at[pl.ds(first + i * piece, piece)],
            target.at[pl.ds(i * piece, piece)],
            sems.at[i],
        )
        for i in range(rows // piece)
    ]


def pieces_of(rows, bit, kept):
    core = lax.axis_index("sub")
    upper = ((lax.axis_index("gene") & bit) != 0) == kept
    half, quarter = rows // 2, rows // 4
    place = jnp.where(upper, quarter, 0)
    return [
        pl.multiple_of((1 - core) * half + place, quarter),
        pl.multiple_of(core * half + place, quarter),
    ]


def piece_copies(bit, kept, counts, target, sems):
    quarter = counts.shape[0] // 4
    copies = []
    for i, place in enumerate(pieces_of(counts.shape[0], bit, kept)):
        copies += row_copies(
            counts, target.at[i * quarter : (i + 1) * quarter], place, sems.at[i * 4 : i * 4 + 4]
        )
    return copies


def load_kernel(
    bit, genes, counts, tile_mask, tile_counts, gram, scales, turned, first,
    genes_here, mask_here, counts_here, gene_sems, row_sems, small_sems,
):
    small_copies = [
        pltpu.make_async_copy(tile_mask, mask_here, small_sems.at[0]),
        pltpu.make_async_copy(tile_counts, counts_here, small_sems.at[1]),
    ]
    gene_copies = row_copies(genes, genes_here, 0, gene_sems)
    row_starts = piece_copies(bit, False, counts, first, row_sems)
    for copy in gene_copies + small_copies:
        copy.start()
    for copy in small_copies:
        copy.wait()
    ratio = mask_here[...].astype(F32) / counts_here[...].astype(F32)
    columns = genes.shape[1]
    tile = columns // ratio.shape[1]
    for row in range(ratio.shape[0]):
        for col in range(ratio.shape[1]):
            scales[row * 8 : row * 8 + 8, col * tile : (col + 1) * tile] = jnp.broadcast_to(
                ratio[row : row + 1, col : col + 1], (8, tile)
            )
    for copy in gene_copies:
        copy.wait()
    for copy in row_starts:
        copy.start()
    wide = min(1024, columns)
    gram[...] = jnp.zeros_like(gram)

    @pl.loop(0, columns // wide)
    def _(step):
        at = pl.ds(pl.multiple_of(step * wide, wide), wide)
        piece = genes_here[:, at]
        turned[at, :] = piece.T
        gram[...] += jnp.dot(piece, turned[at, :], preferred_element_type=F32)

    for copy in row_starts:
        copy.wait()


def load(bit, genes, counts, tile_mask, tile_counts):
    width, columns = genes.shape
    rows = counts.shape[0]
    here = pl.BlockSpec(memory_space=pltpu.VMEM)
    there = pl.BlockSpec(memory_space=pltpu.HBM)
    return pl.pallas_call(
        functools.partial(load_kernel, bit),
        out_shape=(
            jax.ShapeDtypeStruct((width, width), F32),
            jax.ShapeDtypeStruct((tile_mask.shape[0] * 8, columns), F32),
            pltpu.VMEM((columns, width), BF16),
            pltpu.VMEM((rows // 2, columns), BF16),
        ),
        in_specs=[there] * 4,
        out_specs=(here,) * 4,
        scratch_shapes=[
            pltpu.VMEM((width, columns), BF16),
            pltpu.VMEM(tile_mask.shape, jnp.int32),
            pltpu.VMEM(tile_mask.shape, jnp.int32),
            pltpu.SemaphoreType.DMA((4,)),
            pltpu.SemaphoreType.DMA((8,)),
            pltpu.SemaphoreType.DMA((2,)),
        ],
        compiler_params=params(),
        cost_estimate=cost(1, 1),
        name="load",
    )(away(genes), away(counts), away(tile_mask), away(tile_counts))


def scaled(counts, at, row_tiles, scales):
    tile = counts.shape[0] // len(row_tiles)
    return jnp.concatenate(
        [
            (
                counts[i * tile : (i + 1) * tile, at].astype(F32)
                * scales[pl.ds(pl.multiple_of(row * 8, 8), 8), at][0:1]
            ).astype(BF16)
            for i, row in enumerate(row_tiles)
        ],
        axis=0,
    )


def cross_rows(row_tiles, scales, counts, turned, total):
    columns = counts.shape[1]
    wide = min(4096, columns)
    total[...] = jnp.zeros_like(total)

    @pl.loop(0, columns // wide)
    def _(step):
        at = pl.ds(pl.multiple_of(step * wide, wide), wide)
        total[...] += jnp.dot(
            scaled(counts, at, row_tiles, scales), turned[at, :], preferred_element_type=F32
        )


def tiles_of(bit, kept, rows, tile):
    quarter = rows // 4
    return [
        place // tile + i
        for place in pieces_of(rows, bit, kept)
        for i in range(quarter // tile)
    ]


def cross_kernel(bit, kept, rows, scales, held_rows, turned, *refs):
    (low, high, mine), total = refs[-5:-2] if kept else refs[1:4], refs[-2]
    if not kept:
        copies = piece_copies(bit, True, refs[0], refs[4], refs[-1])
        for copy in copies:
            copy.start()
    quarter, tile = rows // 4, rows // (scales.shape[0] // 8)
    cross_rows(tiles_of(bit, kept, rows, tile), scales, held_rows, turned, total)
    low[...] = total[: quarter // 2].T
    high[...] = total[quarter // 2 : quarter].T
    mine[...] = total[quarter:].T
    if not kept:
        for copy in copies:
            copy.wait()


def cross(bit, kept, scales, held_rows, turned, counts):
    rows, columns = counts.shape
    width = turned.shape[1]
    here = pl.BlockSpec(memory_space=pltpu.VMEM)
    piece = jax.ShapeDtypeStruct((width, rows // 4), F32)
    small_piece = jax.ShapeDtypeStruct((width, rows // 8), F32)
    out_shape = (small_piece, small_piece, piece)
    in_specs, args = [here] * 3, [scales, held(held_rows), held(turned)]
    if not kept:
        out_shape += (pltpu.VMEM((rows // 2, columns), BF16),)
        in_specs.append(pl.BlockSpec(memory_space=pltpu.HBM))
        args.append(away(counts))
    return pl.pallas_call(
        functools.partial(cross_kernel, bit, kept, rows),
        out_shape=out_shape,
        in_specs=in_specs,
        out_specs=(here,) * len(out_shape),
        scratch_shapes=[pltpu.VMEM((rows // 2, width), F32), pltpu.SemaphoreType.DMA((8,))],
        compiler_params=params(),
        cost_estimate=cost(1, 1),
        name="cross_kept" if kept else "cross_sent",
    )(*args)


def plus_pieces_kernel(left, low, high, out):
    half = low.shape[1]
    out[:, :half] = left[:, :half] + low[...]
    out[:, half:] = left[:, half:] + high[...]


def call(kernel, name, out_shape, token, *args, scratch=(), aliases=None, out=None):
    here = pl.BlockSpec(memory_space=pltpu.VMEM)
    wherever = pl.BlockSpec(memory_space=pl.ANY)
    single = not isinstance(out_shape, tuple)
    specs = [here] * len(args)
    if aliases:
        specs[-1] = wherever
    out = out or here
    return pl.pallas_call(
        lambda token, *refs: kernel(*refs),
        out_shape=out_shape,
        in_specs=[wherever] + specs,
        out_specs=out if single else (out,) * len(out_shape),
        scratch_shapes=list(scratch),
        input_output_aliases=aliases or {},
        compiler_params=params(),
        cost_estimate=cost(1, 1),
        name=name,
    )(token, *args)


def fold_kernel(axis, bit, left, right, kept, sent):
    half = kept.shape[1]
    upper = (lax.axis_index(axis) & bit) != 0

    @pl.when(upper)
    def _():
        kept[...] = left[:, half:] + right[:, half:]
        sent[...] = left[:, :half] + right[:, :half]

    @pl.when(jnp.logical_not(upper))
    def _():
        kept[...] = left[:, :half] + right[:, :half]
        sent[...] = left[:, half:] + right[:, half:]


def half_sum_kernel(axis, left, right, out):
    half = out.shape[1]
    upper = lax.axis_index(axis) != 0

    @pl.when(upper)
    def _():
        out[...] = left[:, half:] + right[:, half:]

    @pl.when(jnp.logical_not(upper))
    def _():
        out[...] = left[:, :half] + right[:, :half]


def fold(axis, bit, token, left, right):
    shape = jax.ShapeDtypeStruct((left.shape[0], left.shape[1] // 2), F32)
    return call(
        functools.partial(fold_kernel, axis, bit), "fold", (shape, shape), token, left, right
    )


def side_kernel(axis, bit, dim, mine, theirs, out):
    size = mine.shape[dim]
    low = (slice(None),) * dim + (slice(0, size),)
    high = (slice(None),) * dim + (slice(size, 2 * size),)
    upper = (lax.axis_index(axis) & bit) != 0

    @pl.when(upper)
    def _():
        out[low], out[high] = theirs[...], mine[...]

    @pl.when(jnp.logical_not(upper))
    def _():
        out[low], out[high] = mine[...], theirs[...]


def side(axis, bit, dim, token, mine, theirs):
    shape = list(mine.shape)
    shape[dim] *= 2
    return call(
        functools.partial(side_kernel, axis, bit, dim),
        "side", jax.ShapeDtypeStruct(tuple(shape), mine.dtype), token, mine, theirs,
    )


def halves(value):
    high = value.astype(BF16)
    return high, (value - high.astype(F32)).astype(BF16)


def product3(left, right):
    left_high, left_low = left
    right_high, right_low = right
    dot = functools.partial(jnp.dot, preferred_element_type=F32)
    return dot(left_high, right_high) + (
        dot(left_high, right_low) + dot(left_low, right_high)
    )


def inverse_kernel(gram_in, inverse, rho_out):
    gram = gram_in[...]
    width = gram.shape[0]
    shape = (width, width)
    diagonal = lax.broadcasted_iota(jnp.int32, shape, 0) == lax.broadcasted_iota(
        jnp.int32, shape, 1
    )
    eye = jnp.where(diagonal, 1.0, 0.0).astype(F32)
    rho = jnp.sum(gram * eye) / width
    rho_out[...] = jnp.full(rho_out.shape, rho, F32)
    scale = 1.0 / jnp.full((1, 1), rho, F32)
    matrix = gram * scale + eye
    low = 2.0 / (width + 2.0)
    guess = low * eye
    image = low * matrix
    first = True
    while True:
        low = low * (2.0 - low)
        gain = 2.0 / (1.0 + low)
        low = gain * low
        done = 1.0 - low < 2e-3
        step = halves(gain * (2.0 * eye - image))
        if first:
            guess = guess[0:1, 0:1] * (gain * (2.0 * eye - image))
        else:
            guess = product3(halves(guess), step)
        first = False
        if done:
            break
        image = product3(halves(image), step)
    rest = eye - jnp.dot(
        matrix, guess, preferred_element_type=F32, precision=lax.Precision.HIGHEST
    )
    rest_halves = halves(rest)
    series = rest + product3(rest_halves, rest_halves)
    inverse[...] = (guess + product3(halves(guess), halves(series))) * scale


def shifted_inverse(gram):
    width = gram.shape[0]
    whole = pl.BlockSpec(memory_space=pltpu.VMEM)
    return pl.pallas_call(
        inverse_kernel,
        out_shape=(
            jax.ShapeDtypeStruct((width, width), F32),
            jax.ShapeDtypeStruct((8, 128), F32),
        ),
        in_specs=[whole],
        out_specs=(whole, whole),
        compiler_params=params(),
        cost_estimate=cost(1, 1),
        name="inverse",
    )(gram)


def admm_kernel(genes, rho_block, cross_a, cross_b, inverse, start, columns_out):
    rows = cross_a.shape[1]
    place = lax.axis_index("sub") * genes + lax.axis_index("gene")
    rho = rho_block[0:1, 0:1]
    cross = cross_a[...] + cross_b[...]
    inverse_halves = halves(inverse[...])
    zvalue = start[pl.ds(pl.multiple_of(place * rows, rows), rows), :].astype(F32).T
    uvalue = jnp.zeros_like(zvalue)
    for _ in range(ITERS):
        vvalue = product3(inverse_halves, halves(cross + rho * (zvalue - uvalue)))
        zvalue = jnp.maximum(vvalue + uvalue, 0.0)
        uvalue = uvalue + vvalue - zvalue
    columns_out[...] = zvalue.astype(BF16)


def products_kernel(tile, bit, line, start, chunk, scales, sent, kept, columns, *outs):
    only_first = len(outs) == 1
    block = line.block(1 if only_first else 2, 0)
    size = kept.shape[1] // line.size
    span = min(tile, chunk)
    wide = 2 * span if chunk % (2 * span) == 0 else span
    steps = chunk // wide
    rows = columns.shape[1]
    quarter = rows // 4
    groups = [(sent, False), (kept, True)]

    @pl.loop(0, steps if only_first else line.size * steps)
    def _(turn):
        order, step = (block, turn) if only_first else (turn // steps, lax.rem(turn, steps))
        genes = pl.ds(pl.multiple_of(order * size + start + step * wide, span), wide)
        total = None
        for counts, stays in groups:
            cells = [columns[:, pl.ds(at, quarter)] for at in pieces_of(rows, bit, stays)]
            part = jnp.dot(
                jnp.concatenate(cells, axis=1),
                scaled(counts, genes, tiles_of(bit, stays, rows, tile), scales),
                preferred_element_type=F32,
            )
            total = part if total is None else total + part
        total = total.astype(BF16)
        at = pl.ds(pl.multiple_of(step * wide, span), wide)
        if only_first:
            outs[0][:, at] = total
        else:
            outs[0][order, :, at] = total

            @pl.when(order == block)
            def _():
                outs[1][:, at] = total


def products(only_first, bit, line, start, chunk, token, scales, sent, kept, columns):
    width, rows = columns.shape
    tile = rows // (scales.shape[0] // 8)
    out_shape = (jax.ShapeDtypeStruct((width, chunk), BF16),)
    if not only_first:
        out_shape = (jax.ShapeDtypeStruct((line.size, width, chunk), BF16),) + out_shape
    return call(
        functools.partial(products_kernel, tile, bit, line, start, chunk),
        "products", out_shape, token, scales, held(sent), held(kept), columns,
    )


def turn_kernel(value, out):
    out[...] = value[...].astype(F32).T.astype(out.dtype)


def turn(token, value):
    shape = jax.ShapeDtypeStruct(value.shape[::-1], value.dtype)
    return call(turn_kernel, "turn", shape, token, value)


def row_share_kernel(columns, out):
    part = out.shape[0]
    place = lax.axis_index("gene")
    share = columns[pl.ds(pl.multiple_of(place * part, part), part), :]
    out[...] = contract_last(share, columns[...]).astype(out.dtype)


def row_share(part, token, columns):
    shape = jax.ShapeDtypeStruct((part, columns.shape[0]), BF16)
    return call(row_share_kernel, "row_share", shape, token, columns)


def plus_kernel(left, right, out):
    out[...] = (left[...].astype(F32) + right[...].astype(F32)).astype(out.dtype)


def hop_kernel(kind, targets, own, arrived, out):
    cell = lax.axis_index("cell")
    reached = cell == targets[0]
    for target in targets[1:]:
        reached = jnp.logical_or(reached, cell == target)
    more = arrived[...].astype(F32)
    base = own[...].astype(F32)
    value = base + more if kind == "sum" else more
    out[...] = jnp.where(reached, value, base).astype(out.dtype)


def hop(kind, targets, token, own, arrived):
    shape = jax.ShapeDtypeStruct(own.shape, own.dtype)
    return call(functools.partial(hop_kernel, kind, targets), "hop", shape, token, own, arrived)


def operand_kernel(line, phase, parity, total, before, *outs):
    own = total.at[line.block(phase, parity)]
    start = 0
    for out in outs:
        at = slice(start, start + out.shape[1])
        out[...] = (own[:, at].astype(F32) + before[:, at].astype(F32)).astype(BF16)
        start += out.shape[1]


def operand(line, phase, parity, parts, token, total, before):
    width = before.shape[0]
    return call(
        functools.partial(operand_kernel, line, phase, parity),
        "operand", tuple(jax.ShapeDtypeStruct((width, part), BF16) for part in parts),
        token, total, before,
    )


def keep_kernel(start, skip, total, first, second, *refs):
    out, turned, sems = refs[-3:]
    pieces = sems.shape[0]
    wide = first.shape[1] // pieces
    own = total.at[lax.axis_index("cell")]
    copies = []
    for piece in range(pieces):
        at = slice(piece * wide, (piece + 1) * wide)
        there = slice(skip + piece * wide, skip + (piece + 1) * wide)
        value = first[:, at].astype(F32) + second[:, there].astype(F32)
        turned[at] = (own[:, there].astype(F32) + value).T
        copies.append(
            pltpu.make_async_copy(
                turned.at[at], out.at[pl.ds(start + skip + piece * wide, wide)], sems.at[piece]
            )
        )
        copies[-1].start()
    for copy in copies:
        copy.wait()


def keep(block, start, skip, token, total, first, second, out):
    width, chunk = first.shape
    pieces = max(1, chunk // 256)
    return call(
        functools.partial(keep_kernel, start, skip),
        "keep", jax.ShapeDtypeStruct((block, width), F32), token,
        total, first, second, *([] if out is None else [out]),
        scratch=[pltpu.VMEM((chunk, width), F32), pltpu.SemaphoreType.DMA((pieces,))],
        aliases=None if out is None else {4: 0},
        out=pl.BlockSpec(memory_space=pl.ANY),
    )


class Line:
    def __init__(self, size):
        self.size = size

    def pairs(self, phase, parity, exchange=False):
        links = range(parity, self.size - 1, 2)
        right = [(i, i + 1) for i in links if i < phase]
        left = [(i + 1, i) for i in links if i + 1 >= self.size - phase]
        pairs = right + left
        if exchange:
            pairs = sorted(set(pairs) | {(b, a) for a, b in pairs})
        return pairs

    def block(self, phase, parity):
        cell = lax.axis_index("cell")
        to_right = (cell & 1) == parity
        block = cell + jnp.where(to_right, self.size - phase, phase)
        return jnp.where(block >= self.size, block - self.size, block)

    def send(self, value, phase, parity):
        return lax.ppermute(value, "cell", self.pairs(phase, parity))


def swap(value, axis, size, step):
    return lax.ppermute(value, axis, [(i, i ^ step) for i in range(size)])


def pair_sums(value, axis, size, event):
    step = 1
    while step < size:
        arrived, event = after(swap(value, axis, size, step), event)
        value = value + arrived
        step *= 2
    return value, event


def after(value, event):
    return lax.optimization_barrier((value, event))


def chunk_sizes(block):
    return [block // 2, block // 2] if block % 1024 == 0 else [block]


def shards(sizes, counts, tile_mask, tile_counts, gene_factor, prev_factor):
    cells, genes, subs = sizes
    rows, columns = counts.shape
    width = gene_factor.shape[0]
    line = Line(cells)

    half_bit = bit = genes // 2
    gram, scales, turned, sent_rows = load(bit, gene_factor, counts, tile_mask, tile_counts)
    token = scales
    piece = jax.ShapeDtypeStruct((width, rows // 4), F32)
    gram_other = swap(gram, "sub", subs, 1)
    low, high, mine, kept_rows = cross(bit, False, scales, sent_rows, turned, counts)
    low, high = [swap(value, "sub", subs, 1) for value in (low, high)]
    token_sent, mine = after(token, mine)
    half = jax.ShapeDtypeStruct((width, width // 2), F32)
    gram_half = call(
        functools.partial(half_sum_kernel, "sub"), "half_sum", half, token_sent, gram, gram_other
    )
    token_sent, gram_half = after(token, gram_half)
    sent = call(plus_pieces_kernel, "plus", piece, token_sent, mine, low, high)
    cross_b = swap(sent, "gene", genes, bit)
    scales_late, _ = after(scales, sent)
    low, high, mine = cross(bit, True, scales_late, kept_rows, turned, counts)
    low, high = [swap(value, "sub", subs, 1) for value in (low, high)]
    gram_half, (mine, _) = pair_sums(gram_half, "gene", genes, (mine, scales))
    gram = side("sub", 1, 1, token, gram_half, swap(gram_half, "sub", subs, 1))
    inverse, rho = shifted_inverse(gram)
    token_late, inverse = after(token, inverse)
    cross_a = call(plus_pieces_kernel, "plus", piece, token_late, mine, low, high)
    bit //= 2
    while bit:
        cross_a, sent = fold("gene", bit, token, cross_a, cross_b)
        cross_b = swap(sent, "gene", genes, bit)
        bit //= 2
    share = jax.ShapeDtypeStruct((width, rows // (genes * subs)), BF16)
    columns_held = call(
        functools.partial(admm_kernel, genes),
        "admm", share, token, rho, cross_a, cross_b, inverse, prev_factor,
    )
    bit = 1
    while bit < genes:
        columns_arrived = swap(columns_held, "gene", genes, bit)
        columns_held = side("gene", bit, 1, token, columns_held, columns_arrived)
        bit *= 2
    token, rows_sum = after(token, row_share(width // genes, token, columns_held))
    columns_arrived = swap(columns_held, "sub", subs, 1)
    whole = side("sub", 1, 1, token, columns_held, columns_arrived)

    block = columns // cells
    chunks = chunk_sizes(block)
    starts = [sum(chunks[:i]) for i in range(len(chunks))]
    every = range(len(chunks))

    arrived = {}
    last_part = []

    def send(value, phase, parity, index):
        pairs = line.pairs(phase, parity, exchange=phase == 1 and index == 0)
        arrived[phase, parity, index] = lax.ppermute(value, "cell", pairs) if pairs else None

    def resend(token, phase, parity, index):
        before = arrived[phase - 1, 1 - parity, index]
        if before is None:
            value = seconds[index]
        else:
            chunk = chunks[index]
            parts = (chunk,)
            if phase == cells - 1 and parity == 0 and index == every[-1] and chunk >= 1024:
                parts = (chunk // 4 * 3, chunk // 4)
            values = operand(line, phase, parity, parts, token, totals[index], before)
            token, values = after(token, values)
            value, rest = values[0], values[1:]
            for part in rest:
                last_part.append(lax.ppermute(part, "cell", line.pairs(phase, parity)))
        send(value, phase, parity, index)
        return token

    middle = cells // 2
    inward = [[(i, i + 1), (cells - 1 - i, cells - 2 - i)] for i in range(middle - 1)]
    outward = [[(b, a) for a, b in pairs] for pairs in reversed(inward)]
    hops = [("sum", p) for p in inward] + [("sum", [(middle - 1, middle), (middle, middle - 1)])]
    hops += [("copy", p) for p in outward]

    def hop_rows(token, rows_sum):
        kind, pairs = hops.pop(0)
        both = sorted(set(pairs) | {(b, a) for a, b in pairs})
        rows_arrived = lax.ppermute(rows_sum, "cell", both)
        targets = [b for _, b in pairs]
        return after(token, hop(kind, targets, token, rows_sum, rows_arrived))

    def side_rows(token, rows_sum, axis, size, bit):
        rows_arrived = swap(rows_sum, axis, size, bit)
        return after(token, side(axis, bit, 0, token, rows_sum, rows_arrived))

    for index in every:
        (first,) = products(
            True, half_bit, line, starts[index], chunks[index], token, scales, sent_rows, kept_rows, whole
        )
        token, first = after(token, first)
        for parity in (0, 1):
            send(first, 1, parity, index)
        if index == 0 and hops:
            token, rows_sum = hop_rows(token, rows_sum)
    totals, seconds = [], []
    for index in every:
        total, second = products(
            False, half_bit, line, starts[index], chunks[index], token, scales, sent_rows, kept_rows, whole
        )
        token, second = after(token, second)
        if hops:
            token, rows_sum = hop_rows(token, rows_sum)
        totals.append(total)
        seconds.append(second)
        for parity in (0, 1):
            token = resend(token, 2, parity, index)
    while hops:
        token, rows_sum = hop_rows(token, rows_sum)
    new_factor = turn(token, whole)
    token, new_factor = after(token, new_factor)
    rows_arrived = swap(rows_sum, "sub", subs, 1)
    shape = jax.ShapeDtypeStruct(rows_sum.shape, F32)
    token, rows_sum = after(token, call(plus_kernel, "plus", shape, token, rows_sum, rows_arrived))
    bits = [1 << i for i in range((genes - 1).bit_length())]
    for phase in range(3, cells):
        for index in every:
            for parity in (0, 1):
                token = resend(token, phase, parity, index)
                if bits:
                    token, rows_sum = side_rows(token, rows_sum, "gene", genes, bits.pop(0))
    data_products = None
    last = cells - 1
    for index in every:
        parts = [arrived[last, 0, index]] + (last_part if index == every[-1] else [])
        skip = 0
        for part in parts:
            data_products = keep(
                block, starts[index], skip, token, totals[index],
                part, arrived[last, 1, index], data_products,
            )
            token, data_products = after(token, data_products)
            skip += part.shape[1]
    return (new_factor, rows_sum, data_products)


def solution(mesh):
    sizes = (mesh.shape["cell"], mesh.shape["gene"], mesh.shape["sub"])
    return jax.shard_map(
        functools.partial(shards, sizes),
        mesh=mesh,
        in_specs=(
            P(("groups", "cell"), ("gene", "sub")),
            P(("groups", "cell"), ("gene", "sub")),
            P(("groups", "cell"), ("gene", "sub")),
            P("groups", ("gene", "sub")),
            P(("groups", "cell"), None),
        ),
        out_specs=(
            P(("groups", "cell"), None),
            P("groups", None),
            P(("groups", "gene", "sub", "cell"), None),
        ),
        check_vma=False,
    )
```
